32 devices in a mesh: seq: 8 (over z, y), head: 4 (over x, core).
Axes of the slice: x: 2, y: 2, z: 4, core: 2. Of those that a mesh axis runs over, the one named last changes fastest.
Arguments:
- tokens: bfloat16 [2048, 2048], P('seq'), may hold values from -6 to 6
- attn_gain: bfloat16 [2048], P('seq'), may hold values from 0.5 to 1.5
- query_weight: bfloat16 [2048, 2048], P('seq', 'head'), may hold values from -0.15625 to 0.15625
- key_weight: bfloat16 [2048, 2048], P('seq', 'head'), may hold values from -0.15625 to 0.15625
- value_weight: bfloat16 [2048, 2048], P('seq', 'head'), may hold values from -0.125 to 0.125
- out_weight: bfloat16 [2048, 2048], P('head', 'seq'), may hold values from -1.796875 to 1.796875
- mlp_gain: bfloat16 [2048], P('seq'), may hold values from 0.5 to 1.5
- gate_weight: bfloat16 [2048, 8192], P('seq', 'head'), may hold values from -0.125 to 0.125
- up_weight: bfloat16 [2048, 8192], P('seq', 'head'), may hold values from -0.125 to 0.125
- down_weight: bfloat16 [8192, 2048], P('head', 'seq'), may hold values from -0.0625 to 0.0625
- cotangent: bfloat16 [2048, 2048], P('seq'), may hold values from -6 to 6
Outputs:
- output: bfloat16 [2048, 2048], P('seq')
- input_grad: bfloat16 [2048, 2048], P('seq')
- attn_gain_grad: float32 [2048], P('seq')
- query_weight_grad: float32 [2048, 2048], P('seq', 'head')
- key_weight_grad: float32 [2048, 2048], P('seq', 'head')
- value_weight_grad: float32 [2048, 2048], P('seq', 'head')
- out_weight_grad: float32 [2048, 2048], P('head', 'seq')
- mlp_gain_grad: float32 [2048], P('seq')
- gate_weight_grad: float32 [2048, 8192], P('seq', 'head')
- up_weight_grad: float32 [2048, 8192], P('seq', 'head')
- down_weight_grad: float32 [8192, 2048], P('head', 'seq')
The draws below stay inside these ranges and needn't reach their ends.
All inputs are finite; a program needn't handle non-finite values.
Results may differ from the reference program's by a relative error of at most 0.015.
Values may be sent and summed in bfloat16 or wider, within the bound.
A program may use at most 192 MiB of HBM per device.

```python
import math
import jax
import jax.numpy as jnp
from jax import lax

D = 2048
HEADS = 16
HD = 128
FF = 8192
TOKENS = 2048


def level_of(stream_key, extent, split, low, high):
    loudness = 1.0
    for dim, parts in split:
        draws = jax.random.uniform(jax.random.fold_in(jax.random.fold_in(stream_key, 6), dim), (parts,), jnp.float32, low / len(split), high / len(split))
        loudness = loudness * jnp.repeat(jnp.exp(draws), extent[dim] // parts).reshape((-1,) + (1,) * (len(extent) - 1 - dim))
    return loudness


def centred(own_key, extent, scale, bound, cuts=(), held_as=jnp.bfloat16):
    factor_of = level_of(own_key, extent, cuts, -0.22, 0.18) if cuts else 1.0
    values = jax.random.normal(own_key, extent, jnp.float32) * scale * factor_of
    return jnp.minimum(jnp.maximum(values, -bound), bound).astype(held_as)


def setup_inputs(seed: int = 0) -> dict:
    keys = jax.random.split(jax.random.key(seed), 12)
    tokens = centred(keys[0], (TOKENS, D), 1.0, 6.0, ((0, 8),))
    attn_gain = jnp.clip(1.0 + 0.1 * jax.random.normal(keys[1], (D,), jnp.float32), 0.5, 1.5).astype(jnp.bfloat16)
    query_weight = centred(keys[2], (D, HEADS * HD), (D * 2 // 3) ** -0.5, 0.15625, ((0, 8), (1, 4)))
    key_weight = centred(keys[3], (D, HEADS * HD), (D * 2 // 3) ** -0.5, 0.15625, ((0, 8), (1, 4)))
    value_weight = centred(keys[4], (D, HEADS * HD), D ** -0.5, 0.125, ((0, 8), (1, 4)))
    out_weight = centred(keys[5], (HEADS * HD, D), 0.3, 1.796875, ((0, 4), (1, 8)))
    mlp_gain = jnp.clip(1.0 + 0.1 * jax.random.normal(keys[6], (D,), jnp.float32), 0.5, 1.5).astype(jnp.bfloat16)
    gate_weight = centred(keys[7], (D, FF), D ** -0.5, 0.125, ((0, 8), (1, 4)))
    up_weight = centred(keys[8], (D, FF), D ** -0.5, 0.125, ((0, 8), (1, 4)))
    down_weight = centred(keys[9], (FF, D), FF ** -0.5, 0.0625, ((0, 4), (1, 8)))
    cotangent = centred(keys[10], (TOKENS, D), 1.0, 6.0, ((0, 8),))
    return dict(tokens=tokens, attn_gain=attn_gain, query_weight=query_weight, key_weight=key_weight, value_weight=value_weight, out_weight=out_weight, mlp_gain=mlp_gain, gate_weight=gate_weight, up_weight=up_weight, down_weight=down_weight, cotangent=cotangent)


epsilon = 1e-05
block_limit = 512

@jax.custom_vjp
def low(v):
    return lax.optimization_barrier(v.astype(jnp.bfloat16)).astype(jnp.float32)

@jax.custom_vjp
def low_back(v):
    return v

def low_keep(v):
    return (low(v), None)

def low_pass(kept, grad):
    return (grad,)

def back_keep(v):
    return (v, None)

def back_low(kept, grad):
    return (low(grad),)
low.defvjp(low_keep, low_pass)
low_back.defvjp(back_keep, back_low)

def tables(offset, length, half_width):
    places = (offset + jnp.arange(length, dtype=jnp.int32)).astype(jnp.float32)
    frequency = jnp.exp(jnp.arange(half_width, dtype=jnp.float32) * (-math.log(10000.0) / half_width))
    angles = places[:, None] * frequency[None, :]
    return (jnp.cos(angles)[:, None, :], jnp.sin(angles)[:, None, :])

def rotary(values, cos_table, sin_table):
    half_width = values.shape[-1] // 2
    front = values[..., :half_width]
    back_half = values[..., half_width:]
    return jnp.concatenate([front * cos_table - back_half * sin_table, back_half * cos_table + front * sin_table], axis=-1)

def rms_gain(values, gain_vector):
    return values * lax.rsqrt(lax.optimization_barrier(jnp.mean(values * values, axis=-1, keepdims=True)) + epsilon) * gain_vector

def forward(token_values, attn_gain, query_weight, key_weight, value_weight, out_weight, mlp_gain, gate_weight, up_weight, down_weight):
    highest = lax.Precision.HIGHEST
    normed_one = low(rms_gain(token_values, attn_gain))
    query_pre = low_back(jnp.dot(normed_one, query_weight, precision=highest))
    key_pre = low_back(jnp.dot(normed_one, key_weight, precision=highest))
    value_rows = low(low_back(jnp.dot(normed_one, value_weight, precision=highest))).reshape(TOKENS, HEADS, HD)
    cos_table, sin_table = tables(0, TOKENS, HD // 2)
    query_rows = low(rotary(query_pre.reshape(TOKENS, HEADS, HD), cos_table, sin_table))
    key_rows = low(rotary(key_pre.reshape(TOKENS, HEADS, HD), cos_table, sin_table))
    score_scale = 1.0 / math.sqrt(HD)
    score_shift = math.log(TOKENS)
    block_rows = math.gcd(TOKENS, block_limit)
    block_count = TOKENS // block_rows
    key_places = jnp.arange(TOKENS, dtype=jnp.int32)

    @jax.checkpoint
    def attend(query_block, block_start):
        scores = low_back(jnp.einsum('qhd,khd->hqk', query_block, key_rows, precision=highest) * score_scale - score_shift)
        query_places = block_start + jnp.arange(block_rows, dtype=jnp.int32)
        visible = key_places[None, :] <= query_places[:, None]
        weights = jnp.where(visible[None], jax.nn.sigmoid(scores), 0.0)
        return jnp.einsum('hqk,khd->qhd', low(weights), value_rows, precision=highest)

    def attend_item(packed):
        return attend(packed[0], packed[1])
    starts = jnp.arange(block_count, dtype=jnp.int32) * block_rows
    mixed_heads = lax.map(attend_item, (query_rows.reshape(block_count, block_rows, HEADS, HD), starts))
    attn_mix = low(low_back(mixed_heads.reshape(TOKENS, HEADS * HD)))
    hidden = token_values + low_back(jnp.dot(attn_mix, out_weight, precision=highest))
    normed_two = low(rms_gain(hidden, mlp_gain))
    gate_pre = low_back(jnp.dot(normed_two, gate_weight, precision=highest))
    up_pre = low_back(jnp.dot(normed_two, up_weight, precision=highest))
    mixed = low(jax.nn.silu(gate_pre) * up_pre)
    return hidden + low_back(jnp.dot(mixed, down_weight, precision=highest))

def reference(tokens, attn_gain, query_weight, key_weight, value_weight, out_weight, mlp_gain, gate_weight, up_weight, down_weight, cotangent):
    primals = tuple((operand.astype(jnp.float32) for operand in (tokens, attn_gain, query_weight, key_weight, value_weight, out_weight, mlp_gain, gate_weight, up_weight, down_weight)))
    output, pullback = jax.vjp(forward, *primals)
    gradients = pullback(cotangent.astype(jnp.float32))
    return (output.astype(jnp.bfloat16), gradients[0].astype(jnp.bfloat16), gradients[1], gradients[2], gradients[3], gradients[4], gradients[5], gradients[6], gradients[7], gradients[8], gradients[9])
```

```python
import functools
import math

import jax
import jax.numpy as jnp
from jax import lax
from jax.experimental import pallas as pl
from jax.experimental.pallas import tpu as pltpu
from jax.sharding import PartitionSpec as P

MESH = pl.DeviceIdType.MESH
F32, BF16 = jnp.float32, jnp.bfloat16

HD = 128


epsilon = 1e-05
block_limit = 512


def tables(offset, length, half_width):
    places = (offset + jnp.arange(length, dtype=jnp.int32)).astype(jnp.float32)
    frequency = jnp.exp(
        jnp.arange(half_width, dtype=jnp.float32) * (-math.log(10000.0) / half_width)
    )
    angles = places[:, None] * frequency[None, :]
    return (jnp.cos(angles)[:, None, :], jnp.sin(angles)[:, None, :])


def rotary(values, cos_table, sin_table):
    half_width = values.shape[-1] // 2
    front = values[..., :half_width]
    back_half = values[..., half_width:]
    return jnp.concatenate(
        [front * cos_table - back_half * sin_table, back_half * cos_table + front * sin_table],
        axis=-1,
    )


def unrotary(gradient, cos_table, sin_table):
    half_width = gradient.shape[-1] // 2
    front = gradient[..., :half_width]
    back_half = gradient[..., half_width:]
    return jnp.concatenate(
        [front * cos_table + back_half * sin_table, back_half * cos_table - front * sin_table],
        axis=-1,
    )


def norm_back(values, inverse, gain_vector, upstream):
    scaled = upstream * gain_vector
    gain_grad = jnp.sum(upstream * values * inverse, axis=0)
    value_grad = inverse * scaled - values * inverse**3 * jnp.mean(
        scaled * values, axis=1, keepdims=True
    )
    return (value_grad, gain_grad)


def gathered_weights(
    tokens,
    attn_gain,
    query_weight,
    key_weight,
    value_weight,
    out_weight,
    mlp_gain,
    gate_weight,
    up_weight,
    down_weight,
    cotangent,
):
    row_count = tokens.shape[0]
    total_rows = row_count * lax.axis_size("seq")
    row_start = lax.axis_index("seq") * row_count
    local_width = query_weight.shape[1]
    local_heads = local_width // HD
    score_scale = 1.0 / math.sqrt(HD)
    score_shift = math.log(total_rows)
    block_rows = math.gcd(total_rows, block_limit)
    block_count = total_rows // block_rows
    attn_gain_full, query_full, key_full, value_full, out_full = (
        lax.all_gather(attn_gain, "seq", axis=0, tiled=True),
        lax.all_gather(query_weight, "seq", axis=0, tiled=True),
        lax.all_gather(key_weight, "seq", axis=0, tiled=True),
        lax.all_gather(value_weight, "seq", axis=0, tiled=True),
        lax.all_gather(out_weight, "seq", axis=1, tiled=True),
    )
    mlp_gain_full, gate_full, up_full, down_full = (
        lax.all_gather(mlp_gain, "seq", axis=0, tiled=True),
        lax.all_gather(gate_weight, "seq", axis=0, tiled=True),
        lax.all_gather(up_weight, "seq", axis=0, tiled=True),
        lax.all_gather(down_weight, "seq", axis=1, tiled=True),
    )
    token_values = tokens.astype(jnp.float32)
    inverse_one = lax.rsqrt(jnp.mean(token_values * token_values, axis=1, keepdims=True) + epsilon)
    normed_one = (token_values * inverse_one * attn_gain_full.astype(jnp.float32)).astype(
        jnp.bfloat16
    )
    query_pre = jnp.dot(normed_one, query_full, preferred_element_type=jnp.float32)
    key_pre = jnp.dot(normed_one, key_full, preferred_element_type=jnp.float32)
    value_rows = (
        jnp.dot(normed_one, value_full, preferred_element_type=jnp.float32)
        .astype(jnp.bfloat16)
        .reshape(row_count, local_heads, HD)
    )
    cos_table, sin_table = tables(row_start, row_count, HD // 2)
    query_rows = (
        rotary(query_pre.reshape(row_count, local_heads, HD), cos_table, sin_table)
        .astype(jnp.bfloat16)
        .reshape(row_count, local_width)
    )
    key_rows = rotary(key_pre.reshape(row_count, local_heads, HD), cos_table, sin_table).astype(
        jnp.bfloat16
    )
    all_queries = lax.all_gather(query_rows, "seq", axis=0, tiled=True)
    key_places = row_start + jnp.arange(row_count, dtype=jnp.int32)

    def weights_for(query_block, block_start):
        scores = (
            jnp.einsum("qhd,khd->hqk", query_block, key_rows, preferred_element_type=jnp.float32)
            * score_scale
            - score_shift
        )
        query_places = block_start + jnp.arange(query_block.shape[0], dtype=jnp.int32)
        visible = key_places[None, :] <= query_places[:, None]
        return jnp.where(visible[None], jax.nn.sigmoid(scores), 0.0)

    step_rows = math.gcd(row_count * lax.axis_size("seq"), block_limit)
    step_count = row_count * lax.axis_size("seq") // step_rows
    picked = all_queries.reshape(step_count, step_rows, local_heads, HD)
    starts = jnp.arange(step_count, dtype=jnp.int32) * step_rows

    def one_block(packed):
        query_block, block_start = packed
        weights = weights_for(query_block, block_start).astype(jnp.bfloat16)
        return jnp.einsum(
            "hqk,khd->qhd", weights, value_rows, preferred_element_type=jnp.float32
        ).reshape(step_rows, local_width)

    attn_mix = lax.psum_scatter(
        lax.map(one_block, (picked, starts)).reshape(row_count * lax.axis_size("seq"), local_width),
        "seq",
        scatter_dimension=0,
        tiled=True,
    ).astype(jnp.bfloat16)
    attn_branch = lax.psum(jnp.dot(attn_mix, out_full, preferred_element_type=jnp.float32), "head")
    hidden = token_values + attn_branch
    inverse_two = lax.rsqrt(jnp.mean(hidden * hidden, axis=1, keepdims=True) + epsilon)
    normed_two = (hidden * inverse_two * mlp_gain_full.astype(jnp.float32)).astype(jnp.bfloat16)
    gate_pre = jnp.dot(normed_two, gate_full, preferred_element_type=jnp.float32)
    up_pre = jnp.dot(normed_two, up_full, preferred_element_type=jnp.float32)
    gate_act = jax.nn.silu(gate_pre)
    mixed = (gate_act * up_pre).astype(jnp.bfloat16)
    mlp_branch = lax.psum(
        jnp.dot(mixed, down_full, preferred_element_type=jnp.float32).astype(jnp.bfloat16), "head"
    ).astype(jnp.float32)
    result = (hidden + mlp_branch).astype(jnp.bfloat16)
    kept_weights = (
        lax.all_gather(attn_gain, "seq", axis=0, tiled=True),
        lax.all_gather(query_weight, "seq", axis=0, tiled=True),
        lax.all_gather(key_weight, "seq", axis=0, tiled=True),
        lax.all_gather(value_weight, "seq", axis=0, tiled=True),
        lax.all_gather(out_weight, "seq", axis=1, tiled=True),
        lax.all_gather(mlp_gain, "seq", axis=0, tiled=True),
        lax.all_gather(gate_weight, "seq", axis=0, tiled=True),
        lax.all_gather(up_weight, "seq", axis=0, tiled=True),
        lax.all_gather(down_weight, "seq", axis=1, tiled=True),
    )
    (
        attn_gain_back,
        query_back,
        key_back,
        value_back,
        out_back,
        mlp_gain_back,
        gate_back,
        up_back,
        down_back,
    ) = kept_weights
    attn_gain_f = attn_gain_back.astype(jnp.float32)
    mlp_gain_f = mlp_gain_back.astype(jnp.float32)
    grad_values = cotangent.astype(jnp.float32)
    grad_down = jnp.einsum("tf,td->fd", mixed, cotangent, preferred_element_type=jnp.float32)
    dmixed = jnp.einsum("td,fd->tf", cotangent, down_back, preferred_element_type=jnp.float32)
    gate_sig = jax.nn.sigmoid(gate_pre)
    dgate = (dmixed * up_pre * gate_sig * (1.0 + gate_pre * (1.0 - gate_sig))).astype(jnp.bfloat16)
    dup = (dmixed * gate_act).astype(jnp.bfloat16)
    grad_gate = jnp.einsum("tk,tf->kf", normed_two, dgate, preferred_element_type=jnp.float32)
    grad_up = jnp.einsum("tk,tf->kf", normed_two, dup, preferred_element_type=jnp.float32)
    dnormed_two = lax.psum(
        jnp.einsum("tf,kf->tk", dgate, gate_back, preferred_element_type=jnp.float32)
        + jnp.einsum("tf,kf->tk", dup, up_back, preferred_element_type=jnp.float32),
        "head",
    )
    dhidden_norm, grad_mlp_gain = norm_back(hidden, inverse_two, mlp_gain_f, dnormed_two)
    dhidden = grad_values + dhidden_norm
    mlp_sums = (grad_mlp_gain, grad_gate, grad_up, grad_down)
    dhidden_low = dhidden.astype(jnp.bfloat16)
    grad_out = jnp.einsum("tc,td->cd", attn_mix, dhidden_low, preferred_element_type=jnp.float32)
    dmix = jnp.einsum(
        "td,cd->tc", dhidden_low, out_back, preferred_element_type=jnp.float32
    ).astype(jnp.bfloat16)
    all_dmix = lax.all_gather(dmix, "seq", axis=0, tiled=True)

    def backward_block(carry, packed):
        key_accum, value_accum = carry
        query_block, grad_block, block_start = packed
        weights = weights_for(query_block, block_start)
        grad_weights = jnp.einsum(
            "qhd,khd->hqk", grad_block, value_rows, preferred_element_type=jnp.float32
        )
        grad_scores = (grad_weights * weights * (1.0 - weights)).astype(jnp.bfloat16)
        value_accum = value_accum + jnp.einsum(
            "hqk,qhd->khd",
            weights.astype(jnp.bfloat16),
            grad_block,
            preferred_element_type=jnp.float32,
        )
        key_accum = key_accum + jnp.einsum(
            "hqk,qhd->khd", grad_scores, query_block, preferred_element_type=jnp.float32
        )
        query_part = (
            jnp.einsum("hqk,khd->qhd", grad_scores, key_rows, preferred_element_type=jnp.float32)
            * score_scale
        )
        return ((key_accum, value_accum), query_part.reshape(block_rows, local_width))

    zero_rows = jnp.zeros((row_count, local_heads, HD), jnp.float32)
    block_starts = jnp.arange(block_count, dtype=jnp.int32) * block_rows
    (key_accum, value_accum), query_parts = lax.scan(
        backward_block,
        (zero_rows, zero_rows),
        (
            all_queries.reshape(block_count, block_rows, local_heads, HD),
            all_dmix.reshape(block_count, block_rows, local_heads, HD),
            block_starts,
        ),
    )
    query_sum = lax.psum_scatter(
        query_parts.reshape(total_rows, local_width), "seq", scatter_dimension=0, tiled=True
    )
    dquery_pre = (
        unrotary(query_sum.reshape(row_count, local_heads, HD), cos_table, sin_table)
        .reshape(row_count, local_width)
        .astype(jnp.bfloat16)
    )
    dkey_pre = (
        unrotary(key_accum * score_scale, cos_table, sin_table)
        .reshape(row_count, local_width)
        .astype(jnp.bfloat16)
    )
    dvalue = value_accum.reshape(row_count, local_width).astype(jnp.bfloat16)
    grad_query = jnp.einsum("tk,tc->kc", normed_one, dquery_pre, preferred_element_type=jnp.float32)
    grad_key = jnp.einsum("tk,tc->kc", normed_one, dkey_pre, preferred_element_type=jnp.float32)
    grad_value = jnp.einsum("tk,tc->kc", normed_one, dvalue, preferred_element_type=jnp.float32)
    dnormed_one = lax.psum(
        jnp.einsum("tc,kc->tk", dquery_pre, query_back, preferred_element_type=jnp.float32)
        + jnp.einsum("tc,kc->tk", dkey_pre, key_back, preferred_element_type=jnp.float32)
        + jnp.einsum("tc,kc->tk", dvalue, value_back, preferred_element_type=jnp.float32),
        "head",
    )
    dinput_norm, grad_attn_gain = norm_back(token_values, inverse_one, attn_gain_f, dnormed_one)
    input_grad = (dhidden + dinput_norm).astype(jnp.bfloat16)
    every_sum = (
        lax.psum_scatter(grad_attn_gain, "seq", scatter_dimension=0, tiled=True),
        lax.psum_scatter(grad_query, "seq", scatter_dimension=0, tiled=True),
        lax.psum_scatter(grad_key, "seq", scatter_dimension=0, tiled=True),
        lax.psum_scatter(grad_value, "seq", scatter_dimension=0, tiled=True),
        lax.psum_scatter(grad_out, "seq", scatter_dimension=1, tiled=True),
        lax.psum_scatter(grad_mlp_gain, "seq", scatter_dimension=0, tiled=True),
        lax.psum_scatter(grad_gate, "seq", scatter_dimension=0, tiled=True),
        lax.psum_scatter(grad_up, "seq", scatter_dimension=0, tiled=True),
        lax.psum_scatter(grad_down, "seq", scatter_dimension=1, tiled=True),
    )
    attn_sums = every_sum[:5]
    mlp_sums = every_sum[5:]
    return (
        result,
        input_grad,
        attn_sums[0],
        attn_sums[1],
        attn_sums[2],
        attn_sums[3],
        attn_sums[4],
        mlp_sums[0],
        mlp_sums[1],
        mlp_sums[2],
        mlp_sums[3],
    )


def place():
    return lax.axis_index("seq"), lax.axis_index("head")


def enter(peers):
    barrier = pltpu.get_barrier_semaphore()
    for peer in peers:
        pl.semaphore_signal(barrier, inc=1, device_id=peer, device_id_type=MESH)
    pl.semaphore_wait(barrier, len(peers))


class Net:
    def __init__(self, send, receive):
        self.send, self.receive, self.copies = send, receive, []

    def put(self, source, target, device):
        i = len(self.copies)
        copy = pltpu.make_async_remote_copy(
            src_ref=source,
            dst_ref=target,
            send_sem=self.send.at[i],
            recv_sem=self.receive.at[i],
            device_id=device,
            device_id_type=MESH,
        )
        copy.start()
        self.copies.append(copy)
        return copy

    def sent(self):
        for copy in self.copies:
            copy.wait_send()


def whole(space):
    return pl.BlockSpec(memory_space=space)


def talk(body, ins, outs, scratch, ident, space=pl.ANY, copies=64):
    return pl.pallas_call(
        body,
        out_shape=outs,
        in_specs=[whole(space)] * len(ins),
        out_specs=[whole(space)] * len(outs),
        scratch_shapes=[
            *scratch,
            pltpu.SemaphoreType.DMA((copies,)),
            pltpu.SemaphoreType.DMA((copies,)),
            pltpu.SemaphoreType.DMA((16,)),
        ],
        compiler_params=pltpu.CompilerParams(
            collective_id=ident, has_side_effects=True, vmem_limit_bytes=56 * 2**20
        ),
    )(*ins)


def lane(start, size):
    return pl.ds(pl.multiple_of(start, 128), size)


def row(start, size):
    return pl.ds(pl.multiple_of(start, 64), size)


def fetch_body(groups, ranks, *refs):
    (tok, cot, gains, q, k, v, o, gate, up, down) = refs[:10]
    (tok_all, cot_all, gains_all, q_all, k_all, v_all, o_all, gate_all, up_all, down_all) = refs[10:20]
    send, receive, local = refs[20:]
    s, h = place()
    g = s // ranks
    enter([(s ^ m, h) for m in range(1, groups * ranks)] + [(s, h ^ 1), (s, h ^ 2)])
    net = Net(send, receive)
    quarter = tok.shape[0] // 4
    width = gains.shape[1]

    def source(ref, group, by_row):
        if by_row:
            size = ref.shape[0] // groups
            return ref.at[pl.ds(pl.multiple_of(group * size, 128), size), :]
        size = ref.shape[1] // groups
        return ref.at[:, lane(group * size, size)]

    def target(ref, shard, by_row):
        if by_row:
            return ref.at[:, lane(shard * width, width)]
        return ref.at[shard]

    mine = []

    def keep(a, b):
        copy = pltpu.make_async_copy(a, b, local.at[len(mine)])
        copy.start()
        mine.append(copy)

    gains_moves = [
        net.put(gains, gains_all.at[:, lane(s * width, width)], (s ^ m, h))
        for m in range(1, groups * ranks)
    ]
    keep(gains, gains_all.at[:, lane(s * width, width)])
    strip = row(h * quarter, quarter)
    pairs = ((tok, tok_all), (cot, cot_all))
    row_moves = {
        (i, m): net.put(a.at[strip], b.at[g, strip], (s ^ (m * ranks), h))
        for i, (a, b) in enumerate(pairs)
        for m in range(1, groups)
    }
    for a, b in pairs:
        keep(a, b.at[g])
    weights = (
        (q, q_all, False),
        (k, k_all, False),
        (v, v_all, False),
        (o, o_all, True),
        (gate, gate_all, False),
        (up, up_all, False),
        (down, down_all, True),
    )
    moves = {}
    for i, (a, b, by_row) in enumerate(weights):
        for m in range(1, groups):
            moves[i, m] = net.put(
                source(a, g ^ m, by_row), target(b, s, by_row), (s ^ (m * ranks), h)
            )
        keep(source(a, g, by_row), target(b, s, by_row))
    arrivals = []
    for i, (a, b, by_row) in enumerate(weights):
        arrivals.append(net.put(source(a, g, by_row), target(b, s, by_row), (s ^ 1, h)))
    across = {}
    for i, (a, b) in enumerate(pairs):
        for m in range(1, groups):
            row_moves[i, m].wait_recv()
            block = b.at[g ^ m, strip]
            across[i, m] = net.put(block, block, (s, h ^ 2))
            arrivals.append(net.put(block, block, (s, h ^ 1)))
    other = row((h ^ 2) * quarter, quarter)
    for i, (a, b) in enumerate(pairs):
        for m in range(1, groups):
            across[i, m].wait_recv()
            block = b.at[g ^ m, other]
            arrivals.append(net.put(block, block, (s, h ^ 1)))
    for i, (a, b, by_row) in enumerate(weights):
        for m in range(1, groups):
            moves[i, m].wait_recv()
            block = target(b, s ^ (m * ranks), by_row)
            arrivals.append(net.put(block, block, (s ^ 1, h)))
    for copy in gains_moves + arrivals:
        copy.wait_recv()
    net.sent()
    for copy in mine:
        copy.wait()


def spread_body(groups, ranks, own, out, send, receive, local):
    s, h = place()
    g = s // ranks
    enter([(s ^ (m * ranks), h) for m in range(1, groups)] + [(s, h ^ 1), (s, h ^ 2)])
    net = Net(send, receive)
    quarter = own.shape[0]
    strip, other = row(h * quarter, quarter), row((h ^ 2) * quarter, quarter)
    keep = pltpu.make_async_copy(own, out.at[g, strip], local.at[0])
    keep.start()
    along = {
        m: net.put(own, out.at[g, strip], (s ^ (m * ranks), h)) for m in range(1, groups)
    }
    across = {0: net.put(own, out.at[g, strip], (s, h ^ 2))}
    last = [net.put(own, out.at[g, strip], (s, h ^ 1))]
    for m in range(1, groups):
        along[m].wait_recv()
        block = out.at[g ^ m, strip]
        across[m] = net.put(block, block, (s, h ^ 2))
        last.append(net.put(block, block, (s, h ^ 1)))
    for m in range(groups):
        across[m].wait_recv()
        block = out.at[g ^ m, other]
        last.append(net.put(block, block, (s, h ^ 1)))
    for copy in last:
        copy.wait_recv()
    net.sent()
    keep.wait()


def collect_body(
    groups, ranks, part, out, near, mid, across_send, across_in, along_send, along_in, send, receive, local
):
    s, h = place()
    g = s // ranks
    enter([(s ^ (m * ranks), h) for m in range(1, groups)] + [(s, h ^ 1), (s, h ^ 2)])
    net = Net(send, receive)
    order = list(range(groups - 1, -1, -1))
    first = {}
    for m in order:
        d = g ^ m
        first[m] = (
            net.put(part.at[d, h ^ 3], near.at[d, 1], (s, h ^ 1)),
            net.put(part.at[d, h ^ 1], near.at[d, 0], (s, h ^ 1)),
        )
    second, third = {}, {}
    for m in order:
        d = g ^ m
        first[m][0].wait_recv()
        across_send[d] = (part[d, h ^ 2].astype(F32) + near[d, 1].astype(F32)).astype(BF16)
        second[m] = net.put(across_send.at[d], across_in.at[d], (s, h ^ 2))
    for m in order:
        d = g ^ m
        first[m][1].wait_recv()
        mid[...] = part[d, h].astype(F32) + near[d, 0].astype(F32)
        second[m].wait_recv()
        total = mid[...] + across_in[d].astype(F32)
        if m:
            along_send[m - 1] = total.astype(BF16)
            third[m] = net.put(along_send.at[m - 1], along_in.at[m - 1], (s ^ (m * ranks), h))
        else:
            out[...] = total
    for m in order[:-1]:
        third[m].wait_recv()
        out[...] += along_in[m - 1].astype(F32)
    net.sent()


def swap_body(ranks, own, out, send, receive, local):
    s, h = place()
    r = s % ranks
    enter([(s ^ 1, h)])
    net = Net(send, receive)
    keep = pltpu.make_async_copy(own, out.at[:, r], local.at[0])
    keep.start()
    net.put(own, out.at[:, r], (s ^ 1, h)).wait_recv()
    net.sent()
    keep.wait()


def hand_body(ranks, own, out, send, receive, local):
    s, h = place()
    r = s % ranks
    enter([(s ^ 1, h)])
    net = Net(send, receive)
    net.put(own.at[:, r ^ 1], out, (s ^ 1, h)).wait_recv()
    net.sent()


def finish_body(groups, ranks, *refs):
    parts, (result, rows_grad, gains) = refs[:7], refs[7:10]
    outs, (result_all, rows_grad_all, gains_out) = refs[10:17], refs[17:20]
    peers, sums, (gains_in, gains_mid, gains_near) = refs[20:27], refs[27:34], refs[34:37]
    send, receive, local = refs[37:]
    s, h = place()
    g, r = s // ranks, s % ranks
    size = groups * ranks
    enter([(s ^ m, h) for m in range(1, size)] + [(s, h ^ m) for m in range(1, 4)])
    net = Net(send, receive)
    quarter = result.shape[0]
    width = gains_out.shape[1]
    strip = row(h * quarter, quarter)
    to_peer = []
    for i, part in enumerate(parts):
        to_peer.append(net.put(part.at[:, r ^ 1], peers[i], (s ^ 1, h)))
    rest = []
    for a, b in ((result, result_all), (rows_grad, rows_grad_all)):
        b[strip, :] = a[...]
        for m in range(1, 4):
            rest.append(net.put(a, b.at[strip], (s, h ^ m)))
    gains_moves = [
        net.put(gains.at[:, lane((s ^ m) * width, width)], gains_in.at[m - 1], (s ^ m, h))
        for m in range(1, size)
    ]

    def target(i, group):
        if outs[i].shape[0] != width:
            n = outs[i].shape[0] // groups
            return outs[i].at[pl.ds(pl.multiple_of(group * n, 128), n), :]
        n = outs[i].shape[1] // groups
        return outs[i].at[:, lane(group * n, n)]

    for i, part in enumerate(parts):
        to_peer[i].wait_recv()
        for m in range(groups - 1, -1, -1):
            d = g ^ m
            total = part[d, r].astype(F32) + peers[i][d].astype(F32)
            sums[i][d] = total.astype(BF16)
            if m:
                rest.append(net.put(sums[i].at[d], target(i, g), (s ^ (m * ranks), h)))
            else:
                keep = pltpu.make_async_copy(sums[i].at[d], target(i, g), local.at[i])
                keep.start()
    total = gains[:, lane(s * width, width)]
    for m in range(1, size):
        gains_moves[m - 1].wait_recv()
        total += gains_in[m - 1]
    gains_mid[...] = total
    near = [net.put(gains_mid, gains_near.at[m - 1], (s, h ^ m)) for m in range(1, 4)]
    for m in range(1, 4):
        near[m - 1].wait_recv()
        total += gains_near[m - 1]
    gains_out[...] = total
    for copy in rest:
        copy.wait_recv()
    net.sent()
    for i in range(len(parts)):
        pltpu.make_async_copy(sums[i].at[g], target(i, g), local.at[i]).wait()


def rotate(values, cos_table, sin_table):
    return values * cos_table + jnp.roll(values, HD // 2, axis=1) * sin_table


def rows_plan(
    groups,
    ranks,
    tokens,
    attn_gain,
    query_weight,
    key_weight,
    value_weight,
    out_weight,
    mlp_gain,
    gate_weight,
    up_weight,
    down_weight,
    cotangent,
):
    count, depth = tokens.shape
    shards = groups * ranks
    quarter = count // 4
    width = query_weight.shape[0]
    units = gate_weight.shape[1] // groups
    total_rows = count * shards
    here = groups * count
    s, h = place()
    r = s % ranks
    shape = jax.ShapeDtypeStruct
    bind = functools.partial

    gains = jnp.zeros((8, width), F32)
    gains = gains.at[0].set(attn_gain.astype(F32)).at[1].set(mlp_gain.astype(F32))
    ins = (tokens, cotangent, gains, query_weight, key_weight, value_weight, out_weight, gate_weight, up_weight, down_weight)
    heads = shape((shards, width, HD), BF16)
    hidden_units = shape((shards, width, units), BF16)
    outs = (
        shape((groups, count, depth), BF16),
        shape((groups, count, depth), BF16),
        shape((8, depth), F32),
        heads,
        heads,
        heads,
        shape((HD, depth), BF16),
        hidden_units,
        hidden_units,
        shape((units, depth), BF16),
    )
    tok, cot, gains, wq, wk, wv, wo, wg, wu, wd = talk(bind(fetch_body, groups, ranks), ins, outs, [], 1, copies=96)
    wq, wk, wv = (w.reshape(depth, HD) for w in (wq, wk, wv))
    wg, wu = (w.reshape(depth, units) for w in (wg, wu))
    tok, cot = tok.reshape(here, depth), cot.reshape(here, depth)
    gain_one, gain_two = gains[0], gains[1]

    def collect(part, ident):
        part = part.astype(BF16).reshape(groups, 4, quarter, depth)
        piece = (quarter, depth)
        return talk(
            bind(collect_body, groups, ranks),
            (part,),
            [shape(piece, F32)],
            [
                pltpu.VMEM((groups, 2, *piece), BF16),
                pltpu.VMEM(piece, F32),
                pltpu.VMEM((groups, *piece), BF16),
                pltpu.VMEM((groups, *piece), BF16),
                pltpu.VMEM((groups - 1, *piece), BF16),
                pltpu.VMEM((groups - 1, *piece), BF16),
            ],
            ident,
            space=pltpu.VMEM,
        )[0]

    def spread(own, ident):
        return talk(
            bind(spread_body, groups, ranks), (own,), [shape((groups, count, depth), BF16)], [], ident
        )[0].reshape(here, depth)

    def dot(a, b):
        return jnp.dot(a, b, preferred_element_type=F32)

    def dot_nt(a, b):
        return lax.dot_general(a, b, (((1,), (1,)), ((), ())), preferred_element_type=F32)

    def dot_tn(a, b):
        return lax.dot_general(a, b, (((0,), (0,)), ((), ())), preferred_element_type=F32)

    x = tok.astype(F32)
    inv = lax.rsqrt(jnp.mean(x * x, axis=1, keepdims=True) + epsilon)
    normed_one = (x * inv * gain_one).astype(BF16)
    own_rows = lax.dynamic_slice_in_dim(tokens, h * quarter, quarter, 0).astype(F32)
    places = (
        (jnp.arange(groups, dtype=jnp.int32) * ranks + r)[:, None] * count
        + jnp.arange(count, dtype=jnp.int32)[None, :]
    ).reshape(here)
    half = HD // 2
    frequency = jnp.exp(jnp.arange(half, dtype=F32) * (-math.log(10000.0) / half))
    angles = places.astype(F32)[:, None] * frequency[None, :]
    cosines, sines = jnp.cos(angles), jnp.sin(angles)
    cos_table = jnp.concatenate([cosines, cosines], 1)
    sin_table = jnp.concatenate([-sines, sines], 1)
    query = rotate(dot(normed_one, wq), cos_table, sin_table).astype(BF16)
    key = rotate(dot(normed_one, wk), cos_table, sin_table).astype(BF16)
    value = dot(normed_one, wv).astype(BF16)
    both = jnp.concatenate([key, value], 1).reshape(groups, count, 2 * HD)
    both = talk(bind(swap_body, ranks), (both,), [shape((groups, ranks, count, 2 * HD), BF16)], [], 2)[0]
    both = both.reshape(total_rows, 2 * HD)
    keys, values = both[:, :HD], both[:, HD:]
    score_scale = 1.0 / math.sqrt(HD)
    score_shift = math.log(total_rows)
    visible = jnp.arange(total_rows, dtype=jnp.int32)[None, :] <= places[:, None]
    weight = jnp.where(visible, jax.nn.sigmoid(dot_nt(query, keys) * score_scale - score_shift), 0.0)
    weight_low = weight.astype(BF16)
    mix = dot(weight_low, values).astype(BF16)
    hidden = own_rows + collect(dot(mix, wo), 3)
    inv_two = lax.rsqrt(jnp.mean(hidden * hidden, axis=1, keepdims=True) + epsilon)
    normed_two = spread((hidden * inv_two * gain_two).astype(BF16), 4)
    gate = dot(normed_two, wg)
    up = dot(normed_two, wu)
    sig = jax.nn.sigmoid(gate)
    act = gate * sig
    mixed = (act * up).astype(BF16)
    result = (hidden + collect(dot(mixed, wd), 5)).astype(BF16)
    grad_down = dot_tn(mixed, cot)
    dmixed = dot_nt(cot, wd)
    dgate = (dmixed * up * sig * (1.0 + gate * (1.0 - sig))).astype(BF16)
    dup = (dmixed * act).astype(BF16)
    dnormed_two = collect(dot_nt(dgate, wg) + dot_nt(dup, wu), 6)
    grad_gate = dot_tn(normed_two, dgate)
    grad_up = dot_tn(normed_two, dup)
    own_cot = lax.dynamic_slice_in_dim(cotangent, h * quarter, quarter, 0).astype(F32)
    back, grad_gain_two = norm_back(hidden, inv_two, gain_two, dnormed_two)
    dhidden = own_cot + back
    dhidden_low = spread(dhidden.astype(BF16), 7)
    grad_out = dot_tn(mix, dhidden_low)
    dmix = dot_nt(dhidden_low, wo).astype(BF16)
    dweight = dot_nt(dmix, values)
    dscore = (dweight * weight * (1.0 - weight)).astype(BF16)
    dvalues = dot_tn(weight_low, dmix)
    dkeys = dot_tn(dscore, query) * score_scale
    dquery = dot(dscore, keys) * score_scale
    both_back = jnp.concatenate([dkeys, dvalues], 1).reshape(groups, ranks, count, 2 * HD)
    other = talk(
        bind(hand_body, ranks), (both_back.astype(BF16),), [shape((groups, count, 2 * HD), BF16)], [], 8
    )[0]
    both_back = lax.dynamic_index_in_dim(both_back, r, 1, keepdims=False) + other.astype(F32)
    both_back = both_back.reshape(here, 2 * HD)
    dquery_pre = rotate(dquery, cos_table, -sin_table).astype(BF16)
    dkey_pre = rotate(both_back[:, :HD], cos_table, -sin_table).astype(BF16)
    dvalue = both_back[:, HD:].astype(BF16)
    dnormed_one = collect(
        dot_nt(dquery_pre, wq) + dot_nt(dkey_pre, wk) + dot_nt(dvalue, wv), 9
    )
    grad_query = dot_tn(normed_one, dquery_pre)
    grad_key = dot_tn(normed_one, dkey_pre)
    grad_value = dot_tn(normed_one, dvalue)
    own_inv = lax.rsqrt(jnp.mean(own_rows * own_rows, axis=1, keepdims=True) + epsilon)
    back, grad_gain_one = norm_back(own_rows, own_inv, gain_one, dnormed_one)
    rows_grad = (dhidden + back).astype(BF16)
    by_row = [
        w.astype(BF16).reshape(groups, ranks, width, w.shape[1])
        for w in (grad_query, grad_key, grad_value, grad_gate, grad_up)
    ]
    by_column = [
        w.astype(BF16).reshape(w.shape[0], groups, ranks, width).transpose(1, 2, 0, 3)
        for w in (grad_out, grad_down)
    ]
    parts = (*by_row[:3], by_column[0], *by_row[3:], by_column[1])
    gain_grads = jnp.zeros((8, depth), F32).at[0].set(grad_gain_one).at[1].set(grad_gain_two)
    owners = (query_weight, key_weight, value_weight, out_weight, gate_weight, up_weight, down_weight)
    rows_all = shape((count, depth), BF16)
    moved = [pltpu.VMEM((groups, *p.shape[2:]), BF16) for p in parts]
    *grads, result, rows_grad, gain_grads = talk(
        bind(finish_body, groups, ranks),
        (*parts, result, rows_grad, gain_grads),
        [*(shape(w.shape, BF16) for w in owners), rows_all, rows_all, shape((8, width), F32)],
        [
            *moved,
            *moved,
            pltpu.VMEM((shards - 1, 8, width), F32),
            pltpu.VMEM((8, width), F32),
            pltpu.VMEM((3, 8, width), F32),
        ],
        10,
        space=pltpu.VMEM,
        copies=64,
    )
    grads = [w.astype(F32) for w in grads]
    return (result, rows_grad, gain_grads[0], *grads[:4], gain_grads[1], *grads[4:])


def on_device(tokens, attn_gain, query_weight, *rest):
    groups = query_weight.shape[1] // HD
    ranks = lax.axis_size("seq") // groups
    fits = lax.axis_size("head") == 4 and groups == 4 and ranks == 2 and query_weight.shape[0] % 128 == 0
    plan = functools.partial(rows_plan, groups, ranks) if fits else gathered_weights
    return plan(tokens, attn_gain, query_weight, *rest)


def solution(mesh):
    in_specs = (
        P("seq", None),
        P("seq"),
        P("seq", "head"),
        P("seq", "head"),
        P("seq", "head"),
        P("head", "seq"),
        P("seq"),
        P("seq", "head"),
        P("seq", "head"),
        P("head", "seq"),
        P("seq", None),
    )
    out_specs = (
        P("seq", None),
        P("seq", None),
        P("seq"),
        P("seq", "head"),
        P("seq", "head"),
        P("seq", "head"),
        P("head", "seq"),
        P("seq"),
        P("seq", "head"),
        P("seq", "head"),
        P("head", "seq"),
    )
    return jax.shard_map(
        on_device, mesh=mesh, in_specs=in_specs, out_specs=out_specs, check_vma=False
    )
```

```python
import functools
import math

import jax
import jax.numpy as jnp
from jax import lax
from jax.experimental import pallas as pl
from jax.experimental.pallas import tpu as pltpu
from jax.sharding import PartitionSpec as P

MESH = pl.DeviceIdType.MESH
F32, BF16 = jnp.float32, jnp.bfloat16

HD = 128


epsilon = 1e-05
block_limit = 512
VMEM_LIMIT = 63 * 2**20


def tables(offset, length, half_width):
    places = (offset + jnp.arange(length, dtype=jnp.int32)).astype(jnp.float32)
    frequency = jnp.exp(
        jnp.arange(half_width, dtype=jnp.float32) * (-math.log(10000.0) / half_width)
    )
    angles = places[:, None] * frequency[None, :]
    return (jnp.cos(angles)[:, None, :], jnp.sin(angles)[:, None, :])


def rotary(values, cos_table, sin_table):
    half_width = values.shape[-1] // 2
    front = values[..., :half_width]
    back_half = values[..., half_width:]
    return jnp.concatenate(
        [front * cos_table - back_half * sin_table, back_half * cos_table + front * sin_table],
        axis=-1,
    )


def unrotary(gradient, cos_table, sin_table):
    half_width = gradient.shape[-1] // 2
    front = gradient[..., :half_width]
    back_half = gradient[..., half_width:]
    return jnp.concatenate(
        [front * cos_table + back_half * sin_table, back_half * cos_table - front * sin_table],
        axis=-1,
    )


def norm_back(values, inverse, gain_vector, upstream):
    scaled = upstream * gain_vector
    gain_grad = jnp.sum(upstream * values * inverse, axis=0)
    value_grad = inverse * scaled - values * inverse**3 * jnp.mean(
        scaled * values, axis=1, keepdims=True
    )
    return (value_grad, gain_grad)


def gathered_weights(
    tokens,
    attn_gain,
    query_weight,
    key_weight,
    value_weight,
    out_weight,
    mlp_gain,
    gate_weight,
    up_weight,
    down_weight,
    cotangent,
):
    row_count = tokens.shape[0]
    total_rows = row_count * lax.axis_size("seq")
    row_start = lax.axis_index("seq") * row_count
    local_width = query_weight.shape[1]
    local_heads = local_width // HD
    score_scale = 1.0 / math.sqrt(HD)
    score_shift = math.log(total_rows)
    block_rows = math.gcd(total_rows, block_limit)
    block_count = total_rows // block_rows
    attn_gain_full, query_full, key_full, value_full, out_full = (
        lax.all_gather(attn_gain, "seq", axis=0, tiled=True),
        lax.all_gather(query_weight, "seq", axis=0, tiled=True),
        lax.all_gather(key_weight, "seq", axis=0, tiled=True),
        lax.all_gather(value_weight, "seq", axis=0, tiled=True),
        lax.all_gather(out_weight, "seq", axis=1, tiled=True),
    )
    mlp_gain_full, gate_full, up_full, down_full = (
        lax.all_gather(mlp_gain, "seq", axis=0, tiled=True),
        lax.all_gather(gate_weight, "seq", axis=0, tiled=True),
        lax.all_gather(up_weight, "seq", axis=0, tiled=True),
        lax.all_gather(down_weight, "seq", axis=1, tiled=True),
    )
    token_values = tokens.astype(jnp.float32)
    inverse_one = lax.rsqrt(jnp.mean(token_values * token_values, axis=1, keepdims=True) + epsilon)
    normed_one = (token_values * inverse_one * attn_gain_full.astype(jnp.float32)).astype(
        jnp.bfloat16
    )
    query_pre = jnp.dot(normed_one, query_full, preferred_element_type=jnp.float32)
    key_pre = jnp.dot(normed_one, key_full, preferred_element_type=jnp.float32)
    value_rows = (
        jnp.dot(normed_one, value_full, preferred_element_type=jnp.float32)
        .astype(jnp.bfloat16)
        .reshape(row_count, local_heads, HD)
    )
    cos_table, sin_table = tables(row_start, row_count, HD // 2)
    query_rows = (
        rotary(query_pre.reshape(row_count, local_heads, HD), cos_table, sin_table)
        .astype(jnp.bfloat16)
        .reshape(row_count, local_width)
    )
    key_rows = rotary(key_pre.reshape(row_count, local_heads, HD), cos_table, sin_table).astype(
        jnp.bfloat16
    )
    all_queries = lax.all_gather(query_rows, "seq", axis=0, tiled=True)
    key_places = row_start + jnp.arange(row_count, dtype=jnp.int32)

    def weights_for(query_block, block_start):
        scores = (
            jnp.einsum("qhd,khd->hqk", query_block, key_rows, preferred_element_type=jnp.float32)
            * score_scale
            - score_shift
        )
        query_places = block_start + jnp.arange(query_block.shape[0], dtype=jnp.int32)
        visible = key_places[None, :] <= query_places[:, None]
        return jnp.where(visible[None], jax.nn.sigmoid(scores), 0.0)

    step_rows = math.gcd(row_count * lax.axis_size("seq"), block_limit)
    step_count = row_count * lax.axis_size("seq") // step_rows
    picked = all_queries.reshape(step_count, step_rows, local_heads, HD)
    starts = jnp.arange(step_count, dtype=jnp.int32) * step_rows

    def one_block(packed):
        query_block, block_start = packed
        weights = weights_for(query_block, block_start).astype(jnp.bfloat16)
        return jnp.einsum(
            "hqk,khd->qhd", weights, value_rows, preferred_element_type=jnp.float32
        ).reshape(step_rows, local_width)

    attn_mix = lax.psum_scatter(
        lax.map(one_block, (picked, starts)).reshape(row_count * lax.axis_size("seq"), local_width),
        "seq",
        scatter_dimension=0,
        tiled=True,
    ).astype(jnp.bfloat16)
    attn_branch = lax.psum(jnp.dot(attn_mix, out_full, preferred_element_type=jnp.float32), "head")
    hidden = token_values + attn_branch
    inverse_two = lax.rsqrt(jnp.mean(hidden * hidden, axis=1, keepdims=True) + epsilon)
    normed_two = (hidden * inverse_two * mlp_gain_full.astype(jnp.float32)).astype(jnp.bfloat16)
    gate_pre = jnp.dot(normed_two, gate_full, preferred_element_type=jnp.float32)
    up_pre = jnp.dot(normed_two, up_full, preferred_element_type=jnp.float32)
    gate_act = jax.nn.silu(gate_pre)
    mixed = (gate_act * up_pre).astype(jnp.bfloat16)
    mlp_branch = lax.psum(
        jnp.dot(mixed, down_full, preferred_element_type=jnp.float32).astype(jnp.bfloat16), "head"
    ).astype(jnp.float32)
    result = (hidden + mlp_branch).astype(jnp.bfloat16)
    kept_weights = (
        lax.all_gather(attn_gain, "seq", axis=0, tiled=True),
        lax.all_gather(query_weight, "seq", axis=0, tiled=True),
        lax.all_gather(key_weight, "seq", axis=0, tiled=True),
        lax.all_gather(value_weight, "seq", axis=0, tiled=True),
        lax.all_gather(out_weight, "seq", axis=1, tiled=True),
        lax.all_gather(mlp_gain, "seq", axis=0, tiled=True),
        lax.all_gather(gate_weight, "seq", axis=0, tiled=True),
        lax.all_gather(up_weight, "seq", axis=0, tiled=True),
        lax.all_gather(down_weight, "seq", axis=1, tiled=True),
    )
    (
        attn_gain_back,
        query_back,
        key_back,
        value_back,
        out_back,
        mlp_gain_back,
        gate_back,
        up_back,
        down_back,
    ) = kept_weights
    attn_gain_f = attn_gain_back.astype(jnp.float32)
    mlp_gain_f = mlp_gain_back.astype(jnp.float32)
    grad_values = cotangent.astype(jnp.float32)
    grad_down = jnp.einsum("tf,td->fd", mixed, cotangent, preferred_element_type=jnp.float32)
    dmixed = jnp.einsum("td,fd->tf", cotangent, down_back, preferred_element_type=jnp.float32)
    gate_sig = jax.nn.sigmoid(gate_pre)
    dgate = (dmixed * up_pre * gate_sig * (1.0 + gate_pre * (1.0 - gate_sig))).astype(jnp.bfloat16)
    dup = (dmixed * gate_act).astype(jnp.bfloat16)
    grad_gate = jnp.einsum("tk,tf->kf", normed_two, dgate, preferred_element_type=jnp.float32)
    grad_up = jnp.einsum("tk,tf->kf", normed_two, dup, preferred_element_type=jnp.float32)
    dnormed_two = lax.psum(
        jnp.einsum("tf,kf->tk", dgate, gate_back, preferred_element_type=jnp.float32)
        + jnp.einsum("tf,kf->tk", dup, up_back, preferred_element_type=jnp.float32),
        "head",
    )
    dhidden_norm, grad_mlp_gain = norm_back(hidden, inverse_two, mlp_gain_f, dnormed_two)
    dhidden = grad_values + dhidden_norm
    mlp_sums = (grad_mlp_gain, grad_gate, grad_up, grad_down)
    dhidden_low = dhidden.astype(jnp.bfloat16)
    grad_out = jnp.einsum("tc,td->cd", attn_mix, dhidden_low, preferred_element_type=jnp.float32)
    dmix = jnp.einsum(
        "td,cd->tc", dhidden_low, out_back, preferred_element_type=jnp.float32
    ).astype(jnp.bfloat16)
    all_dmix = lax.all_gather(dmix, "seq", axis=0, tiled=True)

    def backward_block(carry, packed):
        key_accum, value_accum = carry
        query_block, grad_block, block_start = packed
        weights = weights_for(query_block, block_start)
        grad_weights = jnp.einsum(
            "qhd,khd->hqk", grad_block, value_rows, preferred_element_type=jnp.float32
        )
        grad_scores = (grad_weights * weights * (1.0 - weights)).astype(jnp.bfloat16)
        value_accum = value_accum + jnp.einsum(
            "hqk,qhd->khd",
            weights.astype(jnp.bfloat16),
            grad_block,
            preferred_element_type=jnp.float32,
        )
        key_accum = key_accum + jnp.einsum(
            "hqk,qhd->khd", grad_scores, query_block, preferred_element_type=jnp.float32
        )
        query_part = (
            jnp.einsum("hqk,khd->qhd", grad_scores, key_rows, preferred_element_type=jnp.float32)
            * score_scale
        )
        return ((key_accum, value_accum), query_part.reshape(block_rows, local_width))

    zero_rows = jnp.zeros((row_count, local_heads, HD), jnp.float32)
    block_starts = jnp.arange(block_count, dtype=jnp.int32) * block_rows
    (key_accum, value_accum), query_parts = lax.scan(
        backward_block,
        (zero_rows, zero_rows),
        (
            all_queries.reshape(block_count, block_rows, local_heads, HD),
            all_dmix.reshape(block_count, block_rows, local_heads, HD),
            block_starts,
        ),
    )
    query_sum = lax.psum_scatter(
        query_parts.reshape(total_rows, local_width), "seq", scatter_dimension=0, tiled=True
    )
    dquery_pre = (
        unrotary(query_sum.reshape(row_count, local_heads, HD), cos_table, sin_table)
        .reshape(row_count, local_width)
        .astype(jnp.bfloat16)
    )
    dkey_pre = (
        unrotary(key_accum * score_scale, cos_table, sin_table)
        .reshape(row_count, local_width)
        .astype(jnp.bfloat16)
    )
    dvalue = value_accum.reshape(row_count, local_width).astype(jnp.bfloat16)
    grad_query = jnp.einsum("tk,tc->kc", normed_one, dquery_pre, preferred_element_type=jnp.float32)
    grad_key = jnp.einsum("tk,tc->kc", normed_one, dkey_pre, preferred_element_type=jnp.float32)
    grad_value = jnp.einsum("tk,tc->kc", normed_one, dvalue, preferred_element_type=jnp.float32)
    dnormed_one = lax.psum(
        jnp.einsum("tc,kc->tk", dquery_pre, query_back, preferred_element_type=jnp.float32)
        + jnp.einsum("tc,kc->tk", dkey_pre, key_back, preferred_element_type=jnp.float32)
        + jnp.einsum("tc,kc->tk", dvalue, value_back, preferred_element_type=jnp.float32),
        "head",
    )
    dinput_norm, grad_attn_gain = norm_back(token_values, inverse_one, attn_gain_f, dnormed_one)
    input_grad = (dhidden + dinput_norm).astype(jnp.bfloat16)
    every_sum = (
        lax.psum_scatter(grad_attn_gain, "seq", scatter_dimension=0, tiled=True),
        lax.psum_scatter(grad_query, "seq", scatter_dimension=0, tiled=True),
        lax.psum_scatter(grad_key, "seq", scatter_dimension=0, tiled=True),
        lax.psum_scatter(grad_value, "seq", scatter_dimension=0, tiled=True),
        lax.psum_scatter(grad_out, "seq", scatter_dimension=1, tiled=True),
        lax.psum_scatter(grad_mlp_gain, "seq", scatter_dimension=0, tiled=True),
        lax.psum_scatter(grad_gate, "seq", scatter_dimension=0, tiled=True),
        lax.psum_scatter(grad_up, "seq", scatter_dimension=0, tiled=True),
        lax.psum_scatter(grad_down, "seq", scatter_dimension=1, tiled=True),
    )
    attn_sums = every_sum[:5]
    mlp_sums = every_sum[5:]
    return (
        result,
        input_grad,
        attn_sums[0],
        attn_sums[1],
        attn_sums[2],
        attn_sums[3],
        attn_sums[4],
        mlp_sums[0],
        mlp_sums[1],
        mlp_sums[2],
        mlp_sums[3],
    )


class Net:
    def __init__(self, send, receive):
        self.send, self.receive, self.copies, self.done = send, receive, [], set()

    def put(self, source, target, device):
        i = len(self.copies)
        copy = pltpu.make_async_remote_copy(
            src_ref=source,
            dst_ref=target,
            send_sem=self.send.at[i],
            recv_sem=self.receive.at[i],
            device_id=device,
            device_id_type=MESH,
        )
        copy.start()
        self.copies.append(copy)
        return copy

    def sent(self, copies=None):
        for copy in self.copies if copies is None else copies:
            if id(copy) not in self.done:
                self.done.add(id(copy))
                copy.wait_send()


class Keep:
    def __init__(self, sems):
        self.sems, self.count = sems, 0

    def put(self, source, target):
        copy = pltpu.make_async_copy(source, target, self.sems.at[self.count])
        self.count += 1
        copy.start()
        return copy


class Where:
    def __init__(self, groups, ranks):
        self.s, self.h = lax.axis_index("seq"), lax.axis_index("head")
        self.g, self.r = self.s // ranks, self.s % ranks
        self.groups, self.ranks = groups, ranks

    def along(self, m):
        return (self.s ^ (m * self.ranks), self.h)

    def beside(self):
        return (self.s ^ 1, self.h)

    def across(self):
        return (self.s, self.h ^ 2)

    def near(self):
        return (self.s, self.h ^ 1)


def lane(start, size):
    return pl.ds(pl.multiple_of(start, 128), size)


def row(start, size):
    return pl.ds(pl.multiple_of(start, size), size)


class Spread:
    def __init__(self, net, at, buffer, quarter, shared):
        self.net, self.at, self.buffer, self.quarter, self.shared = net, at, buffer, quarter, shared
        self.z, self.x, self.c, self.d = {}, {}, {}, {}

    def block(self, m, k):
        at = self.at
        return self.buffer.at[row(((at.g ^ m) * 4 + (at.h ^ k)) * self.quarter, self.quarter), :]

    def pass_on(self, m, source=None):
        block = self.block(m, 0)
        source = block if source is None else source
        self.x[m] = self.net.put(source, block, self.at.across())
        self.c[m] = self.net.put(source, block, self.at.near())

    def start(self, own):
        block = self.block(0, 0)
        self.z[2] = self.net.put(own, block, self.at.along(2))
        self.z[1] = self.net.put(own, block, self.at.along(1))
        if not self.shared:
            self.pass_on(0, own)

    def arrive(self, m):
        self.z[m].wait_recv()
        if m == 2:
            block = self.block(2, 0)
            self.z[3] = self.net.put(block, block, self.at.along(1))
        self.pass_on(m)

    def second(self, m):
        self.x[m].wait_recv()
        block = self.block(m, 2)
        self.d[m] = self.net.put(block, block, self.at.near())

    def ready(self, m):
        if m or not self.shared:
            self.c[m].wait_recv()
            self.d[m].wait_recv()

    def sent(self, m):
        if m or not self.shared:
            self.net.sent([self.x[m], self.c[m], self.d[m]])
        if m == 2:
            self.net.sent([self.z[3]])


class Collect:
    def __init__(self, net, at, refs, quarter):
        self.net, self.at, self.quarter = net, at, quarter
        self.part, self.near, self.xin, self.zin = refs
        self.a, self.b, self.z = {}, {}, {}
        self.own = None

    def rows(self, m, k):
        at = self.at
        return row(((at.g ^ m) * 4 + (at.h ^ k)) * self.quarter, self.quarter)

    def first(self, m):
        d, at = self.at.g ^ m, self.at
        self.a[m] = (
            self.net.put(self.part.at[self.rows(m, 3), :], self.near.at[d, 1], at.near()),
            self.net.put(self.part.at[self.rows(m, 1), :], self.near.at[d, 0], at.near()),
        )

    def second(self, m):
        d = self.at.g ^ m
        rows = self.rows(m, 2)
        self.a[m][0].wait_recv()
        self.part[rows, :] = (self.part[rows, :].astype(F32) + self.near[d, 1].astype(F32)).astype(BF16)
        self.b[m] = self.net.put(self.part.at[rows, :], self.xin.at[d], self.at.across())

    def third(self, m):
        d = self.at.g ^ m
        rows = self.rows(m, 0)
        self.a[m][1].wait_recv()
        self.b[m].wait_recv()
        total = self.part[rows, :].astype(F32) + self.near[d, 0].astype(F32) + self.xin[d].astype(F32)
        if m == 0:
            return total
        if m == 2:
            self.z[3].wait_recv()
            total += self.zin[0].astype(F32)
        self.part[rows, :] = total.astype(BF16)
        slot, hop = {3: (0, 1), 2: (2, 2), 1: (1, 1)}[m]
        self.z[m] = self.net.put(self.part.at[rows, :], self.zin.at[slot], self.at.along(hop))
        return None

    def last(self):
        total = self.third(0)
        self.z[1].wait_recv()
        total += self.zin[1].astype(F32)
        self.z[2].wait_recv()
        return total + self.zin[2].astype(F32)

    def sent(self):
        for m in range(4):
            self.net.sent(list(self.a[m]) + [self.b[m]] + ([self.z[m]] if m else []))


class Turn:
    def __init__(self, net, keep, at, sources, buffer, block, views):
        self.net, self.keep, self.at = net, keep, at
        self.sources, self.buffer, self.block, self.views = sources, buffer, block, views
        self.z, self.y, self.own = {}, [], []

    def start(self, m, i):
        at = self.at
        copy = self.net.put(self.sources(i, at.g ^ m), self.views(i, at.s), at.along(m))
        self.z.setdefault(m, []).append(copy)

    def mine(self, i):
        at = self.at
        source = self.sources(i, at.g)
        self.own.append(self.keep.put(source, self.views(i, at.s)))
        self.y.append(self.net.put(source, self.views(i, at.s), at.beside()))

    def pass_on(self, m):
        at = self.at
        for copy in self.z[m]:
            copy.wait_recv()
        block = self.block(at.s ^ (m * at.ranks))
        self.y.append(self.net.put(block, block, at.beside()))

    def ready(self):
        for copy in self.own:
            copy.wait()
        for copy in self.y:
            copy.wait_recv()

    def sent(self):
        self.net.sent(self.y)


def dot(a, b):
    return jnp.dot(a, b, preferred_element_type=F32)


def dot_nt(a, b):
    return lax.dot_general(a, b, (((1,), (1,)), ((), ())), preferred_element_type=F32)


def dot_tn(a, b):
    return lax.dot_general(a, b, (((0,), (0,)), ((), ())), preferred_element_type=F32)


def turned(values, cos_table, sin_table):
    return values * cos_table + pltpu.roll(values, HD // 2, 1) * sin_table


def mean_square(values):
    return jnp.mean(values * values, axis=1, keepdims=True)


def layer_body(groups, ranks, *refs):
    (tok, cot, gains, qw, kw, vw, ow, gw, uw, dw, cosines, sines) = refs[:12]
    (result_out, rows_out, gains_out, q_out, k_out, v_out, o_out, g_out, u_out, d_out) = refs[12:22]
    (
        gains_all, rows_one, rows_cot, rows_two, rows_dh, w_qkv, w_o, w_gu, w_d, queries, pairs, mix, dmix, dqkv, accum, pair_send,
        pair_in, mixed, dgu, dmixed, own_x, hidden, dhidden, part_a, near_a, xin_a, zin_a, part_b, near_b, xin_b, zin_b, in_gu, in_d,
        in_qkv, in_o, gain_part, gain_in, gain_mid, gain_near, result_own, rows_own, send, receive, local,
    ) = refs[22:]
    at = Where(groups, ranks)
    s, h, g, r = at.s, at.h, at.g, at.r
    shards = groups * ranks
    count, depth = tok.shape
    quarter = count // 4
    width = gains.shape[1]
    units = gw.shape[1] // groups
    total_rows = count * shards
    score_scale = 1.0 / math.sqrt(HD)
    score_shift = math.log(total_rows)
    peers = [(s ^ m, h) for m in range(1, shards)] + [(s, h ^ m) for m in range(1, 4)]
    barrier = pltpu.get_barrier_semaphore()
    for peer in peers:
        pl.semaphore_signal(barrier, inc=1, device_id=peer, device_id_type=MESH)
    pl.semaphore_wait(barrier, len(peers))
    net, keep = Net(send, receive), Keep(local)

    def chunk(m):
        return row((g ^ m) * count, count)

    def shard_rows(shard):
        return row(shard * width, width)

    def by_column(size):
        return lambda refs_: lambda i, group: refs_[i].at[:, lane(group * size, size)]

    def by_row(size):
        return lambda refs_: lambda i, group: refs_[i].at[row(group * size, size), :]

    turn_qkv = Turn(
        net, keep, at, by_column(HD)((qw, kw, vw)), w_qkv,
        lambda shard: w_qkv.at[shard_rows(shard), :],
        lambda i, shard: w_qkv.at[shard_rows(shard), i * HD : (i + 1) * HD],
    )
    turn_gu = Turn(
        net, keep, at, by_column(units)((gw, uw)), w_gu,
        lambda shard: w_gu.at[shard_rows(shard), :],
        lambda i, shard: w_gu.at[shard_rows(shard), i * units : (i + 1) * units],
    )
    turn_o = Turn(
        net, keep, at, by_row(HD)((ow,)), w_o,
        lambda shard: w_o.at[:, lane(shard * width, width)],
        lambda i, shard: w_o.at[:, lane(shard * width, width)],
    )
    turn_d = Turn(
        net, keep, at, by_row(units)((dw,)), w_d,
        lambda shard: w_d.at[:, lane(shard * width, width)],
        lambda i, shard: w_d.at[:, lane(shard * width, width)],
    )

    gain_slot = gains_all.at[:, lane(s * width, width)]
    gain_moves = [net.put(gains, gain_slot, (s ^ m, h)) for m in range(1, shards)]
    gain_own = keep.put(gains, gain_slot)
    strip = row(h * quarter, quarter)
    one = Spread(net, at, rows_one, quarter, True)
    one.start(tok.at[strip, :])
    own_rows = keep.put(tok, rows_one.at[chunk(0), :])
    own_strip = keep.put(tok.at[strip, :], own_x)
    for m in (3, 2, 1):
        for i in range(3):
            turn_qkv.start(m, i)
    for i in range(3):
        turn_qkv.mine(i)
    for m in (3, 2, 1):
        turn_o.start(m, 0)
    turn_o.mine(0)
    for m in (3, 2, 1):
        turn_d.start(m, 0)
    turn_d.mine(0)
    grad = Spread(net, at, rows_cot, quarter, True)
    grad.start(cot.at[strip, :])
    own_cot = keep.put(cot, rows_cot.at[chunk(0), :])
    turn_gu.mine(0)
    turn_gu.mine(1)
    gain_part[...] = jnp.zeros_like(gain_part)

    gain_own.wait()
    for copy in gain_moves:
        copy.wait_recv()

    def norm_one(m):
        def some(i, carry):
            rows = row((g ^ m) * count + i * 64, 64)
            values = rows_one[rows, :].astype(F32)
            inverse = lax.rsqrt(mean_square(values) + epsilon)
            rows_one[rows, :] = (values * inverse * gains_all[0:1, :]).astype(BF16)
            return carry

        lax.fori_loop(0, count // 64, some, 0)

    own_rows.wait()
    own_strip.wait()
    norm_one(0)
    one.arrive(1)
    one.arrive(2)
    one.second(1)
    one.second(2)
    one.arrive(3)
    for m in (3, 2, 1):
        turn_qkv.pass_on(m)
    one.second(3)
    for m in (1, 2, 3):
        one.ready(m)
        one.sent(m)
        norm_one(m)
    for m in (3, 2, 1):
        turn_o.pass_on(m)
    turn_qkv.ready()
    pair_moves = {}
    for m in (0, 1, 2, 3):
        rows = chunk(m)
        heads = dot(rows_one[rows, :], w_qkv[...])
        cos_part, sin_part = cosines[rows, :], sines[rows, :]
        queries[rows, :] = turned(heads[:, :HD], cos_part, sin_part).astype(BF16)
        place = row(((g ^ m) * ranks + r) * count, count)
        pairs[place, :HD] = turned(heads[:, HD : 2 * HD], cos_part, sin_part).astype(BF16)
        pairs[place, HD:] = heads[:, 2 * HD :].astype(BF16)
        pair_moves[m] = net.put(pairs.at[place, :], pairs.at[place, :], at.beside())
    for m in (0, 1, 2, 3):
        pair_moves[m].wait_recv()
    turn_o.ready()
    span = ranks * count

    def weights_of(m, j, query):
        keys = pairs[row(j * span, span), :HD]
        scores = dot_nt(query, keys) * score_scale - score_shift
        q_place = ((g ^ m) * ranks + r) * count + lax.broadcasted_iota(jnp.int32, (count, span), 0)
        k_place = j * span + lax.broadcasted_iota(jnp.int32, (count, span), 1)
        return jnp.where(k_place <= q_place, jax.nn.sigmoid(scores), 0.0)

    def attend(m, collect):
        rows = chunk(m)
        query = queries[rows, :]

        def step(j, total):
            weight = weights_of(m, j, query).astype(BF16)
            return total + dot(weight, pairs[row(j * span, span), HD:])

        total = lax.fori_loop(0, (g ^ m) + 1, step, jnp.zeros((count, HD), F32))
        low = total.astype(BF16)
        mix[rows, :] = low
        collect.part[rows, :] = dot(low, w_o[...]).astype(BF16)

    first = Collect(net, at, (part_a, near_a, xin_a, zin_a), quarter)
    attend(3, first)
    first.first(3)
    attend(2, first)
    first.first(2)
    first.second(3)
    attend(1, first)
    first.first(1)
    first.second(2)
    first.third(3)
    turn_gu.start(3, 0)
    attend(0, first)
    first.first(0)
    first.second(1)
    first.third(2)
    turn_gu.start(2, 0)
    first.second(0)
    first.third(1)
    turn_gu.start(1, 0)
    for m in (3, 2, 1):
        turn_d.pass_on(m)
    total = first.last()
    hidden_rows = own_x[...].astype(F32) + total
    hidden[...] = hidden_rows
    inverse = lax.rsqrt(mean_square(hidden_rows) + epsilon)
    two = Spread(net, at, rows_two, quarter, False)
    mine = row((g * 4 + h) * quarter, quarter)
    rows_two[mine, :] = (hidden_rows * inverse * gains_all[1:2, :]).astype(BF16)
    two.start(rows_two.at[mine, :])
    turn_gu.start(3, 1)
    turn_gu.start(2, 1)
    turn_gu.start(1, 1)
    grad.arrive(1)
    grad.arrive(2)
    grad.second(1)
    two.second(0)
    two.arrive(1)
    two.arrive(2)
    grad.second(2)
    grad.arrive(3)
    two.second(1)
    two.second(2)
    two.arrive(3)
    grad.second(3)
    two.second(3)
    turn_d.ready()
    own_cot.wait()
    for m in (0, 1, 2, 3):
        grad.ready(m)
        dmixed[chunk(m), :] = dot_nt(rows_cot[chunk(m), :], w_d[...])
    for m in (3, 2, 1):
        turn_gu.pass_on(m)
    for m in (0, 1, 2, 3):
        two.ready(m)
    turn_gu.ready()

    def feed(m, collect):
        rows = chunk(m)
        both = dot(rows_two[rows, :], w_gu[...])
        gate, up = both[:, :units], both[:, units:]
        sig = jax.nn.sigmoid(gate)
        act = gate * sig
        mixed[rows, :] = (act * up).astype(BF16)
        back = dmixed[rows, :]
        dgu[rows, :units] = (back * up * sig * (1.0 + gate * (1.0 - sig))).astype(BF16)
        dgu[rows, units:] = (back * act).astype(BF16)
        collect.part[rows, :] = dot_nt(dgu[rows, :], w_gu[...]).astype(BF16)

    first.sent()
    second = Collect(net, at, (part_a, near_a, xin_a, zin_a), quarter)
    feed(3, second)
    second.first(3)
    feed(2, second)
    second.first(2)
    second.second(3)
    feed(1, second)
    second.first(1)
    second.second(2)
    second.third(3)
    feed(0, second)
    second.first(0)
    second.second(1)
    second.third(2)
    turn_gu.sent()
    turn_d.sent()

    moves_gu, moves_d, moves_qkv, moves_o = {}, {}, {}, {}

    def grads_gu(m):
        d = g ^ m
        for k in (1, 0):
            shard = d * ranks + (r ^ k)
            w_gu[shard_rows(shard), :] = dot_tn(rows_two[:, lane(shard * width, width)], dgu[...]).astype(BF16)
            if k:
                moves_gu[m] = net.put(w_gu.at[shard_rows(shard), :], in_gu.at[d], at.beside())

    def grads_d(m):
        d = g ^ m
        for k in (1, 0):
            shard = d * ranks + (r ^ k)
            columns = lane(shard * width, width)
            w_d[:, columns] = dot_tn(mixed[...], rows_cot[:, columns]).astype(BF16)
            if k:
                moves_d[m] = net.put(w_d.at[:, columns], in_d.at[d], at.beside())

    grads_gu(3)
    second.second(0)
    second.third(1)
    for m in (0, 1, 2, 3):
        part_b[chunk(m), :] = dot(mixed[chunk(m), :], w_d[...]).astype(BF16)
    dn_two = second.last()
    hidden_rows = hidden[...]
    inverse = lax.rsqrt(mean_square(hidden_rows) + epsilon)
    scaled = dn_two * gains_all[1:2, :]
    gain_part[1:2, :] = jnp.sum(dn_two * hidden_rows * inverse, axis=0, keepdims=True)
    back = inverse * scaled - hidden_rows * (inverse * inverse * inverse) * jnp.mean(
        scaled * hidden_rows, axis=1, keepdims=True
    )
    dh_rows = rows_cot[mine, :].astype(F32) + back
    dhidden[...] = dh_rows
    three = Spread(net, at, rows_dh, quarter, False)
    rows_dh[mine, :] = dh_rows.astype(BF16)
    three.start(rows_dh.at[mine, :])
    grads_gu(2)
    grads_gu(1)
    three.second(0)
    three.arrive(1)
    three.arrive(2)
    grads_gu(0)
    final = []

    def give(source, target, m):
        if m:
            final.append(net.put(source, target, at.along(m)))
        else:
            final_own.append(keep.put(source, target))

    final_own = []

    def sums_gu(m):
        d = g ^ m
        rows = shard_rows(d * ranks + r)
        moves_gu[m].wait_recv()
        w_gu[rows, :] = (w_gu[rows, :].astype(F32) + in_gu[d].astype(F32)).astype(BF16)
        for i, out in enumerate((g_out, u_out)):
            give(w_gu.at[rows, i * units : (i + 1) * units], out.at[:, lane(g * units, units)], m)

    def sums_d(m):
        d = g ^ m
        columns = lane((d * ranks + r) * width, width)
        moves_d[m].wait_recv()
        w_d[:, columns] = (w_d[:, columns].astype(F32) + in_d[d].astype(F32)).astype(BF16)
        give(w_d.at[:, columns], d_out.at[row(g * units, units), :], m)

    three.second(1)
    three.second(2)
    three.arrive(3)
    three.second(3)
    sums_gu(3)
    for m in (3, 2, 1, 0):
        grads_d(m)
    out_sum = Collect(net, at, (part_b, near_b, xin_b, zin_b), quarter)
    for m in (3, 2, 1, 0):
        out_sum.first(m)
    sums_gu(2)
    sums_gu(1)
    sums_gu(0)

    accum[...] = jnp.zeros_like(accum)

    def attend_back(m):
        rows = chunk(m)
        query = queries[rows, :]
        dm = dot_nt(rows_dh[rows, :], w_o[...]).astype(BF16)
        dmix[rows, :] = dm

        def step(j, total):
            block = row(j * span, span)
            weight = weights_of(m, j, query)
            dweight = dot_nt(dm, pairs[block, HD:])
            dscore = (dweight * weight * (1.0 - weight)).astype(BF16)
            accum[block, HD:] += dot_tn(weight.astype(BF16), dm)
            accum[block, :HD] += dot_tn(dscore, query)
            return total + dot(dscore, pairs[block, :HD])

        total = lax.fori_loop(0, (g ^ m) + 1, step, jnp.zeros((count, HD), F32))
        dqkv[rows, :HD] = turned(total * score_scale, cosines[rows, :], -sines[rows, :]).astype(BF16)

    for m in (0, 1, 2, 3):
        three.ready(m)
        attend_back(m)
        out_sum.second((3, 2, 1, 0)[m])
    pair_back = {}
    for m in (3, 2, 1, 0):
        d = g ^ m
        rows = row((d * ranks + (r ^ 1)) * count, count)
        pair_send[d] = accum[rows, :].astype(BF16)
        pair_back[m] = net.put(pair_send.at[d], pair_in.at[d], at.beside())
    turn_o.sent()
    for k in (1, 0):
        for m in (3, 2, 1, 0):
            d = g ^ m
            columns = lane((d * ranks + (r ^ k)) * width, width)
            w_o[:, columns] = dot_tn(mix[...], rows_dh[:, columns]).astype(BF16)
            if k:
                moves_o[m] = net.put(w_o.at[:, columns], in_o.at[d], at.beside())
    for m in (3, 2, 1, 0):
        sums_d(m)
    out_sum.third(3)
    out_sum.third(2)
    out_sum.third(1)
    second.sent()
    third = Collect(net, at, (part_a, near_a, xin_a, zin_a), quarter)

    def back_one(m):
        d = g ^ m
        rows = chunk(m)
        pair_back[m].wait_recv()
        both = accum[row((d * ranks + r) * count, count), :] + pair_in[d].astype(F32)
        dqkv[rows, HD : 2 * HD] = turned(both[:, :HD] * score_scale, cosines[rows, :], -sines[rows, :]).astype(BF16)
        dqkv[rows, 2 * HD :] = both[:, HD:].astype(BF16)
        third.part[rows, :] = dot_nt(dqkv[rows, :], w_qkv[...]).astype(BF16)

    back_one(3)
    third.first(3)
    back_one(2)
    third.first(2)
    third.second(3)
    back_one(1)
    third.first(1)
    third.second(2)
    third.third(3)
    back_one(0)
    third.first(0)
    third.second(1)
    third.third(2)
    third.second(0)
    third.third(1)
    turn_qkv.sent()

    def grads_qkv(m):
        d = g ^ m
        for k in (1, 0):
            shard = d * ranks + (r ^ k)
            w_qkv[shard_rows(shard), :] = dot_tn(rows_one[:, lane(shard * width, width)], dqkv[...]).astype(BF16)
            if k:
                moves_qkv[m] = net.put(w_qkv.at[shard_rows(shard), :], in_qkv.at[d], at.beside())

    for m in (3, 2, 1, 0):
        grads_qkv(m)
    for m in (3, 2, 1, 0):
        d = g ^ m
        columns = lane((d * ranks + r) * width, width)
        moves_o[m].wait_recv()
        w_o[:, columns] = (w_o[:, columns].astype(F32) + in_o[d].astype(F32)).astype(BF16)
        give(w_o.at[:, columns], o_out.at[row(g * HD, HD), :], m)
    result_own[...] = (hidden[...] + out_sum.last()).astype(BF16)
    ends = []

    def share(source, target):
        place = target.at[strip, :]
        final_own.append(keep.put(source, place))
        final.append(net.put(source, place, at.near()))
        ends.append((net.put(source, place, at.across()), target))

    def relay():
        copy, target = ends.pop()
        copy.wait_recv()
        block = target.at[row((h ^ 2) * quarter, quarter), :]
        final.append(net.put(block, block, at.near()))

    share(result_own, result_out)
    for m in (3, 2, 1, 0):
        d = g ^ m
        rows = shard_rows(d * ranks + r)
        moves_qkv[m].wait_recv()
        w_qkv[rows, :] = (w_qkv[rows, :].astype(F32) + in_qkv[d].astype(F32)).astype(BF16)
        for i, out in enumerate((q_out, k_out, v_out)):
            give(w_qkv.at[rows, i * HD : (i + 1) * HD], out.at[:, lane(g * HD, HD)], m)
    dn_one = third.last()
    values = own_x[...].astype(F32)
    inverse = lax.rsqrt(mean_square(values) + epsilon)
    scaled = dn_one * gains_all[0:1, :]
    gain_part[0:1, :] = jnp.sum(dn_one * values * inverse, axis=0, keepdims=True)
    back = inverse * scaled - values * (inverse * inverse * inverse) * jnp.mean(
        scaled * values, axis=1, keepdims=True
    )
    gain_moves = [
        net.put(gain_part.at[:, lane((s ^ m) * width, width)], gain_in.at[m - 1], (s ^ m, h))
        for m in range(1, shards)
    ]
    rows_own[...] = (dhidden[...] + back).astype(BF16)
    relay()
    share(rows_own, rows_out)
    total = gain_part[:, lane(s * width, width)]
    for m in range(1, shards):
        gain_moves[m - 1].wait_recv()
        total += gain_in[m - 1]
    gain_mid[...] = total
    gain_ends = [net.put(gain_mid, gain_near.at[m - 1], (s, h ^ m)) for m in range(1, 4)]
    relay()
    for m in range(1, 4):
        gain_ends[m - 1].wait_recv()
        total += gain_near[m - 1]
    gains_out[...] = total
    for copy in final:
        copy.wait_recv()
    net.sent()
    for copy in final_own:
        copy.wait()


def rows_plan(
    groups,
    ranks,
    tokens,
    attn_gain,
    query_weight,
    key_weight,
    value_weight,
    out_weight,
    mlp_gain,
    gate_weight,
    up_weight,
    down_weight,
    cotangent,
):
    count, depth = tokens.shape
    shards = groups * ranks
    quarter = count // 4
    width = query_weight.shape[0]
    units = gate_weight.shape[1] // groups
    total_rows = count * shards
    here = groups * count
    r = lax.axis_index("seq") % ranks
    gains = jnp.concatenate([attn_gain[None], mlp_gain[None], jnp.zeros((6, width), BF16)]).astype(F32)
    places = (
        (jnp.arange(groups, dtype=jnp.int32) * ranks + r)[:, None] * count
        + jnp.arange(count, dtype=jnp.int32)[None, :]
    ).reshape(here)
    lanes = jnp.arange(HD, dtype=jnp.int32)
    half = HD // 2
    frequency = jnp.exp((lanes % half).astype(F32) * (-math.log(10000.0) / half))
    angles = places.astype(F32)[:, None] * frequency[None, :]
    cosines = jnp.cos(angles)
    sines = jnp.sin(angles) * jnp.where(lanes < half, -1.0, 1.0)[None, :]
    ins = (tokens, cotangent, gains, query_weight, key_weight, value_weight, out_weight, gate_weight, up_weight, down_weight, cosines, sines)
    shape = jax.ShapeDtypeStruct
    hbm, vmem = pl.BlockSpec(memory_space=pl.ANY), pl.BlockSpec(memory_space=pltpu.VMEM)
    owners = (query_weight, key_weight, value_weight, out_weight, gate_weight, up_weight, down_weight)
    outs = [
        shape((count, depth), BF16),
        shape((count, depth), BF16),
        shape((8, width), F32),
        *(shape(w.shape, BF16) for w in owners),
    ]

    def low(*extent):
        return pltpu.VMEM(extent, BF16)

    def full(*extent):
        return pltpu.VMEM(extent, F32)

    def collector():
        return [
            low(here, depth),
            low(groups, 2, quarter, depth),
            low(groups, quarter, depth),
            low(3, quarter, depth),
        ]

    scratch = [
        full(8, depth),
        low(here, depth), low(here, depth), low(here, depth), low(here, depth),
        low(depth, 3 * HD), low(HD, depth), low(depth, 2 * units), low(units, depth),
        low(here, HD), low(total_rows, 2 * HD), low(here, HD), low(here, HD), low(here, 3 * HD),
        full(total_rows, 2 * HD), low(groups, count, 2 * HD), low(groups, count, 2 * HD),
        low(here, units), low(here, 2 * units), full(here, units),
        low(quarter, depth), full(quarter, depth), full(quarter, depth),
        *collector(), *collector(),
        low(groups, width, 2 * units), low(groups, units, width), low(groups, width, 3 * HD), low(groups, HD, width),
        full(8, depth), full(shards - 1, 8, width), full(8, width), full(3, 8, width),
        low(quarter, depth), low(quarter, depth),
        pltpu.SemaphoreType.DMA((320,)), pltpu.SemaphoreType.DMA((320,)), pltpu.SemaphoreType.DMA((48,)),
    ]
    result, rows_grad, gain_grads, *grads = pl.pallas_call(
        functools.partial(layer_body, groups, ranks),
        out_shape=outs,
        in_specs=[hbm] * 10 + [vmem] * 2,
        out_specs=[hbm, hbm, vmem] + [hbm] * 7,
        scratch_shapes=scratch,
        compiler_params=pltpu.CompilerParams(
            collective_id=1, has_side_effects=True, vmem_limit_bytes=VMEM_LIMIT
        ),
    )(*ins)
    grads = [w.astype(F32) for w in grads]
    return (result, rows_grad, gain_grads[0], *grads[:4], gain_grads[1], *grads[4:])


def on_device(tokens, attn_gain, query_weight, *rest):
    groups = query_weight.shape[1] // HD
    ranks = lax.axis_size("seq") // groups
    fits = lax.axis_size("head") == 4 and groups == 4 and ranks == 2 and query_weight.shape[0] % 128 == 0
    plan = functools.partial(rows_plan, groups, ranks) if fits else gathered_weights
    return plan(tokens, attn_gain, query_weight, *rest)


def solution(mesh):
    in_specs = (
        P("seq", None),
        P("seq"),
        P("seq", "head"),
        P("seq", "head"),
        P("seq", "head"),
        P("head", "seq"),
        P("seq"),
        P("seq", "head"),
        P("seq", "head"),
        P("head", "seq"),
        P("seq", None),
    )
    out_specs = (
        P("seq", None),
        P("seq", None),
        P("seq"),
        P("seq", "head"),
        P("seq", "head"),
        P("seq", "head"),
        P("head", "seq"),
        P("seq"),
        P("seq", "head"),
        P("seq", "head"),
        P("head", "seq"),
    )
    return jax.shard_map(
        on_device, mesh=mesh, in_specs=in_specs, out_specs=out_specs, check_vma=False
    )
```

```python
import functools
import math

import jax
import jax.numpy as jnp
from jax import lax
from jax.experimental import pallas as pl
from jax.experimental.pallas import tpu as pltpu
from jax.sharding import PartitionSpec as P

MESH = pl.DeviceIdType.MESH
F32, BF16 = jnp.float32, jnp.bfloat16

HD = 128


epsilon = 1e-05
block_limit = 512
VMEM_LIMIT = 63 * 2**20


def tables(offset, length, half_width):
    places = (offset + jnp.arange(length, dtype=jnp.int32)).astype(jnp.float32)
    frequency = jnp.exp(
        jnp.arange(half_width, dtype=jnp.float32) * (-math.log(10000.0) / half_width)
    )
    angles = places[:, None] * frequency[None, :]
    return (jnp.cos(angles)[:, None, :], jnp.sin(angles)[:, None, :])


def rotary(values, cos_table, sin_table):
    half_width = values.shape[-1] // 2
    front = values[..., :half_width]
    back_half = values[..., half_width:]
    return jnp.concatenate(
        [front * cos_table - back_half * sin_table, back_half * cos_table + front * sin_table],
        axis=-1,
    )


def unrotary(gradient, cos_table, sin_table):
    half_width = gradient.shape[-1] // 2
    front = gradient[..., :half_width]
    back_half = gradient[..., half_width:]
    return jnp.concatenate(
        [front * cos_table + back_half * sin_table, back_half * cos_table - front * sin_table],
        axis=-1,
    )


def norm_back(values, inverse, gain_vector, upstream):
    scaled = upstream * gain_vector
    gain_grad = jnp.sum(upstream * values * inverse, axis=0)
    value_grad = inverse * scaled - values * inverse**3 * jnp.mean(
        scaled * values, axis=1, keepdims=True
    )
    return (value_grad, gain_grad)


def gathered_weights(
    tokens,
    attn_gain,
    query_weight,
    key_weight,
    value_weight,
    out_weight,
    mlp_gain,
    gate_weight,
    up_weight,
    down_weight,
    cotangent,
):
    row_count = tokens.shape[0]
    total_rows = row_count * lax.axis_size("seq")
    row_start = lax.axis_index("seq") * row_count
    local_width = query_weight.shape[1]
    local_heads = local_width // HD
    score_scale = 1.0 / math.sqrt(HD)
    score_shift = math.log(total_rows)
    block_rows = math.gcd(total_rows, block_limit)
    block_count = total_rows // block_rows
    attn_gain_full, query_full, key_full, value_full, out_full = (
        lax.all_gather(attn_gain, "seq", axis=0, tiled=True),
        lax.all_gather(query_weight, "seq", axis=0, tiled=True),
        lax.all_gather(key_weight, "seq", axis=0, tiled=True),
        lax.all_gather(value_weight, "seq", axis=0, tiled=True),
        lax.all_gather(out_weight, "seq", axis=1, tiled=True),
    )
    mlp_gain_full, gate_full, up_full, down_full = (
        lax.all_gather(mlp_gain, "seq", axis=0, tiled=True),
        lax.all_gather(gate_weight, "seq", axis=0, tiled=True),
        lax.all_gather(up_weight, "seq", axis=0, tiled=True),
        lax.all_gather(down_weight, "seq", axis=1, tiled=True),
    )
    token_values = tokens.astype(jnp.float32)
    inverse_one = lax.rsqrt(jnp.mean(token_values * token_values, axis=1, keepdims=True) + epsilon)
    normed_one = (token_values * inverse_one * attn_gain_full.astype(jnp.float32)).astype(
        jnp.bfloat16
    )
    query_pre = jnp.dot(normed_one, query_full, preferred_element_type=jnp.float32)
    key_pre = jnp.dot(normed_one, key_full, preferred_element_type=jnp.float32)
    value_rows = (
        jnp.dot(normed_one, value_full, preferred_element_type=jnp.float32)
        .astype(jnp.bfloat16)
        .reshape(row_count, local_heads, HD)
    )
    cos_table, sin_table = tables(row_start, row_count, HD // 2)
    query_rows = (
        rotary(query_pre.reshape(row_count, local_heads, HD), cos_table, sin_table)
        .astype(jnp.bfloat16)
        .reshape(row_count, local_width)
    )
    key_rows = rotary(key_pre.reshape(row_count, local_heads, HD), cos_table, sin_table).astype(
        jnp.bfloat16
    )
    all_queries = lax.all_gather(query_rows, "seq", axis=0, tiled=True)
    key_places = row_start + jnp.arange(row_count, dtype=jnp.int32)

    def weights_for(query_block, block_start):
        scores = (
            jnp.einsum("qhd,khd->hqk", query_block, key_rows, preferred_element_type=jnp.float32)
            * score_scale
            - score_shift
        )
        query_places = block_start + jnp.arange(query_block.shape[0], dtype=jnp.int32)
        visible = key_places[None, :] <= query_places[:, None]
        return jnp.where(visible[None], jax.nn.sigmoid(scores), 0.0)

    step_rows = math.gcd(row_count * lax.axis_size("seq"), block_limit)
    step_count = row_count * lax.axis_size("seq") // step_rows
    picked = all_queries.reshape(step_count, step_rows, local_heads, HD)
    starts = jnp.arange(step_count, dtype=jnp.int32) * step_rows

    def one_block(packed):
        query_block, block_start = packed
        weights = weights_for(query_block, block_start).astype(jnp.bfloat16)
        return jnp.einsum(
            "hqk,khd->qhd", weights, value_rows, preferred_element_type=jnp.float32
        ).reshape(step_rows, local_width)

    attn_mix = lax.psum_scatter(
        lax.map(one_block, (picked, starts)).reshape(row_count * lax.axis_size("seq"), local_width),
        "seq",
        scatter_dimension=0,
        tiled=True,
    ).astype(jnp.bfloat16)
    attn_branch = lax.psum(jnp.dot(attn_mix, out_full, preferred_element_type=jnp.float32), "head")
    hidden = token_values + attn_branch
    inverse_two = lax.rsqrt(jnp.mean(hidden * hidden, axis=1, keepdims=True) + epsilon)
    normed_two = (hidden * inverse_two * mlp_gain_full.astype(jnp.float32)).astype(jnp.bfloat16)
    gate_pre = jnp.dot(normed_two, gate_full, preferred_element_type=jnp.float32)
    up_pre = jnp.dot(normed_two, up_full, preferred_element_type=jnp.float32)
    gate_act = jax.nn.silu(gate_pre)
    mixed = (gate_act * up_pre).astype(jnp.bfloat16)
    mlp_branch = lax.psum(
        jnp.dot(mixed, down_full, preferred_element_type=jnp.float32).astype(jnp.bfloat16), "head"
    ).astype(jnp.float32)
    result = (hidden + mlp_branch).astype(jnp.bfloat16)
    kept_weights = (
        lax.all_gather(attn_gain, "seq", axis=0, tiled=True),
        lax.all_gather(query_weight, "seq", axis=0, tiled=True),
        lax.all_gather(key_weight, "seq", axis=0, tiled=True),
        lax.all_gather(value_weight, "seq", axis=0, tiled=True),
        lax.all_gather(out_weight, "seq", axis=1, tiled=True),
        lax.all_gather(mlp_gain, "seq", axis=0, tiled=True),
        lax.all_gather(gate_weight, "seq", axis=0, tiled=True),
        lax.all_gather(up_weight, "seq", axis=0, tiled=True),
        lax.all_gather(down_weight, "seq", axis=1, tiled=True),
    )
    (
        attn_gain_back,
        query_back,
        key_back,
        value_back,
        out_back,
        mlp_gain_back,
        gate_back,
        up_back,
        down_back,
    ) = kept_weights
    attn_gain_f = attn_gain_back.astype(jnp.float32)
    mlp_gain_f = mlp_gain_back.astype(jnp.float32)
    grad_values = cotangent.astype(jnp.float32)
    grad_down = jnp.einsum("tf,td->fd", mixed, cotangent, preferred_element_type=jnp.float32)
    dmixed = jnp.einsum("td,fd->tf", cotangent, down_back, preferred_element_type=jnp.float32)
    gate_sig = jax.nn.sigmoid(gate_pre)
    dgate = (dmixed * up_pre * gate_sig * (1.0 + gate_pre * (1.0 - gate_sig))).astype(jnp.bfloat16)
    dup = (dmixed * gate_act).astype(jnp.bfloat16)
    grad_gate = jnp.einsum("tk,tf->kf", normed_two, dgate, preferred_element_type=jnp.float32)
    grad_up = jnp.einsum("tk,tf->kf", normed_two, dup, preferred_element_type=jnp.float32)
    dnormed_two = lax.psum(
        jnp.einsum("tf,kf->tk", dgate, gate_back, preferred_element_type=jnp.float32)
        + jnp.einsum("tf,kf->tk", dup, up_back, preferred_element_type=jnp.float32),
        "head",
    )
    dhidden_norm, grad_mlp_gain = norm_back(hidden, inverse_two, mlp_gain_f, dnormed_two)
    dhidden = grad_values + dhidden_norm
    mlp_sums = (grad_mlp_gain, grad_gate, grad_up, grad_down)
    dhidden_low = dhidden.astype(jnp.bfloat16)
    grad_out = jnp.einsum("tc,td->cd", attn_mix, dhidden_low, preferred_element_type=jnp.float32)
    dmix = jnp.einsum(
        "td,cd->tc", dhidden_low, out_back, preferred_element_type=jnp.float32
    ).astype(jnp.bfloat16)
    all_dmix = lax.all_gather(dmix, "seq", axis=0, tiled=True)

    def backward_block(carry, packed):
        key_accum, value_accum = carry
        query_block, grad_block, block_start = packed
        weights = weights_for(query_block, block_start)
        grad_weights = jnp.einsum(
            "qhd,khd->hqk", grad_block, value_rows, preferred_element_type=jnp.float32
        )
        grad_scores = (grad_weights * weights * (1.0 - weights)).astype(jnp.bfloat16)
        value_accum = value_accum + jnp.einsum(
            "hqk,qhd->khd",
            weights.astype(jnp.bfloat16),
            grad_block,
            preferred_element_type=jnp.float32,
        )
        key_accum = key_accum + jnp.einsum(
            "hqk,qhd->khd", grad_scores, query_block, preferred_element_type=jnp.float32
        )
        query_part = (
            jnp.einsum("hqk,khd->qhd", grad_scores, key_rows, preferred_element_type=jnp.float32)
            * score_scale
        )
        return ((key_accum, value_accum), query_part.reshape(block_rows, local_width))

    zero_rows = jnp.zeros((row_count, local_heads, HD), jnp.float32)
    block_starts = jnp.arange(block_count, dtype=jnp.int32) * block_rows
    (key_accum, value_accum), query_parts = lax.scan(
        backward_block,
        (zero_rows, zero_rows),
        (
            all_queries.reshape(block_count, block_rows, local_heads, HD),
            all_dmix.reshape(block_count, block_rows, local_heads, HD),
            block_starts,
        ),
    )
    query_sum = lax.psum_scatter(
        query_parts.reshape(total_rows, local_width), "seq", scatter_dimension=0, tiled=True
    )
    dquery_pre = (
        unrotary(query_sum.reshape(row_count, local_heads, HD), cos_table, sin_table)
        .reshape(row_count, local_width)
        .astype(jnp.bfloat16)
    )
    dkey_pre = (
        unrotary(key_accum * score_scale, cos_table, sin_table)
        .reshape(row_count, local_width)
        .astype(jnp.bfloat16)
    )
    dvalue = value_accum.reshape(row_count, local_width).astype(jnp.bfloat16)
    grad_query = jnp.einsum("tk,tc->kc", normed_one, dquery_pre, preferred_element_type=jnp.float32)
    grad_key = jnp.einsum("tk,tc->kc", normed_one, dkey_pre, preferred_element_type=jnp.float32)
    grad_value = jnp.einsum("tk,tc->kc", normed_one, dvalue, preferred_element_type=jnp.float32)
    dnormed_one = lax.psum(
        jnp.einsum("tc,kc->tk", dquery_pre, query_back, preferred_element_type=jnp.float32)
        + jnp.einsum("tc,kc->tk", dkey_pre, key_back, preferred_element_type=jnp.float32)
        + jnp.einsum("tc,kc->tk", dvalue, value_back, preferred_element_type=jnp.float32),
        "head",
    )
    dinput_norm, grad_attn_gain = norm_back(token_values, inverse_one, attn_gain_f, dnormed_one)
    input_grad = (dhidden + dinput_norm).astype(jnp.bfloat16)
    every_sum = (
        lax.psum_scatter(grad_attn_gain, "seq", scatter_dimension=0, tiled=True),
        lax.psum_scatter(grad_query, "seq", scatter_dimension=0, tiled=True),
        lax.psum_scatter(grad_key, "seq", scatter_dimension=0, tiled=True),
        lax.psum_scatter(grad_value, "seq", scatter_dimension=0, tiled=True),
        lax.psum_scatter(grad_out, "seq", scatter_dimension=1, tiled=True),
        lax.psum_scatter(grad_mlp_gain, "seq", scatter_dimension=0, tiled=True),
        lax.psum_scatter(grad_gate, "seq", scatter_dimension=0, tiled=True),
        lax.psum_scatter(grad_up, "seq", scatter_dimension=0, tiled=True),
        lax.psum_scatter(grad_down, "seq", scatter_dimension=1, tiled=True),
    )
    attn_sums = every_sum[:5]
    mlp_sums = every_sum[5:]
    return (
        result,
        input_grad,
        attn_sums[0],
        attn_sums[1],
        attn_sums[2],
        attn_sums[3],
        attn_sums[4],
        mlp_sums[0],
        mlp_sums[1],
        mlp_sums[2],
        mlp_sums[3],
    )


class Net:
    def __init__(self, send, receive):
        self.send, self.receive, self.count, self.lots = send, receive, 0, []

    def lot(self, size, describe):
        return Lot(self, size, describe)

    def finish(self):
        for lot in self.lots:
            for j in sorted(lot.open):
                lot.sent(j)


class Lot:
    def __init__(self, net, size, describe):
        self.net, self.base, self.describe, self.open = net, net.count, describe, set()
        net.count += size
        net.lots.append(self)

    def copy(self, j):
        source, target, device = self.describe(j)
        return pltpu.make_async_remote_copy(
            src_ref=source,
            dst_ref=target,
            send_sem=self.net.send.at[self.base + j],
            recv_sem=self.net.receive.at[self.base + j],
            device_id=device,
            device_id_type=MESH,
        )

    def start(self, j):
        self.copy(j).start()
        if isinstance(j, int):
            self.open.add(j)

    def arrived(self, j):
        self.copy(j).wait_recv()

    def sent(self, j):
        if j in self.open:
            self.open.remove(j)
            self.copy(j).wait_send()


class Keep:
    def __init__(self, sems):
        self.sems, self.count = sems, 0

    def put(self, source, target):
        copy = pltpu.make_async_copy(source, target, self.sems.at[self.count])
        self.count += 1
        copy.start()
        return copy


class Where:
    def __init__(self, groups, ranks):
        self.s, self.h = lax.axis_index("seq"), lax.axis_index("head")
        self.g, self.r = self.s // ranks, self.s % ranks
        self.groups, self.ranks = groups, ranks

    def along(self, m):
        return (self.s ^ (m * self.ranks), self.h)

    def beside(self):
        return (self.s ^ 1, self.h)

    def across(self):
        return (self.s, self.h ^ 2)

    def near(self):
        return (self.s, self.h ^ 1)


def lane(start, size):
    return pl.ds(pl.multiple_of(start, 128), size)


def row(start, size):
    return pl.ds(pl.multiple_of(start, size), size)


def each(count, step):
    def body(i, carry):
        step(i)
        return carry

    lax.fori_loop(0, count, body, 0)


class Spread:
    def __init__(self, net, at, buffer, quarter, own=None):
        self.at, self.buffer, self.quarter, self.shared = at, buffer, quarter, own is not None
        first = self.block(0, 0) if own is None else own
        self.z = net.lot(
            4,
            lambda m: (self.block(2, 0), self.block(2, 0), at.along(1))
            if m == 3
            else (first, self.block(0, 0), at.along(m)),
        )
        self.x = net.lot(4, lambda m: (self.block(m, 0), self.block(m, 0), at.across()))
        self.c = net.lot(4, lambda m: (self.block(m, 0), self.block(m, 0), at.near()))
        self.d = net.lot(4, lambda m: (self.block(m, 2), self.block(m, 2), at.near()))

    def block(self, m, k):
        at = self.at
        return self.buffer.at[row(((at.g ^ m) * 4 + (at.h ^ k)) * self.quarter, self.quarter), :]

    def pass_on(self, m):
        self.x.start(m)
        self.c.start(m)

    def start(self):
        self.z.start(2)
        self.z.start(1)
        if not self.shared:
            self.pass_on(0)

    def arrive(self, m):
        self.z.arrived(m)
        if m == 2:
            self.z.start(3)
        self.pass_on(m)

    def second(self, m):
        self.x.arrived(m)
        self.d.start(m)

    def ready(self, m):
        self.c.arrived(m)
        self.d.arrived(m)

    def sent(self, m):
        for lot in (self.x, self.c, self.d):
            lot.sent(m)
        if m == 2:
            self.z.sent(3)


class Collect:
    def __init__(self, net, at, refs, quarter, out):
        self.at, self.quarter, self.out = at, quarter, out
        self.part, self.near, self.xin, self.zin = refs
        self.a = net.lot(4, lambda m: (self.part.at[self.rows(m, 3), :], self.near.at[at.g ^ m, 1], at.near()))
        self.e = net.lot(4, lambda m: (self.part.at[self.rows(m, 1), :], self.near.at[at.g ^ m, 0], at.near()))
        self.b = net.lot(4, lambda m: (self.part.at[self.rows(m, 2), :], self.xin.at[at.g ^ m], at.across()))
        hops = {3: (0, 1), 2: (2, 2), 1: (1, 1)}
        self.z = net.lot(
            4, lambda m: (self.part.at[self.rows(m, 0), :], self.zin.at[hops[m][0]], at.along(hops[m][1]))
        )

    def rows(self, m, k):
        at = self.at
        return row(((at.g ^ m) * 4 + (at.h ^ k)) * self.quarter, self.quarter)

    def first(self, m):
        self.a.start(m)
        self.e.start(m)

    def slices(self, m, k, step):
        at = self.at
        start = ((at.g ^ m) * 4 + (at.h ^ k)) * self.quarter
        each(self.quarter // 16, lambda i: step(row(start + i * 16, 16), row(i * 16, 16)))

    def second(self, m):
        d = self.at.g ^ m
        self.a.arrived(m)

        def step(rows, few):
            total = self.part[rows, :].astype(F32) + self.near[d, 1, few, :].astype(F32)
            self.part[rows, :] = total.astype(BF16)

        self.slices(m, 2, step)
        self.b.start(m)

    def third(self, m):
        d = self.at.g ^ m
        self.e.arrived(m)
        self.b.arrived(m)
        if m == 2:
            self.z.arrived(3)

        def step(rows, few):
            total = self.part[rows, :].astype(F32) + self.near[d, 0, few, :].astype(F32)
            total += self.xin[d, few, :].astype(F32)
            if m == 2:
                total += self.zin[0, few, :].astype(F32)
            if m:
                self.part[rows, :] = total.astype(BF16)
            else:
                self.out[few, :] = total

        self.slices(m, 0, step)
        if m:
            self.z.start(m)

    def last(self):
        self.third(0)
        self.z.arrived(1)
        self.z.arrived(2)

    def total(self, few):
        return self.out[few, :] + self.zin[1, few, :].astype(F32) + self.zin[2, few, :].astype(F32)

    def produce(self, work):
        def step(i):
            m = 3 - i
            work(m)
            self.first(m)

            @pl.when(i > 0)
            def _():
                self.second(m + 1)

        each(4, step)
        for lot in (self.a, self.e):
            lot.open.update(range(4))
        self.b.open.update((1, 2, 3))

    def sent(self):
        for m in range(4):
            for lot in (self.a, self.e, self.b, self.z):
                lot.sent(m)


class Turn:
    def __init__(self, net, keep, at, source, view, blocks):
        self.keep, self.at, self.source, self.view, self.blocks = keep, at, source, view, blocks
        n = sum(len(items) for items, _ in blocks)
        self.n = n
        self.z = net.lot(
            4 * n,
            lambda j: (source(j % n, at.g ^ (j // n)), view(j % n, at.s), at.along(j // n)),
        )
        self.o = net.lot(n, lambda i: (source(i, at.g), view(i, at.s), at.beside()))
        self.y = net.lot(4 * len(blocks), self.sent_on)
        self.own = {}

    def sent_on(self, j):
        at = self.at
        block = self.blocks[j // 4][1](at.s ^ (j % 4 * at.ranks))
        return (block, block, at.beside())

    def start(self, m, b=0):
        for i in self.blocks[b][0]:
            self.z.start(m * self.n + i)

    def mine(self, b=0):
        at = self.at
        for i in self.blocks[b][0]:
            self.own[i] = self.keep.put(self.source(i, at.g), self.view(i, at.s))
            self.o.start(i)

    def pass_on(self, m, b=0):
        for i in self.blocks[b][0]:
            self.z.arrived(m * self.n + i)
        self.y.start(b * 4 + m)

    def ready(self, b=0):
        for i in self.blocks[b][0]:
            self.own[i].wait()
            self.o.arrived(i)
        for m in (1, 2, 3):
            self.y.arrived(b * 4 + m)

    def sent(self, b=0):
        for m in (1, 2, 3):
            self.y.sent(b * 4 + m)


def dot(a, b):
    return jnp.dot(a, b, preferred_element_type=F32)


def dot_nt(a, b):
    return lax.dot_general(a, b, (((1,), (1,)), ((), ())), preferred_element_type=F32)


def dot_tn(a, b):
    return lax.dot_general(a, b, (((0,), (0,)), ((), ())), preferred_element_type=F32)


def turned(values, cos_table, sin_table):
    return values * cos_table + pltpu.roll(values, HD // 2, 1) * sin_table


def mean_square(values):
    return jnp.mean(values * values, axis=1, keepdims=True)


def layer_body(groups, ranks, *refs):
    (tok, cot, gains, qw, kw, vw, ow, gw, uw, dw, cosines, sines) = refs[:12]
    (result_out, rows_out, gains_out, q_out, k_out, v_out, o_out, g_out, u_out, d_out) = refs[12:22]
    (
        gains_all, rows_one, rows_cot, rows_two, rows_dh, w_qkv, w_o, w_gu, w_d, queries, pairs, mix, dqkv, accum, pair_send,
        pair_in, mixed, dgu, dmixed, own_x, hidden, dhidden, summed, part_a, near_a, xin_a, zin_a, part_b, near_b, xin_b, zin_b,
        in_gu, in_d, in_qkv, in_o, gain_part, gain_in, gain_mid, gain_near, result_own, rows_own, send, receive, local,
    ) = refs[22:]
    at = Where(groups, ranks)
    s, h, g, r = at.s, at.h, at.g, at.r
    shards = groups * ranks
    count, depth = tok.shape
    quarter = count // 4
    width = gains.shape[1]
    units = gw.shape[1] // groups
    half = units // 2
    total_rows = count * shards
    score_scale = 1.0 / math.sqrt(HD)
    score_shift = math.log(total_rows)
    peers = [(s ^ m, h) for m in range(1, shards)] + [(s, h ^ m) for m in range(1, 4)]
    barrier = pltpu.get_barrier_semaphore()
    for peer in peers:
        pl.semaphore_signal(barrier, inc=1, device_id=peer, device_id_type=MESH)
    pl.semaphore_wait(barrier, len(peers))
    net, keep = Net(send, receive), Keep(local)

    def chunk(m):
        return row((g ^ m) * count, count)

    def shard_rows(shard):
        return row(shard * width, width)

    def columns_of(shard):
        return lane(shard * width, width)

    turn_qkv = Turn(
        net, keep, at,
        lambda i, group: (qw, kw, vw)[i].at[:, lane(group * HD, HD)],
        lambda i, shard: w_qkv.at[shard_rows(shard), i * HD : (i + 1) * HD],
        [((0, 1, 2), lambda shard: w_qkv.at[shard_rows(shard), :])],
    )
    turn_gu = Turn(
        net, keep, at,
        lambda i, group: (gw, uw)[i % 2].at[:, lane(group * units + (i // 2) * half, half)],
        lambda i, shard: w_gu.at[shard_rows(shard), i * half : (i + 1) * half],
        [((2 * b, 2 * b + 1), lambda shard, b=b: w_gu.at[shard_rows(shard), b * units : (b + 1) * units]) for b in (0, 1)],
    )
    turn_o = Turn(
        net, keep, at,
        lambda i, group: ow.at[row(group * HD, HD), :],
        lambda i, shard: w_o.at[:, columns_of(shard)],
        [((0,), lambda shard: w_o.at[:, columns_of(shard)])],
    )
    turn_d = Turn(
        net, keep, at,
        lambda i, group: dw.at[row(group * units + i * half, half), :],
        lambda i, shard: w_d.at[i * half : (i + 1) * half, columns_of(shard)],
        [((b,), lambda shard, b=b: w_d.at[b * half : (b + 1) * half, columns_of(shard)]) for b in (0, 1)],
    )

    gain_slot = gains_all.at[:, columns_of(s)]
    gain_moves = net.lot(shards, lambda m: (gains, gain_slot, (s ^ m, h)))
    for m in range(1, shards):
        gain_moves.start(m)
    gain_own = keep.put(gains, gain_slot)
    strip = row(h * quarter, quarter)
    one = Spread(net, at, rows_one, quarter, tok.at[strip, :])
    one.start()
    own_rows = keep.put(tok, rows_one.at[chunk(0), :])
    own_strip = keep.put(tok.at[strip, :], own_x)
    turn_qkv.start(3)
    turn_qkv.mine()
    turn_o.mine()
    own_cot = keep.put(cot, rows_cot.at[chunk(0), :])
    gain_part[...] = jnp.zeros_like(gain_part)

    def clear(i):
        rows = row(i * 64, 64)
        accum[rows, :] = jnp.zeros_like(accum[rows, :])

    each(total_rows // 64, clear)

    gain_own.wait()
    for m in range(1, shards):
        gain_moves.arrived(m)

    def norm_one(m):
        def some(i):
            rows = row((g ^ m) * count + i * 32, 32)
            values = rows_one[rows, :].astype(F32)
            inverse = lax.rsqrt(mean_square(values) + epsilon)
            rows_one[rows, :] = (values * inverse * gains_all[0:1, :]).astype(BF16)

        each(count // 32, some)

    own_rows.wait()
    own_strip.wait()
    norm_one(0)
    one.arrive(1)
    one.arrive(2)
    turn_qkv.start(2)
    turn_qkv.start(1)
    for m in (3, 2, 1):
        turn_o.start(m)
    one.second(1)
    one.second(2)
    turn_qkv.pass_on(3)
    one.arrive(3)
    grad = Spread(net, at, rows_cot, quarter, cot.at[strip, :])
    grad.start()
    one.ready(1)
    one.sent(1)
    norm_one(1)
    one.ready(2)
    one.sent(2)
    norm_one(2)
    turn_qkv.pass_on(1)
    one.second(3)
    turn_qkv.pass_on(2)
    one.ready(3)
    one.sent(3)
    norm_one(3)
    for m in (3, 2, 1):
        turn_d.start(m, 0)
    turn_qkv.ready()

    def own_place(m):
        return row(((g ^ m) * ranks + r) * count, count)

    pair_moves = net.lot(4, lambda m: (pairs.at[own_place(m), :], pairs.at[own_place(m), :], at.beside()))

    def project(m):
        rows, place = chunk(m), own_place(m)
        heads = dot(rows_one[rows, :], w_qkv[...])
        cos_part, sin_part = cosines[rows, :], sines[rows, :]
        queries[rows, :] = turned(heads[:, :HD], cos_part, sin_part).astype(BF16)
        pairs[place, :HD] = turned(heads[:, HD : 2 * HD], cos_part, sin_part).astype(BF16)
        pairs[place, HD:] = heads[:, 2 * HD :].astype(BF16)
        pair_moves.start(m)

    each(4, project)
    pair_moves.open.update(range(4))
    for m in (3, 2, 1):
        turn_o.pass_on(m)
    turn_gu.start(3, 0)
    turn_gu.start(1, 0)
    for m in (3, 2, 1):
        turn_d.start(m, 1)
    grad.arrive(1)
    grad.arrive(2)
    turn_d.mine(0)
    turn_gu.mine(0)
    for m in (0, 1, 2, 3):
        pair_moves.arrived(m)
    turn_o.ready()
    span = ranks * count

    def weights_of(m, j, query):
        keys = pairs[row(j * span, span), :HD]
        scores = dot_nt(query, keys) * score_scale - score_shift
        q_place = ((g ^ m) * ranks + r) * count + lax.broadcasted_iota(jnp.int32, (count, span), 0)
        k_place = j * span + lax.broadcasted_iota(jnp.int32, (count, span), 1)
        return jnp.where(k_place <= q_place, jax.nn.sigmoid(scores), 0.0)

    def attend(m):
        rows = chunk(m)
        query = queries[rows, :]

        def step(j, total):
            weight = weights_of(m, j, query).astype(BF16)
            return total + dot(weight, pairs[row(j * span, span), HD:])

        total = lax.fori_loop(0, (g ^ m) + 1, step, jnp.zeros((count, HD), F32))
        low = total.astype(BF16)
        mix[rows, :] = low
        part_a[rows, :] = dot(low, w_o[...]).astype(BF16)

    set_a, set_b = (part_a, near_a, xin_a, zin_a), (part_b, near_b, xin_b, zin_b)
    first = Collect(net, at, set_a, quarter, summed)
    first.produce(attend)
    first.third(3)
    first.second(0)
    turn_gu.start(1, 1)
    turn_d.mine(1)
    turn_gu.mine(1)
    for m in (3, 2, 1):
        turn_d.pass_on(m, 0)
    first.third(2)
    grad.second(1)
    grad.second(2)
    grad.arrive(3)
    first.third(1)
    first.last()
    two = Spread(net, at, rows_two, quarter)
    mine_start = (g * 4 + h) * quarter

    def norm_two(i):
        few = row(i * 16, 16)
        values = own_x[few, :].astype(F32) + first.total(few)
        hidden[few, :] = values
        inverse = lax.rsqrt(mean_square(values) + epsilon)
        rows_two[row(mine_start + i * 16, 16), :] = (values * inverse * gains_all[1:2, :]).astype(BF16)

    each(quarter // 16, norm_two)
    two.start()
    turn_gu.start(2, 0)
    turn_gu.start(3, 1)
    turn_gu.start(2, 1)
    turn_gu.pass_on(3, 0)
    turn_gu.pass_on(1, 0)
    for m in (3, 2, 1):
        turn_d.pass_on(m, 1)
    grad.second(3)
    two.second(0)
    two.arrive(1)
    turn_gu.pass_on(1, 1)
    turn_d.ready(0)
    own_cot.wait()

    def early(m, b):
        lanes = slice(b * half, (b + 1) * half)
        dmixed[chunk(m), lanes] = dot_nt(rows_cot[chunk(m), :], w_d[lanes, :])

    for m in (1, 2, 3):
        grad.ready(m)
    each(4, lambda m: early(m, 0))
    two.arrive(2)
    two.second(1)
    two.second(2)
    two.arrive(3)
    turn_gu.pass_on(2, 0)
    two.second(3)
    turn_gu.pass_on(3, 1)
    for m in (0, 1, 2, 3):
        two.ready(m)
    turn_gu.ready(0)

    def feed(m, b):
        rows = chunk(m)
        lanes, pair = slice(b * half, (b + 1) * half), slice(b * units, (b + 1) * units)
        both = dot(rows_two[rows, :], w_gu[:, pair])
        gate, up = both[:, :half], both[:, half:]
        sig = jax.nn.sigmoid(gate)
        act = gate * sig
        mixed[rows, lanes] = (act * up).astype(BF16)
        back = dmixed[rows, lanes]
        dgu[rows, b * units : b * units + half] = (back * up * sig * (1.0 + gate * (1.0 - sig))).astype(BF16)
        dgu[rows, b * units + half : (b + 1) * units] = (back * act).astype(BF16)
        total = dot_nt(dgu[rows, pair], w_gu[:, pair])
        if b:
            total += part_a[rows, :].astype(F32)
        part_a[rows, :] = total.astype(BF16)

    def out_part(m, b):
        rows = chunk(m)
        lanes = slice(b * half, (b + 1) * half)
        total = dot(mixed[rows, lanes], w_d[lanes, :])
        if b:
            total += part_b[rows, :].astype(F32)
        part_b[rows, :] = total.astype(BF16)

    def halves(m, work, lot):
        d = g ^ m

        def step(k):
            work(d * ranks + (r ^ 1 ^ k))

            @pl.when(k == 0)
            def _():
                lot.start(m)

        each(2, step)

    def several(groups_, work, lot):
        first_, last_ = groups_
        each(first_ - last_ + 1, lambda i: halves(first_ - i, work, lot))
        lot.open.update(range(last_, first_ + 1))

    def beside(source, target):
        def describe(m):
            d = g ^ m
            return (source(d * ranks + (r ^ 1)), target(d), at.beside())

        return net.lot(4, describe)

    pairs_of = [slice(b * units, (b + 1) * units) for b in (0, 1)]
    lanes_of = [slice(b * half, (b + 1) * half) for b in (0, 1)]
    moves_gu = [
        beside(lambda shard, p=p: w_gu.at[shard_rows(shard), p], lambda d, p=p: in_gu.at[d, :, p]) for p in pairs_of
    ]
    moves_d = [
        beside(lambda shard, p=p: w_d.at[p, columns_of(shard)], lambda d, p=p: in_d.at[d, p, :]) for p in lanes_of
    ]
    moves_qkv = beside(lambda shard: w_qkv.at[shard_rows(shard), :], lambda d: in_qkv.at[d])
    moves_o = beside(lambda shard: w_o.at[:, columns_of(shard)], lambda d: in_o.at[d])

    def grads_gu(groups_, b):
        def work(shard):
            w_gu[shard_rows(shard), pairs_of[b]] = dot_tn(rows_two[:, columns_of(shard)], dgu[:, pairs_of[b]]).astype(BF16)

        several(groups_, work, moves_gu[b])

    def grads_d(groups_, b):
        def work(shard):
            columns = columns_of(shard)
            w_d[lanes_of[b], columns] = dot_tn(mixed[:, lanes_of[b]], rows_cot[:, columns]).astype(BF16)

        several(groups_, work, moves_d[b])

    def grads_o(groups_):
        def work(shard):
            columns = columns_of(shard)
            w_o[:, columns] = dot_tn(mix[...], rows_dh[:, columns]).astype(BF16)

        several(groups_, work, moves_o)

    def grads_qkv(groups_):
        def work(shard):
            w_qkv[shard_rows(shard), :] = dot_tn(rows_one[:, columns_of(shard)], dqkv[...]).astype(BF16)

        several(groups_, work, moves_qkv)

    final, final_own = [], []

    def give(source, target, m):
        if m:
            lot = net.lot(1, lambda j: (source, target, at.along(m)))
            lot.start(0)
            final.append(lot)
        else:
            final_own.append(keep.put(source, target))

    def sums(m, lot, mine_of, other_of, size):
        lot.arrived(m)

        def step(i):
            a, rows, lanes = mine_of(i)
            b, d, few, others = other_of(i)
            a[rows, lanes] = (a[rows, lanes].astype(F32) + b[d, few, others].astype(F32)).astype(BF16)

        each(size // 32, step)

    def sums_gu(m, b):
        d, p = g ^ m, pairs_of[b]
        start = (d * ranks + r) * width
        sums(
            m, moves_gu[b],
            lambda i: (w_gu, row(start + i * 32, 32), p), lambda i: (in_gu, d, row(i * 32, 32), p), width,
        )
        for i, out in enumerate((g_out, u_out)):
            place = b * units + i * half
            give(w_gu.at[row(start, width), place : place + half], out.at[:, lane(g * units + b * half, half)], m)

    def sums_d(m, b):
        d, base = g ^ m, b * half
        columns = columns_of(d * ranks + r)
        sums(
            m, moves_d[b],
            lambda i: (w_d, row(base + i * 32, 32), columns),
            lambda i: (in_d, d, row(base + i * 32, 32), slice(None)), half,
        )
        give(w_d.at[lanes_of[b], columns], d_out.at[row(g * units + base, half), :], m)

    def sums_o(m):
        d = g ^ m
        columns = columns_of(d * ranks + r)
        sums(
            m, moves_o,
            lambda i: (w_o, row(i * 32, 32), columns), lambda i: (in_o, d, row(i * 32, 32), slice(None)), HD,
        )
        give(w_o.at[:, columns], o_out.at[row(g * HD, HD), :], m)

    def sums_qkv(m):
        d = g ^ m
        start = (d * ranks + r) * width
        sums(
            m, moves_qkv,
            lambda i: (w_qkv, row(start + i * 32, 32), slice(None)),
            lambda i: (in_qkv, d, row(i * 32, 32), slice(None)), width,
        )
        for i, out in enumerate((q_out, k_out, v_out)):
            give(w_qkv.at[row(start, width), i * HD : (i + 1) * HD], out.at[:, lane(g * HD, HD)], m)

    first.sent()
    second = Collect(net, at, set_a, quarter, summed)
    each(4, lambda m: feed(m, 0))
    turn_gu.sent(0)
    turn_gu.pass_on(2, 1)
    grads_gu((3, 2), 0)
    turn_d.ready(1)
    each(4, lambda m: early(m, 1))
    each(4, lambda m: out_part(m, 0))
    turn_d.sent(0)
    grads_gu((1, 1), 0)
    turn_gu.ready(1)
    second.produce(lambda m: feed(m, 1))
    second.third(3)
    sums_gu(3, 0)
    second.second(0)
    second.third(2)
    sums_gu(2, 0)
    turn_gu.sent(1)
    turn_d.sent(1)
    grads_d((3, 1), 0)
    second.third(1)
    grads_gu((3, 1), 1)
    each(4, lambda m: out_part(m, 1))
    sums_gu(1, 0)
    second.last()
    three = Spread(net, at, rows_dh, quarter)

    def back_two(i, gain_grad):
        few = row(i * 16, 16)
        own = row(mine_start + i * 16, 16)
        upstream, values = second.total(few), hidden[few, :]
        inverse = lax.rsqrt(mean_square(values) + epsilon)
        scaled = upstream * gains_all[1:2, :]
        back = inverse * scaled - values * (inverse * inverse * inverse) * jnp.mean(
            scaled * values, axis=1, keepdims=True
        )
        total = rows_cot[own, :].astype(F32) + back
        dhidden[few, :] = total
        rows_dh[own, :] = total.astype(BF16)
        return gain_grad + jnp.sum(upstream * values * inverse, axis=0, keepdims=True)

    gain_part[1:2, :] = lax.fori_loop(0, quarter // 16, back_two, jnp.zeros((1, depth), F32))
    three.start()
    for m in (3, 2, 1):
        sums_d(m, 0)
    grads_d((3, 1), 1)
    three.second(0)
    three.arrive(1)
    three.arrive(2)
    sums_gu(3, 1)
    three.second(1)
    for b in (0, 1):
        grads_gu((0, 0), b)
    sums_gu(2, 1)
    three.second(2)
    three.arrive(3)
    for b in (0, 1):
        grads_d((0, 0), b)
    out_sum = Collect(net, at, set_b, quarter, summed)
    for m in (3, 2, 1, 0):
        out_sum.first(m)
    sums_gu(1, 1)
    three.second(3)

    def attend_back(m):
        three.ready(m)
        rows = chunk(m)
        query = queries[rows, :]
        dm = dot_nt(rows_dh[rows, :], w_o[...]).astype(BF16)

        def step(j, total):
            block = row(j * span, span)
            weight = weights_of(m, j, query)
            dweight = dot_nt(dm, pairs[block, HD:])
            dscore = (dweight * weight * (1.0 - weight)).astype(BF16)
            accum[block, HD:] += dot_tn(weight.astype(BF16), dm)
            accum[block, :HD] += dot_tn(dscore, query)
            return total + dot(dscore, pairs[block, :HD])

        total = lax.fori_loop(0, (g ^ m) + 1, step, jnp.zeros((count, HD), F32))
        dqkv[rows, :HD] = turned(total * score_scale, cosines[rows, :], -sines[rows, :]).astype(BF16)

    each(4, attend_back)
    pair_back = net.lot(4, lambda m: (pair_send.at[g ^ m], pair_in.at[g ^ m], at.beside()))

    def send_pair(i):
        m = 3 - i
        d = g ^ m
        rows = row((d * ranks + (r ^ 1)) * count, count)
        pair_send[d] = accum[rows, :].astype(BF16)
        pair_back.start(m)

    each(4, send_pair)
    pair_back.open.update(range(4))
    for m in (3, 2, 1, 0):
        out_sum.second(m)
    for m in (3, 2, 1):
        sums_d(m, 1)
    turn_o.sent()
    grads_o((3, 0))
    out_sum.third(3)
    out_sum.third(2)
    out_sum.third(1)
    second.sent()
    third = Collect(net, at, set_a, quarter, summed)

    def back_one(m):
        d = g ^ m
        rows = chunk(m)
        pair_back.arrived(m)
        both = accum[own_place(m), :] + pair_in[d].astype(F32)
        dqkv[rows, HD : 2 * HD] = turned(both[:, :HD] * score_scale, cosines[rows, :], -sines[rows, :]).astype(BF16)
        dqkv[rows, 2 * HD :] = both[:, HD:].astype(BF16)
        part_a[rows, :] = dot_nt(dqkv[rows, :], w_qkv[...]).astype(BF16)

    third.produce(back_one)
    third.second(0)
    turn_qkv.sent()
    grads_qkv((3, 0))
    third.third(3)
    for m in (3, 2, 1):
        sums_o(m)
    third.third(2)
    third.third(1)
    for b in (0, 1):
        sums_gu(0, b)
        sums_d(0, b)
    ends = []

    def share(source, target):
        place = target.at[strip, :]
        final_own.append(keep.put(source, place))
        lot = net.lot(2, lambda j: (source, place, (at.near(), at.across())[j]))
        lot.start(0)
        lot.start(1)
        ends.append((lot, target))

    def relay():
        lot, target = ends.pop()
        lot.arrived(1)
        final.append(lot)
        block = target.at[row((h ^ 2) * quarter, quarter), :]
        on = net.lot(1, lambda j: (block, block, at.near()))
        on.start(0)
        final.append(on)

    for m in (3, 2, 1, 0):
        sums_qkv(m)
    out_sum.last()

    def result_rows(i):
        few = row(i * 16, 16)
        result_own[few, :] = (hidden[few, :] + out_sum.total(few)).astype(BF16)

    each(quarter // 16, result_rows)
    share(result_own, result_out)
    third.last()

    def back_rows(i, gain_grad):
        few = row(i * 16, 16)
        upstream, values = third.total(few), own_x[few, :].astype(F32)
        inverse = lax.rsqrt(mean_square(values) + epsilon)
        scaled = upstream * gains_all[0:1, :]
        back = inverse * scaled - values * (inverse * inverse * inverse) * jnp.mean(
            scaled * values, axis=1, keepdims=True
        )
        rows_own[few, :] = (dhidden[few, :] + back).astype(BF16)
        return gain_grad + jnp.sum(upstream * values * inverse, axis=0, keepdims=True)

    gain_part[0:1, :] = lax.fori_loop(0, quarter // 16, back_rows, jnp.zeros((1, depth), F32))
    gain_sums = net.lot(shards, lambda m: (gain_part.at[:, columns_of(s ^ m)], gain_in.at[m - 1], (s ^ m, h)))
    for m in range(1, shards):
        gain_sums.start(m)
    relay()
    share(rows_own, rows_out)
    total = gain_part[:, columns_of(s)]
    for m in range(1, shards):
        gain_sums.arrived(m)
        total += gain_in[m - 1]
    gain_mid[...] = total
    gain_ends = net.lot(4, lambda m: (gain_mid, gain_near.at[m - 1], (s, h ^ m)))
    for m in range(1, 4):
        gain_ends.start(m)
    sums_o(0)
    relay()
    for m in range(1, 4):
        gain_ends.arrived(m)
        total += gain_near[m - 1]
    gains_out[...] = total
    for lot in final:
        lot.arrived(0)
    net.finish()
    for copy in final_own:
        copy.wait()


def rows_plan(
    groups,
    ranks,
    tokens,
    attn_gain,
    query_weight,
    key_weight,
    value_weight,
    out_weight,
    mlp_gain,
    gate_weight,
    up_weight,
    down_weight,
    cotangent,
):
    count, depth = tokens.shape
    shards = groups * ranks
    quarter = count // 4
    width = query_weight.shape[0]
    units = gate_weight.shape[1] // groups
    total_rows = count * shards
    here = groups * count
    r = lax.axis_index("seq") % ranks
    gains = jnp.concatenate([attn_gain[None], mlp_gain[None], jnp.zeros((6, width), BF16)]).astype(F32)
    places = (
        (jnp.arange(groups, dtype=jnp.int32) * ranks + r)[:, None] * count
        + jnp.arange(count, dtype=jnp.int32)[None, :]
    ).reshape(here)
    lanes = jnp.arange(HD, dtype=jnp.int32)
    half = HD // 2
    frequency = jnp.exp((lanes % half).astype(F32) * (-math.log(10000.0) / half))
    angles = places.astype(F32)[:, None] * frequency[None, :]
    cosines = jnp.cos(angles)
    sines = jnp.sin(angles) * jnp.where(lanes < half, -1.0, 1.0)[None, :]
    ins = (tokens, cotangent, gains, query_weight, key_weight, value_weight, out_weight, gate_weight, up_weight, down_weight, cosines, sines)
    shape = jax.ShapeDtypeStruct
    hbm, vmem = pl.BlockSpec(memory_space=pl.ANY), pl.BlockSpec(memory_space=pltpu.VMEM)
    owners = (query_weight, key_weight, value_weight, out_weight, gate_weight, up_weight, down_weight)
    outs = [
        shape((count, depth), BF16),
        shape((count, depth), BF16),
        shape((8, width), F32),
        *(shape(w.shape, BF16) for w in owners),
    ]

    def low(*extent):
        return pltpu.VMEM(extent, BF16)

    def full(*extent):
        return pltpu.VMEM(extent, F32)

    def collector():
        return [
            low(here, depth),
            low(groups, 2, quarter, depth),
            low(groups, quarter, depth),
            low(3, quarter, depth),
        ]

    scratch = [
        full(8, depth),
        low(here, depth), low(here, depth), low(here, depth), low(here, depth),
        low(depth, 3 * HD), low(HD, depth), low(depth, 2 * units), low(units, depth),
        low(here, HD), low(total_rows, 2 * HD), low(here, HD), low(here, 3 * HD),
        full(total_rows, 2 * HD), low(groups, count, 2 * HD), low(groups, count, 2 * HD),
        low(here, units), low(here, 2 * units), full(here, units),
        low(quarter, depth), full(quarter, depth), full(quarter, depth), full(quarter, depth),
        *collector(), *collector(),
        low(groups, width, 2 * units), low(groups, units, width), low(groups, width, 3 * HD), low(groups, HD, width),
        full(8, depth), full(shards - 1, 8, width), full(8, width), full(3, 8, width),
        low(quarter, depth), low(quarter, depth),
        pltpu.SemaphoreType.DMA((400,)), pltpu.SemaphoreType.DMA((400,)), pltpu.SemaphoreType.DMA((48,)),
    ]
    result, rows_grad, gain_grads, *grads = pl.pallas_call(
        functools.partial(layer_body, groups, ranks),
        out_shape=outs,
        in_specs=[hbm] * 10 + [vmem] * 2,
        out_specs=[hbm, hbm, vmem] + [hbm] * 7,
        scratch_shapes=scratch,
        compiler_params=pltpu.CompilerParams(
            collective_id=1, has_side_effects=True, vmem_limit_bytes=VMEM_LIMIT
        ),
    )(*ins)
    grads = [w.astype(F32) for w in grads]
    return (result, rows_grad, gain_grads[0], *grads[:4], gain_grads[1], *grads[4:])


def on_device(tokens, attn_gain, query_weight, *rest):
    groups = query_weight.shape[1] // HD
    ranks = lax.axis_size("seq") // groups
    fits = lax.axis_size("head") == 4 and groups == 4 and ranks == 2 and query_weight.shape[0] % 128 == 0
    plan = functools.partial(rows_plan, groups, ranks) if fits else gathered_weights
    return plan(tokens, attn_gain, query_weight, *rest)


def solution(mesh):
    in_specs = (
        P("seq", None),
        P("seq"),
        P("seq", "head"),
        P("seq", "head"),
        P("seq", "head"),
        P("head", "seq"),
        P("seq"),
        P("seq", "head"),
        P("seq", "head"),
        P("head", "seq"),
        P("seq", None),
    )
    out_specs = (
        P("seq", None),
        P("seq", None),
        P("seq"),
        P("seq", "head"),
        P("seq", "head"),
        P("seq", "head"),
        P("head", "seq"),
        P("seq"),
        P("seq", "head"),
        P("seq", "head"),
        P("head", "seq"),
    )
    return jax.shard_map(
        on_device, mesh=mesh, in_specs=in_specs, out_specs=out_specs, check_vma=False
    )
```

```python
import functools
import math

import jax
import jax.numpy as jnp
from jax import lax
from jax.experimental import pallas as pl
from jax.experimental.pallas import tpu as pltpu
from jax.sharding import PartitionSpec as P

MESH = pl.DeviceIdType.MESH
F32, BF16 = jnp.float32, jnp.bfloat16

HD = 128


epsilon = 1e-05
block_limit = 512
VMEM_LIMIT = 63 * 2**20
SENDS, RECEIVES, KEEPS = 103, 213, 26


def tables(offset, length, half_width):
    places = (offset + jnp.arange(length, dtype=jnp.int32)).astype(jnp.float32)
    frequency = jnp.exp(
        jnp.arange(half_width, dtype=jnp.float32) * (-math.log(10000.0) / half_width)
    )
    angles = places[:, None] * frequency[None, :]
    return (jnp.cos(angles)[:, None, :], jnp.sin(angles)[:, None, :])


def rotary(values, cos_table, sin_table):
    half_width = values.shape[-1] // 2
    front = values[..., :half_width]
    back_half = values[..., half_width:]
    return jnp.concatenate(
        [front * cos_table - back_half * sin_table, back_half * cos_table + front * sin_table],
        axis=-1,
    )


def unrotary(gradient, cos_table, sin_table):
    half_width = gradient.shape[-1] // 2
    front = gradient[..., :half_width]
    back_half = gradient[..., half_width:]
    return jnp.concatenate(
        [front * cos_table + back_half * sin_table, back_half * cos_table - front * sin_table],
        axis=-1,
    )


def norm_back(values, inverse, gain_vector, upstream):
    scaled = upstream * gain_vector
    gain_grad = jnp.sum(upstream * values * inverse, axis=0)
    value_grad = inverse * scaled - values * inverse**3 * jnp.mean(
        scaled * values, axis=1, keepdims=True
    )
    return (value_grad, gain_grad)


def gathered_weights(
    tokens,
    attn_gain,
    query_weight,
    key_weight,
    value_weight,
    out_weight,
    mlp_gain,
    gate_weight,
    up_weight,
    down_weight,
    cotangent,
):
    row_count = tokens.shape[0]
    total_rows = row_count * lax.axis_size("seq")
    row_start = lax.axis_index("seq") * row_count
    local_width = query_weight.shape[1]
    local_heads = local_width // HD
    score_scale = 1.0 / math.sqrt(HD)
    score_shift = math.log(total_rows)
    block_rows = math.gcd(total_rows, block_limit)
    block_count = total_rows // block_rows
    attn_gain_full, query_full, key_full, value_full, out_full = (
        lax.all_gather(attn_gain, "seq", axis=0, tiled=True),
        lax.all_gather(query_weight, "seq", axis=0, tiled=True),
        lax.all_gather(key_weight, "seq", axis=0, tiled=True),
        lax.all_gather(value_weight, "seq", axis=0, tiled=True),
        lax.all_gather(out_weight, "seq", axis=1, tiled=True),
    )
    mlp_gain_full, gate_full, up_full, down_full = (
        lax.all_gather(mlp_gain, "seq", axis=0, tiled=True),
        lax.all_gather(gate_weight, "seq", axis=0, tiled=True),
        lax.all_gather(up_weight, "seq", axis=0, tiled=True),
        lax.all_gather(down_weight, "seq", axis=1, tiled=True),
    )
    token_values = tokens.astype(jnp.float32)
    inverse_one = lax.rsqrt(jnp.mean(token_values * token_values, axis=1, keepdims=True) + epsilon)
    normed_one = (token_values * inverse_one * attn_gain_full.astype(jnp.float32)).astype(
        jnp.bfloat16
    )
    query_pre = jnp.dot(normed_one, query_full, preferred_element_type=jnp.float32)
    key_pre = jnp.dot(normed_one, key_full, preferred_element_type=jnp.float32)
    value_rows = (
        jnp.dot(normed_one, value_full, preferred_element_type=jnp.float32)
        .astype(jnp.bfloat16)
        .reshape(row_count, local_heads, HD)
    )
    cos_table, sin_table = tables(row_start, row_count, HD // 2)
    query_rows = (
        rotary(query_pre.reshape(row_count, local_heads, HD), cos_table, sin_table)
        .astype(jnp.bfloat16)
        .reshape(row_count, local_width)
    )
    key_rows = rotary(key_pre.reshape(row_count, local_heads, HD), cos_table, sin_table).astype(
        jnp.bfloat16
    )
    all_queries = lax.all_gather(query_rows, "seq", axis=0, tiled=True)
    key_places = row_start + jnp.arange(row_count, dtype=jnp.int32)

    def weights_for(query_block, block_start):
        scores = (
            jnp.einsum("qhd,khd->hqk", query_block, key_rows, preferred_element_type=jnp.float32)
            * score_scale
            - score_shift
        )
        query_places = block_start + jnp.arange(query_block.shape[0], dtype=jnp.int32)
        visible = key_places[None, :] <= query_places[:, None]
        return jnp.where(visible[None], jax.nn.sigmoid(scores), 0.0)

    step_rows = math.gcd(row_count * lax.axis_size("seq"), block_limit)
    step_count = row_count * lax.axis_size("seq") // step_rows
    picked = all_queries.reshape(step_count, step_rows, local_heads, HD)
    starts = jnp.arange(step_count, dtype=jnp.int32) * step_rows

    def one_block(packed):
        query_block, block_start = packed
        weights = weights_for(query_block, block_start).astype(jnp.bfloat16)
        return jnp.einsum(
            "hqk,khd->qhd", weights, value_rows, preferred_element_type=jnp.float32
        ).reshape(step_rows, local_width)

    attn_mix = lax.psum_scatter(
        lax.map(one_block, (picked, starts)).reshape(row_count * lax.axis_size("seq"), local_width),
        "seq",
        scatter_dimension=0,
        tiled=True,
    ).astype(jnp.bfloat16)
    attn_branch = lax.psum(jnp.dot(attn_mix, out_full, preferred_element_type=jnp.float32), "head")
    hidden = token_values + attn_branch
    inverse_two = lax.rsqrt(jnp.mean(hidden * hidden, axis=1, keepdims=True) + epsilon)
    normed_two = (hidden * inverse_two * mlp_gain_full.astype(jnp.float32)).astype(jnp.bfloat16)
    gate_pre = jnp.dot(normed_two, gate_full, preferred_element_type=jnp.float32)
    up_pre = jnp.dot(normed_two, up_full, preferred_element_type=jnp.float32)
    gate_act = jax.nn.silu(gate_pre)
    mixed = (gate_act * up_pre).astype(jnp.bfloat16)
    mlp_branch = lax.psum(
        jnp.dot(mixed, down_full, preferred_element_type=jnp.float32).astype(jnp.bfloat16), "head"
    ).astype(jnp.float32)
    result = (hidden + mlp_branch).astype(jnp.bfloat16)
    kept_weights = (
        lax.all_gather(attn_gain, "seq", axis=0, tiled=True),
        lax.all_gather(query_weight, "seq", axis=0, tiled=True),
        lax.all_gather(key_weight, "seq", axis=0, tiled=True),
        lax.all_gather(value_weight, "seq", axis=0, tiled=True),
        lax.all_gather(out_weight, "seq", axis=1, tiled=True),
        lax.all_gather(mlp_gain, "seq", axis=0, tiled=True),
        lax.all_gather(gate_weight, "seq", axis=0, tiled=True),
        lax.all_gather(up_weight, "seq", axis=0, tiled=True),
        lax.all_gather(down_weight, "seq", axis=1, tiled=True),
    )
    (
        attn_gain_back,
        query_back,
        key_back,
        value_back,
        out_back,
        mlp_gain_back,
        gate_back,
        up_back,
        down_back,
    ) = kept_weights
    attn_gain_f = attn_gain_back.astype(jnp.float32)
    mlp_gain_f = mlp_gain_back.astype(jnp.float32)
    grad_values = cotangent.astype(jnp.float32)
    grad_down = jnp.einsum("tf,td->fd", mixed, cotangent, preferred_element_type=jnp.float32)
    dmixed = jnp.einsum("td,fd->tf", cotangent, down_back, preferred_element_type=jnp.float32)
    gate_sig = jax.nn.sigmoid(gate_pre)
    dgate = (dmixed * up_pre * gate_sig * (1.0 + gate_pre * (1.0 - gate_sig))).astype(jnp.bfloat16)
    dup = (dmixed * gate_act).astype(jnp.bfloat16)
    grad_gate = jnp.einsum("tk,tf->kf", normed_two, dgate, preferred_element_type=jnp.float32)
    grad_up = jnp.einsum("tk,tf->kf", normed_two, dup, preferred_element_type=jnp.float32)
    dnormed_two = lax.psum(
        jnp.einsum("tf,kf->tk", dgate, gate_back, preferred_element_type=jnp.float32)
        + jnp.einsum("tf,kf->tk", dup, up_back, preferred_element_type=jnp.float32),
        "head",
    )
    dhidden_norm, grad_mlp_gain = norm_back(hidden, inverse_two, mlp_gain_f, dnormed_two)
    dhidden = grad_values + dhidden_norm
    mlp_sums = (grad_mlp_gain, grad_gate, grad_up, grad_down)
    dhidden_low = dhidden.astype(jnp.bfloat16)
    grad_out = jnp.einsum("tc,td->cd", attn_mix, dhidden_low, preferred_element_type=jnp.float32)
    dmix = jnp.einsum(
        "td,cd->tc", dhidden_low, out_back, preferred_element_type=jnp.float32
    ).astype(jnp.bfloat16)
    all_dmix = lax.all_gather(dmix, "seq", axis=0, tiled=True)

    def backward_block(carry, packed):
        key_accum, value_accum = carry
        query_block, grad_block, block_start = packed
        weights = weights_for(query_block, block_start)
        grad_weights = jnp.einsum(
            "qhd,khd->hqk", grad_block, value_rows, preferred_element_type=jnp.float32
        )
        grad_scores = (grad_weights * weights * (1.0 - weights)).astype(jnp.bfloat16)
        value_accum = value_accum + jnp.einsum(
            "hqk,qhd->khd",
            weights.astype(jnp.bfloat16),
            grad_block,
            preferred_element_type=jnp.float32,
        )
        key_accum = key_accum + jnp.einsum(
            "hqk,qhd->khd", grad_scores, query_block, preferred_element_type=jnp.float32
        )
        query_part = (
            jnp.einsum("hqk,khd->qhd", grad_scores, key_rows, preferred_element_type=jnp.float32)
            * score_scale
        )
        return ((key_accum, value_accum), query_part.reshape(block_rows, local_width))

    zero_rows = jnp.zeros((row_count, local_heads, HD), jnp.float32)
    block_starts = jnp.arange(block_count, dtype=jnp.int32) * block_rows
    (key_accum, value_accum), query_parts = lax.scan(
        backward_block,
        (zero_rows, zero_rows),
        (
            all_queries.reshape(block_count, block_rows, local_heads, HD),
            all_dmix.reshape(block_count, block_rows, local_heads, HD),
            block_starts,
        ),
    )
    query_sum = lax.psum_scatter(
        query_parts.reshape(total_rows, local_width), "seq", scatter_dimension=0, tiled=True
    )
    dquery_pre = (
        unrotary(query_sum.reshape(row_count, local_heads, HD), cos_table, sin_table)
        .reshape(row_count, local_width)
        .astype(jnp.bfloat16)
    )
    dkey_pre = (
        unrotary(key_accum * score_scale, cos_table, sin_table)
        .reshape(row_count, local_width)
        .astype(jnp.bfloat16)
    )
    dvalue = value_accum.reshape(row_count, local_width).astype(jnp.bfloat16)
    grad_query = jnp.einsum("tk,tc->kc", normed_one, dquery_pre, preferred_element_type=jnp.float32)
    grad_key = jnp.einsum("tk,tc->kc", normed_one, dkey_pre, preferred_element_type=jnp.float32)
    grad_value = jnp.einsum("tk,tc->kc", normed_one, dvalue, preferred_element_type=jnp.float32)
    dnormed_one = lax.psum(
        jnp.einsum("tc,kc->tk", dquery_pre, query_back, preferred_element_type=jnp.float32)
        + jnp.einsum("tc,kc->tk", dkey_pre, key_back, preferred_element_type=jnp.float32)
        + jnp.einsum("tc,kc->tk", dvalue, value_back, preferred_element_type=jnp.float32),
        "head",
    )
    dinput_norm, grad_attn_gain = norm_back(token_values, inverse_one, attn_gain_f, dnormed_one)
    input_grad = (dhidden + dinput_norm).astype(jnp.bfloat16)
    every_sum = (
        lax.psum_scatter(grad_attn_gain, "seq", scatter_dimension=0, tiled=True),
        lax.psum_scatter(grad_query, "seq", scatter_dimension=0, tiled=True),
        lax.psum_scatter(grad_key, "seq", scatter_dimension=0, tiled=True),
        lax.psum_scatter(grad_value, "seq", scatter_dimension=0, tiled=True),
        lax.psum_scatter(grad_out, "seq", scatter_dimension=1, tiled=True),
        lax.psum_scatter(grad_mlp_gain, "seq", scatter_dimension=0, tiled=True),
        lax.psum_scatter(grad_gate, "seq", scatter_dimension=0, tiled=True),
        lax.psum_scatter(grad_up, "seq", scatter_dimension=0, tiled=True),
        lax.psum_scatter(grad_down, "seq", scatter_dimension=1, tiled=True),
    )
    attn_sums = every_sum[:5]
    mlp_sums = every_sum[5:]
    return (
        result,
        input_grad,
        attn_sums[0],
        attn_sums[1],
        attn_sums[2],
        attn_sums[3],
        attn_sums[4],
        mlp_sums[0],
        mlp_sums[1],
        mlp_sums[2],
        mlp_sums[3],
    )


class Net:
    def __init__(self, send, receive):
        self.send, self.receive, self.sends, self.receives, self.lots = send, receive, 0, 0, []

    def lot(self, *args, **options):
        return Lot(self, *args, **options)

    def finish(self):
        for lot in self.lots:
            lot.sent()


class Lot:
    def __init__(self, net, indices, describe, bulk, arrival=None, apart=False):
        self.net, self.describe, self.bulk, self.arrival, self.apart = net, describe, bulk, arrival, apart
        self.place = {j: net.receives + i for i, j in enumerate(indices)}
        self.low = min(indices)
        self.send_base, self.receive_base = net.sends, net.receives
        net.receives += len(indices)
        net.sends += len(indices) if apart else 1
        self.started, self.open = set(), set()
        net.lots.append(self)

    def receive_at(self, j):
        return self.net.receive.at[self.receive_base + (j - self.low)]

    def send_at(self, j):
        return self.net.send.at[self.send_base + (j - self.low if self.apart else 0)]

    def start(self, j, pieces=None):
        described = self.describe(j)
        for i, (source, target, device) in enumerate(described if isinstance(described, list) else [described]):
            if pieces is None or i in pieces:
                pltpu.make_async_remote_copy(
                    src_ref=source,
                    dst_ref=target,
                    send_sem=self.send_at(j),
                    recv_sem=self.receive_at(j),
                    device_id=device,
                    device_id_type=MESH,
                ).start()
        if isinstance(j, int):
            self.mark((j,))

    def mark(self, indices):
        self.started.update(indices)
        self.open.update(indices if self.apart else (self.low,))

    def arrived(self, j):
        described = self.describe(j)
        target = self.arrival(j) if self.arrival else described[1]
        self.wait(target, self.receive_at(j))

    def wait(self, like, sem):
        pltpu.make_async_copy(like, like, sem).wait()

    def sent(self, j=None):
        for k in sorted(self.open) if j is None else [j] if j in self.open else []:
            self.open.remove(k)
            self.wait(self.bulk(k) if self.apart else self.bulk, self.send_at(k))


class Keep:
    def __init__(self, sems):
        self.sems, self.count = sems, 0

    def put(self, source, target):
        copy = pltpu.make_async_copy(source, target, self.sems.at[self.count])
        self.count += 1
        copy.start()
        return copy


class Where:
    def __init__(self, groups, ranks):
        self.s, self.h = lax.axis_index("seq"), lax.axis_index("head")
        self.g, self.r = self.s // ranks, self.s % ranks
        self.groups, self.ranks = groups, ranks
        self.q = self.h % 2 * 2 + self.h // 2

    def along(self, m):
        return (self.s ^ (m * self.ranks), self.h)

    def beside(self):
        return (self.s ^ 1, self.h)

    def across(self):
        return (self.s, self.h ^ 2)

    def near(self):
        return (self.s, self.h ^ 1)


def lane(start, size):
    return pl.ds(pl.multiple_of(start, 128), size)


def row(start, size):
    return pl.ds(pl.multiple_of(start, size), size)


def each(count, step):
    def body(i, carry):
        step(i)
        return carry

    lax.fori_loop(0, count, body, 0)


class Spread:
    def __init__(self, net, at, buffer, quarter, own=None):
        self.at, self.buffer, self.quarter, self.shared = at, buffer, quarter, own is not None
        first = self.block(0, 0) if own is None else own
        self.z = net.lot(
            (1, 2, 3),
            lambda m: (self.block(2, 0), self.block(2, 0), at.along(1))
            if m == 3
            else (first, self.block(0, 0), at.along(m)),
            self.some(3),
        )
        indices = (1, 2, 3) if self.shared else (0, 1, 2, 3)
        size = len(indices)
        self.x = net.lot(indices, lambda m: (self.block(m, 0), self.block(m, 0), at.across()), self.some(size))
        self.c = net.lot(indices, lambda m: (self.block(m, 0), self.block(m, 0), at.near()), self.some(size))
        self.d = net.lot(indices, lambda m: (self.block(m, 1), self.block(m, 1), at.near()), self.some(size))

    def some(self, size):
        return self.buffer.at[0 : size * self.quarter, :]

    def block(self, m, k):
        at = self.at
        return self.buffer.at[row(((at.g ^ m) * 4 + (at.q ^ k)) * self.quarter, self.quarter), :]

    def pass_on(self, m):
        self.x.start(m)
        self.c.start(m)

    def start(self):
        self.z.start(2)
        self.z.start(1)
        if not self.shared:
            self.pass_on(0)

    def arrive(self, m):
        self.z.arrived(m)
        if m == 2:
            self.z.start(3)
        self.pass_on(m)

    def second(self, m):
        self.x.arrived(m)
        self.d.start(m)

    def ready(self, m):
        self.c.arrived(m)
        self.d.arrived(m)

    def sent(self):
        for lot in (self.z, self.x, self.c, self.d):
            lot.sent()


class Collect:
    def __init__(self, net, at, refs, quarter, out):
        self.at, self.quarter, self.out = at, quarter, out
        self.part, self.near, self.xin, self.zin = refs
        every = (0, 1, 2, 3)
        self.a = net.lot(every, lambda m: (self.pair(m), self.near.at[at.g ^ m], at.near()), self.near)
        self.b = net.lot(
            every, lambda m: (self.part.at[self.rows(m, 1), :], self.xin.at[at.g ^ m], at.across()), self.xin
        )
        hops = {3: (0, 1), 2: (2, 2), 1: (1, 1)}
        self.z = net.lot(
            (1, 2, 3),
            lambda m: (self.part.at[self.rows(m, 0), :], self.zin.at[hops[m][0]], at.along(hops[m][1])),
            self.zin,
        )

    def rows(self, m, k):
        at = self.at
        return row(((at.g ^ m) * 4 + (at.q ^ k)) * self.quarter, self.quarter)

    def pair(self, m):
        at = self.at
        return self.part.at[row(((at.g ^ m) * 2 + (1 - at.h % 2)) * 2 * self.quarter, 2 * self.quarter), :]

    def first(self, m):
        self.a.start(m)

    def lines(self, few, k):
        start = (self.at.h // 2 ^ k) * self.quarter
        return pl.ds(pl.multiple_of(start + few.start, 16), few.size)

    def slices(self, m, k, step):
        at = self.at
        start = ((at.g ^ m) * 4 + (at.q ^ k)) * self.quarter
        each(self.quarter // 16, lambda i: step(row(start + i * 16, 16), row(i * 16, 16)))

    def second(self, m):
        d = self.at.g ^ m
        self.a.arrived(m)

        def step(rows, few):
            total = self.part[rows, :].astype(F32) + self.near[d, self.lines(few, 1), :].astype(F32)
            self.part[rows, :] = total.astype(BF16)

        self.slices(m, 1, step)
        self.b.start(m)

    def third(self, m):
        d = self.at.g ^ m
        self.b.arrived(m)
        if m == 2:
            self.z.arrived(3)

        def step(rows, few):
            total = self.part[rows, :].astype(F32) + self.near[d, self.lines(few, 0), :].astype(F32)
            total += self.xin[d, few, :].astype(F32)
            if m == 2:
                total += self.zin[0, few, :].astype(F32)
            if m:
                self.part[rows, :] = total.astype(BF16)
            else:
                self.out[few, :] = total

        self.slices(m, 0, step)
        if m:
            self.z.start(m)

    def last(self):
        self.third(0)
        self.z.arrived(1)
        self.z.arrived(2)

    def total(self, few):
        return self.out[few, :] + self.zin[1, few, :].astype(F32) + self.zin[2, few, :].astype(F32)

    def produce(self, work):
        def step(i):
            m = 3 - i
            work(m)
            self.first(m)

            @pl.when(i > 0)
            def _():
                self.second(m + 1)

        each(4, step)
        self.a.mark(range(4))
        self.b.mark((1, 2, 3))

    def sent(self):
        for lot in (self.a, self.b, self.z):
            lot.sent()


class Turn:
    def __init__(self, net, keep, at, source, view, blocks):
        self.keep, self.at, self.source, self.view, self.blocks = keep, at, source, view, blocks
        self.z, self.o, self.y, self.own = [], [], [], {}
        for b, (items, place) in enumerate(blocks):

            def out(m, items=items):
                return [(source(i, at.g ^ m), view(i, at.s), at.along(m)) for i in items]

            def beside(m, items=items):
                return [(source(i, at.g), view(i, at.s), at.beside()) for i in items]

            def on(m, place=place):
                block = place(at.s ^ (m * at.ranks))
                return (block, block, at.beside())

            def arrival(m, place=place):
                return place(at.s ^ (m * at.ranks))

            self.z.append(net.lot((1, 2, 3), out, lambda m, place=place: place(at.s), arrival, apart=True))
            self.o.append(net.lot((0,), beside, place(at.s), arrival))
            self.y.append(net.lot((1, 2, 3), on, lambda m, place=place: place(at.s), apart=True))

    def start(self, m, b=0, pieces=None):
        self.z[b].start(m, pieces)

    def mine(self, b=0):
        at = self.at
        for i in self.blocks[b][0]:
            self.own[i] = self.keep.put(self.source(i, at.g), self.view(i, at.s))
        self.o[b].start(0)

    def pass_on(self, m, b=0):
        self.z[b].arrived(m)
        self.y[b].start(m)

    def ready(self, b=0):
        for i in self.blocks[b][0]:
            self.own[i].wait()
        self.o[b].arrived(0)
        for m in (1, 2, 3):
            self.y[b].arrived(m)

    def sent(self, b=0):
        self.y[b].sent()


def dot(a, b):
    return jnp.dot(a, b, preferred_element_type=F32)


def dot_nt(a, b):
    return lax.dot_general(a, b, (((1,), (1,)), ((), ())), preferred_element_type=F32)


def dot_tn(a, b):
    return lax.dot_general(a, b, (((0,), (0,)), ((), ())), preferred_element_type=F32)


def turned(values, cos_table, sin_table):
    return values * cos_table + pltpu.roll(values, HD // 2, 1) * sin_table


def mean_square(values):
    return jnp.mean(values * values, axis=1, keepdims=True)


def layer_body(groups, ranks, *refs):
    (tok, cot, gain_one, gain_two, qw, kw, vw, ow, gw, uw, dw) = refs[:11]
    (result_out, rows_out, gains_out, q_out, k_out, v_out, o_out, g_out, u_out, d_out) = refs[11:21]
    (
        gains, gains_all, cosines, sines, rows_one, rows_cot, rows_two, rows_dh, w_qkv, w_o, w_gu, w_d, queries, pairs, mix, dqkv, accum, pair_send,
        pair_in, mixed, dgu, dmixed, own_x, hidden, dhidden, summed, part_a, near_a, xin_a, zin_a, part_b, near_b, xin_b, zin_b,
        in_gu, in_d, in_qkv, in_o, gain_part, gain_in, gain_mid, gain_near, result_own, rows_own, send, receive, local,
    ) = refs[21:]
    at = Where(groups, ranks)
    s, h, g, r = at.s, at.h, at.g, at.r
    shards = groups * ranks
    count, depth = tok.shape
    quarter = count // 4
    width = gains.shape[1]
    units = gw.shape[1] // groups
    half = units // 2
    total_rows = count * shards
    score_scale = 1.0 / math.sqrt(HD)
    score_shift = math.log(total_rows)
    peers = [(s ^ m, h) for m in range(1, shards)] + [(s, h ^ m) for m in range(1, 4)]
    barrier = pltpu.get_barrier_semaphore()
    for peer in peers:
        pl.semaphore_signal(barrier, inc=1, device_id=peer, device_id_type=MESH)
    pl.semaphore_wait(barrier, len(peers))
    net, keep = Net(send, receive), Keep(local)

    def chunk(m):
        return row((g ^ m) * count, count)

    def shard_rows(shard):
        return row(shard * width, width)

    def columns_of(shard):
        return lane(shard * width, width)

    turn_qkv = Turn(
        net, keep, at,
        lambda i, group: (qw, kw, vw)[i].at[:, lane(group * HD, HD)],
        lambda i, shard: w_qkv.at[shard_rows(shard), i * HD : (i + 1) * HD],
        [((0, 1, 2), lambda shard: w_qkv.at[shard_rows(shard), :])],
    )
    turn_gu = Turn(
        net, keep, at,
        lambda i, group: (gw, uw)[i % 2].at[:, lane(group * units + (i // 2) * half, half)],
        lambda i, shard: w_gu.at[shard_rows(shard), i * half : (i + 1) * half],
        [((2 * b, 2 * b + 1), lambda shard, b=b: w_gu.at[shard_rows(shard), b * units : (b + 1) * units]) for b in (0, 1)],
    )
    turn_o = Turn(
        net, keep, at,
        lambda i, group: ow.at[row(group * HD, HD), :],
        lambda i, shard: w_o.at[:, columns_of(shard)],
        [((0,), lambda shard: w_o.at[:, columns_of(shard)])],
    )
    turn_d = Turn(
        net, keep, at,
        lambda i, group: dw.at[row(group * units + i * half, half), :],
        lambda i, shard: w_d.at[i * half : (i + 1) * half, columns_of(shard)],
        [((b,), lambda shard, b=b: w_d.at[b * half : (b + 1) * half, columns_of(shard)]) for b in (0, 1)],
    )

    gains[...] = jnp.zeros_like(gains)
    gains[0:1, :] = gain_one[...].astype(F32).reshape(1, width)
    gains[1:2, :] = gain_two[...].astype(F32).reshape(1, width)
    gain_slot = gains_all.at[:, columns_of(s)]
    gain_moves = net.lot(range(1, shards), lambda m: (gains, gain_slot, (s ^ m, h)), gain_in)
    for m in range(1, shards):
        gain_moves.start(m)
    gain_own = keep.put(gains, gain_slot)
    strip = row(at.q * quarter, quarter)
    one = Spread(net, at, rows_one, quarter, tok.at[strip, :])
    one.start()
    own_rows = keep.put(tok, rows_one.at[chunk(0), :])
    own_strip = keep.put(tok.at[strip, :], own_x)
    turn_qkv.start(3)
    turn_qkv.start(2)
    turn_qkv.mine()
    turn_o.mine()
    own_cot = keep.put(cot, rows_cot.at[chunk(0), :])
    gain_part[...] = jnp.zeros_like(gain_part)

    def clear(i):
        rows = row(i * 64, 64)
        accum[rows, :] = jnp.zeros_like(accum[rows, :])

    each(total_rows // 64, clear)

    def tables(i):
        rows = row(i * 64, 64)
        first_row = (i // (count // 64) * ranks + r) * count + i % (count // 64) * 64
        places = (first_row + lax.broadcasted_iota(jnp.int32, (64, HD), 0)).astype(F32)
        lanes = lax.broadcasted_iota(jnp.int32, (64, HD), 1)
        low_half = lanes < HD // 2
        order = jnp.where(low_half, lanes, lanes - HD // 2).astype(F32)
        angles = places * jnp.exp(order * (-math.log(10000.0) / (HD // 2)))
        cosines[rows, :] = jnp.cos(angles)
        sines[rows, :] = jnp.where(low_half, -jnp.sin(angles), jnp.sin(angles))

    each(groups * count // 64, tables)

    gain_own.wait()
    for m in range(1, shards):
        gain_moves.arrived(m)

    def norm_one(m):
        def some(i):
            rows = row((g ^ m) * count + i * 32, 32)
            values = rows_one[rows, :].astype(F32)
            inverse = lax.rsqrt(mean_square(values) + epsilon)
            rows_one[rows, :] = (values * inverse * gains_all[0:1, :]).astype(BF16)

        each(count // 32, some)

    own_rows.wait()
    own_strip.wait()
    norm_one(0)
    one.arrive(1)
    one.arrive(2)
    turn_qkv.start(1)
    for m in (3, 2, 1):
        turn_o.start(m)
    one.second(1)
    one.second(2)
    turn_qkv.pass_on(3)
    one.arrive(3)
    turn_qkv.pass_on(2)
    turn_qkv.pass_on(1)
    grad = Spread(net, at, rows_cot, quarter, cot.at[strip, :])
    grad.start()
    one.second(3)
    for m in (1, 2, 3):
        one.ready(m)
    one.sent()
    for m in (1, 2, 3):
        norm_one(m)
    for m in (3, 2, 1):
        turn_d.start(m, 0)
    turn_qkv.ready()

    def own_place(m):
        return row(((g ^ m) * ranks + r) * count, count)

    pair_moves = net.lot(
        range(4),
        lambda m: (pairs.at[own_place(m), :], pairs.at[own_place(m), :], at.beside()),
        pairs.at[0 : groups * count, :],
    )

    def project(m):
        rows, place = chunk(m), own_place(m)
        heads = dot(rows_one[rows, :], w_qkv[...])
        cos_part, sin_part = cosines[rows, :], sines[rows, :]
        queries[rows, :] = turned(heads[:, :HD], cos_part, sin_part).astype(BF16)
        pairs[place, :HD] = turned(heads[:, HD : 2 * HD], cos_part, sin_part).astype(BF16)
        pairs[place, HD:] = heads[:, 2 * HD :].astype(BF16)
        pair_moves.start(m)

    each(4, project)
    pair_moves.mark(range(4))
    for m in (3, 2, 1):
        turn_o.pass_on(m)
    for m in (3, 2, 1):
        turn_d.start(m, 1)
    turn_gu.start(3, 0, (0,))
    grad.arrive(1)
    grad.arrive(2)
    turn_d.mine(0)
    turn_gu.mine(0)
    for m in (0, 1, 2, 3):
        pair_moves.arrived(m)
    span = ranks * count

    def weights_of(m, j, query):
        keys = pairs[row(j * span, span), :HD]
        scores = dot_nt(query, keys) * score_scale - score_shift
        q_place = ((g ^ m) * ranks + r) * count + lax.broadcasted_iota(jnp.int32, (count, span), 0)
        k_place = j * span + lax.broadcasted_iota(jnp.int32, (count, span), 1)
        return jnp.where(k_place <= q_place, jax.nn.sigmoid(scores), 0.0)

    def attend(m):
        rows = chunk(m)
        query = queries[rows, :]

        def step(j, total):
            weight = weights_of(m, j, query).astype(BF16)
            return total + dot(weight, pairs[row(j * span, span), HD:])

        total = lax.fori_loop(0, (g ^ m) + 1, step, jnp.zeros((count, HD), F32))
        low = total.astype(BF16)
        mix[rows, :] = low

        @pl.when(m == 3)
        def _():
            turn_o.ready()

        part_a[rows, :] = dot(low, w_o[...]).astype(BF16)

    set_a, set_b = (part_a, near_a, xin_a, zin_a), (part_b, near_b, xin_b, zin_b)
    first = Collect(net, at, set_a, quarter, summed)
    first.produce(attend)
    first.third(3)
    first.second(0)
    turn_gu.start(1, 0)
    turn_d.mine(1)
    turn_gu.mine(1)
    for m in (3, 2, 1):
        turn_d.pass_on(m, 0)
    first.third(2)
    turn_gu.start(3, 0, (1,))
    grad.second(1)
    grad.second(2)
    grad.arrive(3)
    first.third(1)
    turn_gu.start(1, 1)
    for m in (3, 2, 1):
        turn_d.pass_on(m, 1)
    turn_gu.pass_on(1, 0)
    first.last()
    two = Spread(net, at, rows_two, quarter)
    mine_start = (g * 4 + at.q) * quarter

    def norm_two(i):
        few = row(i * 16, 16)
        values = own_x[few, :].astype(F32) + first.total(few)
        hidden[few, :] = values
        inverse = lax.rsqrt(mean_square(values) + epsilon)
        rows_two[row(mine_start + i * 16, 16), :] = (values * inverse * gains_all[1:2, :]).astype(BF16)

    each(quarter // 16, norm_two)
    two.start()
    turn_gu.start(2, 0)
    grad.second(3)
    two.second(0)
    two.arrive(1)
    turn_gu.pass_on(3, 0)
    turn_gu.pass_on(1, 1)
    turn_d.ready(0)
    own_cot.wait()

    def early(m, b):
        lanes = slice(b * half, (b + 1) * half)
        dmixed[chunk(m), lanes] = dot_nt(rows_cot[chunk(m), :], w_d[lanes, :])

    for m in (1, 2, 3):
        grad.ready(m)
    each(4, lambda m: early(m, 0))
    two.arrive(2)
    for m in (3, 2):
        turn_gu.start(m, 1)
    two.second(1)
    two.second(2)
    two.arrive(3)
    turn_gu.pass_on(2, 0)
    two.second(3)
    for m in (0, 1, 2, 3):
        two.ready(m)
    turn_gu.ready(0)

    def feed(m, b):
        rows = chunk(m)
        lanes, pair = slice(b * half, (b + 1) * half), slice(b * units, (b + 1) * units)
        both = dot(rows_two[rows, :], w_gu[:, pair])
        gate, up = both[:, :half], both[:, half:]
        sig = jax.nn.sigmoid(gate)
        act = gate * sig
        mixed[rows, lanes] = (act * up).astype(BF16)
        back = dmixed[rows, lanes]
        dgu[rows, b * units : b * units + half] = (back * up * sig * (1.0 + gate * (1.0 - sig))).astype(BF16)
        dgu[rows, b * units + half : (b + 1) * units] = (back * act).astype(BF16)
        total = dot_nt(dgu[rows, pair], w_gu[:, pair])
        if b:
            total += part_a[rows, :].astype(F32)
        part_a[rows, :] = total.astype(BF16)

    def out_part(m, b):
        rows = chunk(m)
        lanes = slice(b * half, (b + 1) * half)
        total = dot(mixed[rows, lanes], w_d[lanes, :])
        if b:
            total += part_b[rows, :].astype(F32)
        part_b[rows, :] = total.astype(BF16)

    def halves(m, work, lot):
        d = g ^ m

        def step(k):
            work(d * ranks + (r ^ 1 ^ k))

            @pl.when(k == 0)
            def _():
                lot.start(m)

        each(2, step)

    def several(groups_, work, lot):
        first_, last_ = groups_
        each(first_ - last_ + 1, lambda i: halves(first_ - i, work, lot))
        lot.mark(range(last_, first_ + 1))

    def beside(source, target, bulk):
        def describe(m):
            d = g ^ m
            return (source(d * ranks + (r ^ 1)), target(d), at.beside())

        return net.lot(range(4), describe, bulk)

    pairs_of = [slice(b * units, (b + 1) * units) for b in (0, 1)]
    lanes_of = [slice(b * half, (b + 1) * half) for b in (0, 1)]
    moves_gu = [
        beside(lambda shard, p=p: w_gu.at[shard_rows(shard), p], lambda d, p=p: in_gu.at[d, :, p], in_gu.at[:, :, p])
        for p in pairs_of
    ]
    moves_d = [
        beside(lambda shard, p=p: w_d.at[p, columns_of(shard)], lambda d, p=p: in_d.at[d, p, :], in_d.at[:, p, :])
        for p in lanes_of
    ]
    moves_qkv = beside(lambda shard: w_qkv.at[shard_rows(shard), :], lambda d: in_qkv.at[d], in_qkv)
    moves_o = beside(lambda shard: w_o.at[:, columns_of(shard)], lambda d: in_o.at[d], in_o)

    def grads_gu(groups_, b):
        def work(shard):
            w_gu[shard_rows(shard), pairs_of[b]] = dot_tn(rows_two[:, columns_of(shard)], dgu[:, pairs_of[b]]).astype(BF16)

        several(groups_, work, moves_gu[b])

    def grads_d(groups_, b):
        def work(shard):
            columns = columns_of(shard)
            w_d[lanes_of[b], columns] = dot_tn(mixed[:, lanes_of[b]], rows_cot[:, columns]).astype(BF16)

        several(groups_, work, moves_d[b])

    def grads_o(groups_):
        def work(shard):
            columns = columns_of(shard)
            w_o[:, columns] = dot_tn(mix[...], rows_dh[:, columns]).astype(BF16)

        several(groups_, work, moves_o)

    def grads_qkv(groups_):
        def work(shard):
            w_qkv[shard_rows(shard), :] = dot_tn(rows_one[:, columns_of(shard)], dqkv[...]).astype(BF16)

        several(groups_, work, moves_qkv)

    final, final_own = [], []

    def give(moves, whole_, m):
        if m:
            lot = net.lot((0,), lambda j: [(a, b, at.along(m)) for a, b in moves], whole_, lambda j: whole_)
            lot.start(0)
            final.append(lot)
        else:
            final_own.extend(keep.put(a, b) for a, b in moves)

    def sums(m, lot, mine_of, other_of, size):
        lot.arrived(m)

        def step(i):
            a, rows, lanes = mine_of(i)
            b, d, few, others = other_of(i)
            a[rows, lanes] = (a[rows, lanes].astype(F32) + b[d, few, others].astype(F32)).astype(BF16)

        each(size // 32, step)

    def sums_gu(m, b):
        d, p = g ^ m, pairs_of[b]
        start = (d * ranks + r) * width
        sums(
            m, moves_gu[b],
            lambda i: (w_gu, row(start + i * 32, 32), p), lambda i: (in_gu, d, row(i * 32, 32), p), width,
        )
        moves = []
        for i, out in enumerate((g_out, u_out)):
            place = b * units + i * half
            moves.append((w_gu.at[row(start, width), place : place + half], out.at[:, lane(g * units + b * half, half)]))
        give(moves, w_gu.at[row(start, width), p], m)

    def sums_d(m, b):
        d, base = g ^ m, b * half
        columns = columns_of(d * ranks + r)
        sums(
            m, moves_d[b],
            lambda i: (w_d, row(base + i * 32, 32), columns),
            lambda i: (in_d, d, row(base + i * 32, 32), slice(None)), half,
        )
        block = w_d.at[lanes_of[b], columns]
        give([(block, d_out.at[row(g * units + base, half), :])], block, m)

    def sums_o(m):
        d = g ^ m
        columns = columns_of(d * ranks + r)
        sums(
            m, moves_o,
            lambda i: (w_o, row(i * 32, 32), columns), lambda i: (in_o, d, row(i * 32, 32), slice(None)), HD,
        )
        give([(w_o.at[:, columns], o_out.at[row(g * HD, HD), :])], w_o.at[:, columns], m)

    def sums_qkv(m):
        d = g ^ m
        start = (d * ranks + r) * width
        sums(
            m, moves_qkv,
            lambda i: (w_qkv, row(start + i * 32, 32), slice(None)),
            lambda i: (in_qkv, d, row(i * 32, 32), slice(None)), width,
        )
        moves = [
            (w_qkv.at[row(start, width), i * HD : (i + 1) * HD], out.at[:, lane(g * HD, HD)])
            for i, out in enumerate((q_out, k_out, v_out))
        ]
        give(moves, w_qkv.at[row(start, width), :], m)

    first.sent()
    second = Collect(net, at, set_a, quarter, summed)
    each(4, lambda m: feed(m, 0))
    turn_gu.pass_on(3, 1)
    turn_gu.sent(0)
    grads_gu((3, 3), 0)
    turn_d.ready(1)
    each(4, lambda m: early(m, 1))
    turn_gu.pass_on(2, 1)
    grads_gu((2, 1), 0)
    each(4, lambda m: out_part(m, 0))
    turn_d.sent(0)
    grads_d((3, 1), 0)
    sums_gu(3, 0)
    turn_gu.ready(1)
    second.produce(lambda m: feed(m, 1))
    sums_gu(2, 0)
    second.third(3)
    second.second(0)
    sums_gu(1, 0)
    second.third(2)
    turn_gu.sent(1)
    turn_d.sent(1)
    grads_gu((3, 2), 1)
    second.third(1)
    grads_gu((1, 1), 1)
    each(4, lambda m: out_part(m, 1))
    out_sum = Collect(net, at, set_b, quarter, summed)
    for m in (3, 2, 1, 0):
        out_sum.first(m)
    second.last()
    three = Spread(net, at, rows_dh, quarter)

    def back_two(i, gain_grad):
        few = row(i * 16, 16)
        own = row(mine_start + i * 16, 16)
        upstream, values = second.total(few), hidden[few, :]
        inverse = lax.rsqrt(mean_square(values) + epsilon)
        scaled = upstream * gains_all[1:2, :]
        back = inverse * scaled - values * (inverse * inverse * inverse) * jnp.mean(
            scaled * values, axis=1, keepdims=True
        )
        total = rows_cot[own, :].astype(F32) + back
        dhidden[few, :] = total
        rows_dh[own, :] = total.astype(BF16)
        return gain_grad + jnp.sum(upstream * values * inverse, axis=0, keepdims=True)

    gain_part[1:2, :] = lax.fori_loop(0, quarter // 16, back_two, jnp.zeros((1, depth), F32))
    three.start()
    for m in (3, 2, 1):
        sums_d(m, 0)
    grads_d((3, 1), 1)
    three.second(0)
    out_sum.second(3)
    out_sum.second(2)
    for b in (0, 1):
        grads_gu((0, 0), b)
    three.arrive(1)
    for b in (0, 1):
        grads_d((0, 0), b)
    three.arrive(2)
    sums_gu(3, 1)
    out_sum.third(3)
    three.second(1)
    three.second(2)
    sums_gu(2, 1)
    three.arrive(3)
    out_sum.second(1)
    out_sum.second(0)
    sums_gu(1, 1)
    three.second(3)

    def attend_back(m):
        three.ready(m)
        rows = chunk(m)
        query = queries[rows, :]
        dm = dot_nt(rows_dh[rows, :], w_o[...]).astype(BF16)

        def step(j, total):
            block = row(j * span, span)
            weight = weights_of(m, j, query)
            dweight = dot_nt(dm, pairs[block, HD:])
            dscore = (dweight * weight * (1.0 - weight)).astype(BF16)
            accum[block, HD:] += dot_tn(weight.astype(BF16), dm)
            accum[block, :HD] += dot_tn(dscore, query)
            return total + dot(dscore, pairs[block, :HD])

        total = lax.fori_loop(0, (g ^ m) + 1, step, jnp.zeros((count, HD), F32))
        dqkv[rows, :HD] = turned(total * score_scale, cosines[rows, :], -sines[rows, :]).astype(BF16)

    pair_back = net.lot(range(4), lambda m: (pair_send.at[g ^ m], pair_in.at[g ^ m], at.beside()), pair_send)

    def send_pair(m):
        d = g ^ m
        rows = row((d * ranks + (r ^ 1)) * count, count)
        pair_send[d] = accum[rows, :].astype(BF16)
        pair_back.start(m)

    def back_from_end(i):
        m = g ^ (groups - 1 - i)
        attend_back(m)
        send_pair(m)

    each(4, back_from_end)
    pair_back.mark(range(4))
    out_sum.third(2)
    for m in (3, 2, 1):
        sums_d(m, 1)
    out_sum.third(1)
    turn_o.sent()
    grads_o((3, 0))
    second.sent()
    third = Collect(net, at, set_a, quarter, summed)

    def back_one(m):
        d = g ^ m
        rows = chunk(m)
        pair_back.arrived(m)
        both = accum[own_place(m), :] + pair_in[d].astype(F32)
        dqkv[rows, HD : 2 * HD] = turned(both[:, :HD] * score_scale, cosines[rows, :], -sines[rows, :]).astype(BF16)
        dqkv[rows, 2 * HD :] = both[:, HD:].astype(BF16)
        part_a[rows, :] = dot_nt(dqkv[rows, :], w_qkv[...]).astype(BF16)

    third.produce(back_one)
    third.second(0)
    third.third(3)
    turn_qkv.sent()
    grads_qkv((3, 2))
    for m in (3, 2, 1):
        sums_o(m)
    third.third(2)
    grads_qkv((1, 0))
    third.third(1)
    for m in (3, 2):
        sums_qkv(m)
    for b in (0, 1):
        sums_gu(0, b)
        sums_d(0, b)
    ends = []

    def share(source, target):
        place = target.at[strip, :]
        final_own.append(keep.put(source, place))
        lot = net.lot((0, 1), lambda j: (source, place, (at.near(), at.across())[j]), target.at[0 : 2 * quarter, :])
        lot.start(0)
        lot.start(1)
        ends.append((lot, target))

    def relay():
        lot, target = ends.pop()
        lot.arrived(1)
        final.append(lot)
        block = target.at[row((at.q ^ 1) * quarter, quarter), :]
        on = net.lot((0,), lambda j: (block, block, at.near()), block)
        on.start(0)
        final.append(on)

    out_sum.last()

    def result_rows(i):
        few = row(i * 16, 16)
        result_own[few, :] = (hidden[few, :] + out_sum.total(few)).astype(BF16)

    each(quarter // 16, result_rows)
    share(result_own, result_out)
    sums_qkv(1)
    sums_o(0)
    sums_qkv(0)
    third.last()

    def back_rows(i, gain_grad):
        few = row(i * 16, 16)
        upstream, values = third.total(few), own_x[few, :].astype(F32)
        inverse = lax.rsqrt(mean_square(values) + epsilon)
        scaled = upstream * gains_all[0:1, :]
        back = inverse * scaled - values * (inverse * inverse * inverse) * jnp.mean(
            scaled * values, axis=1, keepdims=True
        )
        rows_own[few, :] = (dhidden[few, :] + back).astype(BF16)
        return gain_grad + jnp.sum(upstream * values * inverse, axis=0, keepdims=True)

    gain_part[0:1, :] = lax.fori_loop(0, quarter // 16, back_rows, jnp.zeros((1, depth), F32))
    gain_sums = net.lot(
        range(1, shards), lambda m: (gain_part.at[:, columns_of(s ^ m)], gain_in.at[m - 1], (s ^ m, h)), gain_in
    )
    for m in range(1, shards):
        gain_sums.start(m)
    relay()
    share(rows_own, rows_out)
    total = gain_part[:, columns_of(s)]
    for m in range(1, shards):
        gain_sums.arrived(m)
        total += gain_in[m - 1]
    gain_mid[...] = total
    gain_ends = net.lot(range(1, 4), lambda m: (gain_mid, gain_near.at[m - 1], (s, h ^ m)), gain_near)
    for m in range(1, 4):
        gain_ends.start(m)
    relay()
    for m in range(1, 4):
        gain_ends.arrived(m)
        total += gain_near[m - 1]
    gains_out[...] = total
    for lot in final:
        lot.arrived(0)
    net.finish()
    for copy in final_own:
        copy.wait()


def rows_plan(
    groups,
    ranks,
    tokens,
    attn_gain,
    query_weight,
    key_weight,
    value_weight,
    out_weight,
    mlp_gain,
    gate_weight,
    up_weight,
    down_weight,
    cotangent,
):
    count, depth = tokens.shape
    shards = groups * ranks
    quarter = count // 4
    width = query_weight.shape[0]
    units = gate_weight.shape[1] // groups
    total_rows = count * shards
    here = groups * count
    ins = (
        tokens, cotangent, attn_gain, mlp_gain,
        query_weight, key_weight, value_weight, out_weight, gate_weight, up_weight, down_weight,
    )
    shape = jax.ShapeDtypeStruct
    hbm, vmem = pl.BlockSpec(memory_space=pl.ANY), pl.BlockSpec(memory_space=pltpu.VMEM)
    owners = (query_weight, key_weight, value_weight, out_weight, gate_weight, up_weight, down_weight)
    outs = [
        shape((count, depth), BF16),
        shape((count, depth), BF16),
        shape((8, width), F32),
        *(shape(w.shape, BF16) for w in owners),
    ]

    def low(*extent):
        return pltpu.VMEM(extent, BF16)

    def full(*extent):
        return pltpu.VMEM(extent, F32)

    def collector():
        return [
            low(here, depth),
            low(groups, 2 * quarter, depth),
            low(groups, quarter, depth),
            low(3, quarter, depth),
        ]

    scratch = [
        full(8, width), full(8, depth), full(here, HD), full(here, HD),
        low(here, depth), low(here, depth), low(here, depth), low(here, depth),
        low(depth, 3 * HD), low(HD, depth), low(depth, 2 * units), low(units, depth),
        low(here, HD), low(total_rows, 2 * HD), low(here, HD), low(here, 3 * HD),
        full(total_rows, 2 * HD), low(groups, count, 2 * HD), low(groups, count, 2 * HD),
        low(here, units), low(here, 2 * units), full(here, units),
        low(quarter, depth), full(quarter, depth), full(quarter, depth), full(quarter, depth),
        *collector(), *collector(),
        low(groups, width, 2 * units), low(groups, units, width), low(groups, width, 3 * HD), low(groups, HD, width),
        full(8, depth), full(shards - 1, 8, width), full(8, width), full(3, 8, width),
        low(quarter, depth), low(quarter, depth),
        pltpu.SemaphoreType.DMA((SENDS,)), pltpu.SemaphoreType.DMA((RECEIVES,)), pltpu.SemaphoreType.DMA((KEEPS,)),
    ]
    moved = pl.pallas_call(
        functools.partial(layer_body, groups, ranks),
        out_shape=outs,
        in_specs=[hbm] * 2 + [vmem] * 2 + [hbm] * 7,
        out_specs=[hbm, hbm, vmem] + [hbm] * 7,
        scratch_shapes=scratch,
        compiler_params=pltpu.CompilerParams(
            collective_id=1, has_side_effects=True, vmem_limit_bytes=VMEM_LIMIT
        ),
    )(*ins)
    steps = 8

    def sliced(array):
        rows, columns = array.shape
        return pl.BlockSpec((rows // steps, columns), lambda i: (i, 0))

    gain_specs = [pl.BlockSpec((8, width), lambda i: (0, 0))]
    row_spec = pl.BlockSpec((width,), lambda i: (0,))
    specs = [sliced(moved[0]), sliced(moved[1]), *(sliced(w) for w in moved[3:])]
    gain_row = shape((width,), F32)
    one, two, result, rows_grad, *grads = pl.pallas_call(
        cast_body,
        grid=(steps,),
        out_shape=[gain_row, gain_row, moved[0], moved[1], *(shape(w.shape, F32) for w in owners)],
        in_specs=gain_specs + specs,
        out_specs=[row_spec, row_spec] + specs,
        compiler_params=pltpu.CompilerParams(vmem_limit_bytes=VMEM_LIMIT),
    )(moved[2], moved[0], moved[1], *moved[3:])
    return (result, rows_grad, one, *grads[:4], two, *grads[4:])


def cast_body(*refs):
    inputs = len(refs) // 2
    gains, sources, (one, two, *targets) = refs[0], refs[1:inputs], refs[inputs:]
    one[...] = gains[0, :]
    two[...] = gains[1, :]
    for source, target in zip(sources, targets):
        target[...] = source[...].astype(target.dtype)


def on_device(tokens, attn_gain, query_weight, *rest):
    groups = query_weight.shape[1] // HD
    ranks = lax.axis_size("seq") // groups
    fits = lax.axis_size("head") == 4 and groups == 4 and ranks == 2 and query_weight.shape[0] % 128 == 0
    plan = functools.partial(rows_plan, groups, ranks) if fits else gathered_weights
    return plan(tokens, attn_gain, query_weight, *rest)


def solution(mesh):
    in_specs = (
        P("seq", None),
        P("seq"),
        P("seq", "head"),
        P("seq", "head"),
        P("seq", "head"),
        P("head", "seq"),
        P("seq"),
        P("seq", "head"),
        P("seq", "head"),
        P("head", "seq"),
        P("seq", None),
    )
    out_specs = (
        P("seq", None),
        P("seq", None),
        P("seq"),
        P("seq", "head"),
        P("seq", "head"),
        P("seq", "head"),
        P("head", "seq"),
        P("seq"),
        P("seq", "head"),
        P("seq", "head"),
        P("head", "seq"),
    )
    return jax.shard_map(
        on_device, mesh=mesh, in_specs=in_specs, out_specs=out_specs, check_vma=False
    )
```

```python
import functools
import math

import jax
import jax.numpy as jnp
from jax import lax
from jax.experimental import pallas as pl
from jax.experimental.pallas import tpu as pltpu
from jax.sharding import PartitionSpec as P

MESH = pl.DeviceIdType.MESH
F32, BF16 = jnp.float32, jnp.bfloat16

HD = 128


epsilon = 1e-05
block_limit = 512
VMEM_LIMIT = 63 * 2**20
SENDS, RECEIVES, KEEPS = 103, 295, 26
PIECES = 2


def tables(offset, length, half_width):
    places = (offset + jnp.arange(length, dtype=jnp.int32)).astype(jnp.float32)
    frequency = jnp.exp(
        jnp.arange(half_width, dtype=jnp.float32) * (-math.log(10000.0) / half_width)
    )
    angles = places[:, None] * frequency[None, :]
    return (jnp.cos(angles)[:, None, :], jnp.sin(angles)[:, None, :])


def rotary(values, cos_table, sin_table):
    half_width = values.shape[-1] // 2
    front = values[..., :half_width]
    back_half = values[..., half_width:]
    return jnp.concatenate(
        [front * cos_table - back_half * sin_table, back_half * cos_table + front * sin_table],
        axis=-1,
    )


def unrotary(gradient, cos_table, sin_table):
    half_width = gradient.shape[-1] // 2
    front = gradient[..., :half_width]
    back_half = gradient[..., half_width:]
    return jnp.concatenate(
        [front * cos_table + back_half * sin_table, back_half * cos_table - front * sin_table],
        axis=-1,
    )


def norm_back(values, inverse, gain_vector, upstream):
    scaled = upstream * gain_vector
    gain_grad = jnp.sum(upstream * values * inverse, axis=0)
    value_grad = inverse * scaled - values * inverse**3 * jnp.mean(
        scaled * values, axis=1, keepdims=True
    )
    return (value_grad, gain_grad)


def gathered_weights(
    tokens,
    attn_gain,
    query_weight,
    key_weight,
    value_weight,
    out_weight,
    mlp_gain,
    gate_weight,
    up_weight,
    down_weight,
    cotangent,
):
    row_count = tokens.shape[0]
    total_rows = row_count * lax.axis_size("seq")
    row_start = lax.axis_index("seq") * row_count
    local_width = query_weight.shape[1]
    local_heads = local_width // HD
    score_scale = 1.0 / math.sqrt(HD)
    score_shift = math.log(total_rows)
    block_rows = math.gcd(total_rows, block_limit)
    block_count = total_rows // block_rows
    attn_gain_full, query_full, key_full, value_full, out_full = (
        lax.all_gather(attn_gain, "seq", axis=0, tiled=True),
        lax.all_gather(query_weight, "seq", axis=0, tiled=True),
        lax.all_gather(key_weight, "seq", axis=0, tiled=True),
        lax.all_gather(value_weight, "seq", axis=0, tiled=True),
        lax.all_gather(out_weight, "seq", axis=1, tiled=True),
    )
    mlp_gain_full, gate_full, up_full, down_full = (
        lax.all_gather(mlp_gain, "seq", axis=0, tiled=True),
        lax.all_gather(gate_weight, "seq", axis=0, tiled=True),
        lax.all_gather(up_weight, "seq", axis=0, tiled=True),
        lax.all_gather(down_weight, "seq", axis=1, tiled=True),
    )
    token_values = tokens.astype(jnp.float32)
    inverse_one = lax.rsqrt(jnp.mean(token_values * token_values, axis=1, keepdims=True) + epsilon)
    normed_one = (token_values * inverse_one * attn_gain_full.astype(jnp.float32)).astype(
        jnp.bfloat16
    )
    query_pre = jnp.dot(normed_one, query_full, preferred_element_type=jnp.float32)
    key_pre = jnp.dot(normed_one, key_full, preferred_element_type=jnp.float32)
    value_rows = (
        jnp.dot(normed_one, value_full, preferred_element_type=jnp.float32)
        .astype(jnp.bfloat16)
        .reshape(row_count, local_heads, HD)
    )
    cos_table, sin_table = tables(row_start, row_count, HD // 2)
    query_rows = (
        rotary(query_pre.reshape(row_count, local_heads, HD), cos_table, sin_table)
        .astype(jnp.bfloat16)
        .reshape(row_count, local_width)
    )
    key_rows = rotary(key_pre.reshape(row_count, local_heads, HD), cos_table, sin_table).astype(
        jnp.bfloat16
    )
    all_queries = lax.all_gather(query_rows, "seq", axis=0, tiled=True)
    key_places = row_start + jnp.arange(row_count, dtype=jnp.int32)

    def weights_for(query_block, block_start):
        scores = (
            jnp.einsum("qhd,khd->hqk", query_block, key_rows, preferred_element_type=jnp.float32)
            * score_scale
            - score_shift
        )
        query_places = block_start + jnp.arange(query_block.shape[0], dtype=jnp.int32)
        visible = key_places[None, :] <= query_places[:, None]
        return jnp.where(visible[None], jax.nn.sigmoid(scores), 0.0)

    step_rows = math.gcd(row_count * lax.axis_size("seq"), block_limit)
    step_count = row_count * lax.axis_size("seq") // step_rows
    picked = all_queries.reshape(step_count, step_rows, local_heads, HD)
    starts = jnp.arange(step_count, dtype=jnp.int32) * step_rows

    def one_block(packed):
        query_block, block_start = packed
        weights = weights_for(query_block, block_start).astype(jnp.bfloat16)
        return jnp.einsum(
            "hqk,khd->qhd", weights, value_rows, preferred_element_type=jnp.float32
        ).reshape(step_rows, local_width)

    attn_mix = lax.psum_scatter(
        lax.map(one_block, (picked, starts)).reshape(row_count * lax.axis_size("seq"), local_width),
        "seq",
        scatter_dimension=0,
        tiled=True,
    ).astype(jnp.bfloat16)
    attn_branch = lax.psum(jnp.dot(attn_mix, out_full, preferred_element_type=jnp.float32), "head")
    hidden = token_values + attn_branch
    inverse_two = lax.rsqrt(jnp.mean(hidden * hidden, axis=1, keepdims=True) + epsilon)
    normed_two = (hidden * inverse_two * mlp_gain_full.astype(jnp.float32)).astype(jnp.bfloat16)
    gate_pre = jnp.dot(normed_two, gate_full, preferred_element_type=jnp.float32)
    up_pre = jnp.dot(normed_two, up_full, preferred_element_type=jnp.float32)
    gate_act = jax.nn.silu(gate_pre)
    mixed = (gate_act * up_pre).astype(jnp.bfloat16)
    mlp_branch = lax.psum(
        jnp.dot(mixed, down_full, preferred_element_type=jnp.float32).astype(jnp.bfloat16), "head"
    ).astype(jnp.float32)
    result = (hidden + mlp_branch).astype(jnp.bfloat16)
    kept_weights = (
        lax.all_gather(attn_gain, "seq", axis=0, tiled=True),
        lax.all_gather(query_weight, "seq", axis=0, tiled=True),
        lax.all_gather(key_weight, "seq", axis=0, tiled=True),
        lax.all_gather(value_weight, "seq", axis=0, tiled=True),
        lax.all_gather(out_weight, "seq", axis=1, tiled=True),
        lax.all_gather(mlp_gain, "seq", axis=0, tiled=True),
        lax.all_gather(gate_weight, "seq", axis=0, tiled=True),
        lax.all_gather(up_weight, "seq", axis=0, tiled=True),
        lax.all_gather(down_weight, "seq", axis=1, tiled=True),
    )
    (
        attn_gain_back,
        query_back,
        key_back,
        value_back,
        out_back,
        mlp_gain_back,
        gate_back,
        up_back,
        down_back,
    ) = kept_weights
    attn_gain_f = attn_gain_back.astype(jnp.float32)
    mlp_gain_f = mlp_gain_back.astype(jnp.float32)
    grad_values = cotangent.astype(jnp.float32)
    grad_down = jnp.einsum("tf,td->fd", mixed, cotangent, preferred_element_type=jnp.float32)
    dmixed = jnp.einsum("td,fd->tf", cotangent, down_back, preferred_element_type=jnp.float32)
    gate_sig = jax.nn.sigmoid(gate_pre)
    dgate = (dmixed * up_pre * gate_sig * (1.0 + gate_pre * (1.0 - gate_sig))).astype(jnp.bfloat16)
    dup = (dmixed * gate_act).astype(jnp.bfloat16)
    grad_gate = jnp.einsum("tk,tf->kf", normed_two, dgate, preferred_element_type=jnp.float32)
    grad_up = jnp.einsum("tk,tf->kf", normed_two, dup, preferred_element_type=jnp.float32)
    dnormed_two = lax.psum(
        jnp.einsum("tf,kf->tk", dgate, gate_back, preferred_element_type=jnp.float32)
        + jnp.einsum("tf,kf->tk", dup, up_back, preferred_element_type=jnp.float32),
        "head",
    )
    dhidden_norm, grad_mlp_gain = norm_back(hidden, inverse_two, mlp_gain_f, dnormed_two)
    dhidden = grad_values + dhidden_norm
    mlp_sums = (grad_mlp_gain, grad_gate, grad_up, grad_down)
    dhidden_low = dhidden.astype(jnp.bfloat16)
    grad_out = jnp.einsum("tc,td->cd", attn_mix, dhidden_low, preferred_element_type=jnp.float32)
    dmix = jnp.einsum(
        "td,cd->tc", dhidden_low, out_back, preferred_element_type=jnp.float32
    ).astype(jnp.bfloat16)
    all_dmix = lax.all_gather(dmix, "seq", axis=0, tiled=True)

    def backward_block(carry, packed):
        key_accum, value_accum = carry
        query_block, grad_block, block_start = packed
        weights = weights_for(query_block, block_start)
        grad_weights = jnp.einsum(
            "qhd,khd->hqk", grad_block, value_rows, preferred_element_type=jnp.float32
        )
        grad_scores = (grad_weights * weights * (1.0 - weights)).astype(jnp.bfloat16)
        value_accum = value_accum + jnp.einsum(
            "hqk,qhd->khd",
            weights.astype(jnp.bfloat16),
            grad_block,
            preferred_element_type=jnp.float32,
        )
        key_accum = key_accum + jnp.einsum(
            "hqk,qhd->khd", grad_scores, query_block, preferred_element_type=jnp.float32
        )
        query_part = (
            jnp.einsum("hqk,khd->qhd", grad_scores, key_rows, preferred_element_type=jnp.float32)
            * score_scale
        )
        return ((key_accum, value_accum), query_part.reshape(block_rows, local_width))

    zero_rows = jnp.zeros((row_count, local_heads, HD), jnp.float32)
    block_starts = jnp.arange(block_count, dtype=jnp.int32) * block_rows
    (key_accum, value_accum), query_parts = lax.scan(
        backward_block,
        (zero_rows, zero_rows),
        (
            all_queries.reshape(block_count, block_rows, local_heads, HD),
            all_dmix.reshape(block_count, block_rows, local_heads, HD),
            block_starts,
        ),
    )
    query_sum = lax.psum_scatter(
        query_parts.reshape(total_rows, local_width), "seq", scatter_dimension=0, tiled=True
    )
    dquery_pre = (
        unrotary(query_sum.reshape(row_count, local_heads, HD), cos_table, sin_table)
        .reshape(row_count, local_width)
        .astype(jnp.bfloat16)
    )
    dkey_pre = (
        unrotary(key_accum * score_scale, cos_table, sin_table)
        .reshape(row_count, local_width)
        .astype(jnp.bfloat16)
    )
    dvalue = value_accum.reshape(row_count, local_width).astype(jnp.bfloat16)
    grad_query = jnp.einsum("tk,tc->kc", normed_one, dquery_pre, preferred_element_type=jnp.float32)
    grad_key = jnp.einsum("tk,tc->kc", normed_one, dkey_pre, preferred_element_type=jnp.float32)
    grad_value = jnp.einsum("tk,tc->kc", normed_one, dvalue, preferred_element_type=jnp.float32)
    dnormed_one = lax.psum(
        jnp.einsum("tc,kc->tk", dquery_pre, query_back, preferred_element_type=jnp.float32)
        + jnp.einsum("tc,kc->tk", dkey_pre, key_back, preferred_element_type=jnp.float32)
        + jnp.einsum("tc,kc->tk", dvalue, value_back, preferred_element_type=jnp.float32),
        "head",
    )
    dinput_norm, grad_attn_gain = norm_back(token_values, inverse_one, attn_gain_f, dnormed_one)
    input_grad = (dhidden + dinput_norm).astype(jnp.bfloat16)
    every_sum = (
        lax.psum_scatter(grad_attn_gain, "seq", scatter_dimension=0, tiled=True),
        lax.psum_scatter(grad_query, "seq", scatter_dimension=0, tiled=True),
        lax.psum_scatter(grad_key, "seq", scatter_dimension=0, tiled=True),
        lax.psum_scatter(grad_value, "seq", scatter_dimension=0, tiled=True),
        lax.psum_scatter(grad_out, "seq", scatter_dimension=1, tiled=True),
        lax.psum_scatter(grad_mlp_gain, "seq", scatter_dimension=0, tiled=True),
        lax.psum_scatter(grad_gate, "seq", scatter_dimension=0, tiled=True),
        lax.psum_scatter(grad_up, "seq", scatter_dimension=0, tiled=True),
        lax.psum_scatter(grad_down, "seq", scatter_dimension=1, tiled=True),
    )
    attn_sums = every_sum[:5]
    mlp_sums = every_sum[5:]
    return (
        result,
        input_grad,
        attn_sums[0],
        attn_sums[1],
        attn_sums[2],
        attn_sums[3],
        attn_sums[4],
        mlp_sums[0],
        mlp_sums[1],
        mlp_sums[2],
        mlp_sums[3],
    )


class Net:
    def __init__(self, send, receive):
        self.send, self.receive, self.sends, self.receives, self.lots = send, receive, 0, 0, []

    def lot(self, *args, **options):
        return Lot(self, *args, **options)

    def finish(self):
        for lot in self.lots:
            lot.sent()


class Lot:
    def __init__(self, net, indices, describe, bulk, arrival=None, apart=False):
        self.net, self.describe, self.bulk, self.arrival, self.apart = net, describe, bulk, arrival, apart
        self.place = {j: net.receives + i for i, j in enumerate(indices)}
        self.low = min(indices)
        self.send_base, self.receive_base = net.sends, net.receives
        net.receives += len(indices)
        net.sends += len(indices) if apart else 1
        self.started, self.open = set(), set()
        net.lots.append(self)

    def receive_at(self, j):
        return self.net.receive.at[self.receive_base + (j - self.low)]

    def send_at(self, j):
        return self.net.send.at[self.send_base + (j - self.low if self.apart else 0)]

    def start(self, j, pieces=None):
        described = self.describe(j)
        for i, (source, target, device) in enumerate(described if isinstance(described, list) else [described]):
            if pieces is None or i in pieces:
                pltpu.make_async_remote_copy(
                    src_ref=source,
                    dst_ref=target,
                    send_sem=self.send_at(j),
                    recv_sem=self.receive_at(j),
                    device_id=device,
                    device_id_type=MESH,
                ).start()
        if isinstance(j, int):
            self.mark((j,))

    def mark(self, indices):
        self.started.update(indices)
        self.open.update(indices if self.apart else (self.low,))

    def arrived(self, j):
        described = self.describe(j)
        target = self.arrival(j) if self.arrival else described[1]
        self.wait(target, self.receive_at(j))

    def wait(self, like, sem):
        pltpu.make_async_copy(like, like, sem).wait()

    def sent(self, j=None):
        for k in sorted(self.open) if j is None else [j] if j in self.open else []:
            self.open.remove(k)
            self.wait(self.bulk(k) if self.apart else self.bulk, self.send_at(k))


class Keep:
    def __init__(self, sems):
        self.sems, self.count = sems, 0

    def put(self, source, target):
        copy = pltpu.make_async_copy(source, target, self.sems.at[self.count])
        self.count += 1
        copy.start()
        return copy


class Where:
    def __init__(self, groups, ranks):
        self.s, self.h = lax.axis_index("seq"), lax.axis_index("head")
        self.g, self.r = self.s // ranks, self.s % ranks
        self.groups, self.ranks = groups, ranks
        self.q = self.h % 2 * 2 + self.h // 2

    def along(self, m):
        return (self.s ^ (m * self.ranks), self.h)

    def beside(self):
        return (self.s ^ 1, self.h)

    def across(self):
        return (self.s, self.h ^ 2)

    def near(self):
        return (self.s, self.h ^ 1)


def lane(start, size):
    return pl.ds(pl.multiple_of(start, 128), size)


def row(start, size):
    return pl.ds(pl.multiple_of(start, size), size)


def each(count, step):
    def body(i, carry):
        step(i)
        return carry

    lax.fori_loop(0, count, body, 0)


class Spread:
    def __init__(self, net, at, buffer, quarter, own=None):
        self.at, self.buffer, self.quarter, self.shared = at, buffer, quarter, own is not None
        self.size = quarter // PIECES

        def along(j):
            m, p = j // PIECES, j % PIECES
            if m == 3:
                return (self.block(2, 0, p), self.block(2, 0, p), at.along(1))
            first = self.block(0, 0, p) if own is None else own.at[row(at.q * quarter + p * self.size, self.size), :]
            return (first, self.block(0, 0, p), at.along(m))

        def moved(k, device):
            def describe(j):
                block = self.block(j // PIECES, k, j % PIECES)
                return (block, block, device)

            return describe

        low = 1 if self.shared else 0
        indices = range(low * PIECES, 4 * PIECES)
        some = buffer.at[0 : (4 - low) * quarter, :]
        self.z = net.lot(range(PIECES, 4 * PIECES), along, buffer.at[0 : 3 * quarter, :])
        self.x = net.lot(indices, moved(0, at.across()), some)
        self.c = net.lot(indices, moved(0, at.near()), some)
        self.d = net.lot(indices, moved(1, at.near()), some)

    def block(self, m, k, p):
        at = self.at
        start = ((at.g ^ m) * 4 + (at.q ^ k)) * self.quarter + p * self.size
        return self.buffer.at[row(start, self.size), :]

    def pass_on(self, j):
        self.x.start(j)
        self.c.start(j)

    def start(self):
        for m in (2, 1):
            for p in range(PIECES):
                self.z.start(m * PIECES + p)
        if not self.shared:
            for p in range(PIECES):
                self.pass_on(p)

    def arrive(self, m):
        for p in range(PIECES):
            j = m * PIECES + p
            self.z.arrived(j)
            if m == 2:
                self.z.start(3 * PIECES + p)
            self.pass_on(j)

    def second(self, m):
        for p in range(PIECES):
            self.x.arrived(m * PIECES + p)
            self.d.start(m * PIECES + p)

    def ready(self, m):
        for p in range(PIECES):
            self.c.arrived(m * PIECES + p)
            self.d.arrived(m * PIECES + p)

    def sent(self):
        for lot in (self.z, self.x, self.c, self.d):
            lot.sent()


class Collect:
    def __init__(self, net, at, refs, quarter, out):
        self.at, self.quarter, self.out = at, quarter, out
        self.size = quarter // PIECES
        self.part, self.near, self.xin, self.zin = refs
        self.a = net.lot(range(4), lambda m: (self.pair(m), self.near.at[at.g ^ m], at.near()), self.near)

        def across(j):
            m, few = j // PIECES, row(j % PIECES * self.size, self.size)
            return (self.part.at[self.rows(m, 1, j % PIECES), :], self.xin.at[at.g ^ m, few, :], at.across())

        hops = {3: (0, 1), 2: (2, 2), 1: (1, 1)}

        def along(j):
            (slot, hop), few = hops[j // PIECES], row(j % PIECES * self.size, self.size)
            return (self.part.at[self.rows(j // PIECES, 0, j % PIECES), :], self.zin.at[slot, few, :], at.along(hop))

        self.b = net.lot(range(4 * PIECES), across, self.xin)
        self.z = net.lot(range(PIECES, 4 * PIECES), along, self.zin)

    def start_of(self, m, k, p):
        at = self.at
        return ((at.g ^ m) * 4 + (at.q ^ k)) * self.quarter + p * self.size

    def rows(self, m, k, p):
        return row(self.start_of(m, k, p), self.size)

    def pair(self, m):
        at = self.at
        return self.part.at[row(((at.g ^ m) * 2 + (1 - at.h % 2)) * 2 * self.quarter, 2 * self.quarter), :]

    def first(self, m):
        self.a.start(m)

    def lines(self, few, k):
        start = (self.at.h // 2 ^ k) * self.quarter
        return pl.ds(pl.multiple_of(start + few.start, 16), few.size)

    def slices(self, m, k, p, step):
        start = self.start_of(m, k, p)
        each(self.size // 16, lambda i: step(row(start + i * 16, 16), row(p * self.size + i * 16, 16)))

    def second(self, m):
        d = self.at.g ^ m
        self.a.arrived(m)

        def step(rows, few):
            total = self.part[rows, :].astype(F32) + self.near[d, self.lines(few, 1), :].astype(F32)
            self.part[rows, :] = total.astype(BF16)

        for p in range(PIECES):
            self.slices(m, 1, p, step)
            self.b.start(m * PIECES + p)

    def third(self, m):
        d = self.at.g ^ m

        def step(rows, few):
            total = self.part[rows, :].astype(F32) + self.near[d, self.lines(few, 0), :].astype(F32)
            total += self.xin[d, few, :].astype(F32)
            if m == 2:
                total += self.zin[0, few, :].astype(F32)
            if m:
                self.part[rows, :] = total.astype(BF16)
            else:
                self.out[few, :] = total

        for p in range(PIECES):
            self.b.arrived(m * PIECES + p)
            if m == 2:
                self.z.arrived(3 * PIECES + p)
            self.slices(m, 0, p, step)
            if m:
                self.z.start(m * PIECES + p)

    def last(self):
        self.third(0)
        for m in (1, 2):
            for p in range(PIECES):
                self.z.arrived(m * PIECES + p)

    def total(self, few):
        return self.out[few, :] + self.zin[1, few, :].astype(F32) + self.zin[2, few, :].astype(F32)

    def produce(self, work):
        def step(i):
            m = 3 - i
            work(m)
            self.first(m)

            @pl.when(i > 0)
            def _():
                self.second(m + 1)

        each(4, step)
        self.a.mark(range(4))
        self.b.mark(range(PIECES, 4 * PIECES))

    def sent(self):
        for lot in (self.a, self.b, self.z):
            lot.sent()


class Turn:
    def __init__(self, net, keep, at, source, view, blocks):
        self.keep, self.at, self.source, self.view, self.blocks = keep, at, source, view, blocks
        self.z, self.o, self.y, self.own = [], [], [], {}
        for b, (items, place) in enumerate(blocks):

            def out(m, items=items):
                return [(source(i, at.g ^ m), view(i, at.s), at.along(m)) for i in items]

            def beside(m, items=items):
                return [(source(i, at.g), view(i, at.s), at.beside()) for i in items]

            def on(m, place=place):
                block = place(at.s ^ (m * at.ranks))
                return (block, block, at.beside())

            def arrival(m, place=place):
                return place(at.s ^ (m * at.ranks))

            self.z.append(net.lot((1, 2, 3), out, lambda m, place=place: place(at.s), arrival, apart=True))
            self.o.append(net.lot((0,), beside, place(at.s), arrival))
            self.y.append(net.lot((1, 2, 3), on, lambda m, place=place: place(at.s), apart=True))

    def start(self, m, b=0, pieces=None):
        self.z[b].start(m, pieces)

    def mine(self, b=0):
        at = self.at
        for i in self.blocks[b][0]:
            self.own[i] = self.keep.put(self.source(i, at.g), self.view(i, at.s))
        self.o[b].start(0)

    def pass_on(self, m, b=0):
        self.z[b].arrived(m)
        self.y[b].start(m)

    def ready(self, b=0):
        for i in self.blocks[b][0]:
            self.own[i].wait()
        self.o[b].arrived(0)
        for m in (1, 2, 3):
            self.y[b].arrived(m)

    def sent(self, b=0):
        self.y[b].sent()


def dot(a, b):
    return jnp.dot(a, b, preferred_element_type=F32)


def dot_nt(a, b):
    return lax.dot_general(a, b, (((1,), (1,)), ((), ())), preferred_element_type=F32)


def dot_tn(a, b):
    return lax.dot_general(a, b, (((0,), (0,)), ((), ())), preferred_element_type=F32)


def turned(values, cos_table, sin_table):
    return values * cos_table + pltpu.roll(values, HD // 2, 1) * sin_table


def mean_square(values):
    return jnp.mean(values * values, axis=1, keepdims=True)


def layer_body(groups, ranks, *refs):
    (tok, cot, gain_one, gain_two, qw, kw, vw, ow, gw, uw, dw) = refs[:11]
    (result_out, rows_out, gains_out, q_out, k_out, v_out, o_out, g_out, u_out, d_out) = refs[11:21]
    (
        gains, gains_all, cosines, sines, rows_one, rows_cot, rows_two, rows_dh, w_qkv, w_o, w_gu, w_d, queries, pairs, mix, dqkv, accum, pair_send,
        pair_in, mixed, dgu, dmixed, own_x, hidden, dhidden, summed, part_a, near_a, xin_a, zin_a, part_b, near_b, xin_b, zin_b,
        in_gu, in_d, in_qkv, in_o, gain_part, gain_in, gain_mid, gain_near, result_own, rows_own, send, receive, local,
    ) = refs[21:]
    at = Where(groups, ranks)
    s, h, g, r = at.s, at.h, at.g, at.r
    shards = groups * ranks
    count, depth = tok.shape
    quarter = count // 4
    width = gains.shape[1]
    units = gw.shape[1] // groups
    half = units // 2
    total_rows = count * shards
    score_scale = 1.0 / math.sqrt(HD)
    score_shift = math.log(total_rows)
    peers = [(s ^ m, h) for m in range(1, shards)] + [(s, h ^ m) for m in range(1, 4)]
    barrier = pltpu.get_barrier_semaphore()
    for peer in peers:
        pl.semaphore_signal(barrier, inc=1, device_id=peer, device_id_type=MESH)
    pl.semaphore_wait(barrier, len(peers))
    net, keep = Net(send, receive), Keep(local)

    def chunk(m):
        return row((g ^ m) * count, count)

    def shard_rows(shard):
        return row(shard * width, width)

    def columns_of(shard):
        return lane(shard * width, width)

    turn_qkv = Turn(
        net, keep, at,
        lambda i, group: (qw, kw, vw)[i].at[:, lane(group * HD, HD)],
        lambda i, shard: w_qkv.at[shard_rows(shard), i * HD : (i + 1) * HD],
        [((0, 1, 2), lambda shard: w_qkv.at[shard_rows(shard), :])],
    )
    turn_gu = Turn(
        net, keep, at,
        lambda i, group: (gw, uw)[i % 2].at[:, lane(group * units + (i // 2) * half, half)],
        lambda i, shard: w_gu.at[shard_rows(shard), i * half : (i + 1) * half],
        [((2 * b, 2 * b + 1), lambda shard, b=b: w_gu.at[shard_rows(shard), b * units : (b + 1) * units]) for b in (0, 1)],
    )
    turn_o = Turn(
        net, keep, at,
        lambda i, group: ow.at[row(group * HD, HD), :],
        lambda i, shard: w_o.at[:, columns_of(shard)],
        [((0,), lambda shard: w_o.at[:, columns_of(shard)])],
    )
    turn_d = Turn(
        net, keep, at,
        lambda i, group: dw.at[row(group * units + i * half, half), :],
        lambda i, shard: w_d.at[i * half : (i + 1) * half, columns_of(shard)],
        [((b,), lambda shard, b=b: w_d.at[b * half : (b + 1) * half, columns_of(shard)]) for b in (0, 1)],
    )

    gains[...] = jnp.zeros_like(gains)
    gains[0:1, :] = gain_one[...].astype(F32).reshape(1, width)
    gains[1:2, :] = gain_two[...].astype(F32).reshape(1, width)
    gain_slot = gains_all.at[:, columns_of(s)]
    gain_moves = net.lot(range(1, shards), lambda m: (gains, gain_slot, (s ^ m, h)), gain_in)
    for m in range(1, shards):
        gain_moves.start(m)
    gain_own = keep.put(gains, gain_slot)
    strip = row(at.q * quarter, quarter)
    one = Spread(net, at, rows_one, quarter, tok)
    one.start()
    own_rows = keep.put(tok, rows_one.at[chunk(0), :])
    own_strip = keep.put(tok.at[strip, :], own_x)
    turn_qkv.start(3)
    turn_qkv.start(2)
    turn_qkv.mine()
    turn_o.mine()
    own_cot = keep.put(cot, rows_cot.at[chunk(0), :])
    gain_part[...] = jnp.zeros_like(gain_part)

    def clear(i):
        rows = row(i * 64, 64)
        accum[rows, :] = jnp.zeros_like(accum[rows, :])

    each(total_rows // 64, clear)

    def tables(i):
        rows = row(i * 64, 64)
        first_row = (i // (count // 64) * ranks + r) * count + i % (count // 64) * 64
        places = (first_row + lax.broadcasted_iota(jnp.int32, (64, HD), 0)).astype(F32)
        lanes = lax.broadcasted_iota(jnp.int32, (64, HD), 1)
        low_half = lanes < HD // 2
        order = jnp.where(low_half, lanes, lanes - HD // 2).astype(F32)
        angles = places * jnp.exp(order * (-math.log(10000.0) / (HD // 2)))
        cosines[rows, :] = jnp.cos(angles)
        sines[rows, :] = jnp.where(low_half, -jnp.sin(angles), jnp.sin(angles))

    each(groups * count // 64, tables)

    gain_own.wait()
    for m in range(1, shards):
        gain_moves.arrived(m)

    def norm_one(m):
        def some(i):
            rows = row((g ^ m) * count + i * 32, 32)
            values = rows_one[rows, :].astype(F32)
            inverse = lax.rsqrt(mean_square(values) + epsilon)
            rows_one[rows, :] = (values * inverse * gains_all[0:1, :]).astype(BF16)

        each(count // 32, some)

    own_rows.wait()
    own_strip.wait()
    norm_one(0)
    one.arrive(1)
    one.arrive(2)
    turn_qkv.start(1)
    for m in (3, 2, 1):
        turn_o.start(m)
    one.second(1)
    one.second(2)
    turn_qkv.pass_on(3)
    one.arrive(3)
    turn_qkv.pass_on(2)
    turn_qkv.pass_on(1)
    grad = Spread(net, at, rows_cot, quarter, cot)
    grad.start()
    one.second(3)
    for m in (1, 2, 3):
        one.ready(m)
    one.sent()
    for m in (1, 2, 3):
        norm_one(m)
    for m in (3, 2, 1):
        turn_d.start(m, 0)
    turn_qkv.ready()

    def own_place(m):
        return row(((g ^ m) * ranks + r) * count, count)

    pair_moves = net.lot(
        range(4),
        lambda m: (pairs.at[own_place(m), :], pairs.at[own_place(m), :], at.beside()),
        pairs.at[0 : groups * count, :],
    )

    def project(m):
        rows, place = chunk(m), own_place(m)
        heads = dot(rows_one[rows, :], w_qkv[...])
        cos_part, sin_part = cosines[rows, :], sines[rows, :]
        queries[rows, :] = turned(heads[:, :HD], cos_part, sin_part).astype(BF16)
        pairs[place, :HD] = turned(heads[:, HD : 2 * HD], cos_part, sin_part).astype(BF16)
        pairs[place, HD:] = heads[:, 2 * HD :].astype(BF16)
        pair_moves.start(m)

    each(4, project)
    pair_moves.mark(range(4))
    for m in (3, 2, 1):
        turn_o.pass_on(m)
    turn_gu.start(3, 0)
    grad.arrive(1)
    grad.arrive(2)
    turn_d.mine(0)
    turn_gu.mine(0)
    for m in (0, 1, 2, 3):
        pair_moves.arrived(m)
    span = ranks * count

    def weights_of(m, j, query):
        keys = pairs[row(j * span, span), :HD]
        scores = dot_nt(query, keys) * score_scale - score_shift
        q_place = ((g ^ m) * ranks + r) * count + lax.broadcasted_iota(jnp.int32, (count, span), 0)
        k_place = j * span + lax.broadcasted_iota(jnp.int32, (count, span), 1)
        return jnp.where(k_place <= q_place, jax.nn.sigmoid(scores), 0.0)

    def attend(m):
        rows = chunk(m)
        query = queries[rows, :]

        def step(j, total):
            weight = weights_of(m, j, query).astype(BF16)
            return total + dot(weight, pairs[row(j * span, span), HD:])

        total = lax.fori_loop(0, (g ^ m) + 1, step, jnp.zeros((count, HD), F32))
        low = total.astype(BF16)
        mix[rows, :] = low

        @pl.when(m == 3)
        def _():
            turn_o.ready()

        part_a[rows, :] = dot(low, w_o[...]).astype(BF16)

    set_a, set_b = (part_a, near_a, xin_a, zin_a), (part_b, near_b, xin_b, zin_b)
    first = Collect(net, at, set_a, quarter, summed)
    first.produce(attend)
    first.third(3)
    first.second(0)
    turn_gu.start(1, 0)
    turn_d.mine(1)
    turn_gu.mine(1)
    for m in (3, 2, 1):
        turn_d.pass_on(m, 0)
    first.third(2)
    turn_gu.pass_on(3, 0)
    grad.second(1)
    grad.second(2)
    grad.arrive(3)
    first.third(1)
    turn_gu.start(2, 0)
    turn_gu.pass_on(1, 0)
    first.last()
    two = Spread(net, at, rows_two, quarter)
    mine_start = (g * 4 + at.q) * quarter

    def norm_two(i):
        few = row(i * 16, 16)
        values = own_x[few, :].astype(F32) + first.total(few)
        hidden[few, :] = values
        inverse = lax.rsqrt(mean_square(values) + epsilon)
        rows_two[row(mine_start + i * 16, 16), :] = (values * inverse * gains_all[1:2, :]).astype(BF16)

    each(quarter // 16, norm_two)
    two.start()
    for m in (3, 2, 1):
        turn_d.start(m, 1)
    grad.second(3)
    two.second(0)
    turn_gu.pass_on(2, 0)
    two.arrive(1)
    turn_d.ready(0)
    own_cot.wait()

    def early(m, b):
        lanes = slice(b * half, (b + 1) * half)
        dmixed[chunk(m), lanes] = dot_nt(rows_cot[chunk(m), :], w_d[lanes, :])

    for m in (1, 2, 3):
        grad.ready(m)
    each(4, lambda m: early(m, 0))
    two.arrive(2)
    for m in (3, 2, 1):
        turn_gu.start(m, 1)
    two.second(1)
    two.second(2)
    two.arrive(3)
    for m in (3, 2, 1):
        turn_d.pass_on(m, 1)
    two.second(3)
    for m in (0, 1, 2, 3):
        two.ready(m)
    turn_gu.ready(0)

    def feed(m, b):
        rows = chunk(m)
        lanes, pair = slice(b * half, (b + 1) * half), slice(b * units, (b + 1) * units)
        both = dot(rows_two[rows, :], w_gu[:, pair])
        gate, up = both[:, :half], both[:, half:]
        sig = jax.nn.sigmoid(gate)
        act = gate * sig
        mixed[rows, lanes] = (act * up).astype(BF16)
        back = dmixed[rows, lanes]
        dgu[rows, b * units : b * units + half] = (back * up * sig * (1.0 + gate * (1.0 - sig))).astype(BF16)
        dgu[rows, b * units + half : (b + 1) * units] = (back * act).astype(BF16)
        total = dot_nt(dgu[rows, pair], w_gu[:, pair])
        if b:
            total += part_a[rows, :].astype(F32)
        part_a[rows, :] = total.astype(BF16)

    def out_part(m, b):
        rows = chunk(m)
        lanes = slice(b * half, (b + 1) * half)
        total = dot(mixed[rows, lanes], w_d[lanes, :])
        if b:
            total += part_b[rows, :].astype(F32)
        part_b[rows, :] = total.astype(BF16)

    def halves(m, work, lot):
        d = g ^ m

        def step(k):
            work(d * ranks + (r ^ 1 ^ k))

            @pl.when(k == 0)
            def _():
                lot.start(m)

        each(2, step)

    def several(groups_, work, lot):
        first_, last_ = groups_
        each(first_ - last_ + 1, lambda i: halves(first_ - i, work, lot))
        lot.mark(range(last_, first_ + 1))

    def beside(source, target, bulk):
        def describe(m):
            d = g ^ m
            return (source(d * ranks + (r ^ 1)), target(d), at.beside())

        return net.lot(range(4), describe, bulk)

    pairs_of = [slice(b * units, (b + 1) * units) for b in (0, 1)]
    lanes_of = [slice(b * half, (b + 1) * half) for b in (0, 1)]
    moves_gu = [
        beside(lambda shard, p=p: w_gu.at[shard_rows(shard), p], lambda d, p=p: in_gu.at[d, :, p], in_gu.at[:, :, p])
        for p in pairs_of
    ]
    moves_d = [
        beside(lambda shard, p=p: w_d.at[p, columns_of(shard)], lambda d, p=p: in_d.at[d, p, :], in_d.at[:, p, :])
        for p in lanes_of
    ]
    moves_qkv = beside(lambda shard: w_qkv.at[shard_rows(shard), :], lambda d: in_qkv.at[d], in_qkv)
    moves_o = beside(lambda shard: w_o.at[:, columns_of(shard)], lambda d: in_o.at[d], in_o)

    def grads_gu(groups_, b):
        def work(shard):
            w_gu[shard_rows(shard), pairs_of[b]] = dot_tn(rows_two[:, columns_of(shard)], dgu[:, pairs_of[b]]).astype(BF16)

        several(groups_, work, moves_gu[b])

    def grads_d(groups_, b):
        def work(shard):
            columns = columns_of(shard)
            w_d[lanes_of[b], columns] = dot_tn(mixed[:, lanes_of[b]], rows_cot[:, columns]).astype(BF16)

        several(groups_, work, moves_d[b])

    def grads_o(groups_):
        def work(shard):
            columns = columns_of(shard)
            w_o[:, columns] = dot_tn(mix[...], rows_dh[:, columns]).astype(BF16)

        several(groups_, work, moves_o)

    def grads_qkv(groups_):
        def work(shard):
            w_qkv[shard_rows(shard), :] = dot_tn(rows_one[:, columns_of(shard)], dqkv[...]).astype(BF16)

        several(groups_, work, moves_qkv)

    final, final_own = [], []

    def give(moves, whole_, m):
        if m:
            lot = net.lot((0,), lambda j: [(a, b, at.along(m)) for a, b in moves], whole_, lambda j: whole_)
            lot.start(0)
            final.append(lot)
        else:
            final_own.extend(keep.put(a, b) for a, b in moves)

    def sums(m, lot, mine_of, other_of, size):
        lot.arrived(m)

        def step(i):
            a, rows, lanes = mine_of(i)
            b, d, few, others = other_of(i)
            a[rows, lanes] = (a[rows, lanes].astype(F32) + b[d, few, others].astype(F32)).astype(BF16)

        each(size // 32, step)

    def sums_gu(m, b):
        d, p = g ^ m, pairs_of[b]
        start = (d * ranks + r) * width
        sums(
            m, moves_gu[b],
            lambda i: (w_gu, row(start + i * 32, 32), p), lambda i: (in_gu, d, row(i * 32, 32), p), width,
        )
        moves = []
        for i, out in enumerate((g_out, u_out)):
            place = b * units + i * half
            moves.append((w_gu.at[row(start, width), place : place + half], out.at[:, lane(g * units + b * half, half)]))
        give(moves, w_gu.at[row(start, width), p], m)

    def sums_d(m, b):
        d, base = g ^ m, b * half
        columns = columns_of(d * ranks + r)
        sums(
            m, moves_d[b],
            lambda i: (w_d, row(base + i * 32, 32), columns),
            lambda i: (in_d, d, row(base + i * 32, 32), slice(None)), half,
        )
        block = w_d.at[lanes_of[b], columns]
        give([(block, d_out.at[row(g * units + base, half), :])], block, m)

    def sums_o(m):
        d = g ^ m
        columns = columns_of(d * ranks + r)
        sums(
            m, moves_o,
            lambda i: (w_o, row(i * 32, 32), columns), lambda i: (in_o, d, row(i * 32, 32), slice(None)), HD,
        )
        give([(w_o.at[:, columns], o_out.at[row(g * HD, HD), :])], w_o.at[:, columns], m)

    def sums_qkv(m):
        d = g ^ m
        start = (d * ranks + r) * width
        sums(
            m, moves_qkv,
            lambda i: (w_qkv, row(start + i * 32, 32), slice(None)),
            lambda i: (in_qkv, d, row(i * 32, 32), slice(None)), width,
        )
        moves = [
            (w_qkv.at[row(start, width), i * HD : (i + 1) * HD], out.at[:, lane(g * HD, HD)])
            for i, out in enumerate((q_out, k_out, v_out))
        ]
        give(moves, w_qkv.at[row(start, width), :], m)

    first.sent()
    second = Collect(net, at, set_a, quarter, summed)
    each(4, lambda m: feed(m, 0))
    turn_gu.pass_on(3, 1)
    turn_gu.sent(0)
    grads_gu((3, 3), 0)
    turn_d.ready(1)
    each(4, lambda m: early(m, 1))
    each(4, lambda m: out_part(m, 0))
    turn_gu.pass_on(1, 1)
    turn_gu.pass_on(2, 1)
    turn_d.sent(0)
    sums_gu(3, 0)
    grads_gu((2, 1), 0)
    grads_d((3, 1), 0)
    turn_gu.ready(1)
    second.produce(lambda m: feed(m, 1))
    sums_gu(2, 0)
    second.third(3)
    second.second(0)
    sums_gu(1, 0)
    second.third(2)
    turn_gu.sent(1)
    turn_d.sent(1)
    grads_gu((3, 2), 1)
    second.third(1)
    grads_gu((1, 1), 1)
    each(4, lambda m: out_part(m, 1))
    out_sum = Collect(net, at, set_b, quarter, summed)
    for m in (3, 2, 1, 0):
        out_sum.first(m)
    second.last()
    three = Spread(net, at, rows_dh, quarter)

    def back_two(i, gain_grad):
        few = row(i * 16, 16)
        own = row(mine_start + i * 16, 16)
        upstream, values = second.total(few), hidden[few, :]
        inverse = lax.rsqrt(mean_square(values) + epsilon)
        scaled = upstream * gains_all[1:2, :]
        back = inverse * scaled - values * (inverse * inverse * inverse) * jnp.mean(
            scaled * values, axis=1, keepdims=True
        )
        total = rows_cot[own, :].astype(F32) + back
        dhidden[few, :] = total
        rows_dh[own, :] = total.astype(BF16)
        return gain_grad + jnp.sum(upstream * values * inverse, axis=0, keepdims=True)

    gain_part[1:2, :] = lax.fori_loop(0, quarter // 16, back_two, jnp.zeros((1, depth), F32))
    three.start()
    for m in (3, 2, 1):
        sums_d(m, 0)
    grads_d((3, 1), 1)
    three.second(0)
    out_sum.second(3)
    out_sum.second(2)
    for b in (0, 1):
        grads_gu((0, 0), b)
    three.arrive(1)
    for b in (0, 1):
        grads_d((0, 0), b)
    three.arrive(2)
    sums_gu(3, 1)
    out_sum.third(3)
    three.second(1)
    three.second(2)
    sums_gu(2, 1)
    three.arrive(3)
    out_sum.second(1)
    out_sum.second(0)
    sums_gu(1, 1)
    three.second(3)

    def attend_back(m):
        three.ready(m)
        rows = chunk(m)
        query = queries[rows, :]
        dm = dot_nt(rows_dh[rows, :], w_o[...]).astype(BF16)

        def step(j, total):
            block = row(j * span, span)
            weight = weights_of(m, j, query)
            dweight = dot_nt(dm, pairs[block, HD:])
            dscore = (dweight * weight * (1.0 - weight)).astype(BF16)
            accum[block, HD:] += dot_tn(weight.astype(BF16), dm)
            accum[block, :HD] += dot_tn(dscore, query)
            return total + dot(dscore, pairs[block, :HD])

        total = lax.fori_loop(0, (g ^ m) + 1, step, jnp.zeros((count, HD), F32))
        dqkv[rows, :HD] = turned(total * score_scale, cosines[rows, :], -sines[rows, :]).astype(BF16)

    pair_back = net.lot(range(4), lambda m: (pair_send.at[g ^ m], pair_in.at[g ^ m], at.beside()), pair_send)

    def send_pair(m):
        d = g ^ m
        rows = row((d * ranks + (r ^ 1)) * count, count)
        pair_send[d] = accum[rows, :].astype(BF16)
        pair_back.start(m)

    def back_from_end(i):
        m = g ^ (groups - 1 - i)
        attend_back(m)
        send_pair(m)

    each(4, back_from_end)
    pair_back.mark(range(4))
    out_sum.third(2)
    for m in (3, 2, 1):
        sums_d(m, 1)
    out_sum.third(1)
    turn_o.sent()
    grads_o((3, 0))
    second.sent()
    third = Collect(net, at, set_a, quarter, summed)

    def back_one(m):
        d = g ^ m
        rows = chunk(m)
        pair_back.arrived(m)
        both = accum[own_place(m), :] + pair_in[d].astype(F32)
        dqkv[rows, HD : 2 * HD] = turned(both[:, :HD] * score_scale, cosines[rows, :], -sines[rows, :]).astype(BF16)
        dqkv[rows, 2 * HD :] = both[:, HD:].astype(BF16)
        part_a[rows, :] = dot_nt(dqkv[rows, :], w_qkv[...]).astype(BF16)

    third.produce(back_one)
    third.second(0)
    third.third(3)
    turn_qkv.sent()
    grads_qkv((3, 2))
    for m in (3, 2, 1):
        sums_o(m)
    third.third(2)
    grads_qkv((1, 0))
    third.third(1)
    for m in (3, 2):
        sums_qkv(m)
    for b in (0, 1):
        sums_gu(0, b)
        sums_d(0, b)
    ends = []

    def share(source, target):
        place = target.at[strip, :]
        final_own.append(keep.put(source, place))
        lot = net.lot((0, 1), lambda j: (source, place, (at.near(), at.across())[j]), target.at[0 : 2 * quarter, :])
        lot.start(0)
        lot.start(1)
        ends.append((lot, target))

    def relay():
        lot, target = ends.pop()
        lot.arrived(1)
        final.append(lot)
        block = target.at[row((at.q ^ 1) * quarter, quarter), :]
        on = net.lot((0,), lambda j: (block, block, at.near()), block)
        on.start(0)
        final.append(on)

    out_sum.last()

    def result_rows(i):
        few = row(i * 16, 16)
        result_own[few, :] = (hidden[few, :] + out_sum.total(few)).astype(BF16)

    each(quarter // 16, result_rows)
    share(result_own, result_out)
    sums_qkv(1)
    sums_o(0)
    sums_qkv(0)
    third.last()

    def back_rows(i, gain_grad):
        few = row(i * 16, 16)
        upstream, values = third.total(few), own_x[few, :].astype(F32)
        inverse = lax.rsqrt(mean_square(values) + epsilon)
        scaled = upstream * gains_all[0:1, :]
        back = inverse * scaled - values * (inverse * inverse * inverse) * jnp.mean(
            scaled * values, axis=1, keepdims=True
        )
        rows_own[few, :] = (dhidden[few, :] + back).astype(BF16)
        return gain_grad + jnp.sum(upstream * values * inverse, axis=0, keepdims=True)

    gain_part[0:1, :] = lax.fori_loop(0, quarter // 16, back_rows, jnp.zeros((1, depth), F32))
    gain_sums = net.lot(
        range(1, shards), lambda m: (gain_part.at[:, columns_of(s ^ m)], gain_in.at[m - 1], (s ^ m, h)), gain_in
    )
    for m in range(1, shards):
        gain_sums.start(m)
    relay()
    share(rows_own, rows_out)
    total = gain_part[:, columns_of(s)]
    for m in range(1, shards):
        gain_sums.arrived(m)
        total += gain_in[m - 1]
    gain_mid[...] = total
    gain_ends = net.lot(range(1, 4), lambda m: (gain_mid, gain_near.at[m - 1], (s, h ^ m)), gain_near)
    for m in range(1, 4):
        gain_ends.start(m)
    relay()
    for m in range(1, 4):
        gain_ends.arrived(m)
        total += gain_near[m - 1]
    gains_out[...] = total
    for lot in final:
        lot.arrived(0)
    net.finish()
    for copy in final_own:
        copy.wait()


def rows_plan(
    groups,
    ranks,
    tokens,
    attn_gain,
    query_weight,
    key_weight,
    value_weight,
    out_weight,
    mlp_gain,
    gate_weight,
    up_weight,
    down_weight,
    cotangent,
):
    count, depth = tokens.shape
    shards = groups * ranks
    quarter = count // 4
    width = query_weight.shape[0]
    units = gate_weight.shape[1] // groups
    total_rows = count * shards
    here = groups * count
    ins = (
        tokens, cotangent, attn_gain, mlp_gain,
        query_weight, key_weight, value_weight, out_weight, gate_weight, up_weight, down_weight,
    )
    shape = jax.ShapeDtypeStruct
    hbm, vmem = pl.BlockSpec(memory_space=pl.ANY), pl.BlockSpec(memory_space=pltpu.VMEM)
    owners = (query_weight, key_weight, value_weight, out_weight, gate_weight, up_weight, down_weight)
    outs = [
        shape((count, depth), BF16),
        shape((count, depth), BF16),
        shape((8, width), F32),
        *(shape(w.shape, BF16) for w in owners),
    ]

    def low(*extent):
        return pltpu.VMEM(extent, BF16)

    def full(*extent):
        return pltpu.VMEM(extent, F32)

    def collector():
        return [
            low(here, depth),
            low(groups, 2 * quarter, depth),
            low(groups, quarter, depth),
            low(3, quarter, depth),
        ]

    scratch = [
        full(8, width), full(8, depth), full(here, HD), full(here, HD),
        low(here, depth), low(here, depth), low(here, depth), low(here, depth),
        low(depth, 3 * HD), low(HD, depth), low(depth, 2 * units), low(units, depth),
        low(here, HD), low(total_rows, 2 * HD), low(here, HD), low(here, 3 * HD),
        full(total_rows, 2 * HD), low(groups, count, 2 * HD), low(groups, count, 2 * HD),
        low(here, units), low(here, 2 * units), full(here, units),
        low(quarter, depth), full(quarter, depth), full(quarter, depth), full(quarter, depth),
        *collector(), *collector(),
        low(groups, width, 2 * units), low(groups, units, width), low(groups, width, 3 * HD), low(groups, HD, width),
        full(8, depth), full(shards - 1, 8, width), full(8, width), full(3, 8, width),
        low(quarter, depth), low(quarter, depth),
        pltpu.SemaphoreType.DMA((SENDS,)), pltpu.SemaphoreType.DMA((RECEIVES,)), pltpu.SemaphoreType.DMA((KEEPS,)),
    ]
    moved = pl.pallas_call(
        functools.partial(layer_body, groups, ranks),
        out_shape=outs,
        in_specs=[hbm] * 2 + [vmem] * 2 + [hbm] * 7,
        out_specs=[hbm, hbm, vmem] + [hbm] * 7,
        scratch_shapes=scratch,
        compiler_params=pltpu.CompilerParams(
            collective_id=1, has_side_effects=True, vmem_limit_bytes=VMEM_LIMIT
        ),
    )(*ins)
    steps = 8

    def sliced(array):
        rows, columns = array.shape
        return pl.BlockSpec((rows // steps, columns), lambda i: (i, 0))

    gain_specs = [pl.BlockSpec((8, width), lambda i: (0, 0))]
    row_spec = pl.BlockSpec((width,), lambda i: (0,))
    specs = [sliced(moved[0]), sliced(moved[1]), *(sliced(w) for w in moved[3:])]
    gain_row = shape((width,), F32)
    one, two, result, rows_grad, *grads = pl.pallas_call(
        cast_body,
        grid=(steps,),
        out_shape=[gain_row, gain_row, moved[0], moved[1], *(shape(w.shape, F32) for w in owners)],
        in_specs=gain_specs + specs,
        out_specs=[row_spec, row_spec] + specs,
        compiler_params=pltpu.CompilerParams(vmem_limit_bytes=VMEM_LIMIT),
    )(moved[2], moved[0], moved[1], *moved[3:])
    return (result, rows_grad, one, *grads[:4], two, *grads[4:])


def cast_body(*refs):
    inputs = len(refs) // 2
    gains, sources, (one, two, *targets) = refs[0], refs[1:inputs], refs[inputs:]
    one[...] = gains[0, :]
    two[...] = gains[1, :]
    for source, target in zip(sources, targets):
        target[...] = source[...].astype(target.dtype)


def on_device(tokens, attn_gain, query_weight, *rest):
    groups = query_weight.shape[1] // HD
    ranks = lax.axis_size("seq") // groups
    fits = lax.axis_size("head") == 4 and groups == 4 and ranks == 2 and query_weight.shape[0] % 128 == 0
    plan = functools.partial(rows_plan, groups, ranks) if fits else gathered_weights
    return plan(tokens, attn_gain, query_weight, *rest)


def solution(mesh):
    in_specs = (
        P("seq", None),
        P("seq"),
        P("seq", "head"),
        P("seq", "head"),
        P("seq", "head"),
        P("head", "seq"),
        P("seq"),
        P("seq", "head"),
        P("seq", "head"),
        P("head", "seq"),
        P("seq", None),
    )
    out_specs = (
        P("seq", None),
        P("seq", None),
        P("seq"),
        P("seq", "head"),
        P("seq", "head"),
        P("seq", "head"),
        P("head", "seq"),
        P("seq"),
        P("seq", "head"),
        P("seq", "head"),
        P("head", "seq"),
    )
    return jax.shard_map(
        on_device, mesh=mesh, in_specs=in_specs, out_specs=out_specs, check_vma=False
    )
```

```python
import functools
import math

import jax
import jax.numpy as jnp
from jax import lax
from jax.experimental import pallas as pl
from jax.experimental.pallas import tpu as pltpu
from jax.sharding import PartitionSpec as P

MESH = pl.DeviceIdType.MESH
F32, BF16 = jnp.float32, jnp.bfloat16

HD = 128


epsilon = 1e-05
block_limit = 512
VMEM_LIMIT = 63 * 2**20
SENDS, RECEIVES, KEEPS = 103, 295, 26
PIECES = 2


def tables(offset, length, half_width):
    places = (offset + jnp.arange(length, dtype=jnp.int32)).astype(jnp.float32)
    frequency = jnp.exp(
        jnp.arange(half_width, dtype=jnp.float32) * (-math.log(10000.0) / half_width)
    )
    angles = places[:, None] * frequency[None, :]
    return (jnp.cos(angles)[:, None, :], jnp.sin(angles)[:, None, :])


def rotary(values, cos_table, sin_table):
    half_width = values.shape[-1] // 2
    front = values[..., :half_width]
    back_half = values[..., half_width:]
    return jnp.concatenate(
        [front * cos_table - back_half * sin_table, back_half * cos_table + front * sin_table],
        axis=-1,
    )


def unrotary(gradient, cos_table, sin_table):
    half_width = gradient.shape[-1] // 2
    front = gradient[..., :half_width]
    back_half = gradient[..., half_width:]
    return jnp.concatenate(
        [front * cos_table + back_half * sin_table, back_half * cos_table - front * sin_table],
        axis=-1,
    )


def norm_back(values, inverse, gain_vector, upstream):
    scaled = upstream * gain_vector
    gain_grad = jnp.sum(upstream * values * inverse, axis=0)
    value_grad = inverse * scaled - values * inverse**3 * jnp.mean(
        scaled * values, axis=1, keepdims=True
    )
    return (value_grad, gain_grad)


def gathered_weights(
    tokens,
    attn_gain,
    query_weight,
    key_weight,
    value_weight,
    out_weight,
    mlp_gain,
    gate_weight,
    up_weight,
    down_weight,
    cotangent,
):
    row_count = tokens.shape[0]
    total_rows = row_count * lax.axis_size("seq")
    row_start = lax.axis_index("seq") * row_count
    local_width = query_weight.shape[1]
    local_heads = local_width // HD
    score_scale = 1.0 / math.sqrt(HD)
    score_shift = math.log(total_rows)
    block_rows = math.gcd(total_rows, block_limit)
    block_count = total_rows // block_rows
    attn_gain_full, query_full, key_full, value_full, out_full = (
        lax.all_gather(attn_gain, "seq", axis=0, tiled=True),
        lax.all_gather(query_weight, "seq", axis=0, tiled=True),
        lax.all_gather(key_weight, "seq", axis=0, tiled=True),
        lax.all_gather(value_weight, "seq", axis=0, tiled=True),
        lax.all_gather(out_weight, "seq", axis=1, tiled=True),
    )
    mlp_gain_full, gate_full, up_full, down_full = (
        lax.all_gather(mlp_gain, "seq", axis=0, tiled=True),
        lax.all_gather(gate_weight, "seq", axis=0, tiled=True),
        lax.all_gather(up_weight, "seq", axis=0, tiled=True),
        lax.all_gather(down_weight, "seq", axis=1, tiled=True),
    )
    token_values = tokens.astype(jnp.float32)
    inverse_one = lax.rsqrt(jnp.mean(token_values * token_values, axis=1, keepdims=True) + epsilon)
    normed_one = (token_values * inverse_one * attn_gain_full.astype(jnp.float32)).astype(
        jnp.bfloat16
    )
    query_pre = jnp.dot(normed_one, query_full, preferred_element_type=jnp.float32)
    key_pre = jnp.dot(normed_one, key_full, preferred_element_type=jnp.float32)
    value_rows = (
        jnp.dot(normed_one, value_full, preferred_element_type=jnp.float32)
        .astype(jnp.bfloat16)
        .reshape(row_count, local_heads, HD)
    )
    cos_table, sin_table = tables(row_start, row_count, HD // 2)
    query_rows = (
        rotary(query_pre.reshape(row_count, local_heads, HD), cos_table, sin_table)
        .astype(jnp.bfloat16)
        .reshape(row_count, local_width)
    )
    key_rows = rotary(key_pre.reshape(row_count, local_heads, HD), cos_table, sin_table).astype(
        jnp.bfloat16
    )
    all_queries = lax.all_gather(query_rows, "seq", axis=0, tiled=True)
    key_places = row_start + jnp.arange(row_count, dtype=jnp.int32)

    def weights_for(query_block, block_start):
        scores = (
            jnp.einsum("qhd,khd->hqk", query_block, key_rows, preferred_element_type=jnp.float32)
            * score_scale
            - score_shift
        )
        query_places = block_start + jnp.arange(query_block.shape[0], dtype=jnp.int32)
        visible = key_places[None, :] <= query_places[:, None]
        return jnp.where(visible[None], jax.nn.sigmoid(scores), 0.0)

    step_rows = math.gcd(row_count * lax.axis_size("seq"), block_limit)
    step_count = row_count * lax.axis_size("seq") // step_rows
    picked = all_queries.reshape(step_count, step_rows, local_heads, HD)
    starts = jnp.arange(step_count, dtype=jnp.int32) * step_rows

    def one_block(packed):
        query_block, block_start = packed
        weights = weights_for(query_block, block_start).astype(jnp.bfloat16)
        return jnp.einsum(
            "hqk,khd->qhd", weights, value_rows, preferred_element_type=jnp.float32
        ).reshape(step_rows, local_width)

    attn_mix = lax.psum_scatter(
        lax.map(one_block, (picked, starts)).reshape(row_count * lax.axis_size("seq"), local_width),
        "seq",
        scatter_dimension=0,
        tiled=True,
    ).astype(jnp.bfloat16)
    attn_branch = lax.psum(jnp.dot(attn_mix, out_full, preferred_element_type=jnp.float32), "head")
    hidden = token_values + attn_branch
    inverse_two = lax.rsqrt(jnp.mean(hidden * hidden, axis=1, keepdims=True) + epsilon)
    normed_two = (hidden * inverse_two * mlp_gain_full.astype(jnp.float32)).astype(jnp.bfloat16)
    gate_pre = jnp.dot(normed_two, gate_full, preferred_element_type=jnp.float32)
    up_pre = jnp.dot(normed_two, up_full, preferred_element_type=jnp.float32)
    gate_act = jax.nn.silu(gate_pre)
    mixed = (gate_act * up_pre).astype(jnp.bfloat16)
    mlp_branch = lax.psum(
        jnp.dot(mixed, down_full, preferred_element_type=jnp.float32).astype(jnp.bfloat16), "head"
    ).astype(jnp.float32)
    result = (hidden + mlp_branch).astype(jnp.bfloat16)
    kept_weights = (
        lax.all_gather(attn_gain, "seq", axis=0, tiled=True),
        lax.all_gather(query_weight, "seq", axis=0, tiled=True),
        lax.all_gather(key_weight, "seq", axis=0, tiled=True),
        lax.all_gather(value_weight, "seq", axis=0, tiled=True),
        lax.all_gather(out_weight, "seq", axis=1, tiled=True),
        lax.all_gather(mlp_gain, "seq", axis=0, tiled=True),
        lax.all_gather(gate_weight, "seq", axis=0, tiled=True),
        lax.all_gather(up_weight, "seq", axis=0, tiled=True),
        lax.all_gather(down_weight, "seq", axis=1, tiled=True),
    )
    (
        attn_gain_back,
        query_back,
        key_back,
        value_back,
        out_back,
        mlp_gain_back,
        gate_back,
        up_back,
        down_back,
    ) = kept_weights
    attn_gain_f = attn_gain_back.astype(jnp.float32)
    mlp_gain_f = mlp_gain_back.astype(jnp.float32)
    grad_values = cotangent.astype(jnp.float32)
    grad_down = jnp.einsum("tf,td->fd", mixed, cotangent, preferred_element_type=jnp.float32)
    dmixed = jnp.einsum("td,fd->tf", cotangent, down_back, preferred_element_type=jnp.float32)
    gate_sig = jax.nn.sigmoid(gate_pre)
    dgate = (dmixed * up_pre * gate_sig * (1.0 + gate_pre * (1.0 - gate_sig))).astype(jnp.bfloat16)
    dup = (dmixed * gate_act).astype(jnp.bfloat16)
    grad_gate = jnp.einsum("tk,tf->kf", normed_two, dgate, preferred_element_type=jnp.float32)
    grad_up = jnp.einsum("tk,tf->kf", normed_two, dup, preferred_element_type=jnp.float32)
    dnormed_two = lax.psum(
        jnp.einsum("tf,kf->tk", dgate, gate_back, preferred_element_type=jnp.float32)
        + jnp.einsum("tf,kf->tk", dup, up_back, preferred_element_type=jnp.float32),
        "head",
    )
    dhidden_norm, grad_mlp_gain = norm_back(hidden, inverse_two, mlp_gain_f, dnormed_two)
    dhidden = grad_values + dhidden_norm
    mlp_sums = (grad_mlp_gain, grad_gate, grad_up, grad_down)
    dhidden_low = dhidden.astype(jnp.bfloat16)
    grad_out = jnp.einsum("tc,td->cd", attn_mix, dhidden_low, preferred_element_type=jnp.float32)
    dmix = jnp.einsum(
        "td,cd->tc", dhidden_low, out_back, preferred_element_type=jnp.float32
    ).astype(jnp.bfloat16)
    all_dmix = lax.all_gather(dmix, "seq", axis=0, tiled=True)

    def backward_block(carry, packed):
        key_accum, value_accum = carry
        query_block, grad_block, block_start = packed
        weights = weights_for(query_block, block_start)
        grad_weights = jnp.einsum(
            "qhd,khd->hqk", grad_block, value_rows, preferred_element_type=jnp.float32
        )
        grad_scores = (grad_weights * weights * (1.0 - weights)).astype(jnp.bfloat16)
        value_accum = value_accum + jnp.einsum(
            "hqk,qhd->khd",
            weights.astype(jnp.bfloat16),
            grad_block,
            preferred_element_type=jnp.float32,
        )
        key_accum = key_accum + jnp.einsum(
            "hqk,qhd->khd", grad_scores, query_block, preferred_element_type=jnp.float32
        )
        query_part = (
            jnp.einsum("hqk,khd->qhd", grad_scores, key_rows, preferred_element_type=jnp.float32)
            * score_scale
        )
        return ((key_accum, value_accum), query_part.reshape(block_rows, local_width))

    zero_rows = jnp.zeros((row_count, local_heads, HD), jnp.float32)
    block_starts = jnp.arange(block_count, dtype=jnp.int32) * block_rows
    (key_accum, value_accum), query_parts = lax.scan(
        backward_block,
        (zero_rows, zero_rows),
        (
            all_queries.reshape(block_count, block_rows, local_heads, HD),
            all_dmix.reshape(block_count, block_rows, local_heads, HD),
            block_starts,
        ),
    )
    query_sum = lax.psum_scatter(
        query_parts.reshape(total_rows, local_width), "seq", scatter_dimension=0, tiled=True
    )
    dquery_pre = (
        unrotary(query_sum.reshape(row_count, local_heads, HD), cos_table, sin_table)
        .reshape(row_count, local_width)
        .astype(jnp.bfloat16)
    )
    dkey_pre = (
        unrotary(key_accum * score_scale, cos_table, sin_table)
        .reshape(row_count, local_width)
        .astype(jnp.bfloat16)
    )
    dvalue = value_accum.reshape(row_count, local_width).astype(jnp.bfloat16)
    grad_query = jnp.einsum("tk,tc->kc", normed_one, dquery_pre, preferred_element_type=jnp.float32)
    grad_key = jnp.einsum("tk,tc->kc", normed_one, dkey_pre, preferred_element_type=jnp.float32)
    grad_value = jnp.einsum("tk,tc->kc", normed_one, dvalue, preferred_element_type=jnp.float32)
    dnormed_one = lax.psum(
        jnp.einsum("tc,kc->tk", dquery_pre, query_back, preferred_element_type=jnp.float32)
        + jnp.einsum("tc,kc->tk", dkey_pre, key_back, preferred_element_type=jnp.float32)
        + jnp.einsum("tc,kc->tk", dvalue, value_back, preferred_element_type=jnp.float32),
        "head",
    )
    dinput_norm, grad_attn_gain = norm_back(token_values, inverse_one, attn_gain_f, dnormed_one)
    input_grad = (dhidden + dinput_norm).astype(jnp.bfloat16)
    every_sum = (
        lax.psum_scatter(grad_attn_gain, "seq", scatter_dimension=0, tiled=True),
        lax.psum_scatter(grad_query, "seq", scatter_dimension=0, tiled=True),
        lax.psum_scatter(grad_key, "seq", scatter_dimension=0, tiled=True),
        lax.psum_scatter(grad_value, "seq", scatter_dimension=0, tiled=True),
        lax.psum_scatter(grad_out, "seq", scatter_dimension=1, tiled=True),
        lax.psum_scatter(grad_mlp_gain, "seq", scatter_dimension=0, tiled=True),
        lax.psum_scatter(grad_gate, "seq", scatter_dimension=0, tiled=True),
        lax.psum_scatter(grad_up, "seq", scatter_dimension=0, tiled=True),
        lax.psum_scatter(grad_down, "seq", scatter_dimension=1, tiled=True),
    )
    attn_sums = every_sum[:5]
    mlp_sums = every_sum[5:]
    return (
        result,
        input_grad,
        attn_sums[0],
        attn_sums[1],
        attn_sums[2],
        attn_sums[3],
        attn_sums[4],
        mlp_sums[0],
        mlp_sums[1],
        mlp_sums[2],
        mlp_sums[3],
    )


class Net:
    def __init__(self, send, receive):
        self.send, self.receive, self.sends, self.receives, self.lots = send, receive, 0, 0, []

    def lot(self, *args, **options):
        return Lot(self, *args, **options)

    def finish(self):
        for lot in self.lots:
            lot.sent()


class Lot:
    def __init__(self, net, indices, describe, bulk, arrival=None, apart=False):
        self.net, self.describe, self.bulk, self.arrival, self.apart = net, describe, bulk, arrival, apart
        self.place = {j: net.receives + i for i, j in enumerate(indices)}
        self.low = min(indices)
        self.send_base, self.receive_base = net.sends, net.receives
        net.receives += len(indices)
        net.sends += len(indices) if apart else 1
        self.started, self.open = set(), set()
        net.lots.append(self)

    def receive_at(self, j):
        return self.net.receive.at[self.receive_base + (j - self.low)]

    def send_at(self, j):
        return self.net.send.at[self.send_base + (j - self.low if self.apart else 0)]

    def start(self, j, pieces=None):
        described = self.describe(j)
        for i, (source, target, device) in enumerate(described if isinstance(described, list) else [described]):
            if pieces is None or i in pieces:
                pltpu.make_async_remote_copy(
                    src_ref=source,
                    dst_ref=target,
                    send_sem=self.send_at(j),
                    recv_sem=self.receive_at(j),
                    device_id=device,
                    device_id_type=MESH,
                ).start()
        if isinstance(j, int):
            self.mark((j,))

    def mark(self, indices):
        self.started.update(indices)
        self.open.update(indices if self.apart else (self.low,))

    def arrived(self, j):
        described = self.describe(j)
        target = self.arrival(j) if self.arrival else described[1]
        self.wait(target, self.receive_at(j))

    def wait(self, like, sem):
        pltpu.make_async_copy(like, like, sem).wait()

    def sent(self, j=None):
        for k in sorted(self.open) if j is None else [j] if j in self.open else []:
            self.open.remove(k)
            self.wait(self.bulk(k) if self.apart else self.bulk, self.send_at(k))


class Keep:
    def __init__(self, sems):
        self.sems, self.count = sems, 0

    def put(self, source, target):
        copy = pltpu.make_async_copy(source, target, self.sems.at[self.count])
        self.count += 1
        copy.start()
        return copy


class Where:
    def __init__(self, groups, ranks):
        self.s, self.h = lax.axis_index("seq"), lax.axis_index("head")
        self.g, self.r = self.s // ranks, self.s % ranks
        self.groups, self.ranks = groups, ranks
        self.q = self.h % 2 * 2 + self.h // 2

    def along(self, m):
        return (self.s ^ (m * self.ranks), self.h)

    def beside(self):
        return (self.s ^ 1, self.h)

    def across(self):
        return (self.s, self.h ^ 2)

    def near(self):
        return (self.s, self.h ^ 1)


def lane(start, size):
    return pl.ds(pl.multiple_of(start, 128), size)


def row(start, size):
    return pl.ds(pl.multiple_of(start, size), size)


def each(count, step):
    def body(i, carry):
        step(i)
        return carry

    lax.fori_loop(0, count, body, 0)


class Spread:
    def __init__(self, net, at, buffer, quarter, own=None):
        self.at, self.buffer, self.quarter, self.shared = at, buffer, quarter, own is not None
        self.size = quarter // PIECES

        def along(j):
            m, p = j // PIECES, j % PIECES
            if m == 3:
                return (self.block(2, 0, p), self.block(2, 0, p), at.along(1))
            first = self.block(0, 0, p) if own is None else own.at[row(at.q * quarter + p * self.size, self.size), :]
            return (first, self.block(0, 0, p), at.along(m))

        def moved(k, device):
            def describe(j):
                block = self.block(j // PIECES, k, j % PIECES)
                return (block, block, device)

            return describe

        low = 1 if self.shared else 0
        indices = range(low * PIECES, 4 * PIECES)
        some = buffer.at[0 : (4 - low) * quarter, :]
        self.z = net.lot(range(PIECES, 4 * PIECES), along, buffer.at[0 : 3 * quarter, :])
        self.x = net.lot(indices, moved(0, at.across()), some)
        self.c = net.lot(indices, moved(0, at.near()), some)
        self.d = net.lot(indices, moved(1, at.near()), some)

    def block(self, m, k, p):
        at = self.at
        start = ((at.g ^ m) * 4 + (at.q ^ k)) * self.quarter + p * self.size
        return self.buffer.at[row(start, self.size), :]

    def pass_on(self, j):
        self.x.start(j)
        self.c.start(j)

    def start(self):
        for m in (2, 1):
            for p in range(PIECES):
                self.z.start(m * PIECES + p)
        if not self.shared:
            for p in range(PIECES):
                self.pass_on(p)

    def arrive(self, m):
        for p in range(PIECES):
            j = m * PIECES + p
            self.z.arrived(j)
            if m == 2:
                self.z.start(3 * PIECES + p)
            self.pass_on(j)

    def second(self, m):
        for p in range(PIECES):
            self.x.arrived(m * PIECES + p)
            self.d.start(m * PIECES + p)

    def ready(self, m):
        for p in range(PIECES):
            self.c.arrived(m * PIECES + p)
            self.d.arrived(m * PIECES + p)

    def sent(self):
        for lot in (self.z, self.x, self.c, self.d):
            lot.sent()


class Collect:
    def __init__(self, net, at, refs, quarter, out):
        self.at, self.quarter, self.out = at, quarter, out
        self.size = quarter // PIECES
        self.part, self.near, self.xin, self.zin = refs
        self.a = net.lot(range(4), lambda m: (self.pair(m), self.near.at[at.g ^ m], at.near()), self.near)

        def across(j):
            m, few = j // PIECES, row(j % PIECES * self.size, self.size)
            return (self.part.at[self.rows(m, 1, j % PIECES), :], self.xin.at[at.g ^ m, few, :], at.across())

        hops = {3: (0, 1), 2: (2, 2), 1: (1, 1)}

        def along(j):
            (slot, hop), few = hops[j // PIECES], row(j % PIECES * self.size, self.size)
            return (self.part.at[self.rows(j // PIECES, 0, j % PIECES), :], self.zin.at[slot, few, :], at.along(hop))

        self.b = net.lot(range(4 * PIECES), across, self.xin)
        self.z = net.lot(range(PIECES, 4 * PIECES), along, self.zin)

    def start_of(self, m, k, p):
        at = self.at
        return ((at.g ^ m) * 4 + (at.q ^ k)) * self.quarter + p * self.size

    def rows(self, m, k, p):
        return row(self.start_of(m, k, p), self.size)

    def pair(self, m):
        at = self.at
        return self.part.at[row(((at.g ^ m) * 2 + (1 - at.h % 2)) * 2 * self.quarter, 2 * self.quarter), :]

    def first(self, m):
        self.a.start(m)

    def lines(self, few, k):
        start = (self.at.h // 2 ^ k) * self.quarter
        return pl.ds(pl.multiple_of(start + few.start, 16), few.size)

    def slices(self, m, k, p, step):
        start = self.start_of(m, k, p)
        each(self.size // 16, lambda i: step(row(start + i * 16, 16), row(p * self.size + i * 16, 16)))

    def second(self, m):
        d = self.at.g ^ m
        self.a.arrived(m)

        def step(rows, few):
            total = self.part[rows, :].astype(F32) + self.near[d, self.lines(few, 1), :].astype(F32)
            self.part[rows, :] = total.astype(BF16)

        for p in range(PIECES):
            self.slices(m, 1, p, step)
            self.b.start(m * PIECES + p)

    def third(self, m):
        d = self.at.g ^ m

        def step(rows, few):
            total = self.part[rows, :].astype(F32) + self.near[d, self.lines(few, 0), :].astype(F32)
            total += self.xin[d, few, :].astype(F32)
            if m == 2:
                total += self.zin[0, few, :].astype(F32)
            if m:
                self.part[rows, :] = total.astype(BF16)
            else:
                self.out[few, :] = total

        for p in range(PIECES):
            self.b.arrived(m * PIECES + p)
            if m == 2:
                self.z.arrived(3 * PIECES + p)
            self.slices(m, 0, p, step)
            if m:
                self.z.start(m * PIECES + p)

    def last(self):
        self.third(0)
        for m in (1, 2):
            for p in range(PIECES):
                self.z.arrived(m * PIECES + p)

    def total(self, few):
        return self.out[few, :] + self.zin[1, few, :].astype(F32) + self.zin[2, few, :].astype(F32)

    def produce(self, work):
        def step(i):
            m = 3 - i
            work(m)
            self.first(m)

            @pl.when(i > 0)
            def _():
                self.second(m + 1)

        each(4, step)
        self.a.mark(range(4))
        self.b.mark(range(PIECES, 4 * PIECES))

    def sent(self):
        for lot in (self.a, self.b, self.z):
            lot.sent()


class Turn:
    def __init__(self, net, keep, at, source, view, blocks):
        self.keep, self.at, self.source, self.view, self.blocks = keep, at, source, view, blocks
        self.z, self.o, self.y, self.own = [], [], [], {}
        for b, (items, place) in enumerate(blocks):

            def out(m, items=items):
                return [(source(i, at.g ^ m), view(i, at.s), at.along(m)) for i in items]

            def beside(m, items=items):
                return [(source(i, at.g), view(i, at.s), at.beside()) for i in items]

            def on(m, place=place):
                block = place(at.s ^ (m * at.ranks))
                return (block, block, at.beside())

            def arrival(m, place=place):
                return place(at.s ^ (m * at.ranks))

            self.z.append(net.lot((1, 2, 3), out, lambda m, place=place: place(at.s), arrival, apart=True))
            self.o.append(net.lot((0,), beside, place(at.s), arrival))
            self.y.append(net.lot((1, 2, 3), on, lambda m, place=place: place(at.s), apart=True))

    def start(self, m, b=0, pieces=None):
        self.z[b].start(m, pieces)

    def mine(self, b=0):
        at = self.at
        for i in self.blocks[b][0]:
            self.own[i] = self.keep.put(self.source(i, at.g), self.view(i, at.s))
        self.o[b].start(0)

    def pass_on(self, m, b=0):
        self.z[b].arrived(m)
        self.y[b].start(m)

    def ready(self, b=0):
        for i in self.blocks[b][0]:
            self.own[i].wait()
        self.o[b].arrived(0)
        for m in (1, 2, 3):
            self.y[b].arrived(m)

    def sent(self, b=0):
        self.y[b].sent()


def dot(a, b):
    return jnp.dot(a, b, preferred_element_type=F32)


def dot_nt(a, b):
    return lax.dot_general(a, b, (((1,), (1,)), ((), ())), preferred_element_type=F32)


def dot_tn(a, b):
    return lax.dot_general(a, b, (((0,), (0,)), ((), ())), preferred_element_type=F32)


def turned(values, cos_table, sin_table):
    return values * cos_table + pltpu.roll(values, HD // 2, 1) * sin_table


def mean_square(values):
    return jnp.mean(values * values, axis=1, keepdims=True)


def layer_body(groups, ranks, *refs):
    (tok, cot, gain_one, gain_two, qw, kw, vw, ow, gw, uw, dw) = refs[:11]
    (result_out, rows_out, gains_out, q_out, k_out, v_out, o_out, g_out, u_out, d_out) = refs[11:21]
    (
        gains, gains_all, cosines, sines, rows_one, rows_cot, rows_two, rows_dh, w_qkv, w_o, w_gu, w_d, queries, pairs, mix, dqkv, accum, pair_send,
        pair_in, mixed, dgu, dmixed, own_x, hidden, dhidden, summed, part_a, near_a, xin_a, zin_a, part_b, near_b, xin_b, zin_b,
        in_gu, in_d, in_qkv, in_o, gain_part, gain_in, gain_mid, gain_near, result_own, rows_own, send, receive, local,
    ) = refs[21:]
    at = Where(groups, ranks)
    s, h, g, r = at.s, at.h, at.g, at.r
    shards = groups * ranks
    count, depth = tok.shape
    quarter = count // 4
    width = gains.shape[1]
    units = gw.shape[1] // groups
    half = units // 2
    total_rows = count * shards
    score_scale = 1.0 / math.sqrt(HD)
    score_shift = math.log(total_rows)
    peers = [(s ^ m, h) for m in range(1, shards)] + [(s, h ^ m) for m in range(1, 4)]
    barrier = pltpu.get_barrier_semaphore()
    for peer in peers:
        pl.semaphore_signal(barrier, inc=1, device_id=peer, device_id_type=MESH)
    pl.semaphore_wait(barrier, len(peers))
    net, keep = Net(send, receive), Keep(local)

    def chunk(m):
        return row((g ^ m) * count, count)

    def shard_rows(shard):
        return row(shard * width, width)

    def columns_of(shard):
        return lane(shard * width, width)

    turn_qkv = Turn(
        net, keep, at,
        lambda i, group: (qw, kw, vw)[i].at[:, lane(group * HD, HD)],
        lambda i, shard: w_qkv.at[shard_rows(shard), i * HD : (i + 1) * HD],
        [((0, 1, 2), lambda shard: w_qkv.at[shard_rows(shard), :])],
    )
    turn_gu = Turn(
        net, keep, at,
        lambda i, group: (gw, uw)[i % 2].at[:, lane(group * units + (i // 2) * half, half)],
        lambda i, shard: w_gu.at[shard_rows(shard), i * half : (i + 1) * half],
        [((2 * b, 2 * b + 1), lambda shard, b=b: w_gu.at[shard_rows(shard), b * units : (b + 1) * units]) for b in (0, 1)],
    )
    turn_o = Turn(
        net, keep, at,
        lambda i, group: ow.at[row(group * HD, HD), :],
        lambda i, shard: w_o.at[:, columns_of(shard)],
        [((0,), lambda shard: w_o.at[:, columns_of(shard)])],
    )
    turn_d = Turn(
        net, keep, at,
        lambda i, group: dw.at[row(group * units + i * half, half), :],
        lambda i, shard: w_d.at[i * half : (i + 1) * half, columns_of(shard)],
        [((b,), lambda shard, b=b: w_d.at[b * half : (b + 1) * half, columns_of(shard)]) for b in (0, 1)],
    )

    gain_slot = gains_all.at[:, columns_of(s)]
    gain_moves = net.lot(range(1, shards), lambda m: (gains, gain_slot, (s ^ m, h)), gain_in)
    strip = row(at.q * quarter, quarter)
    mine_start = (g * 4 + at.q) * quarter
    span = ranks * count
    one = Spread(net, at, rows_one, quarter, tok)
    grad = Spread(net, at, rows_cot, quarter, cot)
    two = Spread(net, at, rows_two, quarter)
    three = Spread(net, at, rows_dh, quarter)
    set_a, set_b = (part_a, near_a, xin_a, zin_a), (part_b, near_b, xin_b, zin_b)
    first = Collect(net, at, set_a, quarter, summed)
    second = Collect(net, at, set_a, quarter, summed)
    out_sum = Collect(net, at, set_b, quarter, summed)
    third = Collect(net, at, set_a, quarter, summed)

    def clear(i):
        rows = row(i * 64, 64)
        accum[rows, :] = jnp.zeros_like(accum[rows, :])

    def tables(i):
        rows = row(i * 64, 64)
        first_row = (i // (count // 64) * ranks + r) * count + i % (count // 64) * 64
        places = (first_row + lax.broadcasted_iota(jnp.int32, (64, HD), 0)).astype(F32)
        lanes = lax.broadcasted_iota(jnp.int32, (64, HD), 1)
        low_half = lanes < HD // 2
        order = jnp.where(low_half, lanes, lanes - HD // 2).astype(F32)
        angles = places * jnp.exp(order * (-math.log(10000.0) / (HD // 2)))
        cosines[rows, :] = jnp.cos(angles)
        sines[rows, :] = jnp.where(low_half, -jnp.sin(angles), jnp.sin(angles))

    def norm_one(m):
        def some(i):
            rows = row((g ^ m) * count + i * 32, 32)
            values = rows_one[rows, :].astype(F32)
            inverse = lax.rsqrt(mean_square(values) + epsilon)
            rows_one[rows, :] = (values * inverse * gains_all[0:1, :]).astype(BF16)

        each(count // 32, some)

    def own_place(m):
        return row(((g ^ m) * ranks + r) * count, count)

    pair_moves = net.lot(
        range(4),
        lambda m: (pairs.at[own_place(m), :], pairs.at[own_place(m), :], at.beside()),
        pairs.at[0 : groups * count, :],
    )

    def project(m):
        rows, place = chunk(m), own_place(m)
        heads = dot(rows_one[rows, :], w_qkv[...])
        cos_part, sin_part = cosines[rows, :], sines[rows, :]
        queries[rows, :] = turned(heads[:, :HD], cos_part, sin_part).astype(BF16)
        pairs[place, :HD] = turned(heads[:, HD : 2 * HD], cos_part, sin_part).astype(BF16)
        pairs[place, HD:] = heads[:, 2 * HD :].astype(BF16)
        pair_moves.start(m)

    def weights_of(m, j, query):
        keys = pairs[row(j * span, span), :HD]
        scores = dot_nt(query, keys) * score_scale - score_shift
        q_place = ((g ^ m) * ranks + r) * count + lax.broadcasted_iota(jnp.int32, (count, span), 0)
        k_place = j * span + lax.broadcasted_iota(jnp.int32, (count, span), 1)
        return jnp.where(k_place <= q_place, jax.nn.sigmoid(scores), 0.0)

    def attend(m):
        rows = chunk(m)
        query = queries[rows, :]

        def step(j, total):
            weight = weights_of(m, j, query).astype(BF16)
            return total + dot(weight, pairs[row(j * span, span), HD:])

        total = lax.fori_loop(0, (g ^ m) + 1, step, jnp.zeros((count, HD), F32))
        low = total.astype(BF16)
        mix[rows, :] = low

        @pl.when(m == 3)
        def _():
            turn_o.ready()

        part_a[rows, :] = dot(low, w_o[...]).astype(BF16)

    def norm_two(i):
        few = row(i * 16, 16)
        values = own_x[few, :].astype(F32) + first.total(few)
        hidden[few, :] = values
        inverse = lax.rsqrt(mean_square(values) + epsilon)
        rows_two[row(mine_start + i * 16, 16), :] = (values * inverse * gains_all[1:2, :]).astype(BF16)

    def early(m, b):
        lanes = slice(b * half, (b + 1) * half)
        dmixed[chunk(m), lanes] = dot_nt(rows_cot[chunk(m), :], w_d[lanes, :])

    def feed(m, b):
        rows = chunk(m)
        lanes, pair = slice(b * half, (b + 1) * half), slice(b * units, (b + 1) * units)
        both = dot(rows_two[rows, :], w_gu[:, pair])
        gate, up = both[:, :half], both[:, half:]
        sig = jax.nn.sigmoid(gate)
        act = gate * sig
        mixed[rows, lanes] = (act * up).astype(BF16)
        back = dmixed[rows, lanes]
        dgu[rows, b * units : b * units + half] = (back * up * sig * (1.0 + gate * (1.0 - sig))).astype(BF16)
        dgu[rows, b * units + half : (b + 1) * units] = (back * act).astype(BF16)
        total = dot_nt(dgu[rows, pair], w_gu[:, pair])
        if b:
            total += part_a[rows, :].astype(F32)
        part_a[rows, :] = total.astype(BF16)

    def out_part(m, b):
        rows = chunk(m)
        lanes = slice(b * half, (b + 1) * half)
        total = dot(mixed[rows, lanes], w_d[lanes, :])
        if b:
            total += part_b[rows, :].astype(F32)
        part_b[rows, :] = total.astype(BF16)

    def halves(m, work, lot):
        d = g ^ m

        def step(k):
            work(d * ranks + (r ^ 1 ^ k))

            @pl.when(k == 0)
            def _():
                lot.start(m)

        each(2, step)

    def several(groups_, work, lot):
        first_, last_ = groups_
        each(first_ - last_ + 1, lambda i: halves(first_ - i, work, lot))
        lot.mark(range(last_, first_ + 1))

    def beside(source, target, bulk):
        def describe(m):
            d = g ^ m
            return (source(d * ranks + (r ^ 1)), target(d), at.beside())

        return net.lot(range(4), describe, bulk)

    pairs_of = [slice(b * units, (b + 1) * units) for b in (0, 1)]
    lanes_of = [slice(b * half, (b + 1) * half) for b in (0, 1)]
    moves_gu = [
        beside(lambda shard, p=p: w_gu.at[shard_rows(shard), p], lambda d, p=p: in_gu.at[d, :, p], in_gu.at[:, :, p])
        for p in pairs_of
    ]
    moves_d = [
        beside(lambda shard, p=p: w_d.at[p, columns_of(shard)], lambda d, p=p: in_d.at[d, p, :], in_d.at[:, p, :])
        for p in lanes_of
    ]
    moves_qkv = beside(lambda shard: w_qkv.at[shard_rows(shard), :], lambda d: in_qkv.at[d], in_qkv)
    moves_o = beside(lambda shard: w_o.at[:, columns_of(shard)], lambda d: in_o.at[d], in_o)

    def grads_gu(groups_, b):
        def work(shard):
            w_gu[shard_rows(shard), pairs_of[b]] = dot_tn(rows_two[:, columns_of(shard)], dgu[:, pairs_of[b]]).astype(BF16)

        several(groups_, work, moves_gu[b])

    def grads_d(groups_, b):
        def work(shard):
            columns = columns_of(shard)
            w_d[lanes_of[b], columns] = dot_tn(mixed[:, lanes_of[b]], rows_cot[:, columns]).astype(BF16)

        several(groups_, work, moves_d[b])

    def grads_o(groups_):
        def work(shard):
            columns = columns_of(shard)
            w_o[:, columns] = dot_tn(mix[...], rows_dh[:, columns]).astype(BF16)

        several(groups_, work, moves_o)

    def grads_qkv(groups_):
        def work(shard):
            w_qkv[shard_rows(shard), :] = dot_tn(rows_one[:, columns_of(shard)], dqkv[...]).astype(BF16)

        several(groups_, work, moves_qkv)

    final, final_own = [], []

    def give(moves, whole_, m):
        if m:
            lot = net.lot((0,), lambda j: [(a, b, at.along(m)) for a, b in moves], whole_, lambda j: whole_)
            lot.start(0)
            final.append(lot)
        else:
            final_own.extend(keep.put(a, b) for a, b in moves)

    def sums(m, lot, mine_of, other_of, size):
        lot.arrived(m)

        def step(i):
            a, rows, lanes = mine_of(i)
            b, d, few, others = other_of(i)
            a[rows, lanes] = (a[rows, lanes].astype(F32) + b[d, few, others].astype(F32)).astype(BF16)

        each(size // 32, step)

    def sums_gu(m, b):
        d, p = g ^ m, pairs_of[b]
        start = (d * ranks + r) * width
        sums(
            m, moves_gu[b],
            lambda i: (w_gu, row(start + i * 32, 32), p), lambda i: (in_gu, d, row(i * 32, 32), p), width,
        )
        moves = []
        for i, out in enumerate((g_out, u_out)):
            place = b * units + i * half
            moves.append((w_gu.at[row(start, width), place : place + half], out.at[:, lane(g * units + b * half, half)]))
        give(moves, w_gu.at[row(start, width), p], m)

    def sums_d(m, b):
        d, base = g ^ m, b * half
        columns = columns_of(d * ranks + r)
        sums(
            m, moves_d[b],
            lambda i: (w_d, row(base + i * 32, 32), columns),
            lambda i: (in_d, d, row(base + i * 32, 32), slice(None)), half,
        )
        block = w_d.at[lanes_of[b], columns]
        give([(block, d_out.at[row(g * units + base, half), :])], block, m)

    def sums_o(m):
        d = g ^ m
        columns = columns_of(d * ranks + r)
        sums(
            m, moves_o,
            lambda i: (w_o, row(i * 32, 32), columns), lambda i: (in_o, d, row(i * 32, 32), slice(None)), HD,
        )
        give([(w_o.at[:, columns], o_out.at[row(g * HD, HD), :])], w_o.at[:, columns], m)

    def sums_qkv(m):
        d = g ^ m
        start = (d * ranks + r) * width
        sums(
            m, moves_qkv,
            lambda i: (w_qkv, row(start + i * 32, 32), slice(None)),
            lambda i: (in_qkv, d, row(i * 32, 32), slice(None)), width,
        )
        moves = [
            (w_qkv.at[row(start, width), i * HD : (i + 1) * HD], out.at[:, lane(g * HD, HD)])
            for i, out in enumerate((q_out, k_out, v_out))
        ]
        give(moves, w_qkv.at[row(start, width), :], m)

    def back_two(i, gain_grad):
        few = row(i * 16, 16)
        own = row(mine_start + i * 16, 16)
        upstream, values = second.total(few), hidden[few, :]
        inverse = lax.rsqrt(mean_square(values) + epsilon)
        scaled = upstream * gains_all[1:2, :]
        back = inverse * scaled - values * (inverse * inverse * inverse) * jnp.mean(
            scaled * values, axis=1, keepdims=True
        )
        total = rows_cot[own, :].astype(F32) + back
        dhidden[few, :] = total
        rows_dh[own, :] = total.astype(BF16)
        return gain_grad + jnp.sum(upstream * values * inverse, axis=0, keepdims=True)

    def attend_back(m):
        three.ready(m)
        rows = chunk(m)
        query = queries[rows, :]
        dm = dot_nt(rows_dh[rows, :], w_o[...]).astype(BF16)

        def step(j, total):
            block = row(j * span, span)
            weight = weights_of(m, j, query)
            dweight = dot_nt(dm, pairs[block, HD:])
            dscore = (dweight * weight * (1.0 - weight)).astype(BF16)
            accum[block, HD:] += dot_tn(weight.astype(BF16), dm)
            accum[block, :HD] += dot_tn(dscore, query)
            return total + dot(dscore, pairs[block, :HD])

        total = lax.fori_loop(0, (g ^ m) + 1, step, jnp.zeros((count, HD), F32))
        dqkv[rows, :HD] = turned(total * score_scale, cosines[rows, :], -sines[rows, :]).astype(BF16)

    pair_back = net.lot(range(4), lambda m: (pair_send.at[g ^ m], pair_in.at[g ^ m], at.beside()), pair_send)

    def send_pair(m):
        d = g ^ m
        rows = row((d * ranks + (r ^ 1)) * count, count)
        pair_send[d] = accum[rows, :].astype(BF16)
        pair_back.start(m)

    def back_from_end(i):
        m = g ^ (groups - 1 - i)
        attend_back(m)
        send_pair(m)

    def back_one(m):
        d = g ^ m
        rows = chunk(m)
        pair_back.arrived(m)
        both = accum[own_place(m), :] + pair_in[d].astype(F32)
        dqkv[rows, HD : 2 * HD] = turned(both[:, :HD] * score_scale, cosines[rows, :], -sines[rows, :]).astype(BF16)
        dqkv[rows, 2 * HD :] = both[:, HD:].astype(BF16)
        part_a[rows, :] = dot_nt(dqkv[rows, :], w_qkv[...]).astype(BF16)

    ends = []

    def share(source, target):
        place = target.at[strip, :]
        final_own.append(keep.put(source, place))
        lot = net.lot((0, 1), lambda j: (source, place, (at.near(), at.across())[j]), target.at[0 : 2 * quarter, :])
        lot.start(0)
        lot.start(1)
        ends.append((lot, target))

    def relay():
        lot, target = ends.pop()
        lot.arrived(1)
        final.append(lot)
        block = target.at[row((at.q ^ 1) * quarter, quarter), :]
        on = net.lot((0,), lambda j: (block, block, at.near()), block)
        on.start(0)
        final.append(on)

    def result_rows(i):
        few = row(i * 16, 16)
        result_own[few, :] = (hidden[few, :] + out_sum.total(few)).astype(BF16)

    def back_rows(i, gain_grad):
        few = row(i * 16, 16)
        upstream, values = third.total(few), own_x[few, :].astype(F32)
        inverse = lax.rsqrt(mean_square(values) + epsilon)
        scaled = upstream * gains_all[0:1, :]
        back = inverse * scaled - values * (inverse * inverse * inverse) * jnp.mean(
            scaled * values, axis=1, keepdims=True
        )
        rows_own[few, :] = (dhidden[few, :] + back).astype(BF16)
        return gain_grad + jnp.sum(upstream * values * inverse, axis=0, keepdims=True)

    gain_sums = net.lot(
        range(1, shards), lambda m: (gain_part.at[:, columns_of(s ^ m)], gain_in.at[m - 1], (s ^ m, h)), gain_in
    )
    gain_ends = net.lot(range(1, 4), lambda m: (gain_mid, gain_near.at[m - 1], (s, h ^ m)), gain_near)
    gains[...] = jnp.zeros_like(gains)
    gains[0:1, :] = gain_one[...].astype(F32).reshape(1, width)
    gains[1:2, :] = gain_two[...].astype(F32).reshape(1, width)
    for m in range(1, shards):
        gain_moves.start(m)
    gain_own = keep.put(gains, gain_slot)
    turn_qkv.start(1)
    turn_o.start(3)
    one.start()
    own_rows = keep.put(tok, rows_one.at[chunk(0), :])
    own_strip = keep.put(tok.at[strip, :], own_x)
    own_cot = keep.put(cot, rows_cot.at[chunk(0), :])
    turn_qkv.start(3)
    one.arrive(1)
    turn_o.start(2)
    turn_o.pass_on(3)
    turn_qkv.start(2)
    turn_o.mine()
    turn_qkv.mine()
    one.arrive(2)
    gain_part[...] = jnp.zeros_like(gain_part)
    each(total_rows // 64, clear)
    each(groups * count // 64, tables)
    gain_own.wait()
    for m in range(1, shards):
        gain_moves.arrived(m)
    own_rows.wait()
    own_strip.wait()
    norm_one(0)
    turn_qkv.pass_on(1)
    grad.start()
    turn_o.start(1)
    turn_d.start(3, 1)
    turn_gu.start(1, 1)
    one.arrive(3)
    turn_qkv.pass_on(3)
    turn_qkv.pass_on(2)
    one.second(2)
    one.second(3)
    turn_d.mine(1)
    turn_gu.start(3, 0)
    turn_d.start(2, 1)
    one.second(1)
    for m in (1, 2, 3):
        one.ready(m)
    one.sent()
    for m in (1, 2, 3):
        norm_one(m)
    turn_d.start(3, 0)
    turn_o.pass_on(2)
    turn_qkv.ready()
    turn_d.start(1, 0)
    each(4, project)
    pair_moves.mark(range(4))
    grad.arrive(2)
    turn_o.pass_on(1)
    grad.arrive(1)
    for m in (0, 1, 2, 3):
        pair_moves.arrived(m)
    turn_d.start(2, 0)
    turn_gu.mine(0)
    first.produce(attend)
    first.third(3)
    turn_d.start(1, 1)
    turn_gu.pass_on(3, 0)
    turn_d.pass_on(1, 0)
    first.third(2)
    first.third(1)
    turn_gu.pass_on(1, 1)
    turn_gu.start(2, 0)
    turn_gu.mine(1)
    turn_d.pass_on(2, 0)
    turn_gu.start(1, 0)
    first.second(0)
    turn_d.pass_on(3, 1)
    turn_d.pass_on(2, 1)
    turn_d.pass_on(1, 1)
    first.last()
    each(quarter // 16, norm_two)
    grad.arrive(3)
    turn_d.mine(0)
    two.start()
    turn_gu.pass_on(1, 0)
    grad.second(3)
    grad.second(2)
    turn_gu.start(2, 1)
    grad.second(1)
    two.arrive(1)
    two.arrive(2)
    turn_d.pass_on(3, 0)
    turn_gu.pass_on(2, 0)
    own_cot.wait()
    for m in (1, 2, 3):
        grad.ready(m)
    turn_d.ready(1)
    each(4, lambda m: early(m, 1))
    turn_gu.start(3, 1)
    two.arrive(3)
    two.second(0)
    turn_d.ready(0)
    turn_gu.pass_on(2, 1)
    each(4, lambda m: early(m, 0))
    two.second(1)
    two.second(3)
    two.second(2)
    turn_gu.pass_on(3, 1)
    for m in (0, 1, 2, 3):
        two.ready(m)
    turn_gu.ready(0)
    first.sent()
    each(4, lambda m: feed(m, 0))
    turn_gu.sent(0)
    grads_gu((3, 3), 0)
    turn_gu.ready(1)
    second.produce(lambda m: feed(m, 1))
    sums_gu(3, 0)
    turn_gu.sent(1)
    grads_gu((3, 3), 1)
    second.third(3)
    each(4, lambda m: out_part(m, 0))
    second.second(0)
    grads_gu((2, 2), 0)
    second.third(2)
    turn_d.sent(0)
    grads_d((1, 1), 0)
    second.third(1)
    grads_d((0, 0), 0)
    each(4, lambda m: out_part(m, 1))
    for m in (3, 2, 1, 0):
        out_sum.first(m)
    grads_gu((1, 1), 1)
    sums_gu(2, 0)
    grads_gu((2, 2), 1)
    out_sum.second(2)
    turn_d.sent(1)
    grads_d((2, 2), 1)
    out_sum.second(3)
    grads_gu((0, 0), 1)
    grads_gu((1, 1), 0)
    grads_d((3, 3), 0)
    second.last()
    gain_part[1:2, :] = lax.fori_loop(0, quarter // 16, back_two, jnp.zeros((1, depth), F32))
    three.start()
    out_sum.third(3)
    grads_d((3, 3), 1)
    grads_gu((0, 0), 0)
    sums_gu(3, 1)
    grads_d((1, 1), 1)
    three.arrive(2)
    three.arrive(1)
    out_sum.third(2)
    sums_d(3, 1)
    three.arrive(3)
    three.second(1)
    grads_d((2, 2), 0)
    sums_gu(2, 1)
    three.second(0)
    sums_d(2, 1)
    sums_d(1, 0)
    out_sum.second(1)
    sums_gu(0, 0)
    out_sum.second(0)
    sums_gu(1, 1)
    three.second(2)
    three.second(3)
    each(4, back_from_end)
    pair_back.mark(range(4))
    out_sum.third(1)
    sums_d(1, 1)
    sums_d(2, 0)
    second.sent()
    third.produce(back_one)
    turn_o.sent()
    grads_o((1, 1))
    third.third(3)
    sums_d(3, 0)
    turn_qkv.sent()
    grads_qkv((2, 2))
    third.second(0)
    third.third(2)
    grads_o((3, 3))
    third.third(1)
    grads_d((0, 0), 1)
    grads_o((0, 0))
    sums_qkv(2)
    sums_gu(1, 0)
    grads_qkv((1, 1))
    grads_o((2, 2))
    grads_qkv((3, 3))
    sums_d(0, 0)
    sums_o(3)
    grads_qkv((0, 0))
    out_sum.last()
    each(quarter // 16, result_rows)
    share(result_own, result_out)
    sums_o(1)
    sums_o(0)
    sums_o(2)
    relay()
    third.last()
    gain_part[0:1, :] = lax.fori_loop(0, quarter // 16, back_rows, jnp.zeros((1, depth), F32))
    for m in range(1, shards):
        gain_sums.start(m)
    share(rows_own, rows_out)
    sums_gu(0, 1)
    sums_qkv(3)
    sums_qkv(1)
    sums_d(0, 1)
    sums_qkv(0)
    relay()
    total = gain_part[:, columns_of(s)]
    for m in range(1, shards):
        gain_sums.arrived(m)
        total += gain_in[m - 1]
    gain_mid[...] = total
    for m in range(1, 4):
        gain_ends.start(m)
    for m in range(1, 4):
        gain_ends.arrived(m)
        total += gain_near[m - 1]
    gains_out[...] = total
    for lot in final:
        lot.arrived(0)
    net.finish()
    for copy in final_own:
        copy.wait()


def rows_plan(
    groups,
    ranks,
    tokens,
    attn_gain,
    query_weight,
    key_weight,
    value_weight,
    out_weight,
    mlp_gain,
    gate_weight,
    up_weight,
    down_weight,
    cotangent,
):
    count, depth = tokens.shape
    shards = groups * ranks
    quarter = count // 4
    width = query_weight.shape[0]
    units = gate_weight.shape[1] // groups
    total_rows = count * shards
    here = groups * count
    ins = (
        tokens, cotangent, attn_gain, mlp_gain,
        query_weight, key_weight, value_weight, out_weight, gate_weight, up_weight, down_weight,
    )
    shape = jax.ShapeDtypeStruct
    hbm, vmem = pl.BlockSpec(memory_space=pl.ANY), pl.BlockSpec(memory_space=pltpu.VMEM)
    owners = (query_weight, key_weight, value_weight, out_weight, gate_weight, up_weight, down_weight)
    outs = [
        shape((count, depth), BF16),
        shape((count, depth), BF16),
        shape((8, width), F32),
        *(shape(w.shape, BF16) for w in owners),
    ]

    def low(*extent):
        return pltpu.VMEM(extent, BF16)

    def full(*extent):
        return pltpu.VMEM(extent, F32)

    def collector():
        return [
            low(here, depth),
            low(groups, 2 * quarter, depth),
            low(groups, quarter, depth),
            low(3, quarter, depth),
        ]

    scratch = [
        full(8, width), full(8, depth), full(here, HD), full(here, HD),
        low(here, depth), low(here, depth), low(here, depth), low(here, depth),
        low(depth, 3 * HD), low(HD, depth), low(depth, 2 * units), low(units, depth),
        low(here, HD), low(total_rows, 2 * HD), low(here, HD), low(here, 3 * HD),
        full(total_rows, 2 * HD), low(groups, count, 2 * HD), low(groups, count, 2 * HD),
        low(here, units), low(here, 2 * units), full(here, units),
        low(quarter, depth), full(quarter, depth), full(quarter, depth), full(quarter, depth),
        *collector(), *collector(),
        low(groups, width, 2 * units), low(groups, units, width), low(groups, width, 3 * HD), low(groups, HD, width),
        full(8, depth), full(shards - 1, 8, width), full(8, width), full(3, 8, width),
        low(quarter, depth), low(quarter, depth),
        pltpu.SemaphoreType.DMA((SENDS,)), pltpu.SemaphoreType.DMA((RECEIVES,)), pltpu.SemaphoreType.DMA((KEEPS,)),
    ]
    moved = pl.pallas_call(
        functools.partial(layer_body, groups, ranks),
        out_shape=outs,
        in_specs=[hbm] * 2 + [vmem] * 2 + [hbm] * 7,
        out_specs=[hbm, hbm, vmem] + [hbm] * 7,
        scratch_shapes=scratch,
        compiler_params=pltpu.CompilerParams(
            collective_id=1, has_side_effects=True, vmem_limit_bytes=VMEM_LIMIT
        ),
    )(*ins)
    steps = 8

    def sliced(array):
        rows, columns = array.shape
        return pl.BlockSpec((rows // steps, columns), lambda i: (i, 0))

    gain_specs = [pl.BlockSpec((8, width), lambda i: (0, 0))]
    row_spec = pl.BlockSpec((width,), lambda i: (0,))
    specs = [sliced(moved[0]), sliced(moved[1]), *(sliced(w) for w in moved[3:])]
    gain_row = shape((width,), F32)
    one, two, result, rows_grad, *grads = pl.pallas_call(
        cast_body,
        grid=(steps,),
        out_shape=[gain_row, gain_row, moved[0], moved[1], *(shape(w.shape, F32) for w in owners)],
        in_specs=gain_specs + specs,
        out_specs=[row_spec, row_spec] + specs,
        compiler_params=pltpu.CompilerParams(vmem_limit_bytes=VMEM_LIMIT),
    )(moved[2], moved[0], moved[1], *moved[3:])
    return (result, rows_grad, one, *grads[:4], two, *grads[4:])


def cast_body(*refs):
    inputs = len(refs) // 2
    gains, sources, (one, two, *targets) = refs[0], refs[1:inputs], refs[inputs:]
    one[...] = gains[0, :]
    two[...] = gains[1, :]
    for source, target in zip(sources, targets):
        target[...] = source[...].astype(target.dtype)


def on_device(tokens, attn_gain, query_weight, *rest):
    groups = query_weight.shape[1] // HD
    ranks = lax.axis_size("seq") // groups
    fits = lax.axis_size("head") == 4 and groups == 4 and ranks == 2 and query_weight.shape[0] % 128 == 0
    plan = functools.partial(rows_plan, groups, ranks) if fits else gathered_weights
    return plan(tokens, attn_gain, query_weight, *rest)


def solution(mesh):
    in_specs = (
        P("seq", None),
        P("seq"),
        P("seq", "head"),
        P("seq", "head"),
        P("seq", "head"),
        P("head", "seq"),
        P("seq"),
        P("seq", "head"),
        P("seq", "head"),
        P("head", "seq"),
        P("seq", None),
    )
    out_specs = (
        P("seq", None),
        P("seq", None),
        P("seq"),
        P("seq", "head"),
        P("seq", "head"),
        P("seq", "head"),
        P("head", "seq"),
        P("seq"),
        P("seq", "head"),
        P("seq", "head"),
        P("head", "seq"),
    )
    return jax.shard_map(
        on_device, mesh=mesh, in_specs=in_specs, out_specs=out_specs, check_vma=False
    )
```

```python
import functools
import math

import jax
import jax.numpy as jnp
from jax import lax
from jax.experimental import pallas as pl
from jax.experimental.pallas import tpu as pltpu
from jax.sharding import PartitionSpec as P

MESH = pl.DeviceIdType.MESH
F32, BF16 = jnp.float32, jnp.bfloat16

HD = 128


epsilon = 1e-05
block_limit = 512
VMEM_LIMIT = 63 * 2**20
SENDS, RECEIVES, KEEPS = 59, 217, 30
PIECES = 2
PARTS = (2, 2)


def tables(offset, length, half_width):
    places = (offset + jnp.arange(length, dtype=jnp.int32)).astype(jnp.float32)
    frequency = jnp.exp(
        jnp.arange(half_width, dtype=jnp.float32) * (-math.log(10000.0) / half_width)
    )
    angles = places[:, None] * frequency[None, :]
    return (jnp.cos(angles)[:, None, :], jnp.sin(angles)[:, None, :])


def rotary(values, cos_table, sin_table):
    half_width = values.shape[-1] // 2
    front = values[..., :half_width]
    back_half = values[..., half_width:]
    return jnp.concatenate(
        [front * cos_table - back_half * sin_table, back_half * cos_table + front * sin_table],
        axis=-1,
    )


def unrotary(gradient, cos_table, sin_table):
    half_width = gradient.shape[-1] // 2
    front = gradient[..., :half_width]
    back_half = gradient[..., half_width:]
    return jnp.concatenate(
        [front * cos_table + back_half * sin_table, back_half * cos_table - front * sin_table],
        axis=-1,
    )


def norm_back(values, inverse, gain_vector, upstream):
    scaled = upstream * gain_vector
    gain_grad = jnp.sum(upstream * values * inverse, axis=0)
    value_grad = inverse * scaled - values * inverse**3 * jnp.mean(
        scaled * values, axis=1, keepdims=True
    )
    return (value_grad, gain_grad)


def gathered_weights(
    tokens,
    attn_gain,
    query_weight,
    key_weight,
    value_weight,
    out_weight,
    mlp_gain,
    gate_weight,
    up_weight,
    down_weight,
    cotangent,
):
    row_count = tokens.shape[0]
    total_rows = row_count * lax.axis_size("seq")
    row_start = lax.axis_index("seq") * row_count
    local_width = query_weight.shape[1]
    local_heads = local_width // HD
    score_scale = 1.0 / math.sqrt(HD)
    score_shift = math.log(total_rows)
    block_rows = math.gcd(total_rows, block_limit)
    block_count = total_rows // block_rows
    attn_gain_full, query_full, key_full, value_full, out_full = (
        lax.all_gather(attn_gain, "seq", axis=0, tiled=True),
        lax.all_gather(query_weight, "seq", axis=0, tiled=True),
        lax.all_gather(key_weight, "seq", axis=0, tiled=True),
        lax.all_gather(value_weight, "seq", axis=0, tiled=True),
        lax.all_gather(out_weight, "seq", axis=1, tiled=True),
    )
    mlp_gain_full, gate_full, up_full, down_full = (
        lax.all_gather(mlp_gain, "seq", axis=0, tiled=True),
        lax.all_gather(gate_weight, "seq", axis=0, tiled=True),
        lax.all_gather(up_weight, "seq", axis=0, tiled=True),
        lax.all_gather(down_weight, "seq", axis=1, tiled=True),
    )
    token_values = tokens.astype(jnp.float32)
    inverse_one = lax.rsqrt(jnp.mean(token_values * token_values, axis=1, keepdims=True) + epsilon)
    normed_one = (token_values * inverse_one * attn_gain_full.astype(jnp.float32)).astype(
        jnp.bfloat16
    )
    query_pre = jnp.dot(normed_one, query_full, preferred_element_type=jnp.float32)
    key_pre = jnp.dot(normed_one, key_full, preferred_element_type=jnp.float32)
    value_rows = (
        jnp.dot(normed_one, value_full, preferred_element_type=jnp.float32)
        .astype(jnp.bfloat16)
        .reshape(row_count, local_heads, HD)
    )
    cos_table, sin_table = tables(row_start, row_count, HD // 2)
    query_rows = (
        rotary(query_pre.reshape(row_count, local_heads, HD), cos_table, sin_table)
        .astype(jnp.bfloat16)
        .reshape(row_count, local_width)
    )
    key_rows = rotary(key_pre.reshape(row_count, local_heads, HD), cos_table, sin_table).astype(
        jnp.bfloat16
    )
    all_queries = lax.all_gather(query_rows, "seq", axis=0, tiled=True)
    key_places = row_start + jnp.arange(row_count, dtype=jnp.int32)

    def weights_for(query_block, block_start):
        scores = (
            jnp.einsum("qhd,khd->hqk", query_block, key_rows, preferred_element_type=jnp.float32)
            * score_scale
            - score_shift
        )
        query_places = block_start + jnp.arange(query_block.shape[0], dtype=jnp.int32)
        visible = key_places[None, :] <= query_places[:, None]
        return jnp.where(visible[None], jax.nn.sigmoid(scores), 0.0)

    step_rows = math.gcd(row_count * lax.axis_size("seq"), block_limit)
    step_count = row_count * lax.axis_size("seq") // step_rows
    picked = all_queries.reshape(step_count, step_rows, local_heads, HD)
    starts = jnp.arange(step_count, dtype=jnp.int32) * step_rows

    def one_block(packed):
        query_block, block_start = packed
        weights = weights_for(query_block, block_start).astype(jnp.bfloat16)
        return jnp.einsum(
            "hqk,khd->qhd", weights, value_rows, preferred_element_type=jnp.float32
        ).reshape(step_rows, local_width)

    attn_mix = lax.psum_scatter(
        lax.map(one_block, (picked, starts)).reshape(row_count * lax.axis_size("seq"), local_width),
        "seq",
        scatter_dimension=0,
        tiled=True,
    ).astype(jnp.bfloat16)
    attn_branch = lax.psum(jnp.dot(attn_mix, out_full, preferred_element_type=jnp.float32), "head")
    hidden = token_values + attn_branch
    inverse_two = lax.rsqrt(jnp.mean(hidden * hidden, axis=1, keepdims=True) + epsilon)
    normed_two = (hidden * inverse_two * mlp_gain_full.astype(jnp.float32)).astype(jnp.bfloat16)
    gate_pre = jnp.dot(normed_two, gate_full, preferred_element_type=jnp.float32)
    up_pre = jnp.dot(normed_two, up_full, preferred_element_type=jnp.float32)
    gate_act = jax.nn.silu(gate_pre)
    mixed = (gate_act * up_pre).astype(jnp.bfloat16)
    mlp_branch = lax.psum(
        jnp.dot(mixed, down_full, preferred_element_type=jnp.float32).astype(jnp.bfloat16), "head"
    ).astype(jnp.float32)
    result = (hidden + mlp_branch).astype(jnp.bfloat16)
    kept_weights = (
        lax.all_gather(attn_gain, "seq", axis=0, tiled=True),
        lax.all_gather(query_weight, "seq", axis=0, tiled=True),
        lax.all_gather(key_weight, "seq", axis=0, tiled=True),
        lax.all_gather(value_weight, "seq", axis=0, tiled=True),
        lax.all_gather(out_weight, "seq", axis=1, tiled=True),
        lax.all_gather(mlp_gain, "seq", axis=0, tiled=True),
        lax.all_gather(gate_weight, "seq", axis=0, tiled=True),
        lax.all_gather(up_weight, "seq", axis=0, tiled=True),
        lax.all_gather(down_weight, "seq", axis=1, tiled=True),
    )
    (
        attn_gain_back,
        query_back,
        key_back,
        value_back,
        out_back,
        mlp_gain_back,
        gate_back,
        up_back,
        down_back,
    ) = kept_weights
    attn_gain_f = attn_gain_back.astype(jnp.float32)
    mlp_gain_f = mlp_gain_back.astype(jnp.float32)
    grad_values = cotangent.astype(jnp.float32)
    grad_down = jnp.einsum("tf,td->fd", mixed, cotangent, preferred_element_type=jnp.float32)
    dmixed = jnp.einsum("td,fd->tf", cotangent, down_back, preferred_element_type=jnp.float32)
    gate_sig = jax.nn.sigmoid(gate_pre)
    dgate = (dmixed * up_pre * gate_sig * (1.0 + gate_pre * (1.0 - gate_sig))).astype(jnp.bfloat16)
    dup = (dmixed * gate_act).astype(jnp.bfloat16)
    grad_gate = jnp.einsum("tk,tf->kf", normed_two, dgate, preferred_element_type=jnp.float32)
    grad_up = jnp.einsum("tk,tf->kf", normed_two, dup, preferred_element_type=jnp.float32)
    dnormed_two = lax.psum(
        jnp.einsum("tf,kf->tk", dgate, gate_back, preferred_element_type=jnp.float32)
        + jnp.einsum("tf,kf->tk", dup, up_back, preferred_element_type=jnp.float32),
        "head",
    )
    dhidden_norm, grad_mlp_gain = norm_back(hidden, inverse_two, mlp_gain_f, dnormed_two)
    dhidden = grad_values + dhidden_norm
    mlp_sums = (grad_mlp_gain, grad_gate, grad_up, grad_down)
    dhidden_low = dhidden.astype(jnp.bfloat16)
    grad_out = jnp.einsum("tc,td->cd", attn_mix, dhidden_low, preferred_element_type=jnp.float32)
    dmix = jnp.einsum(
        "td,cd->tc", dhidden_low, out_back, preferred_element_type=jnp.float32
    ).astype(jnp.bfloat16)
    all_dmix = lax.all_gather(dmix, "seq", axis=0, tiled=True)

    def backward_block(carry, packed):
        key_accum, value_accum = carry
        query_block, grad_block, block_start = packed
        weights = weights_for(query_block, block_start)
        grad_weights = jnp.einsum(
            "qhd,khd->hqk", grad_block, value_rows, preferred_element_type=jnp.float32
        )
        grad_scores = (grad_weights * weights * (1.0 - weights)).astype(jnp.bfloat16)
        value_accum = value_accum + jnp.einsum(
            "hqk,qhd->khd",
            weights.astype(jnp.bfloat16),
            grad_block,
            preferred_element_type=jnp.float32,
        )
        key_accum = key_accum + jnp.einsum(
            "hqk,qhd->khd", grad_scores, query_block, preferred_element_type=jnp.float32
        )
        query_part = (
            jnp.einsum("hqk,khd->qhd", grad_scores, key_rows, preferred_element_type=jnp.float32)
            * score_scale
        )
        return ((key_accum, value_accum), query_part.reshape(block_rows, local_width))

    zero_rows = jnp.zeros((row_count, local_heads, HD), jnp.float32)
    block_starts = jnp.arange(block_count, dtype=jnp.int32) * block_rows
    (key_accum, value_accum), query_parts = lax.scan(
        backward_block,
        (zero_rows, zero_rows),
        (
            all_queries.reshape(block_count, block_rows, local_heads, HD),
            all_dmix.reshape(block_count, block_rows, local_heads, HD),
            block_starts,
        ),
    )
    query_sum = lax.psum_scatter(
        query_parts.reshape(total_rows, local_width), "seq", scatter_dimension=0, tiled=True
    )
    dquery_pre = (
        unrotary(query_sum.reshape(row_count, local_heads, HD), cos_table, sin_table)
        .reshape(row_count, local_width)
        .astype(jnp.bfloat16)
    )
    dkey_pre = (
        unrotary(key_accum * score_scale, cos_table, sin_table)
        .reshape(row_count, local_width)
        .astype(jnp.bfloat16)
    )
    dvalue = value_accum.reshape(row_count, local_width).astype(jnp.bfloat16)
    grad_query = jnp.einsum("tk,tc->kc", normed_one, dquery_pre, preferred_element_type=jnp.float32)
    grad_key = jnp.einsum("tk,tc->kc", normed_one, dkey_pre, preferred_element_type=jnp.float32)
    grad_value = jnp.einsum("tk,tc->kc", normed_one, dvalue, preferred_element_type=jnp.float32)
    dnormed_one = lax.psum(
        jnp.einsum("tc,kc->tk", dquery_pre, query_back, preferred_element_type=jnp.float32)
        + jnp.einsum("tc,kc->tk", dkey_pre, key_back, preferred_element_type=jnp.float32)
        + jnp.einsum("tc,kc->tk", dvalue, value_back, preferred_element_type=jnp.float32),
        "head",
    )
    dinput_norm, grad_attn_gain = norm_back(token_values, inverse_one, attn_gain_f, dnormed_one)
    input_grad = (dhidden + dinput_norm).astype(jnp.bfloat16)
    every_sum = (
        lax.psum_scatter(grad_attn_gain, "seq", scatter_dimension=0, tiled=True),
        lax.psum_scatter(grad_query, "seq", scatter_dimension=0, tiled=True),
        lax.psum_scatter(grad_key, "seq", scatter_dimension=0, tiled=True),
        lax.psum_scatter(grad_value, "seq", scatter_dimension=0, tiled=True),
        lax.psum_scatter(grad_out, "seq", scatter_dimension=1, tiled=True),
        lax.psum_scatter(grad_mlp_gain, "seq", scatter_dimension=0, tiled=True),
        lax.psum_scatter(grad_gate, "seq", scatter_dimension=0, tiled=True),
        lax.psum_scatter(grad_up, "seq", scatter_dimension=0, tiled=True),
        lax.psum_scatter(grad_down, "seq", scatter_dimension=1, tiled=True),
    )
    attn_sums = every_sum[:5]
    mlp_sums = every_sum[5:]
    return (
        result,
        input_grad,
        attn_sums[0],
        attn_sums[1],
        attn_sums[2],
        attn_sums[3],
        attn_sums[4],
        mlp_sums[0],
        mlp_sums[1],
        mlp_sums[2],
        mlp_sums[3],
    )


class Net:
    def __init__(self, send, receive):
        self.send, self.receive, self.sends, self.receives, self.lots = send, receive, 0, 0, []

    def lot(self, *args, **options):
        return Lot(self, *args, **options)

    def finish(self):
        for lot in self.lots:
            lot.sent()


class Lot:
    def __init__(self, net, indices, describe, bulk, arrival=None, apart=False):
        self.net, self.describe, self.bulk, self.arrival, self.apart = net, describe, bulk, arrival, apart
        self.place = {j: net.receives + i for i, j in enumerate(indices)}
        self.low = min(indices)
        self.send_base, self.receive_base = net.sends, net.receives
        net.receives += len(indices)
        net.sends += len(indices) if apart else 1
        self.started, self.open = set(), set()
        net.lots.append(self)

    def receive_at(self, j):
        return self.net.receive.at[self.receive_base + (j - self.low)]

    def send_at(self, j):
        return self.net.send.at[self.send_base + (j - self.low if self.apart else 0)]

    def start(self, j, pieces=None):
        described = self.describe(j)
        for i, (source, target, device) in enumerate(described if isinstance(described, list) else [described]):
            if pieces is None or i in pieces:
                pltpu.make_async_remote_copy(
                    src_ref=source,
                    dst_ref=target,
                    send_sem=self.send_at(j),
                    recv_sem=self.receive_at(j),
                    device_id=device,
                    device_id_type=MESH,
                ).start()
        if isinstance(j, int):
            self.mark((j,))

    def mark(self, indices):
        self.started.update(indices)
        self.open.update(indices if self.apart else (self.low,))

    def arrived(self, j):
        described = self.describe(j)
        target = self.arrival(j) if self.arrival else described[1]
        self.wait(target, self.receive_at(j))

    def wait(self, like, sem):
        pltpu.make_async_copy(like, like, sem).wait()

    def sent(self, j=None):
        for k in sorted(self.open) if j is None else [j] if j in self.open else []:
            self.open.remove(k)
            self.wait(self.bulk(k) if self.apart else self.bulk, self.send_at(k))


class Keep:
    def __init__(self, sems):
        self.sems, self.count = sems, 0

    def put(self, source, target):
        copy = pltpu.make_async_copy(source, target, self.sems.at[self.count])
        self.count += 1
        copy.start()
        return copy


class Where:
    def __init__(self, groups, ranks):
        self.s, self.h = lax.axis_index("seq"), lax.axis_index("head")
        self.g, self.r = self.s // ranks, self.s % ranks
        self.groups, self.ranks = groups, ranks
        self.q = self.h % 2 * 2 + self.h // 2

    def along(self, m):
        return (self.s ^ (m * self.ranks), self.h)

    def beside(self):
        return (self.s ^ 1, self.h)

    def across(self):
        return (self.s, self.h ^ 2)

    def near(self):
        return (self.s, self.h ^ 1)


def lane(start, size):
    return pl.ds(pl.multiple_of(start, 128), size)


def row(start, size):
    return pl.ds(pl.multiple_of(start, size), size)


def each(count, step):
    def body(i, carry):
        step(i)
        return carry

    lax.fori_loop(0, count, body, 0)


class Spread:
    def __init__(self, net, at, buffer, quarter, own=None):
        self.at, self.buffer, self.quarter, self.shared = at, buffer, quarter, own is not None
        self.size = quarter // PIECES

        def along(j):
            m, p = j // PIECES, j % PIECES
            if m == 3:
                return (self.block(2, 0, p), self.block(2, 0, p), at.along(1))
            first = self.block(0, 0, p) if own is None else own.at[row(at.q * quarter + p * self.size, self.size), :]
            return (first, self.block(0, 0, p), at.along(m))

        def moved(k, device):
            def describe(j):
                block = self.block(j // PIECES, k, j % PIECES)
                return (block, block, device)

            return describe

        low = 1 if self.shared else 0
        indices = range(low * PIECES, 4 * PIECES)
        some = buffer.at[0 : (4 - low) * quarter, :]
        self.z = net.lot(range(PIECES, 4 * PIECES), along, buffer.at[0 : 3 * quarter, :])
        self.x = net.lot(indices, moved(0, at.across()), some)

        def near(m):
            blocks = [self.block(m, k, p) for k in (0, 1) for p in range(PIECES)]
            return [(block, block, at.near()) for block in blocks]

        self.n = net.lot(
            range(low, 4), near, buffer.at[0 : 2 * (4 - low) * quarter, :], lambda m: buffer.at[0 : 2 * quarter, :]
        )

    def block(self, m, k, p):
        at = self.at
        start = ((at.g ^ m) * 4 + (at.q ^ k)) * self.quarter + p * self.size
        return self.buffer.at[row(start, self.size), :]

    def pass_on(self, j):
        self.x.start(j)
        self.n.start(j // PIECES, (j % PIECES,))

    def start(self, m):
        for p in range(PIECES):
            self.z.start(m * PIECES + p)

    def start_own(self):
        for p in range(PIECES):
            self.pass_on(p)

    def arrive(self, m):
        for p in range(PIECES):
            j = m * PIECES + p
            self.z.arrived(j)
            if m == 2:
                self.z.start(3 * PIECES + p)
            self.pass_on(j)

    def second(self, m):
        for p in range(PIECES):
            self.x.arrived(m * PIECES + p)
            self.n.start(m, (PIECES + p,))

    def ready(self, m):
        self.n.arrived(m)

    def sent(self):
        for lot in (self.z, self.x, self.n):
            lot.sent()


class Collect:
    def __init__(self, net, at, refs, quarter, out):
        self.at, self.quarter, self.out = at, quarter, out
        self.size = quarter // PIECES
        self.part, self.near, self.xin, self.zin = refs
        self.a = net.lot(range(4), lambda m: (self.pair(m), self.near.at[at.g ^ m], at.near()), self.near)

        def across(j):
            m, few = j // PIECES, row(j % PIECES * self.size, self.size)
            return (self.part.at[self.rows(m, 1, j % PIECES), :], self.xin.at[at.g ^ m, few, :], at.across())

        hops = {3: (0, 1), 2: (2, 2), 1: (1, 1)}

        def along(j):
            (slot, hop), few = hops[j // PIECES], row(j % PIECES * self.size, self.size)
            return (self.part.at[self.rows(j // PIECES, 0, j % PIECES), :], self.zin.at[slot, few, :], at.along(hop))

        self.b = net.lot(range(4 * PIECES), across, self.xin)
        self.z = net.lot(range(PIECES, 4 * PIECES), along, self.zin)

    def start_of(self, m, k, p):
        at = self.at
        return ((at.g ^ m) * 4 + (at.q ^ k)) * self.quarter + p * self.size

    def rows(self, m, k, p):
        return row(self.start_of(m, k, p), self.size)

    def pair(self, m):
        at = self.at
        return self.part.at[row(((at.g ^ m) * 2 + (1 - at.h % 2)) * 2 * self.quarter, 2 * self.quarter), :]

    def first(self, m):
        self.a.start(m)

    def lines(self, few, k):
        start = (self.at.h // 2 ^ k) * self.quarter
        return pl.ds(pl.multiple_of(start + few.start, 16), few.size)

    def slices(self, m, k, p, step):
        start = self.start_of(m, k, p)
        each(self.size // 16, lambda i: step(row(start + i * 16, 16), row(p * self.size + i * 16, 16)))

    def second(self, m):
        d = self.at.g ^ m
        self.a.arrived(m)

        def step(rows, few):
            total = self.part[rows, :].astype(F32) + self.near[d, self.lines(few, 1), :].astype(F32)
            self.part[rows, :] = total.astype(BF16)

        for p in range(PIECES):
            self.slices(m, 1, p, step)
            self.b.start(m * PIECES + p)

    def third(self, m):
        d = self.at.g ^ m

        def step(rows, few):
            total = self.part[rows, :].astype(F32) + self.near[d, self.lines(few, 0), :].astype(F32)
            total += self.xin[d, few, :].astype(F32)
            if m == 2:
                total += self.zin[0, few, :].astype(F32)
            if m:
                self.part[rows, :] = total.astype(BF16)
            else:
                self.out[few, :] = total

        for p in range(PIECES):
            self.b.arrived(m * PIECES + p)
            if m == 2:
                self.z.arrived(3 * PIECES + p)
            self.slices(m, 0, p, step)
            if m:
                self.z.start(m * PIECES + p)

    def last(self):
        self.third(0)
        for m in (1, 2):
            for p in range(PIECES):
                self.z.arrived(m * PIECES + p)

    def total(self, few):
        return self.out[few, :] + self.zin[1, few, :].astype(F32) + self.zin[2, few, :].astype(F32)

    def produce(self, work):
        def step(i):
            m = 3 - i
            work(m)
            self.first(m)

            @pl.when(i > 0)
            def _():
                self.second(m + 1)

        each(4, step)
        self.a.mark(range(4))
        self.b.mark(range(PIECES, 4 * PIECES))

    def sent(self):
        for lot in (self.a, self.b, self.z):
            lot.sent()


class Turn:
    def __init__(self, net, keep, at, source, view, blocks):
        self.keep, self.at, self.source, self.view, self.blocks = keep, at, source, view, blocks
        self.z, self.y, self.own = [], [], {}
        for b, (items, place, several) in enumerate(blocks):

            def out(m, items=items):
                return [(source(i, at.g ^ m), view(i, at.s), at.along(m)) for i in items]

            def beside(_, items=items, place=place):
                own = [(source(i, at.g), view(i, at.s), at.beside()) for i in items]
                others = [place(at.s ^ (m * at.ranks)) for m in (1, 2, 3)]
                return own + [(block, block, at.beside()) for block in others]

            def arrival(m, place=place):
                return place(at.s ^ (m * at.ranks))

            self.z.append(net.lot((1, 2, 3), out, several(3), arrival))
            self.y.append(net.lot((0,), beside, several(4), lambda _, several=several: several(4)))

    def start(self, m, b=0, pieces=None):
        self.z[b].start(m, pieces)

    def mine(self, b=0):
        items = self.blocks[b][0]
        for i in items:
            self.own[i] = self.keep.put(self.source(i, self.at.g), self.view(i, self.at.s))
        self.y[b].start(0, range(len(items)))

    def pass_on(self, m, b=0):
        self.z[b].arrived(m)
        self.y[b].start(0, (len(self.blocks[b][0]) + m - 1,))

    def ready(self, b=0):
        for i in self.blocks[b][0]:
            self.own[i].wait()
        self.y[b].arrived(0)

    def sent(self, b=0):
        self.y[b].sent()


def dot(a, b):
    return jnp.dot(a, b, preferred_element_type=F32)


def dot_nt(a, b):
    return lax.dot_general(a, b, (((1,), (1,)), ((), ())), preferred_element_type=F32)


def dot_tn(a, b):
    return lax.dot_general(a, b, (((0,), (0,)), ((), ())), preferred_element_type=F32)


def turned(values, cos_table, sin_table):
    return values * cos_table + pltpu.roll(values, HD // 2, 1) * sin_table


def mean_square(values):
    return jnp.mean(values * values, axis=1, keepdims=True)


def layer_body(groups, ranks, *refs):
    (tok, cot, gain_one, gain_two, qw, kw, vw, ow, gw, uw, dw) = refs[:11]
    (result_out, rows_out, gains_out, q_out, k_out, v_out, o_out, g_out, u_out, d_out) = refs[11:21]
    (
        gains, gains_all, cosines, sines, rows_one, rows_cot, rows_two, rows_dh, w_qkv, w_o, w_gu, w_d, queries, pairs, mix, dqkv, accum, pair_send,
        pair_in, mixed, dgu, dmixed, own_x, hidden, dhidden, summed, part_a, near_a, xin_a, zin_a, part_b, near_b, xin_b, zin_b,
        in_gu, in_d, in_qkv, in_o, gain_part, gain_in, gain_mid, gain_near, result_own, rows_own, send, receive, local,
    ) = refs[21:]
    at = Where(groups, ranks)
    s, h, g, r = at.s, at.h, at.g, at.r
    shards = groups * ranks
    count, depth = tok.shape
    quarter = count // 4
    width = gains.shape[1]
    units = gw.shape[1] // groups
    bounds = [units * sum(PARTS[:b]) // sum(PARTS) for b in range(len(PARTS) + 1)]
    lanes_of = [slice(a, b) for a, b in zip(bounds, bounds[1:])]
    pairs_of = [slice(2 * a, 2 * b) for a, b in zip(bounds, bounds[1:])]
    size_of = [b - a for a, b in zip(bounds, bounds[1:])]

    def gate_up(b, i):
        start = pairs_of[b].start + i * size_of[b]
        return slice(start, start + size_of[b])

    total_rows = count * shards
    score_scale = 1.0 / math.sqrt(HD)
    score_shift = math.log(total_rows)
    peers = [(s ^ m, h) for m in range(1, shards)] + [(s, h ^ m) for m in range(1, 4)]
    barrier = pltpu.get_barrier_semaphore()
    for peer in peers:
        pl.semaphore_signal(barrier, inc=1, device_id=peer, device_id_type=MESH)
    pl.semaphore_wait(barrier, len(peers))
    net, keep = Net(send, receive), Keep(local)

    def chunk(m):
        return row((g ^ m) * count, count)

    def shard_rows(shard):
        return row(shard * width, width)

    def columns_of(shard):
        return lane(shard * width, width)

    turn_qkv = Turn(
        net, keep, at,
        lambda i, group: (qw, kw, vw)[i].at[:, lane(group * HD, HD)],
        lambda i, shard: w_qkv.at[shard_rows(shard), i * HD : (i + 1) * HD],
        [((0, 1, 2), lambda shard: w_qkv.at[shard_rows(shard), :], lambda n: w_qkv.at[0 : n * width, :])],
    )
    few = width // 2
    turn_gu = Turn(
        net, keep, at,
        lambda i, group: (gw, uw)[i // 2 % 2].at[
            i % 2 * few : (i % 2 + 1) * few, lane(group * units + lanes_of[i // 4].start, size_of[i // 4])
        ],
        lambda i, shard: w_gu.at[row(shard * width + i % 2 * few, few), gate_up(i // 4, i // 2 % 2)],
        [
            (range(4 * b, 4 * b + 4), lambda shard, p=p: w_gu.at[shard_rows(shard), p], lambda n, p=p: w_gu.at[0 : n * width, p])
            for b, p in enumerate(pairs_of)
        ],
    )
    turn_o = Turn(
        net, keep, at,
        lambda i, group: ow.at[row(group * HD, HD), :],
        lambda i, shard: w_o.at[:, columns_of(shard)],
        [((0,), lambda shard: w_o.at[:, columns_of(shard)], lambda n: w_o.at[:, 0 : n * width])],
    )
    turn_d = Turn(
        net, keep, at,
        lambda i, group: dw.at[lane(group * units + lanes_of[i].start, size_of[i]), :],
        lambda i, shard: w_d.at[lanes_of[i], columns_of(shard)],
        [
            ((b,), lambda shard, p=p: w_d.at[p, columns_of(shard)], lambda n, p=p: w_d.at[p, 0 : n * width])
            for b, p in enumerate(lanes_of)
        ],
    )

    gain_slot = gains_all.at[:, columns_of(s)]
    gain_moves = net.lot(
        (0,), lambda _: [(gains, gain_slot, (s ^ m, h)) for m in range(1, shards)], gain_in, lambda _: gain_in
    )
    strip = row(at.q * quarter, quarter)
    mine_start = (g * 4 + at.q) * quarter
    span = ranks * count
    one = Spread(net, at, rows_dh, quarter, tok)
    grad = Spread(net, at, rows_cot, quarter, cot)
    two = Spread(net, at, rows_two, quarter)
    three = Spread(net, at, rows_dh, quarter)
    set_a, set_b = (part_a, near_a, xin_a, zin_a), (part_b, near_b, xin_b, zin_b)
    first = Collect(net, at, set_a, quarter, summed)
    second = Collect(net, at, set_a, quarter, summed)
    out_sum = Collect(net, at, set_b, quarter, summed)
    third = Collect(net, at, set_a, quarter, summed)

    def clear(i):
        rows = row(i * 64, 64)
        accum[rows, :] = jnp.zeros_like(accum[rows, :])

    def tables(i):
        rows = row(i * 64, 64)
        first_row = (i // (count // 64) * ranks + r) * count + i % (count // 64) * 64
        places = (first_row + lax.broadcasted_iota(jnp.int32, (64, HD), 0)).astype(F32)
        lanes = lax.broadcasted_iota(jnp.int32, (64, HD), 1)
        low_half = lanes < HD // 2
        order = jnp.where(low_half, lanes, lanes - HD // 2).astype(F32)
        angles = places * jnp.exp(order * (-math.log(10000.0) / (HD // 2)))
        cosines[rows, :] = jnp.cos(angles)
        sines[rows, :] = jnp.where(low_half, -jnp.sin(angles), jnp.sin(angles))

    def norm_one(m):
        def some(i):
            rows = row((g ^ m) * count + i * 32, 32)
            values = rows_dh[rows, :].astype(F32)
            inverse = lax.rsqrt(mean_square(values) + epsilon)
            rows_one[rows, :] = (values * inverse * gains_all[0:1, :]).astype(BF16)

        each(count // 32, some)

    def own_place(m):
        return row(((g ^ m) * ranks + r) * count, count)

    pair_moves = net.lot(
        range(4),
        lambda m: (pairs.at[own_place(m), :], pairs.at[own_place(m), :], at.beside()),
        pairs.at[0 : groups * count, :],
    )

    def project(m):
        rows, place = chunk(m), own_place(m)
        heads = dot(rows_one[rows, :], w_qkv[...])
        cos_part, sin_part = cosines[rows, :], sines[rows, :]
        queries[rows, :] = turned(heads[:, :HD], cos_part, sin_part).astype(BF16)
        pairs[place, :HD] = turned(heads[:, HD : 2 * HD], cos_part, sin_part).astype(BF16)
        pairs[place, HD:] = heads[:, 2 * HD :].astype(BF16)
        pair_moves.start(m)

    def weights_of(m, j, query):
        keys = pairs[row(j * span, span), :HD]
        scores = dot_nt(query, keys) * score_scale - score_shift
        q_place = ((g ^ m) * ranks + r) * count + lax.broadcasted_iota(jnp.int32, (count, span), 0)
        k_place = j * span + lax.broadcasted_iota(jnp.int32, (count, span), 1)
        return jnp.where(k_place <= q_place, jax.nn.sigmoid(scores), 0.0)

    def attend(m):
        rows = chunk(m)
        query = queries[rows, :]

        def step(j, total):
            weight = weights_of(m, j, query).astype(BF16)
            return total + dot(weight, pairs[row(j * span, span), HD:])

        total = lax.fori_loop(0, (g ^ m) + 1, step, jnp.zeros((count, HD), F32))
        low = total.astype(BF16)
        mix[rows, :] = low

        if m == 3:
            turn_o.ready()
        part_a[rows, :] = dot(low, w_o[...]).astype(BF16)

    def norm_two(i):
        few = row(i * 16, 16)
        values = own_x[few, :].astype(F32) + first.total(few)
        hidden[few, :] = values
        inverse = lax.rsqrt(mean_square(values) + epsilon)
        rows_two[row(mine_start + i * 16, 16), :] = (values * inverse * gains_all[1:2, :]).astype(BF16)

    def early(m, b):
        lanes = lanes_of[b]
        dmixed[chunk(m), lanes] = dot_nt(rows_cot[chunk(m), :], w_d[lanes, :])

    def feed(m, b):
        rows = chunk(m)
        lanes, pair, size = lanes_of[b], pairs_of[b], size_of[b]
        both = dot(rows_two[rows, :], w_gu[:, pair])
        gate, up = both[:, :size], both[:, size:]
        sig = jax.nn.sigmoid(gate)
        act = gate * sig
        mixed[rows, lanes] = (act * up).astype(BF16)
        back = dmixed[rows, lanes]
        dgu[rows, gate_up(b, 0)] = (back * up * sig * (1.0 + gate * (1.0 - sig))).astype(BF16)
        dgu[rows, gate_up(b, 1)] = (back * act).astype(BF16)
        total = dot_nt(dgu[rows, pair], w_gu[:, pair])
        if b:
            total += part_a[rows, :].astype(F32)
        part_a[rows, :] = total.astype(BF16)

    def out_part(m, b):
        rows = chunk(m)
        lanes = lanes_of[b]
        total = dot(mixed[rows, lanes], w_d[lanes, :])
        if b:
            total += part_b[rows, :].astype(F32)
        part_b[rows, :] = total.astype(BF16)

    def halves(m, work, lot):
        d = g ^ m

        def step(k):
            work(d * ranks + (r ^ 1 ^ k))

            @pl.when(k == 0)
            def _():
                lot.start(m)

        each(2, step)

    def several(groups_, work, lot):
        first_, last_ = groups_
        each(first_ - last_ + 1, lambda i: halves(first_ - i, work, lot))
        lot.mark(range(last_, first_ + 1))

    def beside(source, target, bulk):
        def describe(m):
            d = g ^ m
            return (source(d * ranks + (r ^ 1)), target(d), at.beside())

        return net.lot(range(4), describe, bulk)

    moves_gu = [
        [
            beside(lambda shard, p=p: w_gu.at[shard_rows(shard), p], lambda d, p=p: in_gu.at[d, :, p], in_gu.at[:, :, p])
            for p in (gate_up(b, 0), gate_up(b, 1))
        ]
        for b in range(len(PARTS))
    ]
    moves_d = [
        beside(lambda shard, p=p: w_d.at[p, columns_of(shard)], lambda d, p=p: in_d.at[d, p, :], in_d.at[:, p, :])
        for p in lanes_of
    ]
    moves_qkv = beside(lambda shard: w_qkv.at[shard_rows(shard), :], lambda d: in_qkv.at[d], in_qkv)
    moves_o = beside(lambda shard: w_o.at[:, columns_of(shard)], lambda d: in_o.at[d], in_o)

    def grads_gu(groups_, b, i):
        def work(shard):
            w_gu[shard_rows(shard), gate_up(b, i)] = dot_tn(
                rows_two[:, columns_of(shard)], dgu[:, gate_up(b, i)]
            ).astype(BF16)

        several(groups_, work, moves_gu[b][i])

    def grads_d(groups_, b):
        def work(shard):
            columns = columns_of(shard)
            w_d[lanes_of[b], columns] = dot_tn(mixed[:, lanes_of[b]], rows_cot[:, columns]).astype(BF16)

        several(groups_, work, moves_d[b])

    def grads_o(groups_):
        def work(shard):
            columns = columns_of(shard)
            w_o[:, columns] = dot_tn(mix[...], rows_dh[:, columns]).astype(BF16)

        several(groups_, work, moves_o)

    def grads_qkv(groups_):
        def work(shard):
            w_qkv[shard_rows(shard), :] = dot_tn(rows_one[:, columns_of(shard)], dqkv[...]).astype(BF16)

        several(groups_, work, moves_qkv)

    final, final_own = [], []

    def owners(moves, several):
        pieces = [(a, b, at.along(m)) for m in (1, 2, 3) for a, b in moves(m)]
        lot = net.lot((0,), lambda _: pieces, several, lambda _: several)
        final.append(lot)

        def give(m, i=None):
            blocks = moves(m)
            for k in range(len(blocks)) if i is None else (i,):
                if m:
                    lot.start(0, ((m - 1) * len(blocks) + k,))
                else:
                    final_own.append(keep.put(*blocks[k]))

        return give

    def shard_of(m):
        return (g ^ m) * ranks + r

    def gate_up_moves(b):
        def moves(m):
            for i, out in enumerate((g_out, u_out)):
                place = out.at[:, lane(g * units + lanes_of[b].start, size_of[b])]
                yield (w_gu.at[shard_rows(shard_of(m)), gate_up(b, i)], place)

        return lambda m: list(moves(m))

    def down_moves(b):
        place = d_out.at[lane(g * units + lanes_of[b].start, size_of[b]), :]
        return lambda m: [(w_d.at[lanes_of[b], columns_of(shard_of(m))], place)]

    def qkv_moves(m):
        rows = shard_rows(shard_of(m))
        return [
            (w_qkv.at[rows, i * HD : (i + 1) * HD], out.at[:, lane(g * HD, HD)])
            for i, out in enumerate((q_out, k_out, v_out))
        ]

    give_gu = [owners(gate_up_moves(b), w_gu.at[0 : 3 * width, p]) for b, p in enumerate(pairs_of)]
    give_d = [owners(down_moves(b), w_d.at[p, 0 : 3 * width]) for b, p in enumerate(lanes_of)]
    give_qkv = owners(qkv_moves, w_qkv.at[0 : 3 * width, :])
    give_o = owners(
        lambda m: [(w_o.at[:, columns_of(shard_of(m))], o_out.at[row(g * HD, HD), :])], w_o.at[:, 0 : 3 * width]
    )

    def sums(m, lot, mine_of, other_of, size):
        lot.arrived(m)

        def step(i):
            a, rows, lanes = mine_of(i)
            b, d, few, others = other_of(i)
            a[rows, lanes] = (a[rows, lanes].astype(F32) + b[d, few, others].astype(F32)).astype(BF16)

        each(size // 32, step)

    def sums_gu(m, b, i):
        d, p = g ^ m, gate_up(b, i)
        start = (d * ranks + r) * width
        sums(
            m, moves_gu[b][i],
            lambda k: (w_gu, row(start + k * 32, 32), p), lambda k: (in_gu, d, row(k * 32, 32), p), width,
        )
        give_gu[b](m, i)

    def sums_d(m, b):
        d, base = g ^ m, lanes_of[b].start
        columns = columns_of(d * ranks + r)
        sums(
            m, moves_d[b],
            lambda i: (w_d, row(base + i * 32, 32), columns),
            lambda i: (in_d, d, row(base + i * 32, 32), slice(None)), size_of[b],
        )
        give_d[b](m)

    def sums_o(m):
        d = g ^ m
        columns = columns_of(d * ranks + r)
        sums(
            m, moves_o,
            lambda i: (w_o, row(i * 32, 32), columns), lambda i: (in_o, d, row(i * 32, 32), slice(None)), HD,
        )
        give_o(m)

    def sums_qkv(m):
        d = g ^ m
        start = (d * ranks + r) * width
        sums(
            m, moves_qkv,
            lambda i: (w_qkv, row(start + i * 32, 32), slice(None)),
            lambda i: (in_qkv, d, row(i * 32, 32), slice(None)), width,
        )
        give_qkv(m)

    def back_two(i, gain_grad):
        few = row(i * 16, 16)
        own = row(mine_start + i * 16, 16)
        upstream, values = second.total(few), hidden[few, :]
        inverse = lax.rsqrt(mean_square(values) + epsilon)
        scaled = upstream * gains_all[1:2, :]
        back = inverse * scaled - values * (inverse * inverse * inverse) * jnp.mean(
            scaled * values, axis=1, keepdims=True
        )
        total = rows_cot[own, :].astype(F32) + back
        dhidden[few, :] = total
        rows_dh[own, :] = total.astype(BF16)
        return gain_grad + jnp.sum(upstream * values * inverse, axis=0, keepdims=True)

    def attend_back(m):
        three.ready(m)
        rows = chunk(m)
        query = queries[rows, :]
        dm = dot_nt(rows_dh[rows, :], w_o[...]).astype(BF16)

        def step(j, total):
            block = row(j * span, span)
            weight = weights_of(m, j, query)
            dweight = dot_nt(dm, pairs[block, HD:])
            dscore = (dweight * weight * (1.0 - weight)).astype(BF16)
            accum[block, HD:] += dot_tn(weight.astype(BF16), dm)
            accum[block, :HD] += dot_tn(dscore, query)
            return total + dot(dscore, pairs[block, :HD])

        total = lax.fori_loop(0, (g ^ m) + 1, step, jnp.zeros((count, HD), F32))
        dqkv[rows, :HD] = turned(total * score_scale, cosines[rows, :], -sines[rows, :]).astype(BF16)

    pair_back = net.lot(range(4), lambda m: (pair_send.at[g ^ m], pair_in.at[g ^ m], at.beside()), pair_send)

    def send_pair(m):
        d = g ^ m
        rows = row((d * ranks + (r ^ 1)) * count, count)
        pair_send[d] = accum[rows, :].astype(BF16)
        pair_back.start(m)

    def back_from_end(i):
        m = g ^ (groups - 1 - i)
        attend_back(m)
        send_pair(m)

    def back_one(m):
        d = g ^ m
        rows = chunk(m)
        pair_back.arrived(m)
        both = accum[own_place(m), :] + pair_in[d].astype(F32)
        dqkv[rows, HD : 2 * HD] = turned(both[:, :HD] * score_scale, cosines[rows, :], -sines[rows, :]).astype(BF16)
        dqkv[rows, 2 * HD :] = both[:, HD:].astype(BF16)
        part_a[rows, :] = dot_nt(dqkv[rows, :], w_qkv[...]).astype(BF16)

    ends = {}

    def share(i, source, target):
        place = target.at[strip, :]
        final_own.append(keep.put(source, place))
        lot = net.lot((0, 1), lambda j: (source, place, (at.near(), at.across())[j]), target.at[0 : 2 * quarter, :])
        lot.start(0)
        lot.start(1)
        ends[i] = (lot, target)

    def relay(i):
        lot, target = ends[i]
        lot.arrived(1)
        final.append(lot)
        block = target.at[row((at.q ^ 1) * quarter, quarter), :]
        on = net.lot((0,), lambda j: (block, block, at.near()), block)
        on.start(0)
        final.append(on)

    def result_rows(i):
        few = row(i * 16, 16)
        result_own[few, :] = (hidden[few, :] + out_sum.total(few)).astype(BF16)

    def back_rows(i, gain_grad):
        few = row(i * 16, 16)
        upstream, values = third.total(few), own_x[few, :].astype(F32)
        inverse = lax.rsqrt(mean_square(values) + epsilon)
        scaled = upstream * gains_all[0:1, :]
        back = inverse * scaled - values * (inverse * inverse * inverse) * jnp.mean(
            scaled * values, axis=1, keepdims=True
        )
        rows_own[few, :] = (dhidden[few, :] + back).astype(BF16)
        return gain_grad + jnp.sum(upstream * values * inverse, axis=0, keepdims=True)

    gain_sums = net.lot(
        (0,),
        lambda _: [(gain_part.at[:, columns_of(s ^ m)], gain_in.at[m - 1], (s ^ m, h)) for m in range(1, shards)],
        gain_in,
        lambda _: gain_in,
    )
    gain_ends = net.lot(
        (0,),
        lambda _: [(gain_mid, gain_near.at[m - 1], (s, h ^ m)) for m in range(1, 4)],
        gain_near,
        lambda _: gain_near,
    )
    gains[...] = jnp.zeros_like(gains)
    gains[0:1, :] = gain_one[...].astype(F32).reshape(1, width)
    gains[1:2, :] = gain_two[...].astype(F32).reshape(1, width)
    gain_moves.start(0)
    gain_own = keep.put(gains, gain_slot)
    own_rows = keep.put(tok, rows_dh.at[chunk(0), :])
    own_strip = keep.put(tok.at[strip, :], own_x)
    own_cot = keep.put(cot, rows_cot.at[chunk(0), :])
    turn_qkv.start(3)
    one.start(2)
    one.start(1)
    turn_qkv.start(1)
    turn_o.start(1)
    one.arrive(1)
    turn_qkv.mine()
    turn_qkv.start(2)
    gain_part[...] = jnp.zeros_like(gain_part)
    each(total_rows // 64, clear)
    each(groups * count // 64, tables)
    grad.z.start(2 * PIECES + 0)
    one.arrive(2)
    turn_o.pass_on(1)
    turn_gu.start(1, 0, (1,))
    turn_gu.start(3, 0, (2,))
    turn_o.start(3)
    gain_own.wait()
    gain_moves.arrived(0)
    own_rows.wait()
    own_strip.wait()
    norm_one(0)
    turn_qkv.pass_on(3)
    one.second(2)
    turn_o.start(2)
    turn_qkv.pass_on(1)
    grad.z.start(2 * PIECES + 1)
    turn_gu.start(2, 0, (3,))
    turn_d.start(1, 0)
    one.ready(2)
    norm_one(2)
    grad.z.start(1 * PIECES + 1)
    turn_qkv.pass_on(2)
    turn_gu.start(1, 0, (2,))
    one.arrive(3)
    turn_o.mine()
    one.second(1)
    turn_qkv.ready()
    project(0)
    turn_d.start(2, 1)
    one.ready(1)
    norm_one(1)
    project(1)
    project(2)
    one.second(3)
    one.ready(3)
    norm_one(3)
    project(3)
    turn_d.start(3, 0)
    turn_gu.start(1, 0, (0,))
    turn_o.pass_on(2)
    turn_d.start(2, 0)
    turn_o.pass_on(3)
    grad.arrive(2)
    for m in (0, 1, 2, 3):
        pair_moves.arrived(m)
    attend(3)
    first.first(3)
    attend(2)
    first.first(2)
    grad.z.start(1 * PIECES + 0)
    first.second(3)
    turn_d.start(3, 1)
    turn_d.mine(1)
    first.second(2)
    attend(1)
    first.first(1)
    turn_gu.mine(1)
    turn_gu.start(3, 0, (0,))
    first.third(3)
    grad.arrive(3)
    turn_d.pass_on(2, 1)
    turn_d.pass_on(1, 0)
    first.second(1)
    first.third(2)
    grad.second(2)
    attend(0)
    first.first(0)
    turn_d.pass_on(2, 0)
    turn_gu.start(3, 0, (3,))
    first.third(1)
    turn_gu.start(2, 0, (1,))
    turn_d.pass_on(3, 1)
    turn_gu.start(3, 0, (1,))
    turn_gu.start(2, 0, (2,))
    turn_d.mine(0)
    turn_d.start(1, 1)
    turn_gu.start(2, 0, (0,))
    turn_gu.start(1, 0, (3,))
    turn_gu.start(1, 1, (1, 0))
    first.second(0)
    grad.arrive(1)
    turn_d.pass_on(3, 0)
    first.last()
    each(quarter // 16, norm_two)
    two.start(1)
    turn_gu.mine(0)
    two.start(2)
    two.start_own()
    turn_d.pass_on(1, 1)
    turn_gu.start(2, 1, (3,))
    turn_gu.pass_on(1, 0)
    turn_gu.start(1, 1, (2,))
    grad.second(3)
    turn_gu.start(1, 1, (3,))
    two.second(0)
    turn_d.ready(0)
    turn_d.ready(1)
    turn_gu.pass_on(2, 0)
    grad.second(1)
    turn_gu.start(2, 1, (1, 0))
    turn_gu.pass_on(3, 0)
    turn_gu.start(2, 1, (2,))
    own_cot.wait()
    for m in (1, 2, 3):
        grad.ready(m)
    each(4, lambda m: early(m, 0))
    two.arrive(1)
    two.arrive(2)
    turn_gu.pass_on(1, 1)
    two.second(1)
    two.ready(1)
    turn_gu.start(3, 1, (1,))
    two.ready(0)
    two.second(2)
    turn_gu.start(3, 1, (2, 0, 3))
    two.ready(2)
    turn_gu.pass_on(2, 1)
    each(4, lambda m: early(m, 1))
    two.arrive(3)
    turn_gu.ready(0)
    first.sent()
    one.sent()
    each(2, lambda i: feed(1 - i, 0))
    turn_gu.pass_on(3, 1)
    two.second(3)
    feed(2, 0)
    two.ready(3)
    feed(3, 0)
    turn_gu.sent(0)
    grads_gu((3, 3), 0, 0)
    grads_gu((3, 3), 0, 1)
    turn_gu.ready(1)
    each(2, lambda i: (feed(3 - i, 1), second.first(3 - i)))
    second.a.mark((3, 2))
    sums_gu(3, 0, 0)
    grads_gu((2, 2), 0, 0)
    second.second(3)
    each(4, lambda m: out_part(m, 0))
    sums_gu(3, 0, 1)
    second.second(2)
    turn_d.sent(0)
    grads_d((1, 1), 0)
    feed(1, 1)
    second.first(1)
    second.third(3)
    feed(0, 1)
    second.first(0)
    second.second(1)
    turn_gu.sent(1)
    grads_gu((3, 3), 1, 1)
    sums_d(1, 0)
    each(4, lambda m: out_part(m, 1))
    for m in (3, 2, 1, 0):
        out_sum.first(m)
    grads_gu((2, 2), 0, 1)
    second.third(2)
    grads_gu((3, 3), 1, 0)
    second.second(0)
    second.third(1)
    out_sum.second(1)
    sums_gu(2, 0, 0)
    sums_gu(2, 0, 1)
    turn_d.sent(1)
    grads_d((3, 3), 1)
    grads_gu((0, 0), 1, 1)
    second.last()
    gain_part[1:2, :] = lax.fori_loop(0, quarter // 16, back_two, jnp.zeros((1, depth), F32))
    three.start(1)
    grads_gu((1, 1), 1, 1)
    three.start(2)
    grads_gu((1, 1), 0, 1)
    out_sum.second(3)
    grads_d((2, 2), 1)
    three.start_own()
    grads_gu((2, 2), 1, 1)
    grads_d((3, 3), 0)
    sums_gu(3, 1, 0)
    grads_gu((1, 1), 1, 0)
    grads_gu((2, 2), 1, 0)
    out_sum.third(3)
    three.arrive(1)
    three.arrive(2)
    sums_d(3, 1)
    grads_d((0, 0), 0)
    sums_d(3, 0)
    three.second(0)
    grads_gu((0, 0), 0, 1)
    grads_gu((0, 0), 1, 0)
    grads_d((0, 0), 1)
    sums_gu(1, 1, 1)
    sums_gu(3, 1, 1)
    sums_d(2, 1)
    sums_gu(2, 1, 0)
    sums_gu(1, 0, 1)
    sums_gu(2, 1, 1)
    three.arrive(3)
    three.second(2)
    sums_gu(1, 1, 0)
    grads_gu((0, 0), 0, 0)
    three.second(1)
    out_sum.second(2)
    grads_d((2, 2), 0)
    three.second(3)
    each(4, back_from_end)
    pair_back.mark(range(4))
    out_sum.second(0)
    out_sum.third(2)
    sums_gu(0, 1, 1)
    grads_gu((1, 1), 0, 0)
    out_sum.third(1)
    turn_o.sent()
    grads_o((1, 0))
    grads_o((3, 3))
    second.sent()
    third.produce(back_one)
    sums_gu(0, 0, 0)
    turn_qkv.sent()
    grads_qkv((2, 2))
    grads_qkv((3, 3))
    grads_d((1, 1), 1)
    grads_o((2, 2))
    third.third(3)
    sums_o(3)
    third.second(0)
    grads_qkv((1, 1))
    sums_d(2, 0)
    sums_gu(1, 0, 0)
    sums_o(1)
    third.third(2)
    third.third(1)
    sums_qkv(3)
    out_sum.last()
    each(quarter // 16, result_rows)
    share(0, result_own, result_out)
    sums_d(1, 1)
    sums_o(0)
    sums_qkv(2)
    grads_qkv((0, 0))
    third.last()
    gain_part[0:1, :] = lax.fori_loop(0, quarter // 16, back_rows, jnp.zeros((1, depth), F32))
    gain_sums.start(0)
    share(1, rows_own, rows_out)
    sums_o(2)
    sums_qkv(0)
    relay(0)
    sums_gu(0, 1, 0)
    sums_qkv(1)
    sums_gu(0, 0, 1)
    sums_d(0, 1)
    sums_d(0, 0)
    relay(1)
    total = gain_part[:, columns_of(s)]
    gain_sums.arrived(0)
    for m in range(1, shards):
        total += gain_in[m - 1]
    gain_mid[...] = total
    gain_ends.start(0)
    gain_ends.arrived(0)
    for m in range(1, 4):
        total += gain_near[m - 1]
    gains_out[...] = total
    for lot in final:
        lot.arrived(0)
    net.finish()
    for copy in final_own:
        copy.wait()


def rows_plan(
    groups,
    ranks,
    tokens,
    attn_gain,
    query_weight,
    key_weight,
    value_weight,
    out_weight,
    mlp_gain,
    gate_weight,
    up_weight,
    down_weight,
    cotangent,
):
    count, depth = tokens.shape
    shards = groups * ranks
    quarter = count // 4
    width = query_weight.shape[0]
    units = gate_weight.shape[1] // groups
    total_rows = count * shards
    here = groups * count
    ins = (
        tokens, cotangent, attn_gain, mlp_gain,
        query_weight, key_weight, value_weight, out_weight, gate_weight, up_weight, down_weight,
    )
    shape = jax.ShapeDtypeStruct
    hbm, vmem = pl.BlockSpec(memory_space=pl.ANY), pl.BlockSpec(memory_space=pltpu.VMEM)
    owners = (query_weight, key_weight, value_weight, out_weight, gate_weight, up_weight, down_weight)
    outs = [
        shape((count, depth), BF16),
        shape((count, depth), BF16),
        shape((8, width), F32),
        *(shape(w.shape, BF16) for w in owners),
    ]

    def low(*extent):
        return pltpu.VMEM(extent, BF16)

    def full(*extent):
        return pltpu.VMEM(extent, F32)

    def collector():
        return [
            low(here, depth),
            low(groups, 2 * quarter, depth),
            low(groups, quarter, depth),
            low(3, quarter, depth),
        ]

    scratch = [
        full(8, width), full(8, depth), full(here, HD), full(here, HD),
        low(here, depth), low(here, depth), low(here, depth), low(here, depth),
        low(depth, 3 * HD), low(HD, depth), low(depth, 2 * units), low(units, depth),
        low(here, HD), low(total_rows, 2 * HD), low(here, HD), low(here, 3 * HD),
        full(total_rows, 2 * HD), low(groups, count, 2 * HD), low(groups, count, 2 * HD),
        low(here, units), low(here, 2 * units), full(here, units),
        low(quarter, depth), full(quarter, depth), full(quarter, depth), full(quarter, depth),
        *collector(), *collector(),
        low(groups, width, 2 * units), low(groups, units, width), low(groups, width, 3 * HD), low(groups, HD, width),
        full(8, depth), full(shards - 1, 8, width), full(8, width), full(3, 8, width),
        low(quarter, depth), low(quarter, depth),
        pltpu.SemaphoreType.DMA((SENDS,)), pltpu.SemaphoreType.DMA((RECEIVES,)), pltpu.SemaphoreType.DMA((KEEPS,)),
    ]
    moved = pl.pallas_call(
        functools.partial(layer_body, groups, ranks),
        out_shape=outs,
        in_specs=[hbm] * 2 + [vmem] * 2 + [hbm] * 7,
        out_specs=[hbm, hbm, vmem] + [hbm] * 7,
        scratch_shapes=scratch,
        compiler_params=pltpu.CompilerParams(
            collective_id=1, has_side_effects=True, vmem_limit_bytes=VMEM_LIMIT
        ),
    )(*ins)
    steps = 8

    def sliced(array):
        rows, columns = array.shape
        return pl.BlockSpec((rows // steps, columns), lambda i: (i, 0))

    gain_specs = [pl.BlockSpec((8, width), lambda i: (0, 0))]
    row_spec = pl.BlockSpec((width,), lambda i: (0,))
    specs = [sliced(moved[0]), sliced(moved[1]), *(sliced(w) for w in moved[3:])]
    gain_row = shape((width,), F32)
    one, two, result, rows_grad, *grads = pl.pallas_call(
        cast_body,
        grid=(steps,),
        out_shape=[gain_row, gain_row, moved[0], moved[1], *(shape(w.shape, F32) for w in owners)],
        in_specs=gain_specs + specs,
        out_specs=[row_spec, row_spec] + specs,
        compiler_params=pltpu.CompilerParams(vmem_limit_bytes=VMEM_LIMIT),
    )(moved[2], moved[0], moved[1], *moved[3:])
    return (result, rows_grad, one, *grads[:4], two, *grads[4:])


def cast_body(*refs):
    inputs = len(refs) // 2
    gains, sources, (one, two, *targets) = refs[0], refs[1:inputs], refs[inputs:]
    one[...] = gains[0, :]
    two[...] = gains[1, :]
    for source, target in zip(sources, targets):
        target[...] = source[...].astype(target.dtype)


def on_device(tokens, attn_gain, query_weight, *rest):
    groups = query_weight.shape[1] // HD
    ranks = lax.axis_size("seq") // groups
    fits = lax.axis_size("head") == 4 and groups == 4 and ranks == 2 and query_weight.shape[0] % 128 == 0
    plan = functools.partial(rows_plan, groups, ranks) if fits else gathered_weights
    return plan(tokens, attn_gain, query_weight, *rest)


def solution(mesh):
    in_specs = (
        P("seq", None),
        P("seq"),
        P("seq", "head"),
        P("seq", "head"),
        P("seq", "head"),
        P("head", "seq"),
        P("seq"),
        P("seq", "head"),
        P("seq", "head"),
        P("head", "seq"),
        P("seq", None),
    )
    out_specs = (
        P("seq", None),
        P("seq", None),
        P("seq"),
        P("seq", "head"),
        P("seq", "head"),
        P("seq", "head"),
        P("head", "seq"),
        P("seq"),
        P("seq", "head"),
        P("seq", "head"),
        P("head", "seq"),
    )
    return jax.shard_map(
        on_device, mesh=mesh, in_specs=in_specs, out_specs=out_specs, check_vma=False
    )
```

```python
import functools
import math

import jax
import jax.numpy as jnp
from jax import lax
from jax.experimental import pallas as pl
from jax.experimental.pallas import tpu as pltpu
from jax.sharding import PartitionSpec as P

MESH = pl.DeviceIdType.MESH
F32, BF16 = jnp.float32, jnp.bfloat16

HD = 128


epsilon = 1e-05
block_limit = 512
VMEM_LIMIT = 63 * 2**20
SENDS, RECEIVES, KEEPS = 59, 217, 30
PIECES = 2
PARTS = (2, 2)


def tables(offset, length, half_width):
    places = (offset + jnp.arange(length, dtype=jnp.int32)).astype(jnp.float32)
    frequency = jnp.exp(
        jnp.arange(half_width, dtype=jnp.float32) * (-math.log(10000.0) / half_width)
    )
    angles = places[:, None] * frequency[None, :]
    return (jnp.cos(angles)[:, None, :], jnp.sin(angles)[:, None, :])


def rotary(values, cos_table, sin_table):
    half_width = values.shape[-1] // 2
    front = values[..., :half_width]
    back_half = values[..., half_width:]
    return jnp.concatenate(
        [front * cos_table - back_half * sin_table, back_half * cos_table + front * sin_table],
        axis=-1,
    )


def unrotary(gradient, cos_table, sin_table):
    half_width = gradient.shape[-1] // 2
    front = gradient[..., :half_width]
    back_half = gradient[..., half_width:]
    return jnp.concatenate(
        [front * cos_table + back_half * sin_table, back_half * cos_table - front * sin_table],
        axis=-1,
    )


def norm_back(values, inverse, gain_vector, upstream):
    scaled = upstream * gain_vector
    gain_grad = jnp.sum(upstream * values * inverse, axis=0)
    value_grad = inverse * scaled - values * inverse**3 * jnp.mean(
        scaled * values, axis=1, keepdims=True
    )
    return (value_grad, gain_grad)


def gathered_weights(
    tokens,
    attn_gain,
    query_weight,
    key_weight,
    value_weight,
    out_weight,
    mlp_gain,
    gate_weight,
    up_weight,
    down_weight,
    cotangent,
):
    row_count = tokens.shape[0]
    total_rows = row_count * lax.axis_size("seq")
    row_start = lax.axis_index("seq") * row_count
    local_width = query_weight.shape[1]
    local_heads = local_width // HD
    score_scale = 1.0 / math.sqrt(HD)
    score_shift = math.log(total_rows)
    block_rows = math.gcd(total_rows, block_limit)
    block_count = total_rows // block_rows
    attn_gain_full, query_full, key_full, value_full, out_full = (
        lax.all_gather(attn_gain, "seq", axis=0, tiled=True),
        lax.all_gather(query_weight, "seq", axis=0, tiled=True),
        lax.all_gather(key_weight, "seq", axis=0, tiled=True),
        lax.all_gather(value_weight, "seq", axis=0, tiled=True),
        lax.all_gather(out_weight, "seq", axis=1, tiled=True),
    )
    mlp_gain_full, gate_full, up_full, down_full = (
        lax.all_gather(mlp_gain, "seq", axis=0, tiled=True),
        lax.all_gather(gate_weight, "seq", axis=0, tiled=True),
        lax.all_gather(up_weight, "seq", axis=0, tiled=True),
        lax.all_gather(down_weight, "seq", axis=1, tiled=True),
    )
    token_values = tokens.astype(jnp.float32)
    inverse_one = lax.rsqrt(jnp.mean(token_values * token_values, axis=1, keepdims=True) + epsilon)
    normed_one = (token_values * inverse_one * attn_gain_full.astype(jnp.float32)).astype(
        jnp.bfloat16
    )
    query_pre = jnp.dot(normed_one, query_full, preferred_element_type=jnp.float32)
    key_pre = jnp.dot(normed_one, key_full, preferred_element_type=jnp.float32)
    value_rows = (
        jnp.dot(normed_one, value_full, preferred_element_type=jnp.float32)
        .astype(jnp.bfloat16)
        .reshape(row_count, local_heads, HD)
    )
    cos_table, sin_table = tables(row_start, row_count, HD // 2)
    query_rows = (
        rotary(query_pre.reshape(row_count, local_heads, HD), cos_table, sin_table)
        .astype(jnp.bfloat16)
        .reshape(row_count, local_width)
    )
    key_rows = rotary(key_pre.reshape(row_count, local_heads, HD), cos_table, sin_table).astype(
        jnp.bfloat16
    )
    all_queries = lax.all_gather(query_rows, "seq", axis=0, tiled=True)
    key_places = row_start + jnp.arange(row_count, dtype=jnp.int32)

    def weights_for(query_block, block_start):
        scores = (
            jnp.einsum("qhd,khd->hqk", query_block, key_rows, preferred_element_type=jnp.float32)
            * score_scale
            - score_shift
        )
        query_places = block_start + jnp.arange(query_block.shape[0], dtype=jnp.int32)
        visible = key_places[None, :] <= query_places[:, None]
        return jnp.where(visible[None], jax.nn.sigmoid(scores), 0.0)

    step_rows = math.gcd(row_count * lax.axis_size("seq"), block_limit)
    step_count = row_count * lax.axis_size("seq") // step_rows
    picked = all_queries.reshape(step_count, step_rows, local_heads, HD)
    starts = jnp.arange(step_count, dtype=jnp.int32) * step_rows

    def one_block(packed):
        query_block, block_start = packed
        weights = weights_for(query_block, block_start).astype(jnp.bfloat16)
        return jnp.einsum(
            "hqk,khd->qhd", weights, value_rows, preferred_element_type=jnp.float32
        ).reshape(step_rows, local_width)

    attn_mix = lax.psum_scatter(
        lax.map(one_block, (picked, starts)).reshape(row_count * lax.axis_size("seq"), local_width),
        "seq",
        scatter_dimension=0,
        tiled=True,
    ).astype(jnp.bfloat16)
    attn_branch = lax.psum(jnp.dot(attn_mix, out_full, preferred_element_type=jnp.float32), "head")
    hidden = token_values + attn_branch
    inverse_two = lax.rsqrt(jnp.mean(hidden * hidden, axis=1, keepdims=True) + epsilon)
    normed_two = (hidden * inverse_two * mlp_gain_full.astype(jnp.float32)).astype(jnp.bfloat16)
    gate_pre = jnp.dot(normed_two, gate_full, preferred_element_type=jnp.float32)
    up_pre = jnp.dot(normed_two, up_full, preferred_element_type=jnp.float32)
    gate_act = jax.nn.silu(gate_pre)
    mixed = (gate_act * up_pre).astype(jnp.bfloat16)
    mlp_branch = lax.psum(
        jnp.dot(mixed, down_full, preferred_element_type=jnp.float32).astype(jnp.bfloat16), "head"
    ).astype(jnp.float32)
    result = (hidden + mlp_branch).astype(jnp.bfloat16)
    kept_weights = (
        lax.all_gather(attn_gain, "seq", axis=0, tiled=True),
        lax.all_gather(query_weight, "seq", axis=0, tiled=True),
        lax.all_gather(key_weight, "seq", axis=0, tiled=True),
        lax.all_gather(value_weight, "seq", axis=0, tiled=True),
        lax.all_gather(out_weight, "seq", axis=1, tiled=True),
        lax.all_gather(mlp_gain, "seq", axis=0, tiled=True),
        lax.all_gather(gate_weight, "seq", axis=0, tiled=True),
        lax.all_gather(up_weight, "seq", axis=0, tiled=True),
        lax.all_gather(down_weight, "seq", axis=1, tiled=True),
    )
    (
        attn_gain_back,
        query_back,
        key_back,
        value_back,
        out_back,
        mlp_gain_back,
        gate_back,
        up_back,
        down_back,
    ) = kept_weights
    attn_gain_f = attn_gain_back.astype(jnp.float32)
    mlp_gain_f = mlp_gain_back.astype(jnp.float32)
    grad_values = cotangent.astype(jnp.float32)
    grad_down = jnp.einsum("tf,td->fd", mixed, cotangent, preferred_element_type=jnp.float32)
    dmixed = jnp.einsum("td,fd->tf", cotangent, down_back, preferred_element_type=jnp.float32)
    gate_sig = jax.nn.sigmoid(gate_pre)
    dgate = (dmixed * up_pre * gate_sig * (1.0 + gate_pre * (1.0 - gate_sig))).astype(jnp.bfloat16)
    dup = (dmixed * gate_act).astype(jnp.bfloat16)
    grad_gate = jnp.einsum("tk,tf->kf", normed_two, dgate, preferred_element_type=jnp.float32)
    grad_up = jnp.einsum("tk,tf->kf", normed_two, dup, preferred_element_type=jnp.float32)
    dnormed_two = lax.psum(
        jnp.einsum("tf,kf->tk", dgate, gate_back, preferred_element_type=jnp.float32)
        + jnp.einsum("tf,kf->tk", dup, up_back, preferred_element_type=jnp.float32),
        "head",
    )
    dhidden_norm, grad_mlp_gain = norm_back(hidden, inverse_two, mlp_gain_f, dnormed_two)
    dhidden = grad_values + dhidden_norm
    mlp_sums = (grad_mlp_gain, grad_gate, grad_up, grad_down)
    dhidden_low = dhidden.astype(jnp.bfloat16)
    grad_out = jnp.einsum("tc,td->cd", attn_mix, dhidden_low, preferred_element_type=jnp.float32)
    dmix = jnp.einsum(
        "td,cd->tc", dhidden_low, out_back, preferred_element_type=jnp.float32
    ).astype(jnp.bfloat16)
    all_dmix = lax.all_gather(dmix, "seq", axis=0, tiled=True)

    def backward_block(carry, packed):
        key_accum, value_accum = carry
        query_block, grad_block, block_start = packed
        weights = weights_for(query_block, block_start)
        grad_weights = jnp.einsum(
            "qhd,khd->hqk", grad_block, value_rows, preferred_element_type=jnp.float32
        )
        grad_scores = (grad_weights * weights * (1.0 - weights)).astype(jnp.bfloat16)
        value_accum = value_accum + jnp.einsum(
            "hqk,qhd->khd",
            weights.astype(jnp.bfloat16),
            grad_block,
            preferred_element_type=jnp.float32,
        )
        key_accum = key_accum + jnp.einsum(
            "hqk,qhd->khd", grad_scores, query_block, preferred_element_type=jnp.float32
        )
        query_part = (
            jnp.einsum("hqk,khd->qhd", grad_scores, key_rows, preferred_element_type=jnp.float32)
            * score_scale
        )
        return ((key_accum, value_accum), query_part.reshape(block_rows, local_width))

    zero_rows = jnp.zeros((row_count, local_heads, HD), jnp.float32)
    block_starts = jnp.arange(block_count, dtype=jnp.int32) * block_rows
    (key_accum, value_accum), query_parts = lax.scan(
        backward_block,
        (zero_rows, zero_rows),
        (
            all_queries.reshape(block_count, block_rows, local_heads, HD),
            all_dmix.reshape(block_count, block_rows, local_heads, HD),
            block_starts,
        ),
    )
    query_sum = lax.psum_scatter(
        query_parts.reshape(total_rows, local_width), "seq", scatter_dimension=0, tiled=True
    )
    dquery_pre = (
        unrotary(query_sum.reshape(row_count, local_heads, HD), cos_table, sin_table)
        .reshape(row_count, local_width)
        .astype(jnp.bfloat16)
    )
    dkey_pre = (
        unrotary(key_accum * score_scale, cos_table, sin_table)
        .reshape(row_count, local_width)
        .astype(jnp.bfloat16)
    )
    dvalue = value_accum.reshape(row_count, local_width).astype(jnp.bfloat16)
    grad_query = jnp.einsum("tk,tc->kc", normed_one, dquery_pre, preferred_element_type=jnp.float32)
    grad_key = jnp.einsum("tk,tc->kc", normed_one, dkey_pre, preferred_element_type=jnp.float32)
    grad_value = jnp.einsum("tk,tc->kc", normed_one, dvalue, preferred_element_type=jnp.float32)
    dnormed_one = lax.psum(
        jnp.einsum("tc,kc->tk", dquery_pre, query_back, preferred_element_type=jnp.float32)
        + jnp.einsum("tc,kc->tk", dkey_pre, key_back, preferred_element_type=jnp.float32)
        + jnp.einsum("tc,kc->tk", dvalue, value_back, preferred_element_type=jnp.float32),
        "head",
    )
    dinput_norm, grad_attn_gain = norm_back(token_values, inverse_one, attn_gain_f, dnormed_one)
    input_grad = (dhidden + dinput_norm).astype(jnp.bfloat16)
    every_sum = (
        lax.psum_scatter(grad_attn_gain, "seq", scatter_dimension=0, tiled=True),
        lax.psum_scatter(grad_query, "seq", scatter_dimension=0, tiled=True),
        lax.psum_scatter(grad_key, "seq", scatter_dimension=0, tiled=True),
        lax.psum_scatter(grad_value, "seq", scatter_dimension=0, tiled=True),
        lax.psum_scatter(grad_out, "seq", scatter_dimension=1, tiled=True),
        lax.psum_scatter(grad_mlp_gain, "seq", scatter_dimension=0, tiled=True),
        lax.psum_scatter(grad_gate, "seq", scatter_dimension=0, tiled=True),
        lax.psum_scatter(grad_up, "seq", scatter_dimension=0, tiled=True),
        lax.psum_scatter(grad_down, "seq", scatter_dimension=1, tiled=True),
    )
    attn_sums = every_sum[:5]
    mlp_sums = every_sum[5:]
    return (
        result,
        input_grad,
        attn_sums[0],
        attn_sums[1],
        attn_sums[2],
        attn_sums[3],
        attn_sums[4],
        mlp_sums[0],
        mlp_sums[1],
        mlp_sums[2],
        mlp_sums[3],
    )


class Net:
    def __init__(self, send, receive):
        self.send, self.receive, self.sends, self.receives, self.lots = send, receive, 0, 0, []

    def lot(self, *args, **options):
        return Lot(self, *args, **options)

    def finish(self):
        for lot in self.lots:
            lot.sent()


class Lot:
    def __init__(self, net, indices, describe, bulk, arrival=None, apart=False):
        self.net, self.describe, self.bulk, self.arrival, self.apart = net, describe, bulk, arrival, apart
        self.place = {j: net.receives + i for i, j in enumerate(indices)}
        self.low = min(indices)
        self.send_base, self.receive_base = net.sends, net.receives
        net.receives += len(indices)
        net.sends += len(indices) if apart else 1
        self.started, self.open = set(), set()
        net.lots.append(self)

    def receive_at(self, j):
        return self.net.receive.at[self.receive_base + (j - self.low)]

    def send_at(self, j):
        return self.net.send.at[self.send_base + (j - self.low if self.apart else 0)]

    def start(self, j, pieces=None):
        described = self.describe(j)
        for i, (source, target, device) in enumerate(described if isinstance(described, list) else [described]):
            if pieces is None or i in pieces:
                pltpu.make_async_remote_copy(
                    src_ref=source,
                    dst_ref=target,
                    send_sem=self.send_at(j),
                    recv_sem=self.receive_at(j),
                    device_id=device,
                    device_id_type=MESH,
                ).start()
        if isinstance(j, int):
            self.mark((j,))

    def mark(self, indices):
        self.started.update(indices)
        self.open.update(indices if self.apart else (self.low,))

    def arrived(self, j):
        described = self.describe(j)
        target = self.arrival(j) if self.arrival else described[1]
        self.wait(target, self.receive_at(j))

    def wait(self, like, sem):
        pltpu.make_async_copy(like, like, sem).wait()

    def sent(self, j=None):
        for k in sorted(self.open) if j is None else [j] if j in self.open else []:
            self.open.remove(k)
            self.wait(self.bulk(k) if self.apart else self.bulk, self.send_at(k))


class Keep:
    def __init__(self, sems):
        self.sems, self.count = sems, 0

    def put(self, source, target):
        copy = pltpu.make_async_copy(source, target, self.sems.at[self.count])
        self.count += 1
        copy.start()
        return copy


class Where:
    def __init__(self, groups, ranks):
        self.s, self.h = lax.axis_index("seq"), lax.axis_index("head")
        self.g, self.r = self.s // ranks, self.s % ranks
        self.groups, self.ranks = groups, ranks
        self.q = self.h % 2 * 2 + self.h // 2

    def along(self, m):
        return (self.s ^ (m * self.ranks), self.h)

    def beside(self):
        return (self.s ^ 1, self.h)

    def across(self):
        return (self.s, self.h ^ 2)

    def near(self):
        return (self.s, self.h ^ 1)


def lane(start, size):
    return pl.ds(pl.multiple_of(start, 128), size)


def row(start, size):
    return pl.ds(pl.multiple_of(start, size), size)


def each(count, step):
    def body(i, carry):
        step(i)
        return carry

    lax.fori_loop(0, count, body, 0)


class Spread:
    def __init__(self, net, at, buffer, quarter, own=None):
        self.at, self.buffer, self.quarter, self.shared = at, buffer, quarter, own is not None
        self.size = quarter // PIECES

        def along(j):
            m, p = j // PIECES, j % PIECES
            if m == 3:
                return (self.block(2, 0, p), self.block(2, 0, p), at.along(1))
            first = self.block(0, 0, p) if own is None else own.at[row(at.q * quarter + p * self.size, self.size), :]
            return (first, self.block(0, 0, p), at.along(m))

        def moved(k, device):
            def describe(j):
                block = self.block(j // PIECES, k, j % PIECES)
                return (block, block, device)

            return describe

        low = 1 if self.shared else 0
        indices = range(low * PIECES, 4 * PIECES)
        some = buffer.at[0 : (4 - low) * quarter, :]
        self.z = net.lot(range(PIECES, 4 * PIECES), along, buffer.at[0 : 3 * quarter, :])
        self.x = net.lot(indices, moved(0, at.across()), some)

        def near(m):
            blocks = [self.block(m, k, p) for k in (0, 1) for p in range(PIECES)]
            return [(block, block, at.near()) for block in blocks]

        self.n = net.lot(
            range(low, 4), near, buffer.at[0 : 2 * (4 - low) * quarter, :], lambda m: buffer.at[0 : 2 * quarter, :]
        )

    def block(self, m, k, p):
        at = self.at
        start = ((at.g ^ m) * 4 + (at.q ^ k)) * self.quarter + p * self.size
        return self.buffer.at[row(start, self.size), :]

    def pass_on(self, j):
        self.x.start(j)
        self.n.start(j // PIECES, (j % PIECES,))

    def start(self, m):
        for p in range(PIECES):
            self.z.start(m * PIECES + p)

    def start_own(self):
        for p in range(PIECES):
            self.pass_on(p)

    def arrive(self, m):
        for p in range(PIECES):
            j = m * PIECES + p
            self.z.arrived(j)
            if m == 2:
                self.z.start(3 * PIECES + p)
            self.pass_on(j)

    def second(self, m):
        for p in range(PIECES):
            self.x.arrived(m * PIECES + p)
            self.n.start(m, (PIECES + p,))

    def ready(self, m):
        self.n.arrived(m)

    def sent(self):
        for lot in (self.z, self.x, self.n):
            lot.sent()


class Collect:
    def __init__(self, net, at, refs, quarter, out):
        self.at, self.quarter, self.out = at, quarter, out
        self.size = quarter // PIECES
        self.part, self.near, self.xin, self.zin = refs
        self.a = net.lot(range(4), lambda m: (self.pair(m), self.near.at[at.g ^ m], at.near()), self.near)

        def across(j):
            m, few = j // PIECES, row(j % PIECES * self.size, self.size)
            return (self.part.at[self.rows(m, 1, j % PIECES), :], self.xin.at[at.g ^ m, few, :], at.across())

        hops = {3: (0, 1), 2: (2, 2), 1: (1, 1)}

        def along(j):
            (slot, hop), few = hops[j // PIECES], row(j % PIECES * self.size, self.size)
            return (self.part.at[self.rows(j // PIECES, 0, j % PIECES), :], self.zin.at[slot, few, :], at.along(hop))

        self.b = net.lot(range(4 * PIECES), across, self.xin)
        self.z = net.lot(range(PIECES, 4 * PIECES), along, self.zin)

    def start_of(self, m, k, p):
        at = self.at
        return ((at.g ^ m) * 4 + (at.q ^ k)) * self.quarter + p * self.size

    def rows(self, m, k, p):
        return row(self.start_of(m, k, p), self.size)

    def pair(self, m):
        at = self.at
        return self.part.at[row(((at.g ^ m) * 2 + (1 - at.h % 2)) * 2 * self.quarter, 2 * self.quarter), :]

    def first(self, m):
        self.a.start(m)

    def lines(self, few, k):
        start = (self.at.h // 2 ^ k) * self.quarter
        return pl.ds(pl.multiple_of(start + few.start, 16), few.size)

    def slices(self, m, k, p, step):
        start = self.start_of(m, k, p)
        each(self.size // 16, lambda i: step(row(start + i * 16, 16), row(p * self.size + i * 16, 16)))

    def second(self, m):
        d = self.at.g ^ m
        self.a.arrived(m)

        def step(rows, few):
            total = self.part[rows, :].astype(F32) + self.near[d, self.lines(few, 1), :].astype(F32)
            self.part[rows, :] = total.astype(BF16)

        for p in range(PIECES):
            self.slices(m, 1, p, step)
            self.b.start(m * PIECES + p)

    def third(self, m):
        d = self.at.g ^ m

        def step(rows, few):
            total = self.part[rows, :].astype(F32) + self.near[d, self.lines(few, 0), :].astype(F32)
            total += self.xin[d, few, :].astype(F32)
            if m == 2:
                total += self.zin[0, few, :].astype(F32)
            if m:
                self.part[rows, :] = total.astype(BF16)
            else:
                self.out[few, :] = total

        for p in range(PIECES):
            self.b.arrived(m * PIECES + p)
            if m == 2:
                self.z.arrived(3 * PIECES + p)
            self.slices(m, 0, p, step)
            if m:
                self.z.start(m * PIECES + p)

    def last(self):
        self.third(0)
        for m in (1, 2):
            for p in range(PIECES):
                self.z.arrived(m * PIECES + p)

    def total(self, few):
        return self.out[few, :] + self.zin[1, few, :].astype(F32) + self.zin[2, few, :].astype(F32)

    def produce(self, work):
        def step(i):
            m = 3 - i
            work(m)
            self.first(m)

            @pl.when(i > 0)
            def _():
                self.second(m + 1)

        each(4, step)
        self.a.mark(range(4))
        self.b.mark(range(PIECES, 4 * PIECES))

    def sent(self):
        for lot in (self.a, self.b, self.z):
            lot.sent()


class Turn:
    def __init__(self, net, keep, at, source, view, blocks):
        self.keep, self.at, self.source, self.view, self.blocks = keep, at, source, view, blocks
        self.z, self.y, self.own = [], [], {}
        for b, (items, place, several) in enumerate(blocks):

            def out(m, items=items):
                return [(source(i, at.g ^ m), view(i, at.s), at.along(m)) for i in items]

            def beside(_, items=items, place=place):
                own = [(source(i, at.g), view(i, at.s), at.beside()) for i in items]
                others = [place(at.s ^ (m * at.ranks)) for m in (1, 2, 3)]
                return own + [(block, block, at.beside()) for block in others]

            def arrival(m, place=place):
                return place(at.s ^ (m * at.ranks))

            self.z.append(net.lot((1, 2, 3), out, several(3), arrival))
            self.y.append(net.lot((0,), beside, several(4), lambda _, several=several: several(4)))

    def start(self, m, b=0, pieces=None):
        self.z[b].start(m, pieces)

    def mine(self, b=0):
        items = self.blocks[b][0]
        for i in items:
            self.own[i] = self.keep.put(self.source(i, self.at.g), self.view(i, self.at.s))
        self.y[b].start(0, range(len(items)))

    def pass_on(self, m, b=0):
        self.z[b].arrived(m)
        self.y[b].start(0, (len(self.blocks[b][0]) + m - 1,))

    def ready(self, b=0):
        for i in self.blocks[b][0]:
            self.own[i].wait()
        self.y[b].arrived(0)

    def sent(self, b=0):
        self.y[b].sent()


def dot(a, b):
    return jnp.dot(a, b, preferred_element_type=F32)


def dot_nt(a, b):
    return lax.dot_general(a, b, (((1,), (1,)), ((), ())), preferred_element_type=F32)


def dot_tn(a, b):
    return lax.dot_general(a, b, (((0,), (0,)), ((), ())), preferred_element_type=F32)


def turned(values, cos_table, sin_table):
    return values * cos_table + pltpu.roll(values, HD // 2, 1) * sin_table


def mean_square(values):
    return jnp.mean(values * values, axis=1, keepdims=True)


def layer_body(groups, ranks, *refs):
    (tok, cot, gain_one, gain_two, qw, kw, vw, ow, gw, uw, dw) = refs[:11]
    (result_out, rows_out, gains_out, q_out, k_out, v_out, o_out, g_out, u_out, d_out) = refs[11:21]
    (
        gains, gains_all, cosines, sines, rows_one, rows_cot, rows_two, rows_dh, w_qkv, w_o, w_gu, w_d, queries, pairs, mix, dqkv, accum, pair_send,
        pair_in, mixed, dgu, dmixed, own_x, hidden, dhidden, summed, part_a, near_a, xin_a, zin_a, part_b, near_b, xin_b, zin_b,
        in_gu, in_d, in_qkv, in_o, gain_part, gain_in, gain_mid, gain_near, result_own, rows_own, send, receive, local,
    ) = refs[21:]
    at = Where(groups, ranks)
    s, h, g, r = at.s, at.h, at.g, at.r
    shards = groups * ranks
    count, depth = tok.shape
    quarter = count // 4
    width = gains.shape[1]
    units = gw.shape[1] // groups
    bounds = [units * sum(PARTS[:b]) // sum(PARTS) for b in range(len(PARTS) + 1)]
    lanes_of = [slice(a, b) for a, b in zip(bounds, bounds[1:])]
    pairs_of = [slice(2 * a, 2 * b) for a, b in zip(bounds, bounds[1:])]
    size_of = [b - a for a, b in zip(bounds, bounds[1:])]

    def gate_up(b, i):
        start = pairs_of[b].start + i * size_of[b]
        return slice(start, start + size_of[b])

    total_rows = count * shards
    score_scale = 1.0 / math.sqrt(HD)
    score_shift = math.log(total_rows)
    peers = [(s ^ m, h) for m in range(1, shards)] + [(s, h ^ m) for m in range(1, 4)]
    barrier = pltpu.get_barrier_semaphore()
    for peer in peers:
        pl.semaphore_signal(barrier, inc=1, device_id=peer, device_id_type=MESH)
    pl.semaphore_wait(barrier, len(peers))
    net, keep = Net(send, receive), Keep(local)

    def chunk(m):
        return row((g ^ m) * count, count)

    def shard_rows(shard):
        return row(shard * width, width)

    def columns_of(shard):
        return lane(shard * width, width)

    turn_qkv = Turn(
        net, keep, at,
        lambda i, group: (qw, kw, vw)[i].at[:, lane(group * HD, HD)],
        lambda i, shard: w_qkv.at[shard_rows(shard), i * HD : (i + 1) * HD],
        [((0, 1, 2), lambda shard: w_qkv.at[shard_rows(shard), :], lambda n: w_qkv.at[0 : n * width, :])],
    )
    few = width // 2
    turn_gu = Turn(
        net, keep, at,
        lambda i, group: (gw, uw)[i // 2 % 2].at[
            i % 2 * few : (i % 2 + 1) * few, lane(group * units + lanes_of[i // 4].start, size_of[i // 4])
        ],
        lambda i, shard: w_gu.at[row(shard * width + i % 2 * few, few), gate_up(i // 4, i // 2 % 2)],
        [
            (range(4 * b, 4 * b + 4), lambda shard, p=p: w_gu.at[shard_rows(shard), p], lambda n, p=p: w_gu.at[0 : n * width, p])
            for b, p in enumerate(pairs_of)
        ],
    )
    turn_o = Turn(
        net, keep, at,
        lambda i, group: ow.at[row(group * HD, HD), :],
        lambda i, shard: w_o.at[:, columns_of(shard)],
        [((0,), lambda shard: w_o.at[:, columns_of(shard)], lambda n: w_o.at[:, 0 : n * width])],
    )
    turn_d = Turn(
        net, keep, at,
        lambda i, group: dw.at[lane(group * units + lanes_of[i].start, size_of[i]), :],
        lambda i, shard: w_d.at[lanes_of[i], columns_of(shard)],
        [
            ((b,), lambda shard, p=p: w_d.at[p, columns_of(shard)], lambda n, p=p: w_d.at[p, 0 : n * width])
            for b, p in enumerate(lanes_of)
        ],
    )

    gain_slot = gains_all.at[:, columns_of(s)]
    gain_moves = net.lot(
        (0,), lambda _: [(gains, gain_slot, (s ^ m, h)) for m in range(1, shards)], gain_in, lambda _: gain_in
    )
    strip = row(at.q * quarter, quarter)
    mine_start = (g * 4 + at.q) * quarter
    span = ranks * count
    one = Spread(net, at, rows_dh, quarter, tok)
    grad = Spread(net, at, rows_cot, quarter, cot)
    two = Spread(net, at, rows_two, quarter)
    three = Spread(net, at, rows_dh, quarter)
    set_a, set_b = (part_a, near_a, xin_a, zin_a), (part_b, near_b, xin_b, zin_b)
    first = Collect(net, at, set_a, quarter, summed)
    second = Collect(net, at, set_a, quarter, summed)
    out_sum = Collect(net, at, set_b, quarter, summed)
    third = Collect(net, at, set_a, quarter, summed)

    def clear(i):
        rows = row(i * 64, 64)
        accum[rows, :] = jnp.zeros_like(accum[rows, :])

    def tables(i):
        rows = row(i * 64, 64)
        first_row = (i // (count // 64) * ranks + r) * count + i % (count // 64) * 64
        places = (first_row + lax.broadcasted_iota(jnp.int32, (64, HD), 0)).astype(F32)
        lanes = lax.broadcasted_iota(jnp.int32, (64, HD), 1)
        low_half = lanes < HD // 2
        order = jnp.where(low_half, lanes, lanes - HD // 2).astype(F32)
        angles = places * jnp.exp(order * (-math.log(10000.0) / (HD // 2)))
        cosines[rows, :] = jnp.cos(angles)
        sines[rows, :] = jnp.where(low_half, -jnp.sin(angles), jnp.sin(angles))

    def norm_one(m):
        def some(i):
            rows = row((g ^ m) * count + i * 32, 32)
            values = rows_dh[rows, :].astype(F32)
            inverse = lax.rsqrt(mean_square(values) + epsilon)
            rows_one[rows, :] = (values * inverse * gains_all[0:1, :]).astype(BF16)

        each(count // 32, some)

    def own_place(m):
        return row(((g ^ m) * ranks + r) * count, count)

    pair_moves = net.lot(
        range(4),
        lambda m: (pairs.at[own_place(m), :], pairs.at[own_place(m), :], at.beside()),
        pairs.at[0 : groups * count, :],
    )

    def project(m):
        rows, place = chunk(m), own_place(m)
        heads = dot(rows_one[rows, :], w_qkv[...])
        cos_part, sin_part = cosines[rows, :], sines[rows, :]
        queries[rows, :] = turned(heads[:, :HD], cos_part, sin_part).astype(BF16)
        pairs[place, :HD] = turned(heads[:, HD : 2 * HD], cos_part, sin_part).astype(BF16)
        pairs[place, HD:] = heads[:, 2 * HD :].astype(BF16)
        pair_moves.start(m)

    def weights_of(m, j, query):
        keys = pairs[row(j * span, span), :HD]
        scores = dot_nt(query, keys) * score_scale - score_shift
        q_place = ((g ^ m) * ranks + r) * count + lax.broadcasted_iota(jnp.int32, (count, span), 0)
        k_place = j * span + lax.broadcasted_iota(jnp.int32, (count, span), 1)
        return jnp.where(k_place <= q_place, jax.nn.sigmoid(scores), 0.0)

    def attend(m):
        rows = chunk(m)
        query = queries[rows, :]

        def step(j, total):
            weight = weights_of(m, j, query).astype(BF16)
            return total + dot(weight, pairs[row(j * span, span), HD:])

        total = lax.fori_loop(0, (g ^ m) + 1, step, jnp.zeros((count, HD), F32))
        low = total.astype(BF16)
        mix[rows, :] = low

        if m == 3:
            turn_o.ready()
        part_a[rows, :] = dot(low, w_o[...]).astype(BF16)

    def norm_two(i):
        few = row(i * 16, 16)
        values = own_x[few, :].astype(F32) + first.total(few)
        hidden[few, :] = values
        inverse = lax.rsqrt(mean_square(values) + epsilon)
        rows_two[row(mine_start + i * 16, 16), :] = (values * inverse * gains_all[1:2, :]).astype(BF16)

    def early(m, b):
        lanes = lanes_of[b]
        dmixed[chunk(m), lanes] = dot_nt(rows_cot[chunk(m), :], w_d[lanes, :])

    def feed(m, b):
        rows = chunk(m)
        lanes, pair, size = lanes_of[b], pairs_of[b], size_of[b]
        both = dot(rows_two[rows, :], w_gu[:, pair])
        gate, up = both[:, :size], both[:, size:]
        sig = jax.nn.sigmoid(gate)
        act = gate * sig
        mixed[rows, lanes] = (act * up).astype(BF16)
        back = dmixed[rows, lanes]
        dgu[rows, gate_up(b, 0)] = (back * up * sig * (1.0 + gate * (1.0 - sig))).astype(BF16)
        dgu[rows, gate_up(b, 1)] = (back * act).astype(BF16)
        total = dot_nt(dgu[rows, pair], w_gu[:, pair])
        if b:
            total += part_a[rows, :].astype(F32)
        part_a[rows, :] = total.astype(BF16)

    def out_part(m, b):
        rows = chunk(m)
        lanes = lanes_of[b]
        total = dot(mixed[rows, lanes], w_d[lanes, :])
        if b:
            total += part_b[rows, :].astype(F32)
        part_b[rows, :] = total.astype(BF16)

    def halves(m, work, lot):
        d = g ^ m

        def step(k):
            work(d * ranks + (r ^ 1 ^ k))

            @pl.when(k == 0)
            def _():
                lot.start(m)

        each(2, step)

    def several(groups_, work, lot):
        first_, last_ = groups_
        each(first_ - last_ + 1, lambda i: halves(first_ - i, work, lot))
        lot.mark(range(last_, first_ + 1))

    def beside(source, target, bulk):
        def describe(m):
            d = g ^ m
            return (source(d * ranks + (r ^ 1)), target(d), at.beside())

        return net.lot(range(4), describe, bulk)

    moves_gu = [
        [
            beside(lambda shard, p=p: w_gu.at[shard_rows(shard), p], lambda d, p=p: in_gu.at[d, :, p], in_gu.at[:, :, p])
            for p in (gate_up(b, 0), gate_up(b, 1))
        ]
        for b in range(len(PARTS))
    ]
    moves_d = [
        beside(lambda shard, p=p: w_d.at[p, columns_of(shard)], lambda d, p=p: in_d.at[d, p, :], in_d.at[:, p, :])
        for p in lanes_of
    ]
    moves_qkv = beside(lambda shard: w_qkv.at[shard_rows(shard), :], lambda d: in_qkv.at[d], in_qkv)
    moves_o = beside(lambda shard: w_o.at[:, columns_of(shard)], lambda d: in_o.at[d], in_o)

    def grads_gu(groups_, b, i):
        def work(shard):
            w_gu[shard_rows(shard), gate_up(b, i)] = dot_tn(
                rows_two[:, columns_of(shard)], dgu[:, gate_up(b, i)]
            ).astype(BF16)

        several(groups_, work, moves_gu[b][i])

    def grads_d(groups_, b):
        def work(shard):
            columns = columns_of(shard)
            w_d[lanes_of[b], columns] = dot_tn(mixed[:, lanes_of[b]], rows_cot[:, columns]).astype(BF16)

        several(groups_, work, moves_d[b])

    def grads_o(groups_):
        def work(shard):
            columns = columns_of(shard)
            w_o[:, columns] = dot_tn(mix[...], rows_dh[:, columns]).astype(BF16)

        several(groups_, work, moves_o)

    def grads_qkv(groups_):
        def work(shard):
            w_qkv[shard_rows(shard), :] = dot_tn(rows_one[:, columns_of(shard)], dqkv[...]).astype(BF16)

        several(groups_, work, moves_qkv)

    final, final_own = [], []

    def owners(moves, several):
        pieces = [(a, b, at.along(m)) for m in (1, 2, 3) for a, b in moves(m)]
        lot = net.lot((0,), lambda _: pieces, several, lambda _: several)
        final.append(lot)

        def give(m, i=None):
            blocks = moves(m)
            for k in range(len(blocks)) if i is None else (i,):
                if m:
                    lot.start(0, ((m - 1) * len(blocks) + k,))
                else:
                    final_own.append(keep.put(*blocks[k]))

        return give

    def shard_of(m):
        return (g ^ m) * ranks + r

    def gate_up_moves(b):
        def moves(m):
            for i, out in enumerate((g_out, u_out)):
                place = out.at[:, lane(g * units + lanes_of[b].start, size_of[b])]
                yield (w_gu.at[shard_rows(shard_of(m)), gate_up(b, i)], place)

        return lambda m: list(moves(m))

    def down_moves(b):
        place = d_out.at[lane(g * units + lanes_of[b].start, size_of[b]), :]
        return lambda m: [(w_d.at[lanes_of[b], columns_of(shard_of(m))], place)]

    def qkv_moves(m):
        rows = shard_rows(shard_of(m))
        return [
            (w_qkv.at[rows, i * HD : (i + 1) * HD], out.at[:, lane(g * HD, HD)])
            for i, out in enumerate((q_out, k_out, v_out))
        ]

    give_gu = [owners(gate_up_moves(b), w_gu.at[0 : 3 * width, p]) for b, p in enumerate(pairs_of)]
    give_d = [owners(down_moves(b), w_d.at[p, 0 : 3 * width]) for b, p in enumerate(lanes_of)]
    give_qkv = owners(qkv_moves, w_qkv.at[0 : 3 * width, :])
    give_o = owners(
        lambda m: [(w_o.at[:, columns_of(shard_of(m))], o_out.at[row(g * HD, HD), :])], w_o.at[:, 0 : 3 * width]
    )

    def sums(m, lot, mine_of, other_of, size):
        lot.arrived(m)

        def step(i):
            a, rows, lanes = mine_of(i)
            b, d, few, others = other_of(i)
            a[rows, lanes] = (a[rows, lanes].astype(F32) + b[d, few, others].astype(F32)).astype(BF16)

        each(size // 32, step)

    def sums_gu(m, b, i):
        d, p = g ^ m, gate_up(b, i)
        start = (d * ranks + r) * width
        sums(
            m, moves_gu[b][i],
            lambda k: (w_gu, row(start + k * 32, 32), p), lambda k: (in_gu, d, row(k * 32, 32), p), width,
        )
        give_gu[b](m, i)

    def sums_d(m, b):
        d, base = g ^ m, lanes_of[b].start
        columns = columns_of(d * ranks + r)
        sums(
            m, moves_d[b],
            lambda i: (w_d, row(base + i * 32, 32), columns),
            lambda i: (in_d, d, row(base + i * 32, 32), slice(None)), size_of[b],
        )
        give_d[b](m)

    def sums_o(m):
        d = g ^ m
        columns = columns_of(d * ranks + r)
        sums(
            m, moves_o,
            lambda i: (w_o, row(i * 32, 32), columns), lambda i: (in_o, d, row(i * 32, 32), slice(None)), HD,
        )
        give_o(m)

    def sums_qkv(m):
        d = g ^ m
        start = (d * ranks + r) * width
        sums(
            m, moves_qkv,
            lambda i: (w_qkv, row(start + i * 32, 32), slice(None)),
            lambda i: (in_qkv, d, row(i * 32, 32), slice(None)), width,
        )
        give_qkv(m)

    def back_two(i, gain_grad):
        few = row(i * 16, 16)
        own = row(mine_start + i * 16, 16)
        upstream, values = second.total(few), hidden[few, :]
        inverse = lax.rsqrt(mean_square(values) + epsilon)
        scaled = upstream * gains_all[1:2, :]
        back = inverse * scaled - values * (inverse * inverse * inverse) * jnp.mean(
            scaled * values, axis=1, keepdims=True
        )
        total = rows_cot[own, :].astype(F32) + back
        dhidden[few, :] = total
        rows_dh[own, :] = total.astype(BF16)
        return gain_grad + jnp.sum(upstream * values * inverse, axis=0, keepdims=True)

    def attend_back(m):
        three.ready(m)
        rows = chunk(m)
        query = queries[rows, :]
        dm = dot_nt(rows_dh[rows, :], w_o[...]).astype(BF16)

        def step(j, total):
            block = row(j * span, span)
            weight = weights_of(m, j, query)
            dweight = dot_nt(dm, pairs[block, HD:])
            dscore = (dweight * weight * (1.0 - weight)).astype(BF16)
            accum[block, HD:] += dot_tn(weight.astype(BF16), dm)
            accum[block, :HD] += dot_tn(dscore, query)
            return total + dot(dscore, pairs[block, :HD])

        total = lax.fori_loop(0, (g ^ m) + 1, step, jnp.zeros((count, HD), F32))
        dqkv[rows, :HD] = turned(total * score_scale, cosines[rows, :], -sines[rows, :]).astype(BF16)

    pair_back = net.lot(range(4), lambda m: (pair_send.at[g ^ m], pair_in.at[g ^ m], at.beside()), pair_send)

    def send_pair(m):
        d = g ^ m
        rows = row((d * ranks + (r ^ 1)) * count, count)
        pair_send[d] = accum[rows, :].astype(BF16)
        pair_back.start(m)

    def back_from_end(i):
        m = g ^ (groups - 1 - i)
        attend_back(m)
        send_pair(m)

    def back_one(m):
        d = g ^ m
        rows = chunk(m)
        pair_back.arrived(m)
        both = accum[own_place(m), :] + pair_in[d].astype(F32)
        dqkv[rows, HD : 2 * HD] = turned(both[:, :HD] * score_scale, cosines[rows, :], -sines[rows, :]).astype(BF16)
        dqkv[rows, 2 * HD :] = both[:, HD:].astype(BF16)
        part_a[rows, :] = dot_nt(dqkv[rows, :], w_qkv[...]).astype(BF16)

    ends = {}

    def share(i, source, target):
        place = target.at[strip, :]
        final_own.append(keep.put(source, place))
        lot = net.lot((0, 1), lambda j: (source, place, (at.near(), at.across())[j]), target.at[0 : 2 * quarter, :])
        lot.start(0)
        lot.start(1)
        ends[i] = (lot, target)

    def relay(i):
        lot, target = ends[i]
        lot.arrived(1)
        final.append(lot)
        block = target.at[row((at.q ^ 1) * quarter, quarter), :]
        on = net.lot((0,), lambda j: (block, block, at.near()), block)
        on.start(0)
        final.append(on)

    def result_rows(i):
        few = row(i * 16, 16)
        result_own[few, :] = (hidden[few, :] + out_sum.total(few)).astype(BF16)

    def back_rows(i, gain_grad):
        few = row(i * 16, 16)
        upstream, values = third.total(few), own_x[few, :].astype(F32)
        inverse = lax.rsqrt(mean_square(values) + epsilon)
        scaled = upstream * gains_all[0:1, :]
        back = inverse * scaled - values * (inverse * inverse * inverse) * jnp.mean(
            scaled * values, axis=1, keepdims=True
        )
        rows_own[few, :] = (dhidden[few, :] + back).astype(BF16)
        return gain_grad + jnp.sum(upstream * values * inverse, axis=0, keepdims=True)

    gain_sums = net.lot(
        (0,),
        lambda _: [(gain_part.at[:, columns_of(s ^ m)], gain_in.at[m - 1], (s ^ m, h)) for m in range(1, shards)],
        gain_in,
        lambda _: gain_in,
    )
    gain_ends = net.lot(
        (0,),
        lambda _: [(gain_mid, gain_near.at[m - 1], (s, h ^ m)) for m in range(1, 4)],
        gain_near,
        lambda _: gain_near,
    )
    gains[...] = jnp.zeros_like(gains)
    gains[0:1, :] = gain_one[...].astype(F32).reshape(1, width)
    gains[1:2, :] = gain_two[...].astype(F32).reshape(1, width)
    gain_moves.start(0)
    gain_own = keep.put(gains, gain_slot)
    own_rows = keep.put(tok, rows_dh.at[chunk(0), :])
    own_strip = keep.put(tok.at[strip, :], own_x)
    own_cot = keep.put(cot, rows_cot.at[chunk(0), :])
    turn_qkv.start(3)
    one.start(2)
    one.start(1)
    turn_qkv.start(1)
    turn_o.start(1)
    one.arrive(1)
    turn_qkv.mine()
    turn_qkv.start(2)
    gain_part[...] = jnp.zeros_like(gain_part)
    each(total_rows // 64, clear)
    each(groups * count // 64, tables)
    grad.z.start(2 * PIECES + 0)
    one.arrive(2)
    turn_o.pass_on(1)
    turn_gu.start(1, 0, (1,))
    turn_gu.start(3, 0, (2,))
    turn_o.start(3)
    gain_own.wait()
    gain_moves.arrived(0)
    own_rows.wait()
    own_strip.wait()
    norm_one(0)
    turn_qkv.pass_on(3)
    one.second(2)
    turn_o.start(2)
    turn_qkv.pass_on(1)
    grad.z.start(2 * PIECES + 1)
    turn_gu.start(2, 0, (3,))
    turn_d.start(1, 0)
    one.ready(2)
    norm_one(2)
    grad.z.start(1 * PIECES + 1)
    turn_qkv.pass_on(2)
    turn_gu.start(1, 0, (2,))
    one.arrive(3)
    turn_o.mine()
    one.second(1)
    turn_qkv.ready()
    project(0)
    turn_d.start(2, 1)
    one.ready(1)
    norm_one(1)
    project(1)
    project(2)
    one.second(3)
    one.ready(3)
    norm_one(3)
    project(3)
    turn_d.start(3, 0)
    turn_gu.start(1, 0, (0,))
    turn_o.pass_on(2)
    turn_d.start(2, 0)
    turn_o.pass_on(3)
    grad.arrive(2)
    for m in (0, 1, 2, 3):
        pair_moves.arrived(m)
    attend(3)
    first.first(3)
    attend(2)
    first.first(2)
    grad.z.start(1 * PIECES + 0)
    first.second(3)
    turn_d.start(3, 1)
    turn_d.mine(1)
    first.second(2)
    attend(1)
    first.first(1)
    turn_gu.mine(1)
    turn_gu.start(3, 0, (0,))
    first.third(3)
    grad.arrive(3)
    turn_d.pass_on(2, 1)
    turn_d.pass_on(1, 0)
    first.second(1)
    first.third(2)
    grad.second(2)
    attend(0)
    first.first(0)
    turn_d.pass_on(2, 0)
    turn_gu.start(3, 0, (3,))
    first.third(1)
    turn_gu.start(2, 0, (1,))
    turn_d.pass_on(3, 1)
    turn_gu.start(3, 0, (1,))
    turn_gu.start(2, 0, (2,))
    turn_d.mine(0)
    turn_d.start(1, 1)
    turn_gu.start(2, 0, (0,))
    turn_gu.start(1, 0, (3,))
    turn_gu.start(1, 1, (1, 0))
    first.second(0)
    grad.arrive(1)
    turn_d.pass_on(3, 0)
    first.last()
    each(quarter // 16, norm_two)
    two.start(1)
    turn_gu.mine(0)
    two.start(2)
    two.start_own()
    turn_d.pass_on(1, 1)
    turn_gu.start(2, 1, (3,))
    turn_gu.pass_on(1, 0)
    turn_gu.start(1, 1, (2,))
    grad.second(3)
    turn_gu.start(1, 1, (3,))
    two.second(0)
    turn_d.ready(0)
    turn_d.ready(1)
    turn_gu.pass_on(2, 0)
    grad.second(1)
    turn_gu.start(2, 1, (1, 0))
    turn_gu.pass_on(3, 0)
    turn_gu.start(2, 1, (2,))
    own_cot.wait()
    for m in (1, 2, 3):
        grad.ready(m)
    each(4, lambda m: early(m, 0))
    two.arrive(1)
    two.arrive(2)
    turn_gu.pass_on(1, 1)
    two.second(1)
    two.ready(1)
    turn_gu.start(3, 1, (1,))
    two.ready(0)
    two.second(2)
    turn_gu.start(3, 1, (2, 0, 3))
    two.ready(2)
    turn_gu.pass_on(2, 1)
    each(4, lambda m: early(m, 1))
    two.arrive(3)
    turn_gu.ready(0)
    first.sent()
    one.sent()
    each(2, lambda i: feed(1 - i, 0))
    turn_gu.pass_on(3, 1)
    two.second(3)
    feed(2, 0)
    two.ready(3)
    feed(3, 0)
    turn_gu.sent(0)
    grads_gu((3, 3), 0, 0)
    grads_gu((3, 3), 0, 1)
    turn_gu.ready(1)
    each(2, lambda i: (feed(3 - i, 1), second.first(3 - i)))
    second.a.mark((3, 2))
    sums_gu(3, 0, 0)
    grads_gu((2, 2), 0, 0)
    second.second(3)
    each(4, lambda m: out_part(m, 0))
    sums_gu(3, 0, 1)
    second.second(2)
    turn_d.sent(0)
    grads_d((1, 1), 0)
    feed(1, 1)
    second.first(1)
    second.third(3)
    feed(0, 1)
    second.first(0)
    second.second(1)
    turn_gu.sent(1)
    grads_gu((3, 3), 1, 1)
    sums_d(1, 0)
    each(4, lambda m: out_part(m, 1))
    for m in (3, 2, 1, 0):
        out_sum.first(m)
    grads_gu((2, 2), 0, 1)
    second.third(2)
    grads_gu((3, 3), 1, 0)
    second.second(0)
    second.third(1)
    out_sum.second(1)
    sums_gu(2, 0, 0)
    sums_gu(2, 0, 1)
    turn_d.sent(1)
    grads_d((3, 3), 1)
    grads_gu((0, 0), 1, 1)
    second.last()
    gain_part[1:2, :] = lax.fori_loop(0, quarter // 16, back_two, jnp.zeros((1, depth), F32))
    three.start(1)
    grads_gu((1, 1), 1, 1)
    three.start(2)
    grads_gu((1, 1), 0, 1)
    out_sum.second(3)
    grads_d((2, 2), 1)
    three.start_own()
    grads_gu((2, 2), 1, 1)
    grads_d((3, 3), 0)
    sums_gu(3, 1, 0)
    grads_gu((1, 1), 1, 0)
    grads_gu((2, 2), 1, 0)
    out_sum.third(3)
    three.arrive(1)
    three.arrive(2)
    sums_d(3, 1)
    grads_d((0, 0), 0)
    sums_d(3, 0)
    three.second(0)
    grads_gu((0, 0), 0, 1)
    grads_gu((0, 0), 1, 0)
    grads_d((0, 0), 1)
    sums_gu(1, 1, 1)
    sums_gu(3, 1, 1)
    sums_d(2, 1)
    sums_gu(2, 1, 0)
    sums_gu(1, 0, 1)
    sums_gu(2, 1, 1)
    three.arrive(3)
    three.second(2)
    sums_gu(1, 1, 0)
    grads_gu((0, 0), 0, 0)
    three.second(1)
    out_sum.second(2)
    grads_d((2, 2), 0)
    three.second(3)
    each(4, back_from_end)
    pair_back.mark(range(4))
    out_sum.second(0)
    out_sum.third(2)
    sums_gu(0, 1, 1)
    grads_gu((1, 1), 0, 0)
    out_sum.third(1)
    turn_o.sent()
    grads_o((1, 0))
    grads_o((3, 3))
    second.sent()
    third.produce(back_one)
    sums_gu(0, 0, 0)
    turn_qkv.sent()
    grads_qkv((2, 2))
    grads_qkv((3, 3))
    grads_d((1, 1), 1)
    grads_o((2, 2))
    third.third(3)
    sums_o(3)
    third.second(0)
    grads_qkv((1, 1))
    sums_d(2, 0)
    sums_gu(1, 0, 0)
    sums_o(1)
    third.third(2)
    third.third(1)
    sums_qkv(3)
    out_sum.last()
    each(quarter // 16, result_rows)
    share(0, result_own, result_out)
    sums_d(1, 1)
    sums_o(0)
    sums_qkv(2)
    grads_qkv((0, 0))
    third.last()
    gain_part[0:1, :] = lax.fori_loop(0, quarter // 16, back_rows, jnp.zeros((1, depth), F32))
    gain_sums.start(0)
    share(1, rows_own, rows_out)
    sums_o(2)
    sums_qkv(0)
    relay(0)
    sums_gu(0, 1, 0)
    sums_qkv(1)
    sums_gu(0, 0, 1)
    sums_d(0, 1)
    sums_d(0, 0)
    relay(1)
    total = gain_part[:, columns_of(s)]
    gain_sums.arrived(0)
    for m in range(1, shards):
        total += gain_in[m - 1]
    gain_mid[...] = total
    gain_ends.start(0)
    gain_ends.arrived(0)
    for m in range(1, 4):
        total += gain_near[m - 1]
    gains_out[...] = total
    for lot in final:
        lot.arrived(0)
    net.finish()
    for copy in final_own:
        copy.wait()


def rows_plan(
    groups,
    ranks,
    tokens,
    attn_gain,
    query_weight,
    key_weight,
    value_weight,
    out_weight,
    mlp_gain,
    gate_weight,
    up_weight,
    down_weight,
    cotangent,
):
    count, depth = tokens.shape
    shards = groups * ranks
    quarter = count // 4
    width = query_weight.shape[0]
    units = gate_weight.shape[1] // groups
    total_rows = count * shards
    here = groups * count
    ins = (
        tokens, cotangent, attn_gain, mlp_gain,
        query_weight, key_weight, value_weight, out_weight, gate_weight, up_weight, down_weight,
    )
    shape = jax.ShapeDtypeStruct
    hbm, vmem = pl.BlockSpec(memory_space=pl.ANY), pl.BlockSpec(memory_space=pltpu.VMEM)
    owners = (query_weight, key_weight, value_weight, out_weight, gate_weight, up_weight, down_weight)
    outs = [
        shape((count, depth), BF16),
        shape((count, depth), BF16),
        shape((8, width), F32),
        *(shape(w.shape, BF16) for w in owners),
    ]

    def low(*extent):
        return pltpu.VMEM(extent, BF16)

    def full(*extent):
        return pltpu.VMEM(extent, F32)

    def collector():
        return [
            low(here, depth),
            low(groups, 2 * quarter, depth),
            low(groups, quarter, depth),
            low(3, quarter, depth),
        ]

    scratch = [
        full(8, width), full(8, depth), full(here, HD), full(here, HD),
        low(here, depth), low(here, depth), low(here, depth), low(here, depth),
        low(depth, 3 * HD), low(HD, depth), low(depth, 2 * units), low(units, depth),
        low(here, HD), low(total_rows, 2 * HD), low(here, HD), low(here, 3 * HD),
        full(total_rows, 2 * HD), low(groups, count, 2 * HD), low(groups, count, 2 * HD),
        low(here, units), low(here, 2 * units), full(here, units),
        low(quarter, depth), full(quarter, depth), full(quarter, depth), full(quarter, depth),
        *collector(), *collector(),
        low(groups, width, 2 * units), low(groups, units, width), low(groups, width, 3 * HD), low(groups, HD, width),
        full(8, depth), full(shards - 1, 8, width), full(8, width), full(3, 8, width),
        low(quarter, depth), low(quarter, depth),
        pltpu.SemaphoreType.DMA((SENDS,)), pltpu.SemaphoreType.DMA((RECEIVES,)), pltpu.SemaphoreType.DMA((KEEPS,)),
    ]
    moved = pl.pallas_call(
        functools.partial(layer_body, groups, ranks),
        out_shape=outs,
        in_specs=[hbm] * 2 + [vmem] * 2 + [hbm] * 7,
        out_specs=[hbm, hbm, vmem] + [hbm] * 7,
        scratch_shapes=scratch,
        compiler_params=pltpu.CompilerParams(
            collective_id=1, has_side_effects=True, vmem_limit_bytes=VMEM_LIMIT
        ),
    )(*ins)
    steps = 2

    def sliced(array):
        rows, columns = array.shape
        return pl.BlockSpec((rows // steps, columns), lambda i: (i, 0))

    gain_specs = [pl.BlockSpec((8, width), lambda i: (0, 0))]
    row_spec = pl.BlockSpec((width,), lambda i: (0,))
    specs = [sliced(moved[0]), sliced(moved[1]), *(sliced(w) for w in moved[3:])]
    gain_row = shape((width,), F32)
    one, two, result, rows_grad, *grads = pl.pallas_call(
        cast_body,
        grid=(steps,),
        out_shape=[gain_row, gain_row, moved[0], moved[1], *(shape(w.shape, F32) for w in owners)],
        in_specs=gain_specs + specs,
        out_specs=[row_spec, row_spec] + specs,
        compiler_params=pltpu.CompilerParams(vmem_limit_bytes=VMEM_LIMIT),
    )(moved[2], moved[0], moved[1], *moved[3:])
    return (result, rows_grad, one, *grads[:4], two, *grads[4:])


def cast_body(*refs):
    inputs = len(refs) // 2
    gains, sources, (one, two, *targets) = refs[0], refs[1:inputs], refs[inputs:]
    one[...] = gains[0, :]
    two[...] = gains[1, :]
    for source, target in zip(sources, targets):
        target[...] = source[...].astype(target.dtype)


def on_device(tokens, attn_gain, query_weight, *rest):
    groups = query_weight.shape[1] // HD
    ranks = lax.axis_size("seq") // groups
    fits = lax.axis_size("head") == 4 and groups == 4 and ranks == 2 and query_weight.shape[0] % 128 == 0
    plan = functools.partial(rows_plan, groups, ranks) if fits else gathered_weights
    return plan(tokens, attn_gain, query_weight, *rest)


def solution(mesh):
    in_specs = (
        P("seq", None),
        P("seq"),
        P("seq", "head"),
        P("seq", "head"),
        P("seq", "head"),
        P("head", "seq"),
        P("seq"),
        P("seq", "head"),
        P("seq", "head"),
        P("head", "seq"),
        P("seq", None),
    )
    out_specs = (
        P("seq", None),
        P("seq", None),
        P("seq"),
        P("seq", "head"),
        P("seq", "head"),
        P("seq", "head"),
        P("head", "seq"),
        P("seq"),
        P("seq", "head"),
        P("seq", "head"),
        P("head", "seq"),
    )
    return jax.shard_map(
        on_device, mesh=mesh, in_specs=in_specs, out_specs=out_specs, check_vma=False
    )
```

```python
import functools
import math

import jax
import jax.numpy as jnp
from jax import lax
from jax.experimental import pallas as pl
from jax.experimental.pallas import tpu as pltpu
from jax.sharding import PartitionSpec as P

MESH = pl.DeviceIdType.MESH
F32, BF16 = jnp.float32, jnp.bfloat16

HD = 128


epsilon = 1e-05
block_limit = 512
VMEM_LIMIT = 63 * 2**20
SENDS, RECEIVES, KEEPS = 59, 217, 30
PIECES = 2
PARTS = (2, 2)


def tables(offset, length, half_width):
    places = (offset + jnp.arange(length, dtype=jnp.int32)).astype(jnp.float32)
    frequency = jnp.exp(
        jnp.arange(half_width, dtype=jnp.float32) * (-math.log(10000.0) / half_width)
    )
    angles = places[:, None] * frequency[None, :]
    return (jnp.cos(angles)[:, None, :], jnp.sin(angles)[:, None, :])


def rotary(values, cos_table, sin_table):
    half_width = values.shape[-1] // 2
    front = values[..., :half_width]
    back_half = values[..., half_width:]
    return jnp.concatenate(
        [front * cos_table - back_half * sin_table, back_half * cos_table + front * sin_table],
        axis=-1,
    )


def unrotary(gradient, cos_table, sin_table):
    half_width = gradient.shape[-1] // 2
    front = gradient[..., :half_width]
    back_half = gradient[..., half_width:]
    return jnp.concatenate(
        [front * cos_table + back_half * sin_table, back_half * cos_table - front * sin_table],
        axis=-1,
    )


def norm_back(values, inverse, gain_vector, upstream):
    scaled = upstream * gain_vector
    gain_grad = jnp.sum(upstream * values * inverse, axis=0)
    value_grad = inverse * scaled - values * inverse**3 * jnp.mean(
        scaled * values, axis=1, keepdims=True
    )
    return (value_grad, gain_grad)


def gathered_weights(
    tokens,
    attn_gain,
    query_weight,
    key_weight,
    value_weight,
    out_weight,
    mlp_gain,
    gate_weight,
    up_weight,
    down_weight,
    cotangent,
):
    row_count = tokens.shape[0]
    total_rows = row_count * lax.axis_size("seq")
    row_start = lax.axis_index("seq") * row_count
    local_width = query_weight.shape[1]
    local_heads = local_width // HD
    score_scale = 1.0 / math.sqrt(HD)
    score_shift = math.log(total_rows)
    block_rows = math.gcd(total_rows, block_limit)
    block_count = total_rows // block_rows
    attn_gain_full, query_full, key_full, value_full, out_full = (
        lax.all_gather(attn_gain, "seq", axis=0, tiled=True),
        lax.all_gather(query_weight, "seq", axis=0, tiled=True),
        lax.all_gather(key_weight, "seq", axis=0, tiled=True),
        lax.all_gather(value_weight, "seq", axis=0, tiled=True),
        lax.all_gather(out_weight, "seq", axis=1, tiled=True),
    )
    mlp_gain_full, gate_full, up_full, down_full = (
        lax.all_gather(mlp_gain, "seq", axis=0, tiled=True),
        lax.all_gather(gate_weight, "seq", axis=0, tiled=True),
        lax.all_gather(up_weight, "seq", axis=0, tiled=True),
        lax.all_gather(down_weight, "seq", axis=1, tiled=True),
    )
    token_values = tokens.astype(jnp.float32)
    inverse_one = lax.rsqrt(jnp.mean(token_values * token_values, axis=1, keepdims=True) + epsilon)
    normed_one = (token_values * inverse_one * attn_gain_full.astype(jnp.float32)).astype(
        jnp.bfloat16
    )
    query_pre = jnp.dot(normed_one, query_full, preferred_element_type=jnp.float32)
    key_pre = jnp.dot(normed_one, key_full, preferred_element_type=jnp.float32)
    value_rows = (
        jnp.dot(normed_one, value_full, preferred_element_type=jnp.float32)
        .astype(jnp.bfloat16)
        .reshape(row_count, local_heads, HD)
    )
    cos_table, sin_table = tables(row_start, row_count, HD // 2)
    query_rows = (
        rotary(query_pre.reshape(row_count, local_heads, HD), cos_table, sin_table)
        .astype(jnp.bfloat16)
        .reshape(row_count, local_width)
    )
    key_rows = rotary(key_pre.reshape(row_count, local_heads, HD), cos_table, sin_table).astype(
        jnp.bfloat16
    )
    all_queries = lax.all_gather(query_rows, "seq", axis=0, tiled=True)
    key_places = row_start + jnp.arange(row_count, dtype=jnp.int32)

    def weights_for(query_block, block_start):
        scores = (
            jnp.einsum("qhd,khd->hqk", query_block, key_rows, preferred_element_type=jnp.float32)
            * score_scale
            - score_shift
        )
        query_places = block_start + jnp.arange(query_block.shape[0], dtype=jnp.int32)
        visible = key_places[None, :] <= query_places[:, None]
        return jnp.where(visible[None], jax.nn.sigmoid(scores), 0.0)

    step_rows = math.gcd(row_count * lax.axis_size("seq"), block_limit)
    step_count = row_count * lax.axis_size("seq") // step_rows
    picked = all_queries.reshape(step_count, step_rows, local_heads, HD)
    starts = jnp.arange(step_count, dtype=jnp.int32) * step_rows

    def one_block(packed):
        query_block, block_start = packed
        weights = weights_for(query_block, block_start).astype(jnp.bfloat16)
        return jnp.einsum(
            "hqk,khd->qhd", weights, value_rows, preferred_element_type=jnp.float32
        ).reshape(step_rows, local_width)

    attn_mix = lax.psum_scatter(
        lax.map(one_block, (picked, starts)).reshape(row_count * lax.axis_size("seq"), local_width),
        "seq",
        scatter_dimension=0,
        tiled=True,
    ).astype(jnp.bfloat16)
    attn_branch = lax.psum(jnp.dot(attn_mix, out_full, preferred_element_type=jnp.float32), "head")
    hidden = token_values + attn_branch
    inverse_two = lax.rsqrt(jnp.mean(hidden * hidden, axis=1, keepdims=True) + epsilon)
    normed_two = (hidden * inverse_two * mlp_gain_full.astype(jnp.float32)).astype(jnp.bfloat16)
    gate_pre = jnp.dot(normed_two, gate_full, preferred_element_type=jnp.float32)
    up_pre = jnp.dot(normed_two, up_full, preferred_element_type=jnp.float32)
    gate_act = jax.nn.silu(gate_pre)
    mixed = (gate_act * up_pre).astype(jnp.bfloat16)
    mlp_branch = lax.psum(
        jnp.dot(mixed, down_full, preferred_element_type=jnp.float32).astype(jnp.bfloat16), "head"
    ).astype(jnp.float32)
    result = (hidden + mlp_branch).astype(jnp.bfloat16)
    kept_weights = (
        lax.all_gather(attn_gain, "seq", axis=0, tiled=True),
        lax.all_gather(query_weight, "seq", axis=0, tiled=True),
        lax.all_gather(key_weight, "seq", axis=0, tiled=True),
        lax.all_gather(value_weight, "seq", axis=0, tiled=True),
        lax.all_gather(out_weight, "seq", axis=1, tiled=True),
        lax.all_gather(mlp_gain, "seq", axis=0, tiled=True),
        lax.all_gather(gate_weight, "seq", axis=0, tiled=True),
        lax.all_gather(up_weight, "seq", axis=0, tiled=True),
        lax.all_gather(down_weight, "seq", axis=1, tiled=True),
    )
    (
        attn_gain_back,
        query_back,
        key_back,
        value_back,
        out_back,
        mlp_gain_back,
        gate_back,
        up_back,
        down_back,
    ) = kept_weights
    attn_gain_f = attn_gain_back.astype(jnp.float32)
    mlp_gain_f = mlp_gain_back.astype(jnp.float32)
    grad_values = cotangent.astype(jnp.float32)
    grad_down = jnp.einsum("tf,td->fd", mixed, cotangent, preferred_element_type=jnp.float32)
    dmixed = jnp.einsum("td,fd->tf", cotangent, down_back, preferred_element_type=jnp.float32)
    gate_sig = jax.nn.sigmoid(gate_pre)
    dgate = (dmixed * up_pre * gate_sig * (1.0 + gate_pre * (1.0 - gate_sig))).astype(jnp.bfloat16)
    dup = (dmixed * gate_act).astype(jnp.bfloat16)
    grad_gate = jnp.einsum("tk,tf->kf", normed_two, dgate, preferred_element_type=jnp.float32)
    grad_up = jnp.einsum("tk,tf->kf", normed_two, dup, preferred_element_type=jnp.float32)
    dnormed_two = lax.psum(
        jnp.einsum("tf,kf->tk", dgate, gate_back, preferred_element_type=jnp.float32)
        + jnp.einsum("tf,kf->tk", dup, up_back, preferred_element_type=jnp.float32),
        "head",
    )
    dhidden_norm, grad_mlp_gain = norm_back(hidden, inverse_two, mlp_gain_f, dnormed_two)
    dhidden = grad_values + dhidden_norm
    mlp_sums = (grad_mlp_gain, grad_gate, grad_up, grad_down)
    dhidden_low = dhidden.astype(jnp.bfloat16)
    grad_out = jnp.einsum("tc,td->cd", attn_mix, dhidden_low, preferred_element_type=jnp.float32)
    dmix = jnp.einsum(
        "td,cd->tc", dhidden_low, out_back, preferred_element_type=jnp.float32
    ).astype(jnp.bfloat16)
    all_dmix = lax.all_gather(dmix, "seq", axis=0, tiled=True)

    def backward_block(carry, packed):
        key_accum, value_accum = carry
        query_block, grad_block, block_start = packed
        weights = weights_for(query_block, block_start)
        grad_weights = jnp.einsum(
            "qhd,khd->hqk", grad_block, value_rows, preferred_element_type=jnp.float32
        )
        grad_scores = (grad_weights * weights * (1.0 - weights)).astype(jnp.bfloat16)
        value_accum = value_accum + jnp.einsum(
            "hqk,qhd->khd",
            weights.astype(jnp.bfloat16),
            grad_block,
            preferred_element_type=jnp.float32,
        )
        key_accum = key_accum + jnp.einsum(
            "hqk,qhd->khd", grad_scores, query_block, preferred_element_type=jnp.float32
        )
        query_part = (
            jnp.einsum("hqk,khd->qhd", grad_scores, key_rows, preferred_element_type=jnp.float32)
            * score_scale
        )
        return ((key_accum, value_accum), query_part.reshape(block_rows, local_width))

    zero_rows = jnp.zeros((row_count, local_heads, HD), jnp.float32)
    block_starts = jnp.arange(block_count, dtype=jnp.int32) * block_rows
    (key_accum, value_accum), query_parts = lax.scan(
        backward_block,
        (zero_rows, zero_rows),
        (
            all_queries.reshape(block_count, block_rows, local_heads, HD),
            all_dmix.reshape(block_count, block_rows, local_heads, HD),
            block_starts,
        ),
    )
    query_sum = lax.psum_scatter(
        query_parts.reshape(total_rows, local_width), "seq", scatter_dimension=0, tiled=True
    )
    dquery_pre = (
        unrotary(query_sum.reshape(row_count, local_heads, HD), cos_table, sin_table)
        .reshape(row_count, local_width)
        .astype(jnp.bfloat16)
    )
    dkey_pre = (
        unrotary(key_accum * score_scale, cos_table, sin_table)
        .reshape(row_count, local_width)
        .astype(jnp.bfloat16)
    )
    dvalue = value_accum.reshape(row_count, local_width).astype(jnp.bfloat16)
    grad_query = jnp.einsum("tk,tc->kc", normed_one, dquery_pre, preferred_element_type=jnp.float32)
    grad_key = jnp.einsum("tk,tc->kc", normed_one, dkey_pre, preferred_element_type=jnp.float32)
    grad_value = jnp.einsum("tk,tc->kc", normed_one, dvalue, preferred_element_type=jnp.float32)
    dnormed_one = lax.psum(
        jnp.einsum("tc,kc->tk", dquery_pre, query_back, preferred_element_type=jnp.float32)
        + jnp.einsum("tc,kc->tk", dkey_pre, key_back, preferred_element_type=jnp.float32)
        + jnp.einsum("tc,kc->tk", dvalue, value_back, preferred_element_type=jnp.float32),
        "head",
    )
    dinput_norm, grad_attn_gain = norm_back(token_values, inverse_one, attn_gain_f, dnormed_one)
    input_grad = (dhidden + dinput_norm).astype(jnp.bfloat16)
    every_sum = (
        lax.psum_scatter(grad_attn_gain, "seq", scatter_dimension=0, tiled=True),
        lax.psum_scatter(grad_query, "seq", scatter_dimension=0, tiled=True),
        lax.psum_scatter(grad_key, "seq", scatter_dimension=0, tiled=True),
        lax.psum_scatter(grad_value, "seq", scatter_dimension=0, tiled=True),
        lax.psum_scatter(grad_out, "seq", scatter_dimension=1, tiled=True),
        lax.psum_scatter(grad_mlp_gain, "seq", scatter_dimension=0, tiled=True),
        lax.psum_scatter(grad_gate, "seq", scatter_dimension=0, tiled=True),
        lax.psum_scatter(grad_up, "seq", scatter_dimension=0, tiled=True),
        lax.psum_scatter(grad_down, "seq", scatter_dimension=1, tiled=True),
    )
    attn_sums = every_sum[:5]
    mlp_sums = every_sum[5:]
    return (
        result,
        input_grad,
        attn_sums[0],
        attn_sums[1],
        attn_sums[2],
        attn_sums[3],
        attn_sums[4],
        mlp_sums[0],
        mlp_sums[1],
        mlp_sums[2],
        mlp_sums[3],
    )


class Net:
    def __init__(self, send, receive):
        self.send, self.receive, self.sends, self.receives, self.lots = send, receive, 0, 0, []

    def lot(self, *args, **options):
        return Lot(self, *args, **options)

    def finish(self):
        for lot in self.lots:
            lot.sent()


class Lot:
    def __init__(self, net, indices, describe, bulk, arrival=None, apart=False):
        self.net, self.describe, self.bulk, self.arrival, self.apart = net, describe, bulk, arrival, apart
        self.place = {j: net.receives + i for i, j in enumerate(indices)}
        self.low = min(indices)
        self.send_base, self.receive_base = net.sends, net.receives
        net.receives += len(indices)
        net.sends += len(indices) if apart else 1
        self.started, self.open = set(), set()
        net.lots.append(self)

    def receive_at(self, j):
        return self.net.receive.at[self.receive_base + (j - self.low)]

    def send_at(self, j):
        return self.net.send.at[self.send_base + (j - self.low if self.apart else 0)]

    def start(self, j, pieces=None):
        described = self.describe(j)
        for i, (source, target, device) in enumerate(described if isinstance(described, list) else [described]):
            if pieces is None or i in pieces:
                pltpu.make_async_remote_copy(
                    src_ref=source,
                    dst_ref=target,
                    send_sem=self.send_at(j),
                    recv_sem=self.receive_at(j),
                    device_id=device,
                    device_id_type=MESH,
                ).start()
        if isinstance(j, int):
            self.mark((j,))

    def mark(self, indices):
        self.started.update(indices)
        self.open.update(indices if self.apart else (self.low,))

    def arrived(self, j):
        described = self.describe(j)
        target = self.arrival(j) if self.arrival else described[1]
        self.wait(target, self.receive_at(j))

    def wait(self, like, sem):
        pltpu.make_async_copy(like, like, sem).wait()

    def sent(self, j=None):
        for k in sorted(self.open) if j is None else [j] if j in self.open else []:
            self.open.remove(k)
            self.wait(self.bulk(k) if self.apart else self.bulk, self.send_at(k))


class Keep:
    def __init__(self, sems):
        self.sems, self.count = sems, 0

    def put(self, source, target):
        copy = pltpu.make_async_copy(source, target, self.sems.at[self.count])
        self.count += 1
        copy.start()
        return copy


class Where:
    def __init__(self, groups, ranks):
        self.s, self.h = lax.axis_index("seq"), lax.axis_index("head")
        self.g, self.r = self.s // ranks, self.s % ranks
        self.groups, self.ranks = groups, ranks
        self.q = self.h % 2 * 2 + self.h // 2

    def along(self, m):
        return (self.s ^ (m * self.ranks), self.h)

    def beside(self):
        return (self.s ^ 1, self.h)

    def across(self):
        return (self.s, self.h ^ 2)

    def near(self):
        return (self.s, self.h ^ 1)


def lane(start, size):
    return pl.ds(pl.multiple_of(start, 128), size)


def row(start, size):
    return pl.ds(pl.multiple_of(start, size), size)


def each(count, step):
    def body(i, carry):
        step(i)
        return carry

    lax.fori_loop(0, count, body, 0)


class Spread:
    def __init__(self, net, at, buffer, quarter, own=None):
        self.at, self.buffer, self.quarter, self.shared = at, buffer, quarter, own is not None
        self.size = quarter // PIECES

        def along(j):
            m, p = j // PIECES, j % PIECES
            if m == 3:
                return (self.block(2, 0, p), self.block(2, 0, p), at.along(1))
            first = self.block(0, 0, p) if own is None else own.at[row(at.q * quarter + p * self.size, self.size), :]
            return (first, self.block(0, 0, p), at.along(m))

        def moved(k, device):
            def describe(j):
                block = self.block(j // PIECES, k, j % PIECES)
                return (block, block, device)

            return describe

        low = 1 if self.shared else 0
        indices = range(low * PIECES, 4 * PIECES)
        some = buffer.at[0 : (4 - low) * quarter, :]
        self.z = net.lot(range(PIECES, 4 * PIECES), along, buffer.at[0 : 3 * quarter, :])
        self.x = net.lot(indices, moved(0, at.across()), some)

        def near(m):
            blocks = [self.block(m, k, p) for k in (0, 1) for p in range(PIECES)]
            return [(block, block, at.near()) for block in blocks]

        self.n = net.lot(
            range(low, 4), near, buffer.at[0 : 2 * (4 - low) * quarter, :], lambda m: buffer.at[0 : 2 * quarter, :]
        )

    def block(self, m, k, p):
        at = self.at
        start = ((at.g ^ m) * 4 + (at.q ^ k)) * self.quarter + p * self.size
        return self.buffer.at[row(start, self.size), :]

    def pass_on(self, j):
        self.x.start(j)
        self.n.start(j // PIECES, (j % PIECES,))

    def start(self, m):
        for p in range(PIECES):
            self.z.start(m * PIECES + p)

    def start_own(self):
        for p in range(PIECES):
            self.pass_on(p)

    def arrive(self, m):
        for p in range(PIECES):
            j = m * PIECES + p
            self.z.arrived(j)
            if m == 2:
                self.z.start(3 * PIECES + p)
            self.pass_on(j)

    def second(self, m):
        for p in range(PIECES):
            self.x.arrived(m * PIECES + p)
            self.n.start(m, (PIECES + p,))

    def ready(self, m):
        self.n.arrived(m)

    def sent(self):
        for lot in (self.z, self.x, self.n):
            lot.sent()


class Collect:
    def __init__(self, net, at, refs, quarter, out):
        self.at, self.quarter, self.out = at, quarter, out
        self.size = quarter // PIECES
        self.part, self.near, self.xin, self.zin = refs
        self.a = net.lot(range(4), lambda m: (self.pair(m), self.near.at[at.g ^ m], at.near()), self.near)

        def across(j):
            m, few = j // PIECES, row(j % PIECES * self.size, self.size)
            return (self.part.at[self.rows(m, 1, j % PIECES), :], self.xin.at[at.g ^ m, few, :], at.across())

        hops = {3: (0, 1), 2: (2, 2), 1: (1, 1)}

        def along(j):
            (slot, hop), few = hops[j // PIECES], row(j % PIECES * self.size, self.size)
            return (self.part.at[self.rows(j // PIECES, 0, j % PIECES), :], self.zin.at[slot, few, :], at.along(hop))

        self.b = net.lot(range(4 * PIECES), across, self.xin)
        self.z = net.lot(range(PIECES, 4 * PIECES), along, self.zin)

    def start_of(self, m, k, p):
        at = self.at
        return ((at.g ^ m) * 4 + (at.q ^ k)) * self.quarter + p * self.size

    def rows(self, m, k, p):
        return row(self.start_of(m, k, p), self.size)

    def pair(self, m):
        at = self.at
        return self.part.at[row(((at.g ^ m) * 2 + (1 - at.h % 2)) * 2 * self.quarter, 2 * self.quarter), :]

    def first(self, m):
        self.a.start(m)

    def lines(self, few, k):
        start = (self.at.h // 2 ^ k) * self.quarter
        return pl.ds(pl.multiple_of(start + few.start, 16), few.size)

    def slices(self, m, k, p, step):
        start = self.start_of(m, k, p)
        each(self.size // 16, lambda i: step(row(start + i * 16, 16), row(p * self.size + i * 16, 16)))

    def second(self, m):
        d = self.at.g ^ m
        self.a.arrived(m)

        def step(rows, few):
            total = self.part[rows, :].astype(F32) + self.near[d, self.lines(few, 1), :].astype(F32)
            self.part[rows, :] = total.astype(BF16)

        for p in range(PIECES):
            self.slices(m, 1, p, step)
            self.b.start(m * PIECES + p)

    def third(self, m):
        d = self.at.g ^ m

        def step(rows, few):
            total = self.part[rows, :].astype(F32) + self.near[d, self.lines(few, 0), :].astype(F32)
            total += self.xin[d, few, :].astype(F32)
            if m == 2:
                total += self.zin[0, few, :].astype(F32)
            if m:
                self.part[rows, :] = total.astype(BF16)
            else:
                self.out[few, :] = total

        for p in range(PIECES):
            self.b.arrived(m * PIECES + p)
            if m == 2:
                self.z.arrived(3 * PIECES + p)
            self.slices(m, 0, p, step)
            if m:
                self.z.start(m * PIECES + p)

    def last(self):
        self.third(0)
        for m in (1, 2):
            for p in range(PIECES):
                self.z.arrived(m * PIECES + p)

    def total(self, few):
        return self.out[few, :] + self.zin[1, few, :].astype(F32) + self.zin[2, few, :].astype(F32)

    def produce(self, work):
        def step(i):
            m = 3 - i
            work(m)
            self.first(m)

            @pl.when(i > 0)
            def _():
                self.second(m + 1)

        each(4, step)
        self.a.mark(range(4))
        self.b.mark(range(PIECES, 4 * PIECES))

    def sent(self):
        for lot in (self.a, self.b, self.z):
            lot.sent()


class Turn:
    def __init__(self, net, keep, at, source, view, blocks):
        self.keep, self.at, self.source, self.view, self.blocks = keep, at, source, view, blocks
        self.z, self.y, self.own = [], [], {}
        for b, (items, place, several) in enumerate(blocks):

            def out(m, items=items):
                return [(source(i, at.g ^ m), view(i, at.s), at.along(m)) for i in items]

            def beside(_, items=items, place=place):
                own = [(source(i, at.g), view(i, at.s), at.beside()) for i in items]
                others = [place(at.s ^ (m * at.ranks)) for m in (1, 2, 3)]
                return own + [(block, block, at.beside()) for block in others]

            def arrival(m, place=place):
                return place(at.s ^ (m * at.ranks))

            self.z.append(net.lot((1, 2, 3), out, several(3), arrival))
            self.y.append(net.lot((0,), beside, several(4), lambda _, several=several: several(4)))

    def start(self, m, b=0, pieces=None):
        self.z[b].start(m, pieces)

    def mine(self, b=0):
        items = self.blocks[b][0]
        for i in items:
            self.own[i] = self.keep.put(self.source(i, self.at.g), self.view(i, self.at.s))
        self.y[b].start(0, range(len(items)))

    def pass_on(self, m, b=0):
        self.z[b].arrived(m)
        self.y[b].start(0, (len(self.blocks[b][0]) + m - 1,))

    def ready(self, b=0):
        for i in self.blocks[b][0]:
            self.own[i].wait()
        self.y[b].arrived(0)

    def sent(self, b=0):
        self.y[b].sent()


def dot(a, b):
    return jnp.dot(a, b, preferred_element_type=F32)


def dot_nt(a, b):
    return lax.dot_general(a, b, (((1,), (1,)), ((), ())), preferred_element_type=F32)


def dot_tn(a, b):
    return lax.dot_general(a, b, (((0,), (0,)), ((), ())), preferred_element_type=F32)


def turned(values, cos_table, sin_table):
    return values * cos_table + pltpu.roll(values, HD // 2, 1) * sin_table


def mean_square(values):
    return jnp.mean(values * values, axis=1, keepdims=True)


def layer_body(groups, ranks, *refs):
    (tok, cot, gain_one, gain_two, qw, kw, vw, ow, gw, uw, dw) = refs[:11]
    (result_out, rows_out, gains_out, q_out, k_out, v_out, o_out, g_out, u_out, d_out) = refs[11:21]
    (
        gains, gains_all, cosines, sines, rows_one, rows_cot, rows_two, rows_dh, w_qkv, w_o, w_gu, w_d, queries, pairs, mix, dqkv, accum, pair_send,
        pair_in, mixed, dgu, dmixed, own_x, hidden, dhidden, summed, part_a, near_a, xin_a, zin_a, part_b, near_b, xin_b, zin_b,
        in_gu, in_d, in_qkv, in_o, gain_part, gain_in, gain_mid, gain_near, result_own, rows_own, send, receive, local,
    ) = refs[21:]
    at = Where(groups, ranks)
    s, h, g, r = at.s, at.h, at.g, at.r
    shards = groups * ranks
    count, depth = tok.shape
    quarter = count // 4
    width = gains.shape[1]
    units = gw.shape[1] // groups
    bounds = [units * sum(PARTS[:b]) // sum(PARTS) for b in range(len(PARTS) + 1)]
    lanes_of = [slice(a, b) for a, b in zip(bounds, bounds[1:])]
    pairs_of = [slice(2 * a, 2 * b) for a, b in zip(bounds, bounds[1:])]
    size_of = [b - a for a, b in zip(bounds, bounds[1:])]

    def gate_up(b, i):
        start = pairs_of[b].start + i * size_of[b]
        return slice(start, start + size_of[b])

    total_rows = count * shards
    score_scale = 1.0 / math.sqrt(HD)
    score_shift = math.log(total_rows)
    peers = [(s ^ m, h) for m in range(1, shards)] + [(s, h ^ m) for m in range(1, 4)]
    barrier = pltpu.get_barrier_semaphore()
    for peer in peers:
        pl.semaphore_signal(barrier, inc=1, device_id=peer, device_id_type=MESH)
    pl.semaphore_wait(barrier, len(peers))
    net, keep = Net(send, receive), Keep(local)

    def chunk(m):
        return row((g ^ m) * count, count)

    def shard_rows(shard):
        return row(shard * width, width)

    def columns_of(shard):
        return lane(shard * width, width)

    turn_qkv = Turn(
        net, keep, at,
        lambda i, group: (qw, kw, vw)[i].at[:, lane(group * HD, HD)],
        lambda i, shard: w_qkv.at[shard_rows(shard), i * HD : (i + 1) * HD],
        [((0, 1, 2), lambda shard: w_qkv.at[shard_rows(shard), :], lambda n: w_qkv.at[0 : n * width, :])],
    )
    few = width // 2
    turn_gu = Turn(
        net, keep, at,
        lambda i, group: (gw, uw)[i // 2 % 2].at[
            i % 2 * few : (i % 2 + 1) * few, lane(group * units + lanes_of[i // 4].start, size_of[i // 4])
        ],
        lambda i, shard: w_gu.at[row(shard * width + i % 2 * few, few), gate_up(i // 4, i // 2 % 2)],
        [
            (range(4 * b, 4 * b + 4), lambda shard, p=p: w_gu.at[shard_rows(shard), p], lambda n, p=p: w_gu.at[0 : n * width, p])
            for b, p in enumerate(pairs_of)
        ],
    )
    turn_o = Turn(
        net, keep, at,
        lambda i, group: ow.at[row(group * HD, HD), :],
        lambda i, shard: w_o.at[:, columns_of(shard)],
        [((0,), lambda shard: w_o.at[:, columns_of(shard)], lambda n: w_o.at[:, 0 : n * width])],
    )
    turn_d = Turn(
        net, keep, at,
        lambda i, group: dw.at[lane(group * units + lanes_of[i].start, size_of[i]), :],
        lambda i, shard: w_d.at[lanes_of[i], columns_of(shard)],
        [
            ((b,), lambda shard, p=p: w_d.at[p, columns_of(shard)], lambda n, p=p: w_d.at[p, 0 : n * width])
            for b, p in enumerate(lanes_of)
        ],
    )

    gain_slot = gains_all.at[:, columns_of(s)]
    gain_moves = net.lot(
        (0,), lambda _: [(gains, gain_slot, (s ^ m, h)) for m in range(1, shards)], gain_in, lambda _: gain_in
    )
    strip = row(at.q * quarter, quarter)
    mine_start = (g * 4 + at.q) * quarter
    span = ranks * count
    one = Spread(net, at, rows_dh, quarter, tok)
    grad = Spread(net, at, rows_cot, quarter, cot)
    two = Spread(net, at, rows_two, quarter)
    three = Spread(net, at, rows_dh, quarter)
    set_a, set_b = (part_a, near_a, xin_a, zin_a), (part_b, near_b, xin_b, zin_b)
    first = Collect(net, at, set_a, quarter, summed)
    second = Collect(net, at, set_a, quarter, summed)
    out_sum = Collect(net, at, set_b, quarter, summed)
    third = Collect(net, at, set_a, quarter, summed)

    def clear(i):
        rows = row(i * 64, 64)
        accum[rows, :] = jnp.zeros_like(accum[rows, :])

    def tables(i):
        rows = row(i * 64, 64)
        first_row = (i // (count // 64) * ranks + r) * count + i % (count // 64) * 64
        places = (first_row + lax.broadcasted_iota(jnp.int32, (64, HD), 0)).astype(F32)
        lanes = lax.broadcasted_iota(jnp.int32, (64, HD), 1)
        low_half = lanes < HD // 2
        order = jnp.where(low_half, lanes, lanes - HD // 2).astype(F32)
        angles = places * jnp.exp(order * (-math.log(10000.0) / (HD // 2)))
        cosines[rows, :] = jnp.cos(angles)
        sines[rows, :] = jnp.where(low_half, -jnp.sin(angles), jnp.sin(angles))

    def norm_one(m):
        def some(i):
            rows = row((g ^ m) * count + i * 32, 32)
            values = rows_dh[rows, :].astype(F32)
            inverse = lax.rsqrt(mean_square(values) + epsilon)
            rows_one[rows, :] = (values * inverse * gains_all[0:1, :]).astype(BF16)

        each(count // 32, some)

    def own_place(m):
        return row(((g ^ m) * ranks + r) * count, count)

    pair_moves = net.lot(
        range(4),
        lambda m: (pairs.at[own_place(m), :], pairs.at[own_place(m), :], at.beside()),
        pairs.at[0 : groups * count, :],
    )

    def project(m):
        rows, place = chunk(m), own_place(m)
        heads = dot(rows_one[rows, :], w_qkv[...])
        cos_part, sin_part = cosines[rows, :], sines[rows, :]
        queries[rows, :] = turned(heads[:, :HD], cos_part, sin_part).astype(BF16)
        pairs[place, :HD] = turned(heads[:, HD : 2 * HD], cos_part, sin_part).astype(BF16)
        pairs[place, HD:] = heads[:, 2 * HD :].astype(BF16)
        pair_moves.start(m)

    def weights_of(m, j, query):
        keys = pairs[row(j * span, span), :HD]
        scores = dot_nt(query, keys) * score_scale - score_shift
        q_place = ((g ^ m) * ranks + r) * count + lax.broadcasted_iota(jnp.int32, (count, span), 0)
        k_place = j * span + lax.broadcasted_iota(jnp.int32, (count, span), 1)
        return jnp.where(k_place <= q_place, jax.nn.sigmoid(scores), 0.0)

    def attend(m):
        rows = chunk(m)
        query = queries[rows, :]

        def step(j, total):
            weight = weights_of(m, j, query).astype(BF16)
            return total + dot(weight, pairs[row(j * span, span), HD:])

        total = lax.fori_loop(0, (g ^ m) + 1, step, jnp.zeros((count, HD), F32))
        low = total.astype(BF16)
        mix[rows, :] = low

        if m == 3:
            turn_o.ready()
        part_a[rows, :] = dot(low, w_o[...]).astype(BF16)

    def norm_two(i):
        few = row(i * 16, 16)
        values = own_x[few, :].astype(F32) + first.total(few)
        hidden[few, :] = values
        inverse = lax.rsqrt(mean_square(values) + epsilon)
        rows_two[row(mine_start + i * 16, 16), :] = (values * inverse * gains_all[1:2, :]).astype(BF16)

    def early(m, b):
        lanes = lanes_of[b]
        dmixed[chunk(m), lanes] = dot_nt(rows_cot[chunk(m), :], w_d[lanes, :])

    def feed(m, b):
        rows = chunk(m)
        lanes, pair, size = lanes_of[b], pairs_of[b], size_of[b]
        both = dot(rows_two[rows, :], w_gu[:, pair])
        gate, up = both[:, :size], both[:, size:]
        sig = jax.nn.sigmoid(gate)
        act = gate * sig
        mixed[rows, lanes] = (act * up).astype(BF16)
        back = dmixed[rows, lanes]
        dgu[rows, gate_up(b, 0)] = (back * up * sig * (1.0 + gate * (1.0 - sig))).astype(BF16)
        dgu[rows, gate_up(b, 1)] = (back * act).astype(BF16)
        total = dot_nt(dgu[rows, pair], w_gu[:, pair])
        if b:
            total += part_a[rows, :].astype(F32)
        part_a[rows, :] = total.astype(BF16)

    def out_part(m, b):
        rows = chunk(m)
        lanes = lanes_of[b]
        total = dot(mixed[rows, lanes], w_d[lanes, :])
        if b:
            total += part_b[rows, :].astype(F32)
        part_b[rows, :] = total.astype(BF16)

    def halves(m, work, lot):
        d = g ^ m

        def step(k):
            work(d * ranks + (r ^ 1 ^ k))

            @pl.when(k == 0)
            def _():
                lot.start(m)

        each(2, step)

    def several(groups_, work, lot):
        first_, last_ = groups_
        each(first_ - last_ + 1, lambda i: halves(first_ - i, work, lot))
        lot.mark(range(last_, first_ + 1))

    def beside(source, target, bulk):
        def describe(m):
            d = g ^ m
            return (source(d * ranks + (r ^ 1)), target(d), at.beside())

        return net.lot(range(4), describe, bulk)

    moves_gu = [
        [
            beside(lambda shard, p=p: w_gu.at[shard_rows(shard), p], lambda d, p=p: in_gu.at[d, :, p], in_gu.at[:, :, p])
            for p in (gate_up(b, 0), gate_up(b, 1))
        ]
        for b in range(len(PARTS))
    ]
    moves_d = [
        beside(lambda shard, p=p: w_d.at[p, columns_of(shard)], lambda d, p=p: in_d.at[d, p, :], in_d.at[:, p, :])
        for p in lanes_of
    ]
    moves_qkv = beside(lambda shard: w_qkv.at[shard_rows(shard), :], lambda d: in_qkv.at[d], in_qkv)
    moves_o = beside(lambda shard: w_o.at[:, columns_of(shard)], lambda d: in_o.at[d], in_o)

    def grads_gu(groups_, b, i):
        def work(shard):
            w_gu[shard_rows(shard), gate_up(b, i)] = dot_tn(
                rows_two[:, columns_of(shard)], dgu[:, gate_up(b, i)]
            ).astype(BF16)

        several(groups_, work, moves_gu[b][i])

    def grads_d(groups_, b):
        def work(shard):
            columns = columns_of(shard)
            w_d[lanes_of[b], columns] = dot_tn(mixed[:, lanes_of[b]], rows_cot[:, columns]).astype(BF16)

        several(groups_, work, moves_d[b])

    def grads_o(groups_):
        def work(shard):
            columns = columns_of(shard)
            w_o[:, columns] = dot_tn(mix[...], rows_dh[:, columns]).astype(BF16)

        several(groups_, work, moves_o)

    def grads_qkv(groups_):
        def work(shard):
            w_qkv[shard_rows(shard), :] = dot_tn(rows_one[:, columns_of(shard)], dqkv[...]).astype(BF16)

        several(groups_, work, moves_qkv)

    final, final_own = [], []

    def owners(moves, several):
        pieces = [(a, b, at.along(m)) for m in (1, 2, 3) for a, b in moves(m)]
        lot = net.lot((0,), lambda _: pieces, several, lambda _: several)
        final.append(lot)

        def give(m, i=None):
            blocks = moves(m)
            for k in range(len(blocks)) if i is None else (i,):
                if m:
                    lot.start(0, ((m - 1) * len(blocks) + k,))
                else:
                    final_own.append(keep.put(*blocks[k]))

        return give

    def shard_of(m):
        return (g ^ m) * ranks + r

    def gate_up_moves(b):
        def moves(m):
            for i, out in enumerate((g_out, u_out)):
                place = out.at[:, lane(g * units + lanes_of[b].start, size_of[b])]
                yield (w_gu.at[shard_rows(shard_of(m)), gate_up(b, i)], place)

        return lambda m: list(moves(m))

    def down_moves(b):
        place = d_out.at[lane(g * units + lanes_of[b].start, size_of[b]), :]
        return lambda m: [(w_d.at[lanes_of[b], columns_of(shard_of(m))], place)]

    def qkv_moves(m):
        rows = shard_rows(shard_of(m))
        return [
            (w_qkv.at[rows, i * HD : (i + 1) * HD], out.at[:, lane(g * HD, HD)])
            for i, out in enumerate((q_out, k_out, v_out))
        ]

    give_gu = [owners(gate_up_moves(b), w_gu.at[0 : 3 * width, p]) for b, p in enumerate(pairs_of)]
    give_d = [owners(down_moves(b), w_d.at[p, 0 : 3 * width]) for b, p in enumerate(lanes_of)]
    give_qkv = owners(qkv_moves, w_qkv.at[0 : 3 * width, :])
    give_o = owners(
        lambda m: [(w_o.at[:, columns_of(shard_of(m))], o_out.at[row(g * HD, HD), :])], w_o.at[:, 0 : 3 * width]
    )

    def sums(m, lot, mine_of, other_of, size):
        lot.arrived(m)

        def step(i):
            a, rows, lanes = mine_of(i)
            b, d, few, others = other_of(i)
            a[rows, lanes] = (a[rows, lanes].astype(F32) + b[d, few, others].astype(F32)).astype(BF16)

        each(size // 32, step)

    def sums_gu(m, b, i):
        d, p = g ^ m, gate_up(b, i)
        start = (d * ranks + r) * width
        sums(
            m, moves_gu[b][i],
            lambda k: (w_gu, row(start + k * 32, 32), p), lambda k: (in_gu, d, row(k * 32, 32), p), width,
        )
        give_gu[b](m, i)

    def sums_d(m, b):
        d, base = g ^ m, lanes_of[b].start
        columns = columns_of(d * ranks + r)
        sums(
            m, moves_d[b],
            lambda i: (w_d, row(base + i * 32, 32), columns),
            lambda i: (in_d, d, row(base + i * 32, 32), slice(None)), size_of[b],
        )
        give_d[b](m)

    def sums_o(m):
        d = g ^ m
        columns = columns_of(d * ranks + r)
        sums(
            m, moves_o,
            lambda i: (w_o, row(i * 32, 32), columns), lambda i: (in_o, d, row(i * 32, 32), slice(None)), HD,
        )
        give_o(m)

    def sums_qkv(m):
        d = g ^ m
        start = (d * ranks + r) * width
        sums(
            m, moves_qkv,
            lambda i: (w_qkv, row(start + i * 32, 32), slice(None)),
            lambda i: (in_qkv, d, row(i * 32, 32), slice(None)), width,
        )
        give_qkv(m)

    def back_two(i, gain_grad):
        few = row(i * 16, 16)
        own = row(mine_start + i * 16, 16)
        upstream, values = second.total(few), hidden[few, :]
        inverse = lax.rsqrt(mean_square(values) + epsilon)
        scaled = upstream * gains_all[1:2, :]
        back = inverse * scaled - values * (inverse * inverse * inverse) * jnp.mean(
            scaled * values, axis=1, keepdims=True
        )
        total = rows_cot[own, :].astype(F32) + back
        dhidden[few, :] = total
        rows_dh[own, :] = total.astype(BF16)
        return gain_grad + jnp.sum(upstream * values * inverse, axis=0, keepdims=True)

    def attend_back(m):
        three.ready(m)
        rows = chunk(m)
        query = queries[rows, :]
        dm = dot_nt(rows_dh[rows, :], w_o[...]).astype(BF16)

        def step(j, total):
            block = row(j * span, span)
            weight = weights_of(m, j, query)
            dweight = dot_nt(dm, pairs[block, HD:])
            dscore = (dweight * weight * (1.0 - weight)).astype(BF16)
            accum[block, HD:] += dot_tn(weight.astype(BF16), dm)
            accum[block, :HD] += dot_tn(dscore, query)
            return total + dot(dscore, pairs[block, :HD])

        total = lax.fori_loop(0, (g ^ m) + 1, step, jnp.zeros((count, HD), F32))
        dqkv[rows, :HD] = turned(total * score_scale, cosines[rows, :], -sines[rows, :]).astype(BF16)

    pair_back = net.lot(range(4), lambda m: (pair_send.at[g ^ m], pair_in.at[g ^ m], at.beside()), pair_send)

    def send_pair(m):
        d = g ^ m
        rows = row((d * ranks + (r ^ 1)) * count, count)
        pair_send[d] = accum[rows, :].astype(BF16)
        pair_back.start(m)

    def back_from_end(i):
        m = g ^ (groups - 1 - i)
        attend_back(m)
        send_pair(m)

    def back_one(m):
        d = g ^ m
        rows = chunk(m)
        pair_back.arrived(m)
        both = accum[own_place(m), :] + pair_in[d].astype(F32)
        dqkv[rows, HD : 2 * HD] = turned(both[:, :HD] * score_scale, cosines[rows, :], -sines[rows, :]).astype(BF16)
        dqkv[rows, 2 * HD :] = both[:, HD:].astype(BF16)
        part_a[rows, :] = dot_nt(dqkv[rows, :], w_qkv[...]).astype(BF16)

    ends = {}

    def share(i, source, target):
        place = target.at[strip, :]
        final_own.append(keep.put(source, place))
        lot = net.lot((0, 1), lambda j: (source, place, (at.near(), at.across())[j]), target.at[0 : 2 * quarter, :])
        lot.start(0)
        lot.start(1)
        ends[i] = (lot, target)

    def relay(i):
        lot, target = ends[i]
        lot.arrived(1)
        final.append(lot)
        block = target.at[row((at.q ^ 1) * quarter, quarter), :]
        on = net.lot((0,), lambda j: (block, block, at.near()), block)
        on.start(0)
        final.append(on)

    def result_rows(i):
        few = row(i * 16, 16)
        result_own[few, :] = (hidden[few, :] + out_sum.total(few)).astype(BF16)

    def back_rows(i, gain_grad):
        few = row(i * 16, 16)
        upstream, values = third.total(few), own_x[few, :].astype(F32)
        inverse = lax.rsqrt(mean_square(values) + epsilon)
        scaled = upstream * gains_all[0:1, :]
        back = inverse * scaled - values * (inverse * inverse * inverse) * jnp.mean(
            scaled * values, axis=1, keepdims=True
        )
        rows_own[few, :] = (dhidden[few, :] + back).astype(BF16)
        return gain_grad + jnp.sum(upstream * values * inverse, axis=0, keepdims=True)

    gain_sums = net.lot(
        (0,),
        lambda _: [(gain_part.at[:, columns_of(s ^ m)], gain_in.at[m - 1], (s ^ m, h)) for m in range(1, shards)],
        gain_in,
        lambda _: gain_in,
    )
    gain_ends = net.lot(
        (0,),
        lambda _: [(gain_mid, gain_near.at[m - 1], (s, h ^ m)) for m in range(1, 4)],
        gain_near,
        lambda _: gain_near,
    )
    gains[...] = jnp.zeros_like(gains)
    gains[0:1, :] = gain_one[...].astype(F32).reshape(1, width)
    gains[1:2, :] = gain_two[...].astype(F32).reshape(1, width)
    gain_moves.start(0)
    gain_own = keep.put(gains, gain_slot)
    own_rows = keep.put(tok, rows_dh.at[chunk(0), :])
    own_strip = keep.put(tok.at[strip, :], own_x)
    own_cot = keep.put(cot, rows_cot.at[chunk(0), :])
    turn_qkv.start(3)
    one.start(2)
    one.start(1)
    turn_qkv.start(1)
    turn_o.start(1)
    one.arrive(1)
    turn_qkv.mine()
    turn_qkv.start(2)
    gain_part[...] = jnp.zeros_like(gain_part)
    each(total_rows // 64, clear)
    each(groups * count // 64, tables)
    grad.z.start(2 * PIECES + 0)
    one.arrive(2)
    turn_o.pass_on(1)
    turn_gu.start(1, 0, (1,))
    turn_gu.start(3, 0, (2,))
    turn_o.start(3)
    gain_own.wait()
    gain_moves.arrived(0)
    own_rows.wait()
    own_strip.wait()
    norm_one(0)
    turn_qkv.pass_on(3)
    one.second(2)
    turn_o.start(2)
    turn_qkv.pass_on(1)
    grad.z.start(2 * PIECES + 1)
    turn_gu.start(2, 0, (3,))
    turn_d.start(1, 0)
    one.ready(2)
    norm_one(2)
    grad.z.start(1 * PIECES + 1)
    turn_qkv.pass_on(2)
    turn_gu.start(1, 0, (2,))
    one.arrive(3)
    turn_o.mine()
    one.second(1)
    turn_qkv.ready()
    project(0)
    turn_d.start(2, 1)
    one.ready(1)
    norm_one(1)
    project(1)
    project(2)
    one.second(3)
    one.ready(3)
    norm_one(3)
    project(3)
    turn_d.start(3, 0)
    turn_gu.start(1, 0, (0,))
    turn_o.pass_on(2)
    turn_d.start(2, 0)
    turn_o.pass_on(3)
    grad.arrive(2)
    for m in (0, 1, 2, 3):
        pair_moves.arrived(m)
    attend(3)
    first.first(3)
    attend(2)
    first.first(2)
    grad.z.start(1 * PIECES + 0)
    first.second(3)
    turn_d.start(3, 1)
    turn_d.mine(1)
    first.second(2)
    attend(1)
    first.first(1)
    turn_gu.mine(1)
    turn_gu.start(3, 0, (0,))
    first.third(3)
    grad.arrive(3)
    turn_d.pass_on(2, 1)
    turn_d.pass_on(1, 0)
    first.second(1)
    first.third(2)
    grad.second(2)
    attend(0)
    first.first(0)
    turn_d.pass_on(2, 0)
    turn_gu.start(3, 0, (3,))
    first.third(1)
    turn_gu.start(2, 0, (1,))
    turn_d.pass_on(3, 1)
    turn_gu.start(3, 0, (1,))
    turn_gu.start(2, 0, (2,))
    turn_d.mine(0)
    turn_d.start(1, 1)
    turn_gu.start(2, 0, (0,))
    turn_gu.start(1, 0, (3,))
    turn_gu.start(1, 1, (1, 0))
    first.second(0)
    grad.arrive(1)
    turn_d.pass_on(3, 0)
    first.last()
    each(quarter // 16, norm_two)
    two.start(2)
    two.start(1)
    turn_gu.mine(0)
    two.start_own()
    turn_d.pass_on(1, 1)
    turn_gu.start(2, 1, (3,))
    turn_gu.pass_on(1, 0)
    turn_gu.start(1, 1, (2,))
    grad.second(3)
    turn_gu.start(1, 1, (3,))
    two.second(0)
    turn_d.ready(0)
    turn_d.ready(1)
    turn_gu.pass_on(2, 0)
    grad.second(1)
    turn_gu.start(2, 1, (1, 0))
    turn_gu.pass_on(3, 0)
    turn_gu.start(2, 1, (2,))
    own_cot.wait()
    for m in (1, 2, 3):
        grad.ready(m)
    each(4, lambda m: early(m, 0))
    two.arrive(1)
    two.arrive(2)
    turn_gu.pass_on(1, 1)
    two.second(1)
    two.ready(1)
    turn_gu.start(3, 1, (1,))
    two.ready(0)
    two.second(2)
    turn_gu.start(3, 1, (2, 0, 3))
    two.ready(2)
    turn_gu.pass_on(2, 1)
    each(4, lambda m: early(m, 1))
    two.arrive(3)
    turn_gu.ready(0)
    first.sent()
    one.sent()
    each(2, lambda i: feed(1 - i, 0))
    turn_gu.pass_on(3, 1)
    two.second(3)
    feed(2, 0)
    two.ready(3)
    feed(3, 0)
    turn_gu.sent(0)
    grads_gu((3, 3), 0, 0)
    grads_gu((3, 3), 0, 1)
    turn_gu.ready(1)
    each(2, lambda i: (feed(3 - i, 1), second.first(3 - i)))
    second.a.mark((3, 2))
    sums_gu(3, 0, 0)
    grads_gu((2, 2), 0, 0)
    second.second(3)
    each(4, lambda m: out_part(m, 0))
    sums_gu(3, 0, 1)
    second.second(2)
    turn_d.sent(0)
    grads_d((1, 1), 0)
    feed(1, 1)
    second.first(1)
    second.third(3)
    feed(0, 1)
    second.first(0)
    second.second(1)
    turn_gu.sent(1)
    grads_gu((3, 3), 1, 1)
    sums_d(1, 0)
    each(4, lambda m: out_part(m, 1))
    for m in (3, 2, 1, 0):
        out_sum.first(m)
    grads_gu((2, 2), 0, 1)
    second.third(2)
    grads_gu((3, 3), 1, 0)
    second.second(0)
    second.third(1)
    out_sum.second(1)
    sums_gu(2, 0, 0)
    sums_gu(2, 0, 1)
    turn_d.sent(1)
    grads_d((3, 3), 1)
    grads_gu((0, 0), 1, 1)
    second.last()
    gain_part[1:2, :] = lax.fori_loop(0, quarter // 16, back_two, jnp.zeros((1, depth), F32))
    three.start(2)
    three.start(1)
    grads_gu((1, 1), 1, 1)
    grads_gu((1, 1), 0, 1)
    out_sum.second(3)
    grads_d((2, 2), 1)
    three.start_own()
    grads_gu((2, 2), 1, 1)
    grads_d((3, 3), 0)
    sums_gu(3, 1, 0)
    grads_gu((1, 1), 1, 0)
    grads_gu((2, 2), 1, 0)
    out_sum.third(3)
    three.arrive(1)
    three.arrive(2)
    sums_d(3, 1)
    grads_d((0, 0), 0)
    sums_d(3, 0)
    three.second(0)
    grads_gu((0, 0), 0, 1)
    grads_gu((0, 0), 1, 0)
    grads_d((0, 0), 1)
    sums_gu(1, 1, 1)
    sums_gu(3, 1, 1)
    sums_d(2, 1)
    sums_gu(2, 1, 0)
    sums_gu(1, 0, 1)
    sums_gu(2, 1, 1)
    three.arrive(3)
    three.second(2)
    sums_gu(1, 1, 0)
    grads_gu((0, 0), 0, 0)
    three.second(1)
    out_sum.second(2)
    grads_d((2, 2), 0)
    three.second(3)
    each(4, back_from_end)
    pair_back.mark(range(4))
    out_sum.second(0)
    out_sum.third(2)
    sums_gu(0, 1, 1)
    grads_gu((1, 1), 0, 0)
    out_sum.third(1)
    turn_o.sent()
    grads_o((1, 0))
    grads_o((3, 3))
    second.sent()
    third.produce(back_one)
    sums_gu(0, 0, 0)
    turn_qkv.sent()
    grads_qkv((2, 2))
    grads_qkv((3, 3))
    grads_d((1, 1), 1)
    grads_o((2, 2))
    third.third(3)
    sums_o(3)
    third.second(0)
    grads_qkv((1, 1))
    sums_d(2, 0)
    sums_gu(1, 0, 0)
    sums_o(1)
    third.third(2)
    third.third(1)
    sums_qkv(3)
    out_sum.last()
    each(quarter // 16, result_rows)
    share(0, result_own, result_out)
    sums_d(1, 1)
    sums_o(0)
    sums_qkv(2)
    grads_qkv((0, 0))
    third.last()
    gain_part[0:1, :] = lax.fori_loop(0, quarter // 16, back_rows, jnp.zeros((1, depth), F32))
    gain_sums.start(0)
    share(1, rows_own, rows_out)
    sums_o(2)
    sums_qkv(0)
    relay(0)
    sums_gu(0, 1, 0)
    sums_qkv(1)
    sums_gu(0, 0, 1)
    sums_d(0, 1)
    sums_d(0, 0)
    relay(1)
    total = gain_part[:, columns_of(s)]
    gain_sums.arrived(0)
    for m in range(1, shards):
        total += gain_in[m - 1]
    gain_mid[...] = total
    gain_ends.start(0)
    gain_ends.arrived(0)
    for m in range(1, 4):
        total += gain_near[m - 1]
    gains_out[...] = total
    for lot in final:
        lot.arrived(0)
    net.finish()
    for copy in final_own:
        copy.wait()


def rows_plan(
    groups,
    ranks,
    tokens,
    attn_gain,
    query_weight,
    key_weight,
    value_weight,
    out_weight,
    mlp_gain,
    gate_weight,
    up_weight,
    down_weight,
    cotangent,
):
    count, depth = tokens.shape
    shards = groups * ranks
    quarter = count // 4
    width = query_weight.shape[0]
    units = gate_weight.shape[1] // groups
    total_rows = count * shards
    here = groups * count
    ins = (
        tokens, cotangent, attn_gain, mlp_gain,
        query_weight, key_weight, value_weight, out_weight, gate_weight, up_weight, down_weight,
    )
    shape = jax.ShapeDtypeStruct
    hbm, vmem = pl.BlockSpec(memory_space=pl.ANY), pl.BlockSpec(memory_space=pltpu.VMEM)
    owners = (query_weight, key_weight, value_weight, out_weight, gate_weight, up_weight, down_weight)
    outs = [
        shape((count, depth), BF16),
        shape((count, depth), BF16),
        shape((8, width), F32),
        *(shape(w.shape, BF16) for w in owners),
    ]

    def low(*extent):
        return pltpu.VMEM(extent, BF16)

    def full(*extent):
        return pltpu.VMEM(extent, F32)

    def collector():
        return [
            low(here, depth),
            low(groups, 2 * quarter, depth),
            low(groups, quarter, depth),
            low(3, quarter, depth),
        ]

    scratch = [
        full(8, width), full(8, depth), full(here, HD), full(here, HD),
        low(here, depth), low(here, depth), low(here, depth), low(here, depth),
        low(depth, 3 * HD), low(HD, depth), low(depth, 2 * units), low(units, depth),
        low(here, HD), low(total_rows, 2 * HD), low(here, HD), low(here, 3 * HD),
        full(total_rows, 2 * HD), low(groups, count, 2 * HD), low(groups, count, 2 * HD),
        low(here, units), low(here, 2 * units), full(here, units),
        low(quarter, depth), full(quarter, depth), full(quarter, depth), full(quarter, depth),
        *collector(), *collector(),
        low(groups, width, 2 * units), low(groups, units, width), low(groups, width, 3 * HD), low(groups, HD, width),
        full(8, depth), full(shards - 1, 8, width), full(8, width), full(3, 8, width),
        low(quarter, depth), low(quarter, depth),
        pltpu.SemaphoreType.DMA((SENDS,)), pltpu.SemaphoreType.DMA((RECEIVES,)), pltpu.SemaphoreType.DMA((KEEPS,)),
    ]
    moved = pl.pallas_call(
        functools.partial(layer_body, groups, ranks),
        out_shape=outs,
        in_specs=[hbm] * 2 + [vmem] * 2 + [hbm] * 7,
        out_specs=[hbm, hbm, vmem] + [hbm] * 7,
        scratch_shapes=scratch,
        compiler_params=pltpu.CompilerParams(
            collective_id=1, has_side_effects=True, vmem_limit_bytes=VMEM_LIMIT
        ),
    )(*ins)
    steps = 2

    def sliced(array):
        rows, columns = array.shape
        return pl.BlockSpec((rows // steps, columns), lambda i: (i, 0))

    gain_specs = [pl.BlockSpec((8, width), lambda i: (0, 0))]
    row_spec = pl.BlockSpec((width,), lambda i: (0,))
    specs = [sliced(moved[0]), sliced(moved[1]), *(sliced(w) for w in moved[3:])]
    gain_row = shape((width,), F32)
    one, two, result, rows_grad, *grads = pl.pallas_call(
        cast_body,
        grid=(steps,),
        out_shape=[gain_row, gain_row, moved[0], moved[1], *(shape(w.shape, F32) for w in owners)],
        in_specs=gain_specs + specs,
        out_specs=[row_spec, row_spec] + specs,
        compiler_params=pltpu.CompilerParams(vmem_limit_bytes=VMEM_LIMIT),
    )(moved[2], moved[0], moved[1], *moved[3:])
    return (result, rows_grad, one, *grads[:4], two, *grads[4:])


def cast_body(*refs):
    inputs = len(refs) // 2
    gains, sources, (one, two, *targets) = refs[0], refs[1:inputs], refs[inputs:]
    one[...] = gains[0, :]
    two[...] = gains[1, :]
    for source, target in zip(sources, targets):
        target[...] = source[...].astype(target.dtype)


def on_device(tokens, attn_gain, query_weight, *rest):
    groups = query_weight.shape[1] // HD
    ranks = lax.axis_size("seq") // groups
    fits = lax.axis_size("head") == 4 and groups == 4 and ranks == 2 and query_weight.shape[0] % 128 == 0
    plan = functools.partial(rows_plan, groups, ranks) if fits else gathered_weights
    return plan(tokens, attn_gain, query_weight, *rest)


def solution(mesh):
    in_specs = (
        P("seq", None),
        P("seq"),
        P("seq", "head"),
        P("seq", "head"),
        P("seq", "head"),
        P("head", "seq"),
        P("seq"),
        P("seq", "head"),
        P("seq", "head"),
        P("head", "seq"),
        P("seq", None),
    )
    out_specs = (
        P("seq", None),
        P("seq", None),
        P("seq"),
        P("seq", "head"),
        P("seq", "head"),
        P("seq", "head"),
        P("head", "seq"),
        P("seq"),
        P("seq", "head"),
        P("seq", "head"),
        P("head", "seq"),
    )
    return jax.shard_map(
        on_device, mesh=mesh, in_specs=in_specs, out_specs=out_specs, check_vma=False
    )
```
